32 devices in a mesh: dp: 4 (over z), expert: 8 (over y, x, core).
Axes of the slice: x: 2, y: 2, z: 4, core: 2. Of those that a mesh axis runs over, the one named last changes fastest.
Arguments:
- tokens: bfloat16 [4096, 1536], P(('dp', 'expert')), may hold values from -6 to 6
- cotangent: bfloat16 [4096, 1536], P(('dp', 'expert')), may hold values from -6 to 6
- routes: int32 [1, 4096, 4], P(None, ('dp', 'expert')), may hold values from 0 to 7, all different within a row; in each aligned block of 128 rows (0 to 127, 128 to 255, ..., all dimensions but the last counted through in order) at most 96 rows name the same one
- gain_attn: bfloat16 [1, 1536], P(None, ('dp', 'expert')), may hold values from 0.099609375 to 1.8984375
- w_query: bfloat16 [1, 1536, 1536], P(None, ('dp', 'expert')), may hold values from -0.21875 to 0.21875
- key_weight: bfloat16 [1, 1536, 256], P(None, ('dp', 'expert')), may hold values from -0.21875 to 0.21875
- value_weight: bfloat16 [1, 1536, 256], P(None, ('dp', 'expert')), may hold values from -0.15625 to 0.15625
- w_output: bfloat16 [1, 1536, 1536], P(None, ('dp', 'expert')), may hold values from -2 to 2
- gain_moe: bfloat16 [1, 1536], P(None, ('dp', 'expert')), may hold values from 0.099609375 to 1.8984375
- w_router: bfloat16 [1, 1536, 8], P(None, ('dp', 'expert')), may hold values from -0.078125 to 0.078125
- w_in: bfloat16 [1, 1536, 8, 1536], P(None, 'dp', 'expert'), may hold values from -0.15625 to 0.15625
- w_out: bfloat16 [1, 768, 8, 1536], P(None, 'dp', 'expert'), may hold values from -0.625 to 0.625
Outputs:
- block_out: bfloat16 [4096, 1536], P(('dp', 'expert'))
- tokens_grad: float32 [4096, 1536], P(('dp', 'expert'))
- gain_attn_grad: float32 [1, 1536], P(None, ('dp', 'expert'))
- w_query_grad: float32 [1, 1536, 1536], P(None, ('dp', 'expert'))
- w_key_grad: float32 [1, 1536, 256], P(None, ('dp', 'expert'))
- w_value_grad: float32 [1, 1536, 256], P(None, ('dp', 'expert'))
- w_output_grad: float32 [1, 1536, 1536], P(None, ('dp', 'expert'))
- gain_moe_grad: float32 [1, 1536], P(None, ('dp', 'expert'))
- w_router_grad: float32 [1, 1536, 8], P(None, ('dp', 'expert'))
- w_in_grad: float32 [1, 1536, 8, 1536], P(None, 'dp', 'expert')
- w_out_grad: float32 [1, 768, 8, 1536], P(None, 'dp', 'expert')
The draws below stay inside these ranges and needn't reach their ends.
Inputs may be any that keep to these rules, and one draw needn't show every extreme that they name: `routes`: in each layer the 128 rows of one device name every expert at most 96 times, a bound that some block reaches; a row names 4 different experts.
All inputs are finite; a program needn't handle non-finite values.
Results may differ from the reference program's by a relative error of at most 0.018.
The reference program's roundings to bfloat16 on the way count: a program that leaves them out, or rounds other values in their place, can miss the bound.
Values may be sent and summed in bfloat16 or wider, within the bound.
A program may use at most 192 MiB of HBM per device.

```python
import math
import jax
import jax.numpy as jnp
import numpy as np
from jax import lax

MODEL_DIM = 1536
QUERY_HEADS = 12
KEY_VALUE_HEADS = 2
HEAD_DIM = 128
FF = 768
TOP = 4
LAYER_TOTAL = 1
TOK_DEV = 128
EXPERTS = 8
LEN = 1024
TOKENS = 4096
CAP = 96


def shard_levels(stream_key, extent, pieces, smallest, high):
    level = 1.0
    for position, shards_of in pieces:
        steps = jax.random.uniform(jax.random.fold_in(jax.random.fold_in(stream_key, 6), position), (shards_of,), jnp.float32, smallest / len(pieces), high / len(pieces))
        level = level * jnp.repeat(jnp.exp(steps), extent[position] // shards_of).reshape((-1,) + (1,) * (len(extent) - 1 - position))
    return level


def assign_block(own_key, own, number, rows, number_of, top, reach, slope):
    ranking = jax.random.permutation(own_key, number_of)
    packed, usual = load_shares(number_of, rows * top, reach, slope, True), load_shares(number_of, rows * top, reach, slope, False)
    places = jnp.arange(number_of)

    def named(lengths, turn):
        used = int((lengths > 0).sum())
        fixed = max(1, used // 4)
        moved = fixed + (places - fixed + turn * (used - fixed)) % max(1, number_of - fixed)
        return jnp.zeros((number_of,), jnp.int32).at[ranking[jnp.where(places < fixed, places, moved)]].set(jnp.asarray(lengths, jnp.int32))

    lengths = jnp.where(number % 4 == 0, named(packed, number // 4), named(usual, number - number // 4 - 1))
    mixed = jax.random.permutation(jax.random.fold_in(own, 3), number_of)
    donor, receiver = mixed[0:number_of // 2 * 2:2], mixed[1:number_of // 2 * 2:2]
    room = jnp.minimum(lengths[donor] - 1, reach - lengths[receiver]) // 2
    room = jnp.where((donor == ranking[0]) | (receiver == ranking[0]) | (lengths[receiver] == 0), 0, jnp.maximum(room, 0))
    moved = jax.random.randint(jax.random.fold_in(own, 4), (number_of // 2,), 0, 1 << 20) % (room + 1)
    lengths = lengths.at[donor].add(-moved).at[receiver].add(moved)
    members = jnp.searchsorted(jnp.cumsum(lengths), jnp.arange(rows * top), side="right").astype(jnp.int32)
    grid = members.reshape(top, rows).T
    grid = grid[jax.random.permutation(jax.random.fold_in(own, 1), rows)]
    turn = jax.random.randint(jax.random.fold_in(own, 2), (rows, 1), 0, top)
    return jnp.take_along_axis(grid, (jnp.arange(top)[None, :] + turn) % top, axis=1)


def load_shares(amount, total, limit, lean, full):
    loads = [(1 << 20) // math.isqrt(rank ** lean) + 1 for rank in range(1, amount + 1)]
    largest = limit if full else min(limit, max(-(-total // amount), total * loads[0] // sum(loads)))
    least = 1 if total - largest >= amount - 1 else 0
    counts, spare = [largest] + [least] * (amount - 1), total - largest - least * (amount - 1)
    while spare > 0:
        free = [i for i in range(1, amount) if counts[i] < largest] or [i for i in range(1, amount) if counts[i] < limit]
        mass, left = sum([loads[i] for i in free]), spare
        for i in free:
            extra = min(limit - counts[i], max(1, left * loads[i] // mass), spare)
            counts[i] = counts[i] + extra
            spare = spare - extra
    return np.array(counts)


def centred(key, dims, deviation, reach, pieces=(), kind=jnp.bfloat16):
    gain = shard_levels(key, dims, pieces, -0.22, 0.18) if pieces else 1.0
    values = jax.random.normal(key, dims, jnp.float32) * deviation * gain
    return jnp.minimum(jnp.maximum(values, -reach), reach).astype(kind)


def setup_inputs(seed: int = 0) -> dict:
    keys = jax.random.split(jax.random.key(seed), 13)
    tokens = centred(keys[0], (TOKENS, MODEL_DIM), 1.0, 6.0, ((0, 32),))
    cotangent = centred(keys[1], (TOKENS, MODEL_DIM), 1.0, 6.0, ((0, 32),))
    routes_keys = jax.random.split(jax.random.fold_in(keys[2], 1), LAYER_TOTAL * TOKENS // TOK_DEV)
    routes_turns = jax.random.permutation(jax.random.fold_in(keys[2], 3), LAYER_TOTAL * TOKENS // TOK_DEV)
    routes = jax.vmap(lambda own, number: assign_block(jax.random.fold_in(keys[2], 2), own, number, TOK_DEV, EXPERTS, TOP, CAP, 2))(routes_keys, routes_turns).reshape((LAYER_TOTAL, TOKENS, TOP))
    gain_attn = jnp.clip(1.0 + 0.18 * jax.random.normal(keys[3], (LAYER_TOTAL, MODEL_DIM), jnp.float32), 0.099609375, 1.8984375).astype(jnp.bfloat16)
    w_query = centred(keys[4], (LAYER_TOTAL, MODEL_DIM, QUERY_HEADS * HEAD_DIM), (MODEL_DIM // 2) ** -0.5, 0.21875, ((1, 32),))
    key_weight = centred(keys[5], (LAYER_TOTAL, MODEL_DIM, KEY_VALUE_HEADS * HEAD_DIM), (MODEL_DIM // 2) ** -0.5, 0.21875, ((1, 32),))
    value_weight = centred(keys[6], (LAYER_TOTAL, MODEL_DIM, KEY_VALUE_HEADS * HEAD_DIM), MODEL_DIM ** -0.5, 0.15625, ((1, 32),))
    w_output = centred(keys[7], (LAYER_TOTAL, QUERY_HEADS * HEAD_DIM, MODEL_DIM), 8 ** -0.5, 2.0, ((1, 32),))
    gain_moe = jnp.clip(1.0 + 0.18 * jax.random.normal(keys[8], (LAYER_TOTAL, MODEL_DIM), jnp.float32), 0.099609375, 1.8984375).astype(jnp.bfloat16)
    w_router = centred(keys[9], (LAYER_TOTAL, MODEL_DIM, EXPERTS), (4 * MODEL_DIM) ** -0.5, 0.078125, ((1, 32),))
    w_in = centred(keys[10], (LAYER_TOTAL, MODEL_DIM, EXPERTS, 2 * FF), MODEL_DIM ** -0.5, 0.15625, ((1, 4), (2, 8)))
    w_out = centred(keys[11], (LAYER_TOTAL, FF, EXPERTS, MODEL_DIM), (FF // 8) ** -0.5, 0.625, ((1, 4), (2, 8)))
    return {"tokens": tokens, "cotangent": cotangent, "routes": routes, "gain_attn": gain_attn, "w_query": w_query, "key_weight": key_weight, "value_weight": value_weight, "w_output": w_output, "gain_moe": gain_moe, "w_router": w_router, "w_in": w_in, "w_out": w_out}


norm_eps = 1e-06
rope_base = 1000000.0
top_precision = lax.Precision.HIGHEST

@jax.custom_vjp
def low(v):
    return lax.optimization_barrier(v.astype(jnp.bfloat16)).astype(jnp.float32)

@jax.custom_vjp
def low_back(v):
    return v

def low_keep(v):
    return (low(v), None)

def low_pass(kept, grad):
    return (grad,)

def back_keep(v):
    return (v, None)

def back_low(kept, grad):
    return (low(grad),)
low.defvjp(low_keep, low_pass)
low_back.defvjp(back_keep, back_low)

def norm_factor(values):
    return lax.rsqrt(lax.optimization_barrier(jnp.mean(values * values, axis=-1, keepdims=True)) + norm_eps)

def rope_tables(positions, head_size):
    half_size = head_size // 2
    inverse = rope_base ** (-(jnp.arange(half_size, dtype=jnp.float32) * 2.0 / head_size))
    angles = positions.astype(jnp.float32)[:, None] * inverse[None, :]
    return (jnp.cos(angles), jnp.sin(angles))

def rotate(values, cos_table, sin_table, orient):
    half_size = values.shape[-1] // 2
    first_half = values[..., :half_size]
    second = values[..., half_size:]
    cos_part = cos_table[:, None, :]
    sin_part = orient * sin_table[:, None, :]
    return jnp.concatenate([first_half * cos_part - second * sin_part, second * cos_part + first_half * sin_part], axis=-1)

def attention(query_rows, key_matrix_rows, value_matrix_rows):
    sequence_total = query_rows.shape[0]
    heads_per_group = QUERY_HEADS // KEY_VALUE_HEADS
    rows_per_block = min(512, sequence_total)
    score_scale = HEAD_DIM ** (-0.5)
    block_list = query_rows.reshape(sequence_total // rows_per_block, rows_per_block, KEY_VALUE_HEADS, heads_per_group, HEAD_DIM)
    starts = jnp.arange(sequence_total // rows_per_block, dtype=jnp.int32) * rows_per_block
    key_pos = jnp.arange(sequence_total, dtype=jnp.int32)

    def one_block(block_item):
        query_block, first_row = block_item
        scores = jnp.einsum('qcgd,kcd->cgqk', query_block, key_matrix_rows, precision=top_precision) * score_scale
        scores = low_back(scores)
        query_pos = first_row + jnp.arange(rows_per_block, dtype=jnp.int32)
        allowed = key_pos[None, :] <= query_pos[:, None]
        scores = jnp.where(allowed[None, None], scores, -1e+30)
        attn_probs = low(jax.nn.softmax(scores, axis=-1))
        return jnp.einsum('cgqk,kcd->qcgd', attn_probs, value_matrix_rows, precision=top_precision)
    out_blocks = lax.map(jax.checkpoint(one_block), (block_list, starts))
    return out_blocks.reshape(sequence_total, QUERY_HEADS * HEAD_DIM)

def experts_layer(normed_two, route, router_w, in_w, out_w):
    sequence_total = normed_two.shape[0]
    block_count = sequence_total // TOK_DEV
    slot_total = TOK_DEV * TOP
    logits = jnp.dot(normed_two, router_w, precision=top_precision)
    chosen = jnp.take_along_axis(logits, route, axis=1)
    gate_probs = jax.nn.softmax(chosen, axis=-1)
    flat_route = route.reshape(block_count, slot_total)
    onehot = (flat_route[:, :, None] == jnp.arange(EXPERTS, dtype=jnp.int32)[None, None, :]).astype(jnp.int32)
    before = jnp.cumsum(onehot, axis=1) - onehot
    target = flat_route * CAP + lax.optimization_barrier(jnp.sum(before * onehot, axis=2))

    def fill_sources(target_row):
        return jnp.full((EXPERTS * CAP,), slot_total, jnp.int32).at[target_row].set(jnp.arange(slot_total, dtype=jnp.int32))
    source = jax.vmap(fill_sources)(target)
    filled = (source < slot_total).astype(jnp.float32)
    source = jnp.minimum(source, slot_total - 1)
    per_slot = low_back(jnp.broadcast_to(normed_two[:, None, :], (sequence_total, TOP, MODEL_DIM)))
    per_slot = per_slot.reshape(block_count, slot_total, MODEL_DIM)
    buffers = jnp.take_along_axis(per_slot, source[:, :, None], axis=1) * filled[:, :, None]
    buffers = buffers.reshape(block_count, EXPERTS, CAP, MODEL_DIM)
    gate_up = low_back(jnp.einsum('becd,def->becf', buffers, in_w, precision=top_precision))
    hidden_act = low(jax.nn.silu(gate_up[..., :FF]) * gate_up[..., FF:])
    expert_out = jnp.einsum('becf,fed->becd', hidden_act, out_w, precision=top_precision)
    expert_out = low(low_back(expert_out)).reshape(block_count, EXPERTS * CAP, MODEL_DIM)
    slot_out = jnp.take_along_axis(expert_out, target[:, :, None], axis=1).reshape(sequence_total, TOP, MODEL_DIM)
    return lax.optimization_barrier(jnp.sum(gate_probs[:, :, None] * slot_out, axis=1))

def one_layer(residual, cos_table, sin_table, route, weights, layer_number):
    gain_a, query_w, key_matrix, value_matrix, output_w, gain_m, router_w, in_w, out_w = [arr[layer_number] for arr in weights]
    sequence_total = residual.shape[0]
    norm_result = low(residual * norm_factor(residual) * gain_a)
    query_rows = low_back(jnp.dot(norm_result, query_w, precision=top_precision)).reshape(sequence_total, QUERY_HEADS, HEAD_DIM)
    query_rows = low(rotate(query_rows, cos_table, sin_table, 1.0))
    key_matrix_rows = low_back(jnp.dot(norm_result, key_matrix, precision=top_precision)).reshape(sequence_total, KEY_VALUE_HEADS, HEAD_DIM)
    key_matrix_rows = low(rotate(key_matrix_rows, cos_table, sin_table, 1.0))
    value_matrix_rows = low(low_back(jnp.dot(norm_result, value_matrix, precision=top_precision))).reshape(sequence_total, KEY_VALUE_HEADS, HEAD_DIM)
    attn = low(low_back(attention(query_rows, key_matrix_rows, value_matrix_rows)))
    after_attn = residual + low_back(jnp.dot(attn, output_w, precision=top_precision))
    normed_two = low(after_attn * norm_factor(after_attn) * gain_m)
    return after_attn + experts_layer(normed_two, route, router_w, in_w, out_w)

def reference(tokens, cotangent, routes, gain_attn, w_query, key_weight, value_weight, w_output, gain_moe, w_router, w_in, w_out):
    weights = tuple((arr.astype(jnp.float32) for arr in (gain_attn, w_query, key_weight, value_weight, w_output, gain_moe, w_router, w_in, w_out)))
    seq_total = TOKENS // LEN
    x_all = tokens.astype(jnp.float32).reshape(seq_total, LEN, MODEL_DIM)
    route_all = jnp.transpose(routes.reshape(LAYER_TOTAL, seq_total, LEN, TOP), (1, 0, 2, 3))
    cos_table, sin_table = rope_tables(jnp.arange(LEN, dtype=jnp.int32), HEAD_DIM)

    def forward(x_seqs, layer_weights):

        def one_sequence(carry, seq_item):
            seq_x, seq_routes = seq_item
            for layer_number in range(LAYER_TOTAL):
                seq_x = one_layer(seq_x, cos_table, sin_table, seq_routes[layer_number], layer_weights, layer_number)
            return (carry, seq_x)
        _, outputs = lax.scan(jax.checkpoint(one_sequence), jnp.zeros((), jnp.float32), (x_seqs, route_all))
        return outputs
    outputs, pullback = jax.vjp(forward, x_all, weights)
    grad_x, grad_w = pullback(cotangent.astype(jnp.float32).reshape(seq_total, LEN, MODEL_DIM))
    return (outputs.reshape(TOKENS, MODEL_DIM).astype(jnp.bfloat16), grad_x.reshape(TOKENS, MODEL_DIM), grad_w[0], grad_w[1], grad_w[2], grad_w[3], grad_w[4], grad_w[5], grad_w[6], grad_w[7], grad_w[8])
```

```python
import functools

import jax
import jax.numpy as jnp
from jax import lax
from jax.experimental import pallas as pl
from jax.experimental.pallas import tpu as pltpu
from jax.sharding import PartitionSpec as P

MESH = pl.DeviceIdType.MESH

QUERY_HEADS = 12
KEY_VALUE_HEADS = 2
HEAD_DIM = 128
FF = 768
TOP = 4


norm_eps = 1e-06
rope_base = 1000000.0
masked_score = -1e30
top_precision = lax.Precision.HIGHEST


def norm_factor(values):
    return lax.rsqrt(jnp.mean(values * values, axis=-1, keepdims=True) + norm_eps)


def norm_back(values, gain, grad_out):
    factor = norm_factor(values)
    scaled = grad_out * gain
    gain_grad = jnp.sum(grad_out * values * factor, axis=0)
    inner_mean = jnp.mean(scaled * values, axis=-1, keepdims=True)
    return (factor * scaled - values * factor * factor * factor * inner_mean, gain_grad)


def rope_tables(positions, head_size):
    half_size = head_size // 2
    inverse = rope_base ** (-(jnp.arange(half_size, dtype=jnp.float32) * 2.0 / head_size))
    angles = positions.astype(jnp.float32)[:, None] * inverse[None, :]
    return (jnp.cos(angles), jnp.sin(angles))


def rotate(values, cos_table, sin_table, orient):
    half_size = values.shape[-1] // 2
    first_half = values[..., :half_size]
    second = values[..., half_size:]
    cos_part = cos_table[:, None, :]
    sin_part = orient * sin_table[:, None, :]
    return jnp.concatenate(
        [first_half * cos_part - second * sin_part, second * cos_part + first_half * sin_part],
        axis=-1,
    )


def plan_slots(route, expert_count, capacity):
    flat_route = route.reshape(-1)
    slot_total = flat_route.shape[0]
    onehot = (flat_route[:, None] == jnp.arange(expert_count, dtype=jnp.int32)[None, :]).astype(
        jnp.int32
    )
    before = jnp.cumsum(onehot, axis=0) - onehot
    target = flat_route * capacity + jnp.sum(before * onehot, axis=1)
    source = (
        jnp.full((expert_count * capacity,), slot_total, jnp.int32)
        .at[target]
        .set(jnp.arange(slot_total, dtype=jnp.int32))
    )
    filled = source < slot_total
    return (target, jnp.minimum(source, slot_total - 1), filled)


def gather_kernel(shard_ref, full_ref, z_send, z_recv, p_send, p_recv, s_send, s_recv, own_sem):
    plane = lax.axis_index("dp")
    member = lax.axis_index("expert")
    sibling = lax.bitwise_xor(member, 1)

    barrier = pltpu.get_barrier_semaphore()
    for step in (1, 2, 3):
        pl.semaphore_signal(
            barrier, inc=1, device_id=(lax.bitwise_xor(plane, step), member), device_id_type=MESH
        )
    for step in (1, 2, 4, 6):
        pl.semaphore_signal(
            barrier, inc=1, device_id=(plane, lax.bitwise_xor(member, step)), device_id_type=MESH
        )
    own = pltpu.make_async_copy(shard_ref, full_ref.at[plane, member], own_sem.at[0])
    own.start()
    pl.semaphore_wait(barrier, 7)

    def z_copy(step):
        return pltpu.make_async_remote_copy(
            src_ref=shard_ref,
            dst_ref=full_ref.at[plane, member],
            send_sem=z_send.at[step],
            recv_sem=z_recv.at[step],
            device_id=(lax.bitwise_xor(plane, step), member),
            device_id_type=MESH,
        )

    def plane_copy(step, chip):
        block = full_ref.at[lax.bitwise_xor(plane, step), member]
        return pltpu.make_async_remote_copy(
            src_ref=block,
            dst_ref=block,
            send_sem=p_send.at[step, chip],
            recv_sem=p_recv.at[step, chip],
            device_id=(plane, lax.bitwise_xor(member, 2 * chip)),
            device_id_type=MESH,
        )

    def sibling_copy(step, chip):
        block = full_ref.at[lax.bitwise_xor(plane, step), lax.bitwise_xor(member, 2 * chip)]
        return pltpu.make_async_remote_copy(
            src_ref=block,
            dst_ref=block,
            send_sem=s_send.at[step, chip],
            recv_sem=s_recv.at[step, chip],
            device_id=(plane, sibling),
            device_id_type=MESH,
        )

    for step in (1, 2, 3):
        z_copy(step).start()
    own.wait()
    for step in range(4):
        if step:
            z_copy(step).wait_recv()
        for chip in (1, 2, 3):
            plane_copy(step, chip).start()
        sibling_copy(step, 0).start()
    for step in range(4):
        for chip in (1, 2, 3):
            plane_copy(step, chip).wait_recv()
            sibling_copy(step, chip).start()
    for step in range(4):
        for chip in range(4):
            sibling_copy(step, chip).wait()
            if chip:
                plane_copy(step, chip).wait_send()
        if step:
            z_copy(step).wait_send()


def gather_dense(shard):
    rows, columns = shard.shape
    planes, members = lax.axis_size("dp"), lax.axis_size("expert")
    full = pl.pallas_call(
        gather_kernel,
        out_shape=jax.ShapeDtypeStruct((planes, members, rows, columns), shard.dtype),
        in_specs=[pl.BlockSpec(memory_space=pl.ANY)],
        out_specs=pl.BlockSpec(memory_space=pl.ANY),
        scratch_shapes=[
            pltpu.SemaphoreType.DMA((4,)),
            pltpu.SemaphoreType.DMA((4,)),
            pltpu.SemaphoreType.DMA((4, 4)),
            pltpu.SemaphoreType.DMA((4, 4)),
            pltpu.SemaphoreType.DMA((4, 4)),
            pltpu.SemaphoreType.DMA((4, 4)),
            pltpu.SemaphoreType.DMA((1,)),
        ],
        compiler_params=pltpu.CompilerParams(collective_id=0, has_side_effects=True),
    )(shard)
    return full.reshape(planes * members * rows, columns)


def body(
    tokens,
    cotangent,
    routes,
    gain_attn,
    w_query,
    key_weight,
    value_weight,
    w_output,
    gain_moe,
    w_router,
    w_in,
    w_out,
):
    total_rows, model_width = tokens.shape
    layer_count = w_query.shape[0]
    group_count = lax.axis_size("expert")
    seq_len = total_rows * group_count
    experts_local = w_in.shape[2]
    expert_count = experts_local * group_count
    capacity = min(total_rows, total_rows * TOP * 3 // (2 * expert_count))
    heads_per_group = QUERY_HEADS // KEY_VALUE_HEADS
    score_scale = HEAD_DIM ** (-0.5)
    positions = lax.axis_index("expert") * total_rows + jnp.arange(total_rows, dtype=jnp.int32)
    cos_table, sin_table = rope_tables(positions, HEAD_DIM)
    allowed = jnp.arange(seq_len, dtype=jnp.int32)[None, :] <= positions[:, None]
    zero_bf = jnp.zeros((), jnp.bfloat16)

    def score_block(query_rows, all_keys, group_of_heads):
        grouped_q = query_rows[
            :, group_of_heads * heads_per_group : (group_of_heads + 1) * heads_per_group, :
        ]
        scores = (
            jnp.einsum(
                "rgd,kd->grk",
                grouped_q,
                all_keys[:, group_of_heads, :],
                preferred_element_type=jnp.float32,
            )
            * score_scale
        )
        return (jnp.where(allowed[None], scores, masked_score), grouped_q)

    residual = tokens.astype(jnp.float32)
    layer_number = 0
    shards = [
        gain_attn[layer_number][:, None],
        w_query[layer_number],
        key_weight[layer_number],
        value_weight[layer_number],
        w_output[layer_number],
        gain_moe[layer_number][:, None],
        w_router[layer_number],
    ]
    widths = [part.shape[1] for part in shards]
    if lax.axis_size("dp") == 4 and group_count == 8 and w_query.shape[1] % 16 == 0:
        order = (1, 4, 2, 3, 0, 5, 6)
        total_width = sum(widths)
        padding = jnp.zeros((w_query.shape[1], -total_width % 128), jnp.bfloat16)
        whole = gather_dense(jnp.concatenate([shards[i] for i in order] + [padding], axis=1))
        dense_w = [None] * 7
        start = 0
        for i in order:
            dense_w[i] = whole[:, start : start + widths[i]]
            start += widths[i]
    else:
        dense_w = [lax.all_gather(part, ("dp", "expert"), axis=0, tiled=True) for part in shards]
    dense_w[0] = dense_w[0][:, 0]
    dense_w[5] = dense_w[5][:, 0]
    dense_w = tuple(dense_w)
    expert_w = (
        lax.all_gather(w_in[layer_number], "dp", axis=0, tiled=True),
        lax.all_gather(w_out[layer_number], "dp", axis=0, tiled=True),
    )
    route = routes[layer_number]
    gain_a = dense_w[0].astype(jnp.float32)
    norm_result = (residual * norm_factor(residual) * gain_a).astype(jnp.bfloat16)
    query_rows = jnp.dot(norm_result, dense_w[1], preferred_element_type=jnp.float32).reshape(
        total_rows, QUERY_HEADS, HEAD_DIM
    )
    query_rows = rotate(query_rows, cos_table, sin_table, 1.0).astype(jnp.bfloat16)
    key_matrix_rows = jnp.dot(norm_result, dense_w[2], preferred_element_type=jnp.float32).reshape(
        total_rows, KEY_VALUE_HEADS, HEAD_DIM
    )
    key_matrix_rows = rotate(key_matrix_rows, cos_table, sin_table, 1.0).astype(jnp.bfloat16)
    value_matrix_rows = (
        jnp.dot(norm_result, dense_w[3], preferred_element_type=jnp.float32)
        .astype(jnp.bfloat16)
        .reshape(total_rows, KEY_VALUE_HEADS, HEAD_DIM)
    )
    all_keys = lax.all_gather(key_matrix_rows, "expert", axis=0, tiled=True)
    all_values = lax.all_gather(value_matrix_rows, "expert", axis=0, tiled=True)
    heads_out = []
    log_totals = []
    for group_of_heads in range(KEY_VALUE_HEADS):
        scores, grouped_q = score_block(query_rows, all_keys, group_of_heads)
        row_peak = jnp.max(scores, axis=-1, keepdims=True)
        expo_vals = jnp.exp(scores - row_peak)
        row_sums = jnp.sum(expo_vals, axis=-1, keepdims=True)
        attn_probs = (expo_vals / row_sums).astype(jnp.bfloat16)
        log_totals.append(row_peak + jnp.log(row_sums))
        heads_out.append(
            jnp.einsum(
                "grk,kd->rgd",
                attn_probs,
                all_values[:, group_of_heads, :],
                preferred_element_type=jnp.float32,
            )
        )
    attn = (
        jnp.concatenate(heads_out, axis=1)
        .reshape(total_rows, QUERY_HEADS * HEAD_DIM)
        .astype(jnp.bfloat16)
    )
    after_attn = residual + jnp.dot(attn, dense_w[4], preferred_element_type=jnp.float32)
    gain_m = dense_w[5].astype(jnp.float32)
    normed_two = (after_attn * norm_factor(after_attn) * gain_m).astype(jnp.bfloat16)
    logits = jnp.dot(normed_two, dense_w[6], preferred_element_type=jnp.float32)
    gate_probs = jax.nn.softmax(jnp.take_along_axis(logits, route, axis=1), axis=-1)
    target, source, filled = plan_slots(route, expert_count, capacity)
    send_rows = jnp.where(filled[:, None], normed_two[source // TOP], zero_bf)
    send_rows = send_rows.reshape(group_count, experts_local, capacity, model_width)
    arrived_rows = lax.all_to_all(send_rows, "expert", split_axis=0, concat_axis=0, tiled=True)
    gate_up_vals = jnp.einsum(
        "secd,def->secf", arrived_rows, expert_w[0], preferred_element_type=jnp.float32
    )
    expert_gate_half = gate_up_vals[..., :FF]
    expert_hidden_act = (
        expert_gate_half * jax.nn.sigmoid(expert_gate_half) * gate_up_vals[..., FF:]
    ).astype(jnp.bfloat16)
    expert_out = jnp.einsum(
        "secf,fed->secd", expert_hidden_act, expert_w[1], preferred_element_type=jnp.float32
    ).astype(jnp.bfloat16)
    arrived, gate_up, expert_out = (arrived_rows, gate_up_vals, expert_out)
    returned = lax.all_to_all(expert_out, "expert", split_axis=0, concat_axis=0, tiled=True)
    slot_out = returned.reshape(expert_count * capacity, model_width)[target].reshape(
        total_rows, TOP, model_width
    )
    new_residual = after_attn + jnp.sum(
        gate_probs[:, :, None] * slot_out.astype(jnp.float32), axis=1
    )
    saved_layers = [
        (
            residual,
            norm_result,
            query_rows,
            key_matrix_rows,
            value_matrix_rows,
            all_keys,
            all_values,
            log_totals,
            attn,
            after_attn,
            normed_two,
            route,
            gate_probs,
            target,
            source,
            filled,
            arrived,
            gate_up,
            slot_out,
            dense_w,
            expert_w,
        )
    ]
    block_out = new_residual.astype(jnp.bfloat16)
    grad_resid = cotangent.astype(jnp.float32)
    grad_lists = [[None] * layer_count for _ in range(9)]
    for layer_number in reversed(range(layer_count)):
        (
            resid_in,
            norm_result,
            query_rows,
            key_matrix_rows,
            value_matrix_rows,
            all_keys,
            all_values,
            log_totals,
            attn,
            after_attn,
            normed_two,
            route,
            gate_probs,
            target,
            source,
            filled,
            arrived,
            gate_up,
            slot_out,
            dense_w,
            expert_w,
        ) = saved_layers[layer_number]
        all_keys, all_values = (
            lax.all_gather(key_matrix_rows, "expert", axis=0, tiled=True),
            lax.all_gather(value_matrix_rows, "expert", axis=0, tiled=True),
        )
        gate_grad = jnp.sum(slot_out.astype(jnp.float32) * grad_resid[:, None, :], axis=-1)
        slot_grad = (
            (gate_probs[:, :, None] * grad_resid[:, None, :])
            .astype(jnp.bfloat16)
            .reshape(total_rows * TOP, model_width)
        )
        grad_rows = jnp.where(filled[:, None], slot_grad[source], zero_bf)
        grad_rows = grad_rows.reshape(group_count, experts_local, capacity, model_width)
        grad_arrived = lax.all_to_all(grad_rows, "expert", split_axis=0, concat_axis=0, tiled=True)
        gate_half = gate_up[..., :FF]
        up_half = gate_up[..., FF:]
        sigmoid_vals = jax.nn.sigmoid(gate_half)
        silu_vals = gate_half * sigmoid_vals
        hidden_act = (silu_vals * up_half).astype(jnp.bfloat16)
        act_grad = jnp.einsum(
            "secd,fed->secf", grad_arrived, expert_w[1], preferred_element_type=jnp.float32
        )
        gate_part = act_grad * up_half * sigmoid_vals * (1.0 + gate_half * (1.0 - sigmoid_vals))
        gate_up_grad = jnp.concatenate([gate_part, act_grad * silu_vals], axis=-1).astype(
            jnp.bfloat16
        )
        input_grad = jnp.einsum(
            "secf,def->secd", gate_up_grad, expert_w[0], preferred_element_type=jnp.float32
        ).astype(jnp.bfloat16)
        returned_grad = lax.all_to_all(
            input_grad, "expert", split_axis=0, concat_axis=0, tiled=True
        )
        grad_lists[7][layer_number] = lax.psum_scatter(
            jnp.einsum(
                "secd,secf->def", arrived, gate_up_grad, preferred_element_type=jnp.float32
            ).astype(jnp.bfloat16),
            "dp",
            scatter_dimension=0,
            tiled=True,
        ).astype(jnp.float32)
        grad_lists[8][layer_number] = lax.psum_scatter(
            jnp.einsum(
                "secf,secd->fed", hidden_act, grad_arrived, preferred_element_type=jnp.float32
            ).astype(jnp.bfloat16),
            "dp",
            scatter_dimension=0,
            tiled=True,
        ).astype(jnp.float32)
        slot_back = returned_grad.reshape(expert_count * capacity, model_width)[target].reshape(
            total_rows, TOP, model_width
        )
        normed_two_grad = jnp.sum(slot_back.astype(jnp.float32), axis=1)
        gate_inner = jnp.sum(gate_probs * gate_grad, axis=-1, keepdims=True)
        chosen_grad = gate_probs * (gate_grad - gate_inner)
        route_hot = (
            route[:, :, None] == jnp.arange(expert_count, dtype=jnp.int32)[None, None, :]
        ).astype(jnp.float32)
        logit_grad = jnp.sum(route_hot * chosen_grad[:, :, None], axis=1)
        router_f = dense_w[6].astype(jnp.float32)
        normed_two_grad = normed_two_grad + jnp.einsum(
            "re,de->rd", logit_grad, router_f, precision=top_precision
        )
        router_grad = jnp.einsum(
            "rd,re->de", normed_two.astype(jnp.float32), logit_grad, precision=top_precision
        )
        gain_m = dense_w[5].astype(jnp.float32)
        norm_two_back, gain_m_grad = norm_back(after_attn, gain_m, normed_two_grad)
        mid_grad = grad_resid + norm_two_back
        out_grad = mid_grad.astype(jnp.bfloat16)
        output_grad = jnp.einsum("rq,rd->qd", attn, out_grad, preferred_element_type=jnp.float32)
        attn_grad = (
            jnp.einsum("rd,qd->rq", out_grad, dense_w[4], preferred_element_type=jnp.float32)
            .astype(jnp.bfloat16)
            .reshape(total_rows, QUERY_HEADS, HEAD_DIM)
        )
        query_grads = []
        key_grads = []
        value_grads = []
        for group_of_heads in range(KEY_VALUE_HEADS):
            scores, grouped_q = score_block(query_rows, all_keys, group_of_heads)
            grouped_do = attn_grad[
                :, group_of_heads * heads_per_group : (group_of_heads + 1) * heads_per_group, :
            ]
            probs = jnp.exp(scores - log_totals[group_of_heads])
            prob_bf = probs.astype(jnp.bfloat16)
            prob_grad = jnp.einsum(
                "rgd,kd->grk",
                grouped_do,
                all_values[:, group_of_heads, :],
                preferred_element_type=jnp.float32,
            )
            row_dot = jnp.sum(probs * prob_grad, axis=-1, keepdims=True)
            score_grad = (probs * (prob_grad - row_dot)).astype(jnp.bfloat16)
            query_grads.append(
                jnp.einsum(
                    "grk,kd->rgd",
                    score_grad,
                    all_keys[:, group_of_heads, :],
                    preferred_element_type=jnp.float32,
                )
                * score_scale
            )
            key_grads.append(
                jnp.einsum("grk,rgd->kd", score_grad, grouped_q, preferred_element_type=jnp.float32)
                * score_scale
            )
            value_grads.append(
                jnp.einsum("grk,rgd->kd", prob_bf, grouped_do, preferred_element_type=jnp.float32)
            )
        key_sum, value_total_sum = (
            lax.psum_scatter(
                jnp.stack(key_grads, axis=1).astype(jnp.bfloat16),
                "expert",
                scatter_dimension=0,
                tiled=True,
            ).astype(jnp.float32),
            lax.psum_scatter(
                jnp.stack(value_grads, axis=1).astype(jnp.bfloat16),
                "expert",
                scatter_dimension=0,
                tiled=True,
            ).astype(jnp.float32),
        )
        query_grad = (
            rotate(jnp.concatenate(query_grads, axis=1), cos_table, sin_table, -1.0)
            .astype(jnp.bfloat16)
            .reshape(total_rows, QUERY_HEADS * HEAD_DIM)
        )
        key_grad = (
            rotate(key_sum, cos_table, sin_table, -1.0)
            .astype(jnp.bfloat16)
            .reshape(total_rows, KEY_VALUE_HEADS * HEAD_DIM)
        )
        value_rows_gradient = value_total_sum.astype(jnp.bfloat16).reshape(
            total_rows, KEY_VALUE_HEADS * HEAD_DIM
        )
        normed_grad = jnp.einsum(
            "rq,dq->rd", query_grad, dense_w[1], preferred_element_type=jnp.float32
        )
        normed_grad = normed_grad + jnp.einsum(
            "rq,dq->rd", key_grad, dense_w[2], preferred_element_type=jnp.float32
        )
        normed_grad = normed_grad + jnp.einsum(
            "rq,dq->rd", value_rows_gradient, dense_w[3], preferred_element_type=jnp.float32
        )
        query_w_grad = jnp.einsum(
            "rd,rq->dq", norm_result, query_grad, preferred_element_type=jnp.float32
        )
        key_w_grad = jnp.einsum(
            "rd,rq->dq", norm_result, key_grad, preferred_element_type=jnp.float32
        )
        value_w_grad = jnp.einsum(
            "rd,rq->dq", norm_result, value_rows_gradient, preferred_element_type=jnp.float32
        )
        gain_a = dense_w[0].astype(jnp.float32)
        norm_one_back, gain_a_grad = norm_back(resid_in, gain_a, normed_grad)
        grad_resid = mid_grad + norm_one_back
        partial = jnp.concatenate(
            [query_w_grad, output_grad, key_w_grad, value_w_grad], axis=1
        ).astype(jnp.bfloat16)
        small = jnp.concatenate([gain_a_grad[:, None], gain_m_grad[:, None], router_grad], axis=1)
        both = ("dp", "expert")
        summed = lax.psum_scatter(partial, both, scatter_dimension=0, tiled=True)
        summed = summed.astype(jnp.float32)
        small = lax.psum_scatter(small, both, scatter_dimension=0, tiled=True)
        q_end = query_w_grad.shape[1]
        o_end = q_end + output_grad.shape[1]
        k_end = o_end + key_w_grad.shape[1]
        shares = (
            small[:, 0],
            summed[:, :q_end],
            summed[:, o_end:k_end],
            summed[:, k_end:],
            summed[:, q_end:o_end],
            small[:, 1],
            small[:, 2:],
        )
        for member in range(7):
            grad_lists[member][layer_number] = shares[member]
    stacked = [jnp.stack(grad_lists[member], axis=0) for member in range(9)]
    return (
        block_out,
        grad_resid,
        stacked[0],
        stacked[1],
        stacked[2],
        stacked[3],
        stacked[4],
        stacked[5],
        stacked[6],
        stacked[7],
        stacked[8],
    )


def solution(mesh):
    in_specs = (
        P(("dp", "expert"), None),
        P(("dp", "expert"), None),
        P(None, ("dp", "expert"), None),
        P(None, ("dp", "expert")),
        P(None, ("dp", "expert"), None),
        P(None, ("dp", "expert"), None),
        P(None, ("dp", "expert"), None),
        P(None, ("dp", "expert"), None),
        P(None, ("dp", "expert")),
        P(None, ("dp", "expert"), None),
        P(None, "dp", "expert", None),
        P(None, "dp", "expert", None),
    )
    out_specs = (
        P(("dp", "expert"), None),
        P(("dp", "expert"), None),
        P(None, ("dp", "expert")),
        P(None, ("dp", "expert"), None),
        P(None, ("dp", "expert"), None),
        P(None, ("dp", "expert"), None),
        P(None, ("dp", "expert"), None),
        P(None, ("dp", "expert")),
        P(None, ("dp", "expert"), None),
        P(None, "dp", "expert", None),
        P(None, "dp", "expert", None),
    )
    return jax.shard_map(body, mesh=mesh, in_specs=in_specs, out_specs=out_specs, check_vma=False)
```

```python
import jax
import jax.numpy as jnp
from jax import lax
from jax.experimental import pallas as pl
from jax.experimental.pallas import tpu as pltpu
from jax.sharding import PartitionSpec as P

MESH = pl.DeviceIdType.MESH

QUERY_HEADS = 12
KEY_VALUE_HEADS = 2
HEAD_DIM = 128
FF = 768
TOP = 4


norm_eps = 1e-06
rope_base = 1000000.0
masked_score = -1e30
top_precision = lax.Precision.HIGHEST


def norm_factor(values):
    return lax.rsqrt(jnp.mean(values * values, axis=-1, keepdims=True) + norm_eps)


def norm_back(values, gain, grad_out):
    factor = norm_factor(values)
    scaled = grad_out * gain
    gain_grad = jnp.sum(grad_out * values * factor, axis=0)
    inner_mean = jnp.mean(scaled * values, axis=-1, keepdims=True)
    return (factor * scaled - values * factor * factor * factor * inner_mean, gain_grad)


def rope_tables(positions, head_size):
    half_size = head_size // 2
    inverse = rope_base ** (-(jnp.arange(half_size, dtype=jnp.float32) * 2.0 / head_size))
    angles = positions.astype(jnp.float32)[:, None] * inverse[None, :]
    return (jnp.cos(angles), jnp.sin(angles))


def rotate(values, cos_table, sin_table, orient):
    half_size = values.shape[-1] // 2
    first_half = values[..., :half_size]
    second = values[..., half_size:]
    cos_part = cos_table[:, None, :]
    sin_part = orient * sin_table[:, None, :]
    return jnp.concatenate(
        [first_half * cos_part - second * sin_part, second * cos_part + first_half * sin_part],
        axis=-1,
    )


def plan_slots(route, expert_count, capacity):
    flat_route = route.reshape(-1)
    slot_total = flat_route.shape[0]
    onehot = (flat_route[:, None] == jnp.arange(expert_count, dtype=jnp.int32)[None, :]).astype(
        jnp.int32
    )
    before = jnp.cumsum(onehot, axis=0) - onehot
    target = flat_route * capacity + jnp.sum(before * onehot, axis=1)
    source = (
        jnp.full((expert_count * capacity,), slot_total, jnp.int32)
        .at[target]
        .set(jnp.arange(slot_total, dtype=jnp.int32))
    )
    filled = source < slot_total
    return (target, jnp.minimum(source, slot_total - 1), filled)


def general_body(
    tokens,
    cotangent,
    routes,
    gain_attn,
    w_query,
    key_weight,
    value_weight,
    w_output,
    gain_moe,
    w_router,
    w_in,
    w_out,
):
    total_rows, model_width = tokens.shape
    layer_count = w_query.shape[0]
    group_count = lax.axis_size("expert")
    seq_len = total_rows * group_count
    experts_local = w_in.shape[2]
    expert_count = experts_local * group_count
    capacity = min(total_rows, total_rows * TOP * 3 // (2 * expert_count))
    heads_per_group = QUERY_HEADS // KEY_VALUE_HEADS
    score_scale = HEAD_DIM ** (-0.5)
    positions = lax.axis_index("expert") * total_rows + jnp.arange(total_rows, dtype=jnp.int32)
    cos_table, sin_table = rope_tables(positions, HEAD_DIM)
    allowed = jnp.arange(seq_len, dtype=jnp.int32)[None, :] <= positions[:, None]
    zero_bf = jnp.zeros((), jnp.bfloat16)

    def score_block(query_rows, all_keys, group_of_heads):
        grouped_q = query_rows[
            :, group_of_heads * heads_per_group : (group_of_heads + 1) * heads_per_group, :
        ]
        scores = (
            jnp.einsum(
                "rgd,kd->grk",
                grouped_q,
                all_keys[:, group_of_heads, :],
                preferred_element_type=jnp.float32,
            )
            * score_scale
        )
        return (jnp.where(allowed[None], scores, masked_score), grouped_q)

    residual = tokens.astype(jnp.float32)
    layer_number = 0
    dense_w = (
        lax.all_gather(gain_attn[layer_number], ("dp", "expert"), axis=0, tiled=True),
        lax.all_gather(w_query[layer_number], ("dp", "expert"), axis=0, tiled=True),
        lax.all_gather(key_weight[layer_number], ("dp", "expert"), axis=0, tiled=True),
        lax.all_gather(value_weight[layer_number], ("dp", "expert"), axis=0, tiled=True),
        lax.all_gather(w_output[layer_number], ("dp", "expert"), axis=0, tiled=True),
        lax.all_gather(gain_moe[layer_number], ("dp", "expert"), axis=0, tiled=True),
        lax.all_gather(w_router[layer_number], ("dp", "expert"), axis=0, tiled=True),
    )
    expert_w = (
        lax.all_gather(w_in[layer_number], "dp", axis=0, tiled=True),
        lax.all_gather(w_out[layer_number], "dp", axis=0, tiled=True),
    )
    route = routes[layer_number]
    gain_a = dense_w[0].astype(jnp.float32)
    norm_result = (residual * norm_factor(residual) * gain_a).astype(jnp.bfloat16)
    query_rows = jnp.dot(norm_result, dense_w[1], preferred_element_type=jnp.float32).reshape(
        total_rows, QUERY_HEADS, HEAD_DIM
    )
    query_rows = rotate(query_rows, cos_table, sin_table, 1.0).astype(jnp.bfloat16)
    key_matrix_rows = jnp.dot(norm_result, dense_w[2], preferred_element_type=jnp.float32).reshape(
        total_rows, KEY_VALUE_HEADS, HEAD_DIM
    )
    key_matrix_rows = rotate(key_matrix_rows, cos_table, sin_table, 1.0).astype(jnp.bfloat16)
    value_matrix_rows = (
        jnp.dot(norm_result, dense_w[3], preferred_element_type=jnp.float32)
        .astype(jnp.bfloat16)
        .reshape(total_rows, KEY_VALUE_HEADS, HEAD_DIM)
    )
    all_keys = lax.all_gather(key_matrix_rows, "expert", axis=0, tiled=True)
    all_values = lax.all_gather(value_matrix_rows, "expert", axis=0, tiled=True)
    heads_out = []
    log_totals = []
    for group_of_heads in range(KEY_VALUE_HEADS):
        scores, grouped_q = score_block(query_rows, all_keys, group_of_heads)
        row_peak = jnp.max(scores, axis=-1, keepdims=True)
        expo_vals = jnp.exp(scores - row_peak)
        row_sums = jnp.sum(expo_vals, axis=-1, keepdims=True)
        attn_probs = (expo_vals / row_sums).astype(jnp.bfloat16)
        log_totals.append(row_peak + jnp.log(row_sums))
        heads_out.append(
            jnp.einsum(
                "grk,kd->rgd",
                attn_probs,
                all_values[:, group_of_heads, :],
                preferred_element_type=jnp.float32,
            )
        )
    attn = (
        jnp.concatenate(heads_out, axis=1)
        .reshape(total_rows, QUERY_HEADS * HEAD_DIM)
        .astype(jnp.bfloat16)
    )
    after_attn = residual + jnp.dot(attn, dense_w[4], preferred_element_type=jnp.float32)
    gain_m = dense_w[5].astype(jnp.float32)
    normed_two = (after_attn * norm_factor(after_attn) * gain_m).astype(jnp.bfloat16)
    logits = jnp.dot(normed_two, dense_w[6], preferred_element_type=jnp.float32)
    gate_probs = jax.nn.softmax(jnp.take_along_axis(logits, route, axis=1), axis=-1)
    target, source, filled = plan_slots(route, expert_count, capacity)
    send_rows = jnp.where(filled[:, None], normed_two[source // TOP], zero_bf)
    send_rows = send_rows.reshape(group_count, experts_local, capacity, model_width)
    arrived_rows = lax.all_to_all(send_rows, "expert", split_axis=0, concat_axis=0, tiled=True)
    gate_up_vals = jnp.einsum(
        "secd,def->secf", arrived_rows, expert_w[0], preferred_element_type=jnp.float32
    )
    expert_gate_half = gate_up_vals[..., :FF]
    expert_hidden_act = (
        expert_gate_half * jax.nn.sigmoid(expert_gate_half) * gate_up_vals[..., FF:]
    ).astype(jnp.bfloat16)
    expert_out = jnp.einsum(
        "secf,fed->secd", expert_hidden_act, expert_w[1], preferred_element_type=jnp.float32
    ).astype(jnp.bfloat16)
    arrived, gate_up, expert_out = (arrived_rows, gate_up_vals, expert_out)
    returned = lax.all_to_all(expert_out, "expert", split_axis=0, concat_axis=0, tiled=True)
    slot_out = returned.reshape(expert_count * capacity, model_width)[target].reshape(
        total_rows, TOP, model_width
    )
    new_residual = after_attn + jnp.sum(
        gate_probs[:, :, None] * slot_out.astype(jnp.float32), axis=1
    )
    saved_layers = [
        (
            residual,
            norm_result,
            query_rows,
            key_matrix_rows,
            value_matrix_rows,
            all_keys,
            all_values,
            log_totals,
            attn,
            after_attn,
            normed_two,
            route,
            gate_probs,
            target,
            source,
            filled,
            arrived,
            gate_up,
            slot_out,
            dense_w,
            expert_w,
        )
    ]
    block_out = new_residual.astype(jnp.bfloat16)
    grad_resid = cotangent.astype(jnp.float32)
    grad_lists = [[None] * layer_count for _ in range(9)]
    for layer_number in reversed(range(layer_count)):
        (
            resid_in,
            norm_result,
            query_rows,
            key_matrix_rows,
            value_matrix_rows,
            all_keys,
            all_values,
            log_totals,
            attn,
            after_attn,
            normed_two,
            route,
            gate_probs,
            target,
            source,
            filled,
            arrived,
            gate_up,
            slot_out,
            dense_w,
            expert_w,
        ) = saved_layers[layer_number]
        dense_w = (
            lax.all_gather(gain_attn[layer_number], ("dp", "expert"), axis=0, tiled=True),
            lax.all_gather(w_query[layer_number], ("dp", "expert"), axis=0, tiled=True),
            lax.all_gather(key_weight[layer_number], ("dp", "expert"), axis=0, tiled=True),
            lax.all_gather(value_weight[layer_number], ("dp", "expert"), axis=0, tiled=True),
            lax.all_gather(w_output[layer_number], ("dp", "expert"), axis=0, tiled=True),
            lax.all_gather(gain_moe[layer_number], ("dp", "expert"), axis=0, tiled=True),
            lax.all_gather(w_router[layer_number], ("dp", "expert"), axis=0, tiled=True),
        )
        expert_w = (
            lax.all_gather(w_in[layer_number], "dp", axis=0, tiled=True),
            lax.all_gather(w_out[layer_number], "dp", axis=0, tiled=True),
        )
        all_keys, all_values = (
            lax.all_gather(key_matrix_rows, "expert", axis=0, tiled=True),
            lax.all_gather(value_matrix_rows, "expert", axis=0, tiled=True),
        )
        gate_grad = jnp.sum(slot_out.astype(jnp.float32) * grad_resid[:, None, :], axis=-1)
        slot_grad = (
            (gate_probs[:, :, None] * grad_resid[:, None, :])
            .astype(jnp.bfloat16)
            .reshape(total_rows * TOP, model_width)
        )
        grad_rows = jnp.where(filled[:, None], slot_grad[source], zero_bf)
        grad_rows = grad_rows.reshape(group_count, experts_local, capacity, model_width)
        grad_arrived = lax.all_to_all(grad_rows, "expert", split_axis=0, concat_axis=0, tiled=True)
        gate_half = gate_up[..., :FF]
        up_half = gate_up[..., FF:]
        sigmoid_vals = jax.nn.sigmoid(gate_half)
        silu_vals = gate_half * sigmoid_vals
        hidden_act = (silu_vals * up_half).astype(jnp.bfloat16)
        act_grad = jnp.einsum(
            "secd,fed->secf", grad_arrived, expert_w[1], preferred_element_type=jnp.float32
        )
        gate_part = act_grad * up_half * sigmoid_vals * (1.0 + gate_half * (1.0 - sigmoid_vals))
        gate_up_grad = jnp.concatenate([gate_part, act_grad * silu_vals], axis=-1).astype(
            jnp.bfloat16
        )
        input_grad = jnp.einsum(
            "secf,def->secd", gate_up_grad, expert_w[0], preferred_element_type=jnp.float32
        ).astype(jnp.bfloat16)
        returned_grad = lax.all_to_all(
            input_grad, "expert", split_axis=0, concat_axis=0, tiled=True
        )
        grad_lists[7][layer_number] = lax.psum_scatter(
            jnp.einsum(
                "secd,secf->def", arrived, gate_up_grad, preferred_element_type=jnp.float32
            ).astype(jnp.bfloat16),
            "dp",
            scatter_dimension=0,
            tiled=True,
        ).astype(jnp.float32)
        grad_lists[8][layer_number] = lax.psum_scatter(
            jnp.einsum(
                "secf,secd->fed", hidden_act, grad_arrived, preferred_element_type=jnp.float32
            ).astype(jnp.bfloat16),
            "dp",
            scatter_dimension=0,
            tiled=True,
        ).astype(jnp.float32)
        slot_back = returned_grad.reshape(expert_count * capacity, model_width)[target].reshape(
            total_rows, TOP, model_width
        )
        normed_two_grad = jnp.sum(slot_back.astype(jnp.float32), axis=1)
        gate_inner = jnp.sum(gate_probs * gate_grad, axis=-1, keepdims=True)
        chosen_grad = gate_probs * (gate_grad - gate_inner)
        route_hot = (
            route[:, :, None] == jnp.arange(expert_count, dtype=jnp.int32)[None, None, :]
        ).astype(jnp.float32)
        logit_grad = jnp.sum(route_hot * chosen_grad[:, :, None], axis=1)
        router_f = dense_w[6].astype(jnp.float32)
        normed_two_grad = normed_two_grad + jnp.einsum(
            "re,de->rd", logit_grad, router_f, precision=top_precision
        )
        router_grad = jnp.einsum(
            "rd,re->de", normed_two.astype(jnp.float32), logit_grad, precision=top_precision
        )
        gain_m = dense_w[5].astype(jnp.float32)
        norm_two_back, gain_m_grad = norm_back(after_attn, gain_m, normed_two_grad)
        mid_grad = grad_resid + norm_two_back
        out_grad = mid_grad.astype(jnp.bfloat16)
        output_grad = jnp.einsum("rq,rd->qd", attn, out_grad, preferred_element_type=jnp.float32)
        attn_grad = (
            jnp.einsum("rd,qd->rq", out_grad, dense_w[4], preferred_element_type=jnp.float32)
            .astype(jnp.bfloat16)
            .reshape(total_rows, QUERY_HEADS, HEAD_DIM)
        )
        query_grads = []
        key_grads = []
        value_grads = []
        for group_of_heads in range(KEY_VALUE_HEADS):
            scores, grouped_q = score_block(query_rows, all_keys, group_of_heads)
            grouped_do = attn_grad[
                :, group_of_heads * heads_per_group : (group_of_heads + 1) * heads_per_group, :
            ]
            probs = jnp.exp(scores - log_totals[group_of_heads])
            prob_bf = probs.astype(jnp.bfloat16)
            prob_grad = jnp.einsum(
                "rgd,kd->grk",
                grouped_do,
                all_values[:, group_of_heads, :],
                preferred_element_type=jnp.float32,
            )
            row_dot = jnp.sum(probs * prob_grad, axis=-1, keepdims=True)
            score_grad = (probs * (prob_grad - row_dot)).astype(jnp.bfloat16)
            query_grads.append(
                jnp.einsum(
                    "grk,kd->rgd",
                    score_grad,
                    all_keys[:, group_of_heads, :],
                    preferred_element_type=jnp.float32,
                )
                * score_scale
            )
            key_grads.append(
                jnp.einsum("grk,rgd->kd", score_grad, grouped_q, preferred_element_type=jnp.float32)
                * score_scale
            )
            value_grads.append(
                jnp.einsum("grk,rgd->kd", prob_bf, grouped_do, preferred_element_type=jnp.float32)
            )
        key_sum, value_total_sum = (
            lax.psum_scatter(
                jnp.stack(key_grads, axis=1).astype(jnp.bfloat16),
                "expert",
                scatter_dimension=0,
                tiled=True,
            ).astype(jnp.float32),
            lax.psum_scatter(
                jnp.stack(value_grads, axis=1).astype(jnp.bfloat16),
                "expert",
                scatter_dimension=0,
                tiled=True,
            ).astype(jnp.float32),
        )
        query_grad = (
            rotate(jnp.concatenate(query_grads, axis=1), cos_table, sin_table, -1.0)
            .astype(jnp.bfloat16)
            .reshape(total_rows, QUERY_HEADS * HEAD_DIM)
        )
        key_grad = (
            rotate(key_sum, cos_table, sin_table, -1.0)
            .astype(jnp.bfloat16)
            .reshape(total_rows, KEY_VALUE_HEADS * HEAD_DIM)
        )
        value_rows_gradient = value_total_sum.astype(jnp.bfloat16).reshape(
            total_rows, KEY_VALUE_HEADS * HEAD_DIM
        )
        normed_grad = jnp.einsum(
            "rq,dq->rd", query_grad, dense_w[1], preferred_element_type=jnp.float32
        )
        normed_grad = normed_grad + jnp.einsum(
            "rq,dq->rd", key_grad, dense_w[2], preferred_element_type=jnp.float32
        )
        normed_grad = normed_grad + jnp.einsum(
            "rq,dq->rd", value_rows_gradient, dense_w[3], preferred_element_type=jnp.float32
        )
        query_w_grad = jnp.einsum(
            "rd,rq->dq", norm_result, query_grad, preferred_element_type=jnp.float32
        )
        key_w_grad = jnp.einsum(
            "rd,rq->dq", norm_result, key_grad, preferred_element_type=jnp.float32
        )
        value_w_grad = jnp.einsum(
            "rd,rq->dq", norm_result, value_rows_gradient, preferred_element_type=jnp.float32
        )
        gain_a = dense_w[0].astype(jnp.float32)
        norm_one_back, gain_a_grad = norm_back(resid_in, gain_a, normed_grad)
        grad_resid = mid_grad + norm_one_back
        shares = (
            lax.psum_scatter(gain_a_grad, ("dp", "expert"), scatter_dimension=0, tiled=True),
            lax.psum_scatter(query_w_grad, ("dp", "expert"), scatter_dimension=0, tiled=True),
            lax.psum_scatter(key_w_grad, ("dp", "expert"), scatter_dimension=0, tiled=True),
            lax.psum_scatter(value_w_grad, ("dp", "expert"), scatter_dimension=0, tiled=True),
            lax.psum_scatter(output_grad, ("dp", "expert"), scatter_dimension=0, tiled=True),
            lax.psum_scatter(gain_m_grad, ("dp", "expert"), scatter_dimension=0, tiled=True),
            lax.psum_scatter(router_grad, ("dp", "expert"), scatter_dimension=0, tiled=True),
        )
        for member in range(7):
            grad_lists[member][layer_number] = shares[member]
    stacked = [jnp.stack(grad_lists[member], axis=0) for member in range(9)]
    return (
        block_out,
        grad_resid,
        stacked[0],
        stacked[1],
        stacked[2],
        stacked[3],
        stacked[4],
        stacked[5],
        stacked[6],
        stacked[7],
        stacked[8],
    )


def product(left, right):
    return lax.dot_general(
        left, right, (((1,), (0,)), ((), ())), preferred_element_type=jnp.float32
    )


def product_rows(left, right):
    return lax.dot_general(
        left, right, (((1,), (1,)), ((), ())), preferred_element_type=jnp.float32
    )


def product_columns(left, right):
    return lax.dot_general(
        left, right, (((0,), (0,)), ((), ())), preferred_element_type=jnp.float32
    )


def split_three(values):
    high = values.astype(jnp.bfloat16)
    rest = values - high.astype(jnp.float32)
    middle = rest.astype(jnp.bfloat16)
    low = (rest - middle.astype(jnp.float32)).astype(jnp.bfloat16)
    return high, middle, low


def masked_gates(rows, router, mask):
    chosen = mask.astype(jnp.float32) > 0.5
    logits = jnp.where(chosen, product(rows, router), masked_score)
    expo_vals = jnp.where(chosen, jnp.exp(logits - jnp.max(logits, axis=1, keepdims=True)), 0.0)
    return expo_vals / jnp.sum(expo_vals, axis=1, keepdims=True)


def layer_kernel(
    x_ref,
    cot_ref,
    mask_ref,
    rope_ref,
    shard_a,
    shard_b,
    shard_c,
    w_in_ref,
    w_out_ref,
    block_out_ref,
    dx_ref,
    grad_in_ref,
    grad_out_ref,
    grad_dense_ref,
    grad_aux_ref,
    spill_b,
    spill_c,
    n2_all,
    cot_all,
    full_a,
    arena,
    gate_buf,
    w_in_half,
    w_out_half,
    hidden_all,
    g_all,
    kv_all,
    k_t,
    v_t,
    q_rows,
    do_rows,
    normed_buf,
    attn_buf,
    after_buf,
    lse_buf,
    turn_send,
    turn_recv,
    og_all,
    qg_all,
    kvg_all,
    dkv_recv,
    aux_send,
    gain_buf,
    z_sems,
    p_sems,
    s_sems,
    kv_sems,
    tok_sems,
    turn_sems,
    win_sems,
    wout_sems,
    sib_sems,
    ret_sems,
    gate_sems,
    gin_sems,
    gout_sems,
    og_sems,
    qg_sems,
    kvg_sems,
    dkv_sems,
    dense_sems,
    aux_sems,
    local_sems,
    credit_sem,
):
    plane = lax.axis_index("dp")
    member = lax.axis_index("expert")
    core = lax.rem(member, 2)
    parity = lax.rem(plane, 2)
    tokens, width = x_ref.shape
    rows = shard_a.shape[0]
    xor = lax.bitwise_xor
    f32, bf16 = jnp.float32, jnp.bfloat16
    half = FF // 2
    score_scale = HEAD_DIM ** (-0.5)
    kv_width = KEY_VALUE_HEADS * HEAD_DIM

    def at_rows(start, count, step=16):
        return pl.ds(pl.multiple_of(start, step), count)

    def remote(source, target, sems, index, device):
        return pltpu.make_async_remote_copy(
            src_ref=source,
            dst_ref=target,
            send_sem=sems.at[(0,) + index],
            recv_sem=sems.at[(1,) + index],
            device_id=device,
            device_id_type=MESH,
        )

    in_plane = lambda step: (plane, xor(member, step))
    sibling = in_plane(1)

    barrier = pltpu.get_barrier_semaphore()
    greeted = [(xor(plane, s), member) for s in (1, 2, 3)]
    greeted += [in_plane(s) for s in range(1, 8)]
    greeted += [(xor(plane, 1), xor(member, s)) for s in (2, 4, 6)]
    for device in greeted:
        pl.semaphore_signal(barrier, inc=1, device_id=device, device_id_type=MESH)

    shards = (shard_a, shard_b, shard_c)

    def dense_block(part, step, chip_step):
        start = (xor(plane, step) * 8 + xor(member, chip_step)) * rows
        if part == 0:
            return full_a.at[at_rows(start, rows)]
        return arena.at[at_rows(start + (part - 1) * width, rows)]

    def z_copy(part, step):
        return remote(
            shards[part],
            dense_block(part, 0, 0),
            z_sems,
            (part, step),
            (xor(plane, step), member),
        )

    def plane_copy(part, step, chip):
        block = dense_block(part, step, 0)
        return remote(block, block, p_sems, (part, step, chip), in_plane(2 * chip))

    def sibling_copy(part, step, chip):
        block = dense_block(part, step, 2 * chip)
        return remote(block, block, s_sems, (part, step, chip), sibling)

    own_rows = (plane * 8 + member) * rows
    full_a[at_rows(own_rows, rows)] = shard_a[...]
    arena[at_rows(own_rows, rows)] = shard_b[...]
    arena[at_rows(own_rows + width, rows)] = shard_c[...]

    def token_rows(plane_step, member_step):
        start = (xor(parity, plane_step) * 8 + xor(member, member_step)) * tokens
        return at_rows(start, tokens, 128)

    cot_all[token_rows(0, 0), pl.ds(0, width)] = cot_ref[...]
    cot_all[token_rows(0, 0), pl.ds(width, 128)] = mask_ref[...]
    pl.semaphore_wait(barrier, len(greeted))

    for part in range(3):
        for step in (3, 2, 1):
            z_copy(part, step).start()
    for part in range(3):
        for chip in (1, 2, 3):
            plane_copy(part, 0, chip).start()
        sibling_copy(part, 0, 0).start()

    def pass_on_plane(part):
        for step in (1, 2, 3):
            z_copy(part, step).wait_recv()
            for chip in (1, 2, 3):
                plane_copy(part, step, chip).start()
            sibling_copy(part, step, 0).start()

    def pass_on_sibling(part):
        for step in range(4):
            for chip in (1, 2, 3):
                plane_copy(part, step, chip).wait_recv()
                sibling_copy(part, step, chip).start()

    def arrived_dense(part):
        for step in range(4):
            for chip in range(4):
                sibling_copy(part, step, chip).wait_recv()

    def sent_dense(part):
        for step in range(4):
            if step:
                z_copy(part, step).wait_send()
            for chip in range(4):
                if chip:
                    plane_copy(part, step, chip).wait_send()
                sibling_copy(part, step, chip).wait_send()

    token_arrays = (cot_all, n2_all)

    def token_z(kind):
        block = token_arrays[kind].at[token_rows(0, 0)]
        return remote(block, block, tok_sems, (kind, 0), (xor(plane, 1), member))

    def token_plane(kind, plane_step, chip):
        block = token_arrays[kind].at[token_rows(plane_step, 0)]
        index = (kind, 1 + plane_step * 3 + chip - 1)
        return remote(block, block, tok_sems, index, in_plane(2 * chip))

    def token_sibling(kind, plane_step, chip):
        block = token_arrays[kind].at[token_rows(plane_step, 2 * chip)]
        return remote(block, block, tok_sems, (kind, 7 + plane_step * 4 + chip), sibling)

    def token_start(kind):
        token_z(kind).start()
        for chip in (1, 2, 3):
            token_plane(kind, 0, chip).start()
        token_sibling(kind, 0, 0).start()

    def token_pass_plane(kind):
        token_z(kind).wait_recv()
        for chip in (1, 2, 3):
            token_plane(kind, 1, chip).start()
        token_sibling(kind, 1, 0).start()

    def token_pass_sibling(kind):
        for plane_step in (0, 1):
            for chip in (1, 2, 3):
                token_plane(kind, plane_step, chip).wait_recv()
                token_sibling(kind, plane_step, chip).start()

    def token_finish(kind):
        token_z(kind).wait_send()
        for plane_step in (0, 1):
            for chip in range(4):
                if chip:
                    token_plane(kind, plane_step, chip).wait_send()
                token_sibling(kind, plane_step, chip).wait()

    quarter = w_in_ref.shape[0]
    quarter_out = w_out_ref.shape[0]

    def win_copy(step, piece):
        other = xor(parity, step % 2)
        source = w_in_ref.at[:, at_rows(piece * FF + other * half, half, 128)]
        target = w_in_half.at[at_rows(plane * quarter, quarter), pl.ds(piece * half, half)]
        if step == 0:
            return pltpu.make_async_copy(source, target, local_sems.at[piece])
        return remote(source, target, win_sems, (step, piece), (xor(plane, step), member))

    out_half = lax.div(plane, 2)

    def wout_arrived(slot):
        target = w_out_half.at[at_rows(slot * quarter_out, quarter_out)]
        return pltpu.make_async_remote_copy(
            src_ref=w_out_ref,
            dst_ref=target,
            send_sem=wout_sems.at[0, slot],
            recv_sem=wout_sems.at[1, slot],
            device_id=(xor(plane, 1), member),
            device_id_type=MESH,
        )

    def wout_local():
        return pltpu.make_async_copy(
            w_out_ref,
            w_out_half.at[at_rows(parity * quarter_out, quarter_out)],
            local_sems.at[2],
        )

    def wout_send(turn):
        return pltpu.make_async_remote_copy(
            src_ref=w_out_ref,
            dst_ref=w_out_half.at[at_rows(parity * quarter_out, quarter_out)],
            send_sem=wout_sems.at[0, turn],
            recv_sem=wout_sems.at[1, parity],
            device_id=(out_half + 2 * turn, member),
            device_id_type=MESH,
        )

    def expert_start():
        for step in (1, 3, 2):
            for piece in (0, 1):
                win_copy(step, piece).start()
        for piece in (0, 1):
            win_copy(0, piece).start()
        for turn in (0, 1):

            @pl.when(out_half + 2 * turn != plane)
            def _():
                wout_send(turn).start()

        @pl.when(out_half == parity)
        def _():
            wout_local().start()

    def expert_finish():
        for step in (1, 3, 2):
            for piece in (0, 1):
                win_copy(step, piece).wait()
        for piece in (0, 1):
            win_copy(0, piece).wait()
        for slot in (0, 1):

            @pl.when(parity * 2 + slot != plane)
            def _():
                wout_arrived(slot).wait_recv()

        for turn in (0, 1):

            @pl.when(out_half + 2 * turn != plane)
            def _():
                wout_send(turn).wait_send()

        @pl.when(out_half == parity)
        def _():
            wout_local().wait()

    pass_on_plane(0)
    pass_on_plane(1)
    pass_on_sibling(0)
    arrived_dense(0)
    expert_start()
    aux = full_a[:, pl.ds(2 * kv_width, 128)]
    pick = (
        lax.broadcasted_iota(jnp.int32, (16, 128), 1)
        == lax.broadcasted_iota(jnp.int32, (16, 128), 0) + EXPERT_LANES
    ).astype(bf16)
    gain_buf[...] = product_rows(pick, aux)
    gain_a = gain_buf[pl.ds(0, 1), :]
    gain_m = gain_buf[pl.ds(1, 1), :]
    residual = x_ref[...].astype(f32)
    normed = (residual * norm_factor(residual) * gain_a).astype(bf16)
    normed_buf[...] = normed
    cos_part = rope_ref[:, pl.ds(0, HEAD_DIM)]
    sin_part = rope_ref[:, pl.ds(HEAD_DIM, HEAD_DIM)]

    def turned(values, orient):
        swapped = pltpu.roll(values, HEAD_DIM // 2, 1)
        return values * cos_part + swapped * (sin_part * orient)

    kv_rows = product(normed, full_a[:, pl.ds(0, 2 * kv_width)])
    for part in range(2 * KEY_VALUE_HEADS):
        piece = kv_rows[:, part * HEAD_DIM : (part + 1) * HEAD_DIM]
        if part < KEY_VALUE_HEADS:
            piece = turned(piece, 1.0)
        kv_all[part, at_rows(member * tokens, tokens, 128)] = piece.astype(bf16)

    def kv_copy(sems, index, owner_step, device):
        block = kv_all.at[:, at_rows(xor(member, owner_step) * tokens, tokens, 128)]
        return remote(block, block, sems, (index,), device)

    for chip in (1, 2, 3):
        kv_copy(kv_sems, chip - 1, 0, in_plane(2 * chip)).start()
    kv_copy(kv_sems, 3, 0, sibling).start()
    turn_send[0] = jnp.transpose(normed).reshape(turn_send.shape[1:])

    def turn_copy(kind, step):
        return remote(
            turn_send.at[kind, :, xor(member, step)],
            turn_recv.at[kind, :, :, at_rows(member * tokens, tokens, 128)],
            turn_sems,
            (kind, step),
            in_plane(step),
        )

    def turn_start(kind):
        for step in range(1, 8):
            turn_copy(kind, step).start()
        turn_recv[kind, :, :, at_rows(member * tokens, tokens, 128)] = turn_send[
            kind, :, pl.ds(member, 1)
        ].reshape(turn_recv.shape[1], rows, tokens)

    pass_on_sibling(1)
    for chip in (1, 2, 3):
        kv_copy(kv_sems, chip - 1, 0, in_plane(2 * chip)).wait_recv()
        kv_copy(kv_sems, 3 + chip, 2 * chip, sibling).start()
    pass_on_plane(2)
    token_start(0)
    arrived_dense(1)
    spill_b_copy = pltpu.make_async_copy(
        arena.at[pl.ds(0, width)], spill_b, local_sems.at[3]
    )
    spill_b_copy.start()
    for head in range(QUERY_HEADS):
        if head % 2 == 0:
            pair = product(normed, arena[pl.ds(0, width), pl.ds(head * HEAD_DIM, 2 * HEAD_DIM)])
        piece = pair[:, (head % 2) * HEAD_DIM : (head % 2 + 1) * HEAD_DIM]
        q_rows[pl.ds(head * tokens, tokens)] = turned(piece, 1.0).astype(bf16)
    for chip in range(4):
        index = 3 if chip == 0 else 3 + chip
        kv_copy(kv_sems, index, 2 * chip, sibling).wait()
    for chip in (1, 2, 3):
        kv_copy(kv_sems, chip - 1, 0, in_plane(2 * chip)).wait_send()
    for group in range(KEY_VALUE_HEADS):
        k_t[group] = jnp.transpose(kv_all[group])
        v_t[group] = jnp.transpose(kv_all[KEY_VALUE_HEADS + group])

    seq_len = kv_all.shape[1]
    pairs = QUERY_HEADS // 2
    pairs_per_group = pairs // KEY_VALUE_HEADS
    key_index = lax.broadcasted_iota(jnp.int32, (seq_len, 2 * tokens), 0)
    query_index = member * tokens + lax.rem(
        lax.broadcasted_iota(jnp.int32, (seq_len, 2 * tokens), 1), tokens
    )
    allowed = key_index <= query_index

    def pair_scores(pair, group):
        queries = q_rows[at_rows(pair * 2 * tokens, 2 * tokens, 128)]
        scores = product_rows(kv_all[group], queries) * score_scale
        return jnp.where(allowed, scores, masked_score), queries

    def attend(pair, carry):
        group = lax.div(pair, pairs_per_group)
        scores, _ = pair_scores(pair, group)
        peak = jnp.max(scores, axis=0, keepdims=True)
        expo_vals = jnp.exp(scores - peak)
        sums = jnp.sum(expo_vals, axis=0, keepdims=True)
        probs = (expo_vals / sums).astype(bf16)
        lse_buf[pair] = jnp.broadcast_to(peak + jnp.log(sums), (8, 2 * tokens))
        part = product(v_t[group], probs)
        for inner in (0, 1):
            piece = part[:, inner * tokens : (inner + 1) * tokens].astype(bf16)
            attn_buf[2 * pair + inner] = piece
        return carry

    lax.fori_loop(0, pairs, attend, 0)
    token_pass_plane(0)
    pass_on_sibling(2)
    attn_t = attn_buf[...].reshape(width, tokens)
    turn_send[1] = attn_t.reshape(turn_send.shape[1:])
    attn = jnp.transpose(attn_t)
    arrived_dense(2)
    spill_c_copy = pltpu.make_async_copy(
        arena.at[pl.ds(width, width)], spill_c, local_sems.at[4]
    )
    spill_c_copy.start()
    for start in range(0, width, 512):
        after_buf[:, pl.ds(start, 512)] = x_ref[:, pl.ds(start, 512)].astype(f32) + product(
            attn, arena[pl.ds(width, width), pl.ds(start, 512)]
        )
    after = after_buf[...]
    normed_two = (after * norm_factor(after) * gain_m).astype(bf16)
    n2_all[token_rows(0, 0)] = normed_two
    spill_b_copy.wait()
    spill_c_copy.wait()
    for part in range(3):
        sent_dense(part)
    token_start(1)
    turn_send[2] = jnp.transpose(normed_two).reshape(turn_send.shape[1:])
    token_pass_sibling(0)
    token_finish(0)
    token_pass_plane(1)
    token_pass_sibling(1)
    token_finish(1)
    for kind in range(3):
        turn_start(kind)
    expert_finish()

    own_lane = lax.broadcasted_iota(jnp.int32, (2 * tokens, 128), 1) == member
    low_lane = lax.broadcasted_iota(jnp.int32, (2 * tokens, 128), 1) == member + 64
    message = 2 * tokens
    stage_base, sib_base, send_base, recv_base = 0, 2 * message, 4 * message, 8 * message

    def arena_slot(base, slot):
        return at_rows(base + slot * message, message, 128)

    def sib_copy(slot):
        return remote(
            arena.at[arena_slot(stage_base, slot)],
            arena.at[arena_slot(sib_base, slot)],
            sib_sems,
            (slot,),
            sibling,
        )

    def sib_gate_copy(slot):
        return remote(
            gate_buf.at[slot], gate_buf.at[2 + slot], sib_sems, (2 + slot,), sibling
        )

    def ret_device(turn):
        return (xor(plane, lax.div(turn, 4)), xor(member, 2 * lax.rem(turn, 4)))

    def ret_copy(turn, slot):
        return remote(
            arena.at[arena_slot(send_base, slot)],
            arena.at[arena_slot(recv_base, turn)],
            ret_sems,
            (turn,),
            ret_device(turn),
        )

    def ret_gate_copy(turn, slot):
        return remote(
            gate_buf.at[4 + slot], gate_buf.at[8 + turn], gate_sems, (turn,), ret_device(turn)
        )

    def expert_step(turn, carry):
        slot2 = lax.rem(turn, 2)
        slot4 = lax.rem(turn, 4)
        other_plane = xor(parity, lax.div(turn, 4))
        chip = xor(lax.div(member, 2), lax.rem(turn, 4))
        start = (other_plane * 4 + chip) * 2 * tokens
        here = at_rows(start, 2 * tokens, 128)
        token_block = n2_all[here, :]
        gate_up = product(token_block, w_in_half[...])
        gates = masked_gates(
            token_block,
            full_a[:, pl.ds(2 * kv_width, 128)],
            cot_all[here, pl.ds(width, 128)],
        )
        gate = jnp.sum(jnp.where(own_lane, gates, 0.0), axis=1, keepdims=True)
        gate_half = gate_up[:, :half]
        up_half = gate_up[:, half:]
        sigmoid_vals = 1.0 / (1.0 + jnp.exp(-gate_half))
        silu_vals = gate_half * sigmoid_vals
        hidden = (silu_vals * up_half).astype(bf16)
        hidden_all[here, :] = hidden
        slot_grad = (gate * cot_all[here, pl.ds(0, width)].astype(f32)).astype(bf16)
        act_grad = product_rows(slot_grad, w_out_half[...])
        gate_part = act_grad * up_half * sigmoid_vals * (1.0 + gate_half * (1.0 - sigmoid_vals))
        g_block = jnp.concatenate([gate_part, act_grad * silu_vals], axis=1).astype(bf16)
        g_all[here, :] = g_block

        @pl.when(turn >= 2)
        def _():
            sib_copy(slot2).wait_send()
            sib_gate_copy(slot2).wait_send()
            pl.semaphore_wait(credit_sem, 1)

        @pl.when(turn > 4)
        def _():
            ret_copy(turn - 4, slot4).wait_send()
            ret_gate_copy(turn - 4, slot4).wait_send()

        def halves(values, first):
            return jnp.where(first, values[:tokens], values[tokens:])

        send_first = core == 1
        stage = stage_base + slot2 * message
        place = jnp.where(turn == 0, recv_base, send_base + slot4 * message)
        sib_start = sib_base + slot2 * message
        gate_grad = jnp.zeros((2 * tokens, 1), f32)
        for start in range(0, width, 512):
            columns = pl.ds(start, 512)
            out_part = product(hidden, w_out_half[:, columns])
            in_part = product_rows(g_block, w_in_half[columns, :])
            gate_grad = gate_grad + jnp.sum(
                out_part * cot_all[here, columns].astype(f32), axis=1, keepdims=True
            )
            out_part = out_part * gate
            arena[at_rows(stage, tokens, 128), columns] = halves(out_part, send_first).astype(bf16)
            arena[at_rows(stage + tokens, tokens, 128), columns] = halves(
                in_part, send_first
            ).astype(bf16)
            arena[at_rows(place, tokens, 128), columns] = halves(out_part, core == 0).astype(bf16)
            arena[at_rows(place + tokens, tokens, 128), columns] = halves(
                in_part, core == 0
            ).astype(bf16)
        cot_all[here, pl.ds(0, width)] = slot_grad
        gate_high = gate_grad.astype(bf16).astype(f32)
        gate_lanes = jnp.where(own_lane, gate_high, 0.0) + jnp.where(
            low_lane, gate_grad - gate_high, 0.0
        )
        gate_buf[slot2] = halves(gate_lanes, send_first).astype(bf16)
        sib_copy(slot2).start()
        sib_gate_copy(slot2).start()
        own_gate = halves(gate_lanes, core == 0)
        sib_copy(slot2).wait_recv()
        sib_gate_copy(slot2).wait_recv()
        both = at_rows(place, message, 128)
        arena[both] = (
            arena[both].astype(f32) + arena[at_rows(sib_start, message, 128)].astype(f32)
        ).astype(bf16)
        own_gate = own_gate + gate_buf[2 + slot2].astype(f32)

        @pl.when(turn < 6)
        def _():
            pl.semaphore_signal(credit_sem, inc=1, device_id=sibling, device_id_type=MESH)

        gate_buf[jnp.where(turn == 0, 8, 4 + slot4)] = own_gate.astype(bf16)

        @pl.when(turn > 0)
        def _():
            ret_copy(turn, slot4).start()
            ret_gate_copy(turn, slot4).start()

        return carry

    lax.fori_loop(0, 8, expert_step, 0)

    for slot in (0, 1):
        sib_copy(slot).wait_send()
        sib_gate_copy(slot).wait_send()

    def gin_copy(step):
        source = w_in_half.at[at_rows(xor(plane, step) * quarter, quarter)]
        if step == 0:
            return pltpu.make_async_copy(source, grad_in_ref.at[0], local_sems.at[5])
        return remote(
            source, grad_in_ref.at[step], gin_sems, (step,), (xor(plane, step), member)
        )

    for step in (2, 1, 3, 0):
        start = xor(plane, step) * quarter
        for piece in range(0, quarter, 128):
            columns = n2_all[:, at_rows(start + piece, 128, 128)]
            w_in_half[at_rows(start + piece, 128, 128)] = product_columns(
                columns, g_all[...]
            ).astype(bf16)
        gin_copy(step).start()

    def gout_copy(slot):
        return pltpu.make_async_remote_copy(
            src_ref=w_out_half.at[pl.ds(slot * quarter_out, quarter_out)],
            dst_ref=grad_out_ref.at[out_half],
            send_sem=gout_sems.at[0, slot],
            recv_sem=gout_sems.at[1, out_half],
            device_id=(parity * 2 + slot, member),
            device_id_type=MESH,
        )

    def gout_local(slot):
        return pltpu.make_async_copy(
            w_out_half.at[pl.ds(slot * quarter_out, quarter_out)],
            grad_out_ref.at[out_half],
            local_sems.at[6],
        )

    def gout_arrived(turn):
        return pltpu.make_async_remote_copy(
            src_ref=w_out_half.at[pl.ds(0, quarter_out)],
            dst_ref=grad_out_ref.at[turn],
            send_sem=gout_sems.at[0, turn],
            recv_sem=gout_sems.at[1, turn],
            device_id=(xor(plane, 1), member),
            device_id_type=MESH,
        )

    for start in range(0, half, 128):
        w_out_half[pl.ds(start, 128)] = product_columns(
            hidden_all[:, pl.ds(start, 128)], cot_all[:, pl.ds(0, width)]
        ).astype(bf16)
    for slot in (0, 1):

        @pl.when(parity * 2 + slot != plane)
        def _():
            gout_copy(slot).start()

        @pl.when(parity * 2 + slot == plane)
        def _():
            gout_local(slot).start()

    load_b = pltpu.make_async_copy(
        spill_b, cot_all.at[pl.ds(0, width), pl.ds(0, width)], local_sems.at[3]
    )
    load_c = pltpu.make_async_copy(spill_c, n2_all.at[pl.ds(0, width)], local_sems.at[4])
    own_n2 = n2_all[token_rows(0, 0), :]
    own_mask = mask_ref[...]
    own_gates = masked_gates(own_n2, full_a[:, pl.ds(2 * kv_width, 128)], own_mask)
    load_b.start()
    load_c.start()

    total_out = after_buf[...]
    total_in = jnp.zeros((tokens, width), f32)
    total_gate = jnp.zeros((tokens, 128), f32)
    for turn in range(8):
        if turn:
            ret_copy(turn, turn % 4).wait_recv()
            ret_gate_copy(turn, turn % 4).wait_recv()
        base = recv_base + turn * message
        total_out = total_out + arena[pl.ds(base, tokens)].astype(f32)
        total_in = total_in + arena[pl.ds(base + tokens, tokens)].astype(f32)
        total_gate = total_gate + gate_buf[8 + turn].astype(f32)
    block_out_ref[...] = total_out.astype(bf16)
    gate_grad = total_gate + pltpu.roll(total_gate, 64, 1)
    gate_inner = jnp.sum(own_gates * gate_grad, axis=1, keepdims=True)
    logit_grad = own_gates * (gate_grad - gate_inner)
    lg_parts = split_three(logit_grad)
    aux_now = full_a[:, pl.ds(2 * kv_width, 128)]
    for part in lg_parts:
        total_in = total_in + product_rows(part, aux_now)
    after = after_buf[...]

    def norm_backward(values, gain, grad):
        factor = norm_factor(values)
        scaled = grad * gain
        gain_row = jnp.sum(grad * values * factor, axis=0, keepdims=True)
        inner = jnp.mean(scaled * values, axis=-1, keepdims=True)
        return factor * scaled - values * factor * factor * factor * inner, gain_row

    two_back, gain_m_row = norm_backward(after, gain_buf[pl.ds(1, 1), :], total_in)
    mid = cot_ref[...].astype(f32) + two_back
    after_buf[...] = mid
    out_grad = mid.astype(bf16)
    own_block = at_rows(member * tokens, tokens, 128)
    og_all[own_block, pl.ds(0, width)] = out_grad
    og_all[own_block, pl.ds(width, 128)] = (
        lg_parts[0].astype(f32)
        + pltpu.roll(lg_parts[1].astype(f32), 8, 1)
        + pltpu.roll(lg_parts[2].astype(f32), 16, 1)
    ).astype(bf16)

    def gather_copy(array, sems, index, owner_step, device, columns=None):
        block = at_rows(xor(member, owner_step) * tokens, tokens, 128)
        piece = array.at[block] if columns is None else array.at[block, columns]
        return remote(piece, piece, sems, index, device)

    def gather_start(array, sems, lead=(), columns=None):
        for chip in (1, 2, 3):
            gather_copy(array, sems, lead + (chip - 1,), 0, in_plane(2 * chip), columns).start()
        gather_copy(array, sems, lead + (3,), 0, sibling, columns).start()

    def gather_pass(array, sems, lead=(), columns=None):
        for chip in (1, 2, 3):
            gather_copy(array, sems, lead + (chip - 1,), 0, in_plane(2 * chip), columns).wait_recv()
            gather_copy(array, sems, lead + (3 + chip,), 2 * chip, sibling, columns).start()

    def gather_finish(array, sems, lead=(), columns=None):
        for chip in (1, 2, 3):
            gather_copy(array, sems, lead + (chip - 1,), 0, in_plane(2 * chip), columns).wait_send()
        for chip in range(4):
            gather_copy(array, sems, lead + (3 + chip,), 2 * chip, sibling, columns).wait()

    gather_start(og_all, og_sems)
    load_c.wait()
    for head in range(0, QUERY_HEADS, 2):
        pair = product_rows(out_grad, n2_all[pl.ds(head * HEAD_DIM, 2 * HEAD_DIM), :])
        for inner in (0, 1):
            do_rows[pl.ds((head + inner) * tokens, tokens)] = pair[
                :, inner * HEAD_DIM : (inner + 1) * HEAD_DIM
            ].astype(bf16)
    gather_pass(og_all, og_sems)

    def dkv_copy(group, step):
        return remote(
            g_all.at[
                at_rows(xor(member, step) * tokens, tokens, 128),
                pl.ds(group * 2 * HEAD_DIM, 2 * HEAD_DIM),
            ],
            dkv_recv.at[group, step],
            dkv_sems,
            (group, step),
            in_plane(step),
        )

    planes = turn_recv.shape[1]
    dense_starts = (0, 2 * kv_width, 2 * kv_width + width, 2 * kv_width + 2 * width)

    def dense_copy(piece, step):
        size = dense_starts[piece + 1] - dense_starts[piece]
        source = arena.at[
            at_rows((piece * planes + xor(plane, step)) * rows, rows), pl.ds(0, size)
        ]
        target = grad_dense_ref.at[step, :, pl.ds(dense_starts[piece], size)]
        if step == 0:
            return pltpu.make_async_copy(source, target, local_sems.at[piece])
        return remote(source, target, dense_sems, (piece, step), (xor(plane, step), member))

    for group in range(KEY_VALUE_HEADS):
        keys = kv_all[group]
        values = kv_all[KEY_VALUE_HEADS + group]
        dk = jnp.zeros((seq_len, HEAD_DIM), f32)
        dv = jnp.zeros((seq_len, HEAD_DIM), f32)
        for pair in range(group * pairs_per_group, (group + 1) * pairs_per_group):
            scores, queries = pair_scores(pair, group)
            probs = jnp.exp(scores - lse_buf[pair][0:1])
            grads = do_rows[pl.ds(pair * 2 * tokens, 2 * tokens)]
            prob_grad = product_rows(values, grads)
            row_dot = jnp.sum(probs * prob_grad, axis=0, keepdims=True)
            score_grad = (probs * (prob_grad - row_dot)).astype(bf16)
            dk = dk + product(score_grad, queries)
            dv = dv + product(probs.astype(bf16), grads)
            dq = product(k_t[group], score_grad) * score_scale
            for inner in (0, 1):
                piece = jnp.transpose(dq[:, inner * tokens : (inner + 1) * tokens])
                qg_all[own_block, pl.ds((2 * pair + inner) * HEAD_DIM, HEAD_DIM)] = turned(
                    piece, -1.0
                ).astype(bf16)
        start = group * 2 * HEAD_DIM
        g_all[pl.ds(0, seq_len), pl.ds(start, HEAD_DIM)] = (dk * score_scale).astype(bf16)
        g_all[pl.ds(0, seq_len), pl.ds(start + HEAD_DIM, HEAD_DIM)] = dv.astype(bf16)
        for step in range(1, 8):
            dkv_copy(group, step).start()
        span = width // KEY_VALUE_HEADS
        gather_start(qg_all, qg_sems, (group,), pl.ds(group * span, span))

    gather_finish(og_all, og_sems)
    for kind in range(3):
        for step in range(1, 8):
            turn_copy(kind, step).wait()
    turned_attn = turn_recv[1].reshape(planes * rows, seq_len)
    for start in range(0, width, 512):
        arena[pl.ds(2 * planes * rows, planes * rows), pl.ds(start, 512)] = product(
            turned_attn, og_all[:, pl.ds(start, 512)]
        ).astype(bf16)
    for step in (2, 3, 1, 0):
        dense_copy(2, step).start()
    router_part = product(
        turn_recv[2].reshape(planes * rows, seq_len), og_all[:, pl.ds(width, 128)]
    )

    for group in range(KEY_VALUE_HEADS):
        start = group * 2 * HEAD_DIM
        dk = g_all[own_block, pl.ds(start, HEAD_DIM)].astype(f32)
        dv = g_all[own_block, pl.ds(start + HEAD_DIM, HEAD_DIM)].astype(f32)
        for step in range(1, 8):
            dkv_copy(group, step).wait_recv()
            dk = dk + dkv_recv[group, step, :, pl.ds(0, HEAD_DIM)].astype(f32)
            dv = dv + dkv_recv[group, step, :, pl.ds(HEAD_DIM, HEAD_DIM)].astype(f32)
        kvg_all[own_block, pl.ds(group * HEAD_DIM, HEAD_DIM)] = turned(dk, -1.0).astype(bf16)
        kvg_all[own_block, pl.ds(kv_width + group * HEAD_DIM, HEAD_DIM)] = dv.astype(bf16)
    gather_start(kvg_all, kvg_sems)
    span = width // KEY_VALUE_HEADS
    for group in range(KEY_VALUE_HEADS):
        gather_pass(qg_all, qg_sems, (group,), pl.ds(group * span, span))
    gather_pass(kvg_all, kvg_sems)

    load_b.wait()
    own_kvg = kvg_all[own_block, :]
    own_qg = qg_all[own_block, :]
    normed_grad = product_rows(own_kvg, full_a[:, pl.ds(0, 2 * kv_width)]) + product_rows(
        own_qg, cot_all[pl.ds(0, width), pl.ds(0, width)]
    )
    one_back, gain_a_row = norm_backward(
        x_ref[...].astype(f32), gain_buf[pl.ds(0, 1), :], normed_grad
    )
    dx_ref[...] = after_buf[...] + one_back
    line = lax.broadcasted_iota(jnp.int32, (128, width), 0)
    gain_lines = jnp.zeros((128, width), f32)
    for offset, part in enumerate(split_three(gain_a_row) + split_three(gain_m_row)):
        gain_lines = jnp.where(line == 32 + offset, part.astype(f32), gain_lines)
    turn_send[3] = jnp.transpose(gain_lines.astype(bf16)).reshape(turn_send.shape[1:])
    turn_start(3)

    turned_normed = turn_recv[0].reshape(planes * rows, seq_len)
    for group in range(KEY_VALUE_HEADS):
        gather_finish(qg_all, qg_sems, (group,), pl.ds(group * span, span))
    for start in range(0, width, 512):
        arena[pl.ds(planes * rows, planes * rows), pl.ds(start, 512)] = product(
            turned_normed, qg_all[:, pl.ds(start, 512)]
        ).astype(bf16)
    for step in (2, 3, 1, 0):
        dense_copy(1, step).start()
    gather_finish(kvg_all, kvg_sems)
    arena[pl.ds(0, planes * rows), pl.ds(0, 2 * kv_width)] = product(
        turned_normed, kvg_all[...]
    ).astype(bf16)
    for step in (2, 3, 1, 0):
        dense_copy(0, step).start()
    for step in range(1, 8):
        turn_copy(3, step).wait()
    aux_total = router_part
    for block in range(8):
        aux_total = aux_total + turn_recv[3, :, :, pl.ds(block * tokens, tokens)].reshape(
            planes * rows, tokens
        ).astype(f32)
    aux_send[...] = aux_total.reshape(planes, rows, 128)

    def aux_copy(step):
        return remote(
            aux_send.at[xor(plane, step)],
            grad_aux_ref.at[step],
            aux_sems,
            (step,),
            (xor(plane, step), member),
        )

    for step in (1, 2, 3):
        aux_copy(step).start()
    own_aux = pltpu.make_async_copy(aux_send.at[plane], grad_aux_ref.at[0], local_sems.at[7])
    own_aux.start()

    for turn in range(4, 8):
        ret_copy(turn, turn % 4).wait_send()
        ret_gate_copy(turn, turn % 4).wait_send()
    for group in range(KEY_VALUE_HEADS):
        for step in range(1, 8):
            dkv_copy(group, step).wait_send()
    gin_copy(0).wait()
    for step in (1, 2, 3):
        gin_copy(step).wait()
    for slot in (0, 1):

        @pl.when(parity * 2 + slot != plane)
        def _():
            gout_copy(slot).wait_send()

        @pl.when(parity * 2 + slot == plane)
        def _():
            gout_local(slot).wait()

    for turn in (0, 1):

        @pl.when(out_half + 2 * turn != plane)
        def _():
            gout_arrived(turn).wait_recv()

    for piece in range(3):
        for step in range(4):
            dense_copy(piece, step).wait()
    for step in (1, 2, 3):
        aux_copy(step).wait()
    own_aux.wait()


EXPERT_LANES = 8


def fast_body(
    tokens,
    cotangent,
    routes,
    gain_attn,
    w_query,
    key_weight,
    value_weight,
    w_output,
    gain_moe,
    w_router,
    w_in,
    w_out,
):
    f32, bf16 = jnp.float32, jnp.bfloat16
    total_rows, width = tokens.shape
    rows = w_query.shape[1]
    planes = lax.axis_size("dp")
    members = lax.axis_size("expert")
    seq_len = total_rows * members
    kv_width = key_weight.shape[2]
    quarter = w_in.shape[1]
    quarter_out = w_out.shape[1]
    half = FF // 2
    positions = lax.axis_index("expert") * total_rows + jnp.arange(total_rows, dtype=jnp.int32)
    cos_table, sin_table = rope_tables(positions, HEAD_DIM)
    rope = jnp.concatenate([cos_table, cos_table, -sin_table, sin_table], axis=1)
    lanes = jnp.arange(128, dtype=jnp.int32)
    mask = jnp.any(routes[0][:, :, None] == lanes[None, None, :], axis=1).astype(bf16)
    padding = jnp.zeros((rows, 128 - EXPERT_LANES - 2), bf16)
    shard_a = jnp.concatenate(
        [
            key_weight[0],
            value_weight[0],
            w_router[0],
            gain_attn[0][:, None],
            gain_moe[0][:, None],
            padding,
        ],
        axis=1,
    )
    dense_width = 2 * kv_width + 2 * width
    in_vmem = pl.BlockSpec(memory_space=pltpu.VMEM)
    anywhere = pl.BlockSpec(memory_space=pl.ANY)
    pair_rows = 2 * seq_len
    shape = jax.ShapeDtypeStruct
    dma = pltpu.SemaphoreType.DMA
    heads = QUERY_HEADS
    (
        block_out,
        tokens_grad,
        grad_in,
        grad_out,
        grad_dense,
        grad_aux,
        _,
        _,
    ) = pl.pallas_call(
        layer_kernel,
        out_shape=(
            shape((total_rows, width), bf16),
            shape((total_rows, width), f32),
            shape((planes, quarter, 2 * half), bf16),
            shape((2, quarter_out, width), bf16),
            shape((planes, rows, dense_width), bf16),
            shape((planes, rows, 128), f32),
            shape((width, width), bf16),
            shape((width, width), bf16),
        ),
        in_specs=[in_vmem] * 7 + [anywhere] * 2,
        out_specs=(in_vmem,) * 2 + (anywhere,) * 6,
        scratch_shapes=[
            pltpu.VMEM((pair_rows, width), bf16),
            pltpu.VMEM((pair_rows, width + 128), bf16),
            pltpu.VMEM((width, 2 * kv_width + 128), bf16),
            pltpu.VMEM((32 * total_rows, width), bf16),
            pltpu.VMEM((16, total_rows, 128), bf16),
            pltpu.VMEM((width, 2 * half), bf16),
            pltpu.VMEM((half, width), bf16),
            pltpu.VMEM((pair_rows, half), bf16),
            pltpu.VMEM((pair_rows, 2 * half), bf16),
            pltpu.VMEM((2 * KEY_VALUE_HEADS, seq_len, HEAD_DIM), bf16),
            pltpu.VMEM((KEY_VALUE_HEADS, HEAD_DIM, seq_len), bf16),
            pltpu.VMEM((KEY_VALUE_HEADS, HEAD_DIM, seq_len), bf16),
            pltpu.VMEM((heads * total_rows, HEAD_DIM), bf16),
            pltpu.VMEM((heads * total_rows, HEAD_DIM), bf16),
            pltpu.VMEM((total_rows, width), bf16),
            pltpu.VMEM((heads, HEAD_DIM, total_rows), bf16),
            pltpu.VMEM((total_rows, width), f32),
            pltpu.VMEM((heads // 2, 8, 2 * total_rows), f32),
            pltpu.VMEM((4, planes, members, rows, total_rows), bf16),
            pltpu.VMEM((4, planes, rows, seq_len), bf16),
            pltpu.VMEM((seq_len, width + 128), bf16),
            pltpu.VMEM((seq_len, width), bf16),
            pltpu.VMEM((seq_len, 2 * kv_width), bf16),
            pltpu.VMEM((KEY_VALUE_HEADS, members, total_rows, 2 * HEAD_DIM), bf16),
            pltpu.VMEM((planes, rows, 128), f32),
            pltpu.VMEM((16, width), f32),
            dma((2, 3, 4)),
            dma((2, 3, 4, 4)),
            dma((2, 3, 4, 4)),
            dma((2, 7)),
            dma((2, 2, 15)),
            dma((2, 4, 8)),
            dma((2, 4, 2)),
            dma((2, 2)),
            dma((2, 4)),
            dma((2, 8)),
            dma((2, 8)),
            dma((2, 4)),
            dma((2, 2)),
            dma((2, 7)),
            dma((2, 2, 7)),
            dma((2, 7)),
            dma((2, 2, 8)),
            dma((2, 3, 4)),
            dma((2, 4)),
            dma((8,)),
            pltpu.SemaphoreType.REGULAR,
        ],
        compiler_params=pltpu.CompilerParams(
            collective_id=0, has_side_effects=True, vmem_limit_bytes=63 * 2**20
        ),
    )(
        tokens,
        cotangent,
        mask,
        rope,
        shard_a,
        w_query[0],
        w_output[0],
        w_in.reshape(quarter, 2 * FF),
        w_out.reshape(quarter_out, width),
    )
    own = grad_in[0].astype(f32) + grad_in[2].astype(f32)
    other = grad_in[1].astype(f32) + grad_in[3].astype(f32)
    even = lax.rem(lax.axis_index("dp"), 2) == 0
    low, high = jnp.where(even, own, other), jnp.where(even, other, own)
    w_in_grad = jnp.concatenate(
        [low[:, :half], high[:, :half], low[:, half:], high[:, half:]], axis=1
    )
    w_out_grad = grad_out[0].astype(f32) + grad_out[1].astype(f32)
    dense = jnp.sum(grad_dense.astype(f32), axis=0)
    aux = jnp.sum(grad_aux, axis=0)
    return (
        block_out,
        tokens_grad,
        jnp.sum(aux[:, 32:35], axis=1)[None],
        dense[None, :, 2 * kv_width : 2 * kv_width + width],
        dense[None, :, :kv_width],
        dense[None, :, kv_width : 2 * kv_width],
        dense[None, :, 2 * kv_width + width :],
        jnp.sum(aux[:, 35:38], axis=1)[None],
        (aux[:, :8] + aux[:, 8:16] + aux[:, 16:24])[None],
        w_in_grad[None, :, None, :],
        w_out_grad[None, :, None, :],
    )


def solution(mesh):
    in_specs = (
        P(("dp", "expert"), None),
        P(("dp", "expert"), None),
        P(None, ("dp", "expert"), None),
        P(None, ("dp", "expert")),
        P(None, ("dp", "expert"), None),
        P(None, ("dp", "expert"), None),
        P(None, ("dp", "expert"), None),
        P(None, ("dp", "expert"), None),
        P(None, ("dp", "expert")),
        P(None, ("dp", "expert"), None),
        P(None, "dp", "expert", None),
        P(None, "dp", "expert", None),
    )
    out_specs = (
        P(("dp", "expert"), None),
        P(("dp", "expert"), None),
        P(None, ("dp", "expert")),
        P(None, ("dp", "expert"), None),
        P(None, ("dp", "expert"), None),
        P(None, ("dp", "expert"), None),
        P(None, ("dp", "expert"), None),
        P(None, ("dp", "expert")),
        P(None, ("dp", "expert"), None),
        P(None, "dp", "expert", None),
        P(None, "dp", "expert", None),
    )
    body = fast_body if mesh.shape["dp"] == 4 and mesh.shape["expert"] == 8 else general_body
    return jax.shard_map(body, mesh=mesh, in_specs=in_specs, out_specs=out_specs, check_vma=False)
```

```python
import jax
import jax.numpy as jnp
from jax import lax
from jax.experimental import pallas as pl
from jax.experimental.pallas import tpu as pltpu
from jax.sharding import PartitionSpec as P

MESH = pl.DeviceIdType.MESH

QUERY_HEADS = 12
KEY_VALUE_HEADS = 2
HEAD_DIM = 128
FF = 768
TOP = 4


norm_eps = 1e-06
rope_base = 1000000.0
masked_score = -1e30
top_precision = lax.Precision.HIGHEST


def norm_factor(values):
    return lax.rsqrt(jnp.mean(values * values, axis=-1, keepdims=True) + norm_eps)


def norm_back(values, gain, grad_out):
    factor = norm_factor(values)
    scaled = grad_out * gain
    gain_grad = jnp.sum(grad_out * values * factor, axis=0)
    inner_mean = jnp.mean(scaled * values, axis=-1, keepdims=True)
    return (factor * scaled - values * factor * factor * factor * inner_mean, gain_grad)


def rope_tables(positions, head_size):
    half_size = head_size // 2
    inverse = rope_base ** (-(jnp.arange(half_size, dtype=jnp.float32) * 2.0 / head_size))
    angles = positions.astype(jnp.float32)[:, None] * inverse[None, :]
    return (jnp.cos(angles), jnp.sin(angles))


def rotate(values, cos_table, sin_table, orient):
    half_size = values.shape[-1] // 2
    first_half = values[..., :half_size]
    second = values[..., half_size:]
    cos_part = cos_table[:, None, :]
    sin_part = orient * sin_table[:, None, :]
    return jnp.concatenate(
        [first_half * cos_part - second * sin_part, second * cos_part + first_half * sin_part],
        axis=-1,
    )


def plan_slots(route, expert_count, capacity):
    flat_route = route.reshape(-1)
    slot_total = flat_route.shape[0]
    onehot = (flat_route[:, None] == jnp.arange(expert_count, dtype=jnp.int32)[None, :]).astype(
        jnp.int32
    )
    before = jnp.cumsum(onehot, axis=0) - onehot
    target = flat_route * capacity + jnp.sum(before * onehot, axis=1)
    source = (
        jnp.full((expert_count * capacity,), slot_total, jnp.int32)
        .at[target]
        .set(jnp.arange(slot_total, dtype=jnp.int32))
    )
    filled = source < slot_total
    return (target, jnp.minimum(source, slot_total - 1), filled)


def general_body(
    tokens,
    cotangent,
    routes,
    gain_attn,
    w_query,
    key_weight,
    value_weight,
    w_output,
    gain_moe,
    w_router,
    w_in,
    w_out,
):
    total_rows, model_width = tokens.shape
    layer_count = w_query.shape[0]
    group_count = lax.axis_size("expert")
    seq_len = total_rows * group_count
    experts_local = w_in.shape[2]
    expert_count = experts_local * group_count
    capacity = min(total_rows, total_rows * TOP * 3 // (2 * expert_count))
    heads_per_group = QUERY_HEADS // KEY_VALUE_HEADS
    score_scale = HEAD_DIM ** (-0.5)
    positions = lax.axis_index("expert") * total_rows + jnp.arange(total_rows, dtype=jnp.int32)
    cos_table, sin_table = rope_tables(positions, HEAD_DIM)
    allowed = jnp.arange(seq_len, dtype=jnp.int32)[None, :] <= positions[:, None]
    zero_bf = jnp.zeros((), jnp.bfloat16)

    def score_block(query_rows, all_keys, group_of_heads):
        grouped_q = query_rows[
            :, group_of_heads * heads_per_group : (group_of_heads + 1) * heads_per_group, :
        ]
        scores = (
            jnp.einsum(
                "rgd,kd->grk",
                grouped_q,
                all_keys[:, group_of_heads, :],
                preferred_element_type=jnp.float32,
            )
            * score_scale
        )
        return (jnp.where(allowed[None], scores, masked_score), grouped_q)

    residual = tokens.astype(jnp.float32)
    layer_number = 0
    dense_w = (
        lax.all_gather(gain_attn[layer_number], ("dp", "expert"), axis=0, tiled=True),
        lax.all_gather(w_query[layer_number], ("dp", "expert"), axis=0, tiled=True),
        lax.all_gather(key_weight[layer_number], ("dp", "expert"), axis=0, tiled=True),
        lax.all_gather(value_weight[layer_number], ("dp", "expert"), axis=0, tiled=True),
        lax.all_gather(w_output[layer_number], ("dp", "expert"), axis=0, tiled=True),
        lax.all_gather(gain_moe[layer_number], ("dp", "expert"), axis=0, tiled=True),
        lax.all_gather(w_router[layer_number], ("dp", "expert"), axis=0, tiled=True),
    )
    expert_w = (
        lax.all_gather(w_in[layer_number], "dp", axis=0, tiled=True),
        lax.all_gather(w_out[layer_number], "dp", axis=0, tiled=True),
    )
    route = routes[layer_number]
    gain_a = dense_w[0].astype(jnp.float32)
    norm_result = (residual * norm_factor(residual) * gain_a).astype(jnp.bfloat16)
    query_rows = jnp.dot(norm_result, dense_w[1], preferred_element_type=jnp.float32).reshape(
        total_rows, QUERY_HEADS, HEAD_DIM
    )
    query_rows = rotate(query_rows, cos_table, sin_table, 1.0).astype(jnp.bfloat16)
    key_matrix_rows = jnp.dot(norm_result, dense_w[2], preferred_element_type=jnp.float32).reshape(
        total_rows, KEY_VALUE_HEADS, HEAD_DIM
    )
    key_matrix_rows = rotate(key_matrix_rows, cos_table, sin_table, 1.0).astype(jnp.bfloat16)
    value_matrix_rows = (
        jnp.dot(norm_result, dense_w[3], preferred_element_type=jnp.float32)
        .astype(jnp.bfloat16)
        .reshape(total_rows, KEY_VALUE_HEADS, HEAD_DIM)
    )
    all_keys = lax.all_gather(key_matrix_rows, "expert", axis=0, tiled=True)
    all_values = lax.all_gather(value_matrix_rows, "expert", axis=0, tiled=True)
    heads_out = []
    log_totals = []
    for group_of_heads in range(KEY_VALUE_HEADS):
        scores, grouped_q = score_block(query_rows, all_keys, group_of_heads)
        row_peak = jnp.max(scores, axis=-1, keepdims=True)
        expo_vals = jnp.exp(scores - row_peak)
        row_sums = jnp.sum(expo_vals, axis=-1, keepdims=True)
        attn_probs = (expo_vals / row_sums).astype(jnp.bfloat16)
        log_totals.append(row_peak + jnp.log(row_sums))
        heads_out.append(
            jnp.einsum(
                "grk,kd->rgd",
                attn_probs,
                all_values[:, group_of_heads, :],
                preferred_element_type=jnp.float32,
            )
        )
    attn = (
        jnp.concatenate(heads_out, axis=1)
        .reshape(total_rows, QUERY_HEADS * HEAD_DIM)
        .astype(jnp.bfloat16)
    )
    after_attn = residual + jnp.dot(attn, dense_w[4], preferred_element_type=jnp.float32)
    gain_m = dense_w[5].astype(jnp.float32)
    normed_two = (after_attn * norm_factor(after_attn) * gain_m).astype(jnp.bfloat16)
    logits = jnp.dot(normed_two, dense_w[6], preferred_element_type=jnp.float32)
    gate_probs = jax.nn.softmax(jnp.take_along_axis(logits, route, axis=1), axis=-1)
    target, source, filled = plan_slots(route, expert_count, capacity)
    send_rows = jnp.where(filled[:, None], normed_two[source // TOP], zero_bf)
    send_rows = send_rows.reshape(group_count, experts_local, capacity, model_width)
    arrived_rows = lax.all_to_all(send_rows, "expert", split_axis=0, concat_axis=0, tiled=True)
    gate_up_vals = jnp.einsum(
        "secd,def->secf", arrived_rows, expert_w[0], preferred_element_type=jnp.float32
    )
    expert_gate_half = gate_up_vals[..., :FF]
    expert_hidden_act = (
        expert_gate_half * jax.nn.sigmoid(expert_gate_half) * gate_up_vals[..., FF:]
    ).astype(jnp.bfloat16)
    expert_out = jnp.einsum(
        "secf,fed->secd", expert_hidden_act, expert_w[1], preferred_element_type=jnp.float32
    ).astype(jnp.bfloat16)
    arrived, gate_up, expert_out = (arrived_rows, gate_up_vals, expert_out)
    returned = lax.all_to_all(expert_out, "expert", split_axis=0, concat_axis=0, tiled=True)
    slot_out = returned.reshape(expert_count * capacity, model_width)[target].reshape(
        total_rows, TOP, model_width
    )
    new_residual = after_attn + jnp.sum(
        gate_probs[:, :, None] * slot_out.astype(jnp.float32), axis=1
    )
    saved_layers = [
        (
            residual,
            norm_result,
            query_rows,
            key_matrix_rows,
            value_matrix_rows,
            all_keys,
            all_values,
            log_totals,
            attn,
            after_attn,
            normed_two,
            route,
            gate_probs,
            target,
            source,
            filled,
            arrived,
            gate_up,
            slot_out,
            dense_w,
            expert_w,
        )
    ]
    block_out = new_residual.astype(jnp.bfloat16)
    grad_resid = cotangent.astype(jnp.float32)
    grad_lists = [[None] * layer_count for _ in range(9)]
    for layer_number in reversed(range(layer_count)):
        (
            resid_in,
            norm_result,
            query_rows,
            key_matrix_rows,
            value_matrix_rows,
            all_keys,
            all_values,
            log_totals,
            attn,
            after_attn,
            normed_two,
            route,
            gate_probs,
            target,
            source,
            filled,
            arrived,
            gate_up,
            slot_out,
            dense_w,
            expert_w,
        ) = saved_layers[layer_number]
        dense_w = (
            lax.all_gather(gain_attn[layer_number], ("dp", "expert"), axis=0, tiled=True),
            lax.all_gather(w_query[layer_number], ("dp", "expert"), axis=0, tiled=True),
            lax.all_gather(key_weight[layer_number], ("dp", "expert"), axis=0, tiled=True),
            lax.all_gather(value_weight[layer_number], ("dp", "expert"), axis=0, tiled=True),
            lax.all_gather(w_output[layer_number], ("dp", "expert"), axis=0, tiled=True),
            lax.all_gather(gain_moe[layer_number], ("dp", "expert"), axis=0, tiled=True),
            lax.all_gather(w_router[layer_number], ("dp", "expert"), axis=0, tiled=True),
        )
        expert_w = (
            lax.all_gather(w_in[layer_number], "dp", axis=0, tiled=True),
            lax.all_gather(w_out[layer_number], "dp", axis=0, tiled=True),
        )
        all_keys, all_values = (
            lax.all_gather(key_matrix_rows, "expert", axis=0, tiled=True),
            lax.all_gather(value_matrix_rows, "expert", axis=0, tiled=True),
        )
        gate_grad = jnp.sum(slot_out.astype(jnp.float32) * grad_resid[:, None, :], axis=-1)
        slot_grad = (
            (gate_probs[:, :, None] * grad_resid[:, None, :])
            .astype(jnp.bfloat16)
            .reshape(total_rows * TOP, model_width)
        )
        grad_rows = jnp.where(filled[:, None], slot_grad[source], zero_bf)
        grad_rows = grad_rows.reshape(group_count, experts_local, capacity, model_width)
        grad_arrived = lax.all_to_all(grad_rows, "expert", split_axis=0, concat_axis=0, tiled=True)
        gate_half = gate_up[..., :FF]
        up_half = gate_up[..., FF:]
        sigmoid_vals = jax.nn.sigmoid(gate_half)
        silu_vals = gate_half * sigmoid_vals
        hidden_act = (silu_vals * up_half).astype(jnp.bfloat16)
        act_grad = jnp.einsum(
            "secd,fed->secf", grad_arrived, expert_w[1], preferred_element_type=jnp.float32
        )
        gate_part = act_grad * up_half * sigmoid_vals * (1.0 + gate_half * (1.0 - sigmoid_vals))
        gate_up_grad = jnp.concatenate([gate_part, act_grad * silu_vals], axis=-1).astype(
            jnp.bfloat16
        )
        input_grad = jnp.einsum(
            "secf,def->secd", gate_up_grad, expert_w[0], preferred_element_type=jnp.float32
        ).astype(jnp.bfloat16)
        returned_grad = lax.all_to_all(
            input_grad, "expert", split_axis=0, concat_axis=0, tiled=True
        )
        grad_lists[7][layer_number] = lax.psum_scatter(
            jnp.einsum(
                "secd,secf->def", arrived, gate_up_grad, preferred_element_type=jnp.float32
            ).astype(jnp.bfloat16),
            "dp",
            scatter_dimension=0,
            tiled=True,
        ).astype(jnp.float32)
        grad_lists[8][layer_number] = lax.psum_scatter(
            jnp.einsum(
                "secf,secd->fed", hidden_act, grad_arrived, preferred_element_type=jnp.float32
            ).astype(jnp.bfloat16),
            "dp",
            scatter_dimension=0,
            tiled=True,
        ).astype(jnp.float32)
        slot_back = returned_grad.reshape(expert_count * capacity, model_width)[target].reshape(
            total_rows, TOP, model_width
        )
        normed_two_grad = jnp.sum(slot_back.astype(jnp.float32), axis=1)
        gate_inner = jnp.sum(gate_probs * gate_grad, axis=-1, keepdims=True)
        chosen_grad = gate_probs * (gate_grad - gate_inner)
        route_hot = (
            route[:, :, None] == jnp.arange(expert_count, dtype=jnp.int32)[None, None, :]
        ).astype(jnp.float32)
        logit_grad = jnp.sum(route_hot * chosen_grad[:, :, None], axis=1)
        router_f = dense_w[6].astype(jnp.float32)
        normed_two_grad = normed_two_grad + jnp.einsum(
            "re,de->rd", logit_grad, router_f, precision=top_precision
        )
        router_grad = jnp.einsum(
            "rd,re->de", normed_two.astype(jnp.float32), logit_grad, precision=top_precision
        )
        gain_m = dense_w[5].astype(jnp.float32)
        norm_two_back, gain_m_grad = norm_back(after_attn, gain_m, normed_two_grad)
        mid_grad = grad_resid + norm_two_back
        out_grad = mid_grad.astype(jnp.bfloat16)
        output_grad = jnp.einsum("rq,rd->qd", attn, out_grad, preferred_element_type=jnp.float32)
        attn_grad = (
            jnp.einsum("rd,qd->rq", out_grad, dense_w[4], preferred_element_type=jnp.float32)
            .astype(jnp.bfloat16)
            .reshape(total_rows, QUERY_HEADS, HEAD_DIM)
        )
        query_grads = []
        key_grads = []
        value_grads = []
        for group_of_heads in range(KEY_VALUE_HEADS):
            scores, grouped_q = score_block(query_rows, all_keys, group_of_heads)
            grouped_do = attn_grad[
                :, group_of_heads * heads_per_group : (group_of_heads + 1) * heads_per_group, :
            ]
            probs = jnp.exp(scores - log_totals[group_of_heads])
            prob_bf = probs.astype(jnp.bfloat16)
            prob_grad = jnp.einsum(
                "rgd,kd->grk",
                grouped_do,
                all_values[:, group_of_heads, :],
                preferred_element_type=jnp.float32,
            )
            row_dot = jnp.sum(probs * prob_grad, axis=-1, keepdims=True)
            score_grad = (probs * (prob_grad - row_dot)).astype(jnp.bfloat16)
            query_grads.append(
                jnp.einsum(
                    "grk,kd->rgd",
                    score_grad,
                    all_keys[:, group_of_heads, :],
                    preferred_element_type=jnp.float32,
                )
                * score_scale
            )
            key_grads.append(
                jnp.einsum("grk,rgd->kd", score_grad, grouped_q, preferred_element_type=jnp.float32)
                * score_scale
            )
            value_grads.append(
                jnp.einsum("grk,rgd->kd", prob_bf, grouped_do, preferred_element_type=jnp.float32)
            )
        key_sum, value_total_sum = (
            lax.psum_scatter(
                jnp.stack(key_grads, axis=1).astype(jnp.bfloat16),
                "expert",
                scatter_dimension=0,
                tiled=True,
            ).astype(jnp.float32),
            lax.psum_scatter(
                jnp.stack(value_grads, axis=1).astype(jnp.bfloat16),
                "expert",
                scatter_dimension=0,
                tiled=True,
            ).astype(jnp.float32),
        )
        query_grad = (
            rotate(jnp.concatenate(query_grads, axis=1), cos_table, sin_table, -1.0)
            .astype(jnp.bfloat16)
            .reshape(total_rows, QUERY_HEADS * HEAD_DIM)
        )
        key_grad = (
            rotate(key_sum, cos_table, sin_table, -1.0)
            .astype(jnp.bfloat16)
            .reshape(total_rows, KEY_VALUE_HEADS * HEAD_DIM)
        )
        value_rows_gradient = value_total_sum.astype(jnp.bfloat16).reshape(
            total_rows, KEY_VALUE_HEADS * HEAD_DIM
        )
        normed_grad = jnp.einsum(
            "rq,dq->rd", query_grad, dense_w[1], preferred_element_type=jnp.float32
        )
        normed_grad = normed_grad + jnp.einsum(
            "rq,dq->rd", key_grad, dense_w[2], preferred_element_type=jnp.float32
        )
        normed_grad = normed_grad + jnp.einsum(
            "rq,dq->rd", value_rows_gradient, dense_w[3], preferred_element_type=jnp.float32
        )
        query_w_grad = jnp.einsum(
            "rd,rq->dq", norm_result, query_grad, preferred_element_type=jnp.float32
        )
        key_w_grad = jnp.einsum(
            "rd,rq->dq", norm_result, key_grad, preferred_element_type=jnp.float32
        )
        value_w_grad = jnp.einsum(
            "rd,rq->dq", norm_result, value_rows_gradient, preferred_element_type=jnp.float32
        )
        gain_a = dense_w[0].astype(jnp.float32)
        norm_one_back, gain_a_grad = norm_back(resid_in, gain_a, normed_grad)
        grad_resid = mid_grad + norm_one_back
        shares = (
            lax.psum_scatter(gain_a_grad, ("dp", "expert"), scatter_dimension=0, tiled=True),
            lax.psum_scatter(query_w_grad, ("dp", "expert"), scatter_dimension=0, tiled=True),
            lax.psum_scatter(key_w_grad, ("dp", "expert"), scatter_dimension=0, tiled=True),
            lax.psum_scatter(value_w_grad, ("dp", "expert"), scatter_dimension=0, tiled=True),
            lax.psum_scatter(output_grad, ("dp", "expert"), scatter_dimension=0, tiled=True),
            lax.psum_scatter(gain_m_grad, ("dp", "expert"), scatter_dimension=0, tiled=True),
            lax.psum_scatter(router_grad, ("dp", "expert"), scatter_dimension=0, tiled=True),
        )
        for member in range(7):
            grad_lists[member][layer_number] = shares[member]
    stacked = [jnp.stack(grad_lists[member], axis=0) for member in range(9)]
    return (
        block_out,
        grad_resid,
        stacked[0],
        stacked[1],
        stacked[2],
        stacked[3],
        stacked[4],
        stacked[5],
        stacked[6],
        stacked[7],
        stacked[8],
    )


def product(left, right):
    return lax.dot_general(
        left, right, (((1,), (0,)), ((), ())), preferred_element_type=jnp.float32
    )


def product_rows(left, right):
    return lax.dot_general(
        left, right, (((1,), (1,)), ((), ())), preferred_element_type=jnp.float32
    )


def product_columns(left, right):
    return lax.dot_general(
        left, right, (((0,), (0,)), ((), ())), preferred_element_type=jnp.float32
    )


def split_three(values):
    high = values.astype(jnp.bfloat16)
    rest = values - high.astype(jnp.float32)
    middle = rest.astype(jnp.bfloat16)
    low = (rest - middle.astype(jnp.float32)).astype(jnp.bfloat16)
    return high, middle, low


def masked_gates(rows, router, mask):
    chosen = mask.astype(jnp.float32) > 0.5
    logits = jnp.where(chosen, product(rows, router), masked_score)
    expo_vals = jnp.where(chosen, jnp.exp(logits - jnp.max(logits, axis=1, keepdims=True)), 0.0)
    return expo_vals / jnp.sum(expo_vals, axis=1, keepdims=True)


def layer_kernel(
    x_ref,
    cot_ref,
    mask_ref,
    rope_ref,
    shard_a,
    shard_b,
    shard_c,
    w_in_ref,
    w_out_ref,
    block_out_ref,
    dx_ref,
    grad_in_ref,
    grad_out_ref,
    grad_dense_ref,
    grad_kv_ref,
    grad_aux_ref,
    spill_b,
    spill_c,
    n2_all,
    cot_all,
    full_a,
    arena,
    gate_buf,
    w_in_half,
    w_out_half,
    hidden_all,
    g_all,
    kv_all,
    k_t,
    v_t,
    q_rows,
    do_rows,
    normed_buf,
    attn_buf,
    after_buf,
    lse_buf,
    turn_send,
    turn_recv,
    og_all,
    qg_all,
    kvg_all,
    dkv_recv,
    aux_send,
    gain_buf,
    z_sems,
    p_sems,
    s_sems,
    kv_sems,
    tok_sems,
    tz_sems,
    turn_sems,
    win_sems,
    wout_sems,
    sib_sems,
    ret_sems,
    gate_sems,
    gin_sems,
    gout_sems,
    og_sems,
    qg_sems,
    kvg_sems,
    dkv_sems,
    dense_sems,
    aux_sems,
    local_sems,
    credit_sem,
):
    plane = lax.axis_index("dp")
    member = lax.axis_index("expert")
    core = lax.rem(member, 2)
    parity = lax.rem(plane, 2)
    tokens, width = x_ref.shape
    rows = shard_a.shape[0]
    xor = lax.bitwise_xor
    f32, bf16 = jnp.float32, jnp.bfloat16
    half = FF // 2
    score_scale = HEAD_DIM ** (-0.5)
    kv_width = KEY_VALUE_HEADS * HEAD_DIM

    def at_rows(start, count, step=16):
        return pl.ds(pl.multiple_of(start, step), count)

    def remote(source, target, sems, index, device, recv_index=None):
        return pltpu.make_async_remote_copy(
            src_ref=source,
            dst_ref=target,
            send_sem=sems.at[(0,) + index],
            recv_sem=sems.at[(1,) + (index if recv_index is None else recv_index)],
            device_id=device,
            device_id_type=MESH,
        )

    in_plane = lambda step: (plane, xor(member, step))
    sibling = in_plane(1)

    barrier = pltpu.get_barrier_semaphore()
    greeted = [(xor(plane, s), member) for s in (1, 2, 3)]
    greeted += [in_plane(s) for s in range(1, 8)]
    greeted += [(xor(plane, 1), xor(member, s)) for s in (2, 4, 6)]
    for device in greeted:
        pl.semaphore_signal(barrier, inc=1, device_id=device, device_id_type=MESH)

    shards = (shard_a, shard_b, shard_c)

    def dense_block(part, step, chip_step):
        start = (xor(plane, step) * 8 + xor(member, chip_step)) * rows
        if part == 0:
            return full_a.at[at_rows(start, rows)]
        return arena.at[at_rows(start + (part - 1) * width, rows)]

    def z_copy(part, step):
        device = (xor(plane, step), member)
        return remote(shards[part], dense_block(part, 0, 0), z_sems, (part, step), device)

    def plane_copy(part, step, chip):
        if chip < 3:
            block = dense_block(part, step, 0)
            return remote(block, block, p_sems, (part, step, chip), in_plane(2 * chip))
        via = 1 + step % 2
        block = dense_block(part, step, 2 * via)
        return remote(block, block, p_sems, (part, step, 3), in_plane(2 * (3 - via)))

    def sibling_copy(part, step, chip):
        block = dense_block(part, step, 2 * chip)
        return remote(block, block, s_sems, (part, step, chip), sibling)

    own_rows = (plane * 8 + member) * rows
    full_a[at_rows(own_rows, rows)] = shard_a[...]
    arena[at_rows(own_rows, rows)] = shard_b[...]
    arena[at_rows(own_rows + width, rows)] = shard_c[...]

    def token_rows(plane_step, member_step):
        start = (xor(parity, plane_step) * 8 + xor(member, member_step)) * tokens
        return at_rows(start, tokens, 128)

    cot_all[token_rows(0, 0), pl.ds(0, width)] = cot_ref[...]
    cot_all[token_rows(0, 0), pl.ds(width, 128)] = mask_ref[...]
    pl.semaphore_wait(barrier, len(greeted))

    for part in range(3):
        for step in (3, 2, 1):
            z_copy(part, step).start()
    for part in range(3):
        for chip in (1, 2):
            plane_copy(part, 0, chip).start()
        sibling_copy(part, 0, 0).start()

    def pass_on_plane(part):
        for step in (1, 2, 3):
            z_copy(part, step).wait_recv()
            for chip in (1, 2):
                plane_copy(part, step, chip).start()
            sibling_copy(part, step, 0).start()

    def pass_on_diagonal(part, steps):
        for step in steps:
            for chip in (1, 2):
                plane_copy(part, step, chip).wait_recv()
                if chip == 1 + step % 2:
                    plane_copy(part, step, 3).start()
                sibling_copy(part, step, chip).start()

    def pass_on_sibling(part):
        for step in range(4):
            plane_copy(part, step, 3).wait_recv()
            sibling_copy(part, step, 3).start()

    def arrived_dense(part):
        for step in range(4):
            for chip in range(4):
                sibling_copy(part, step, chip).wait_recv()

    def sent_dense(part):
        for step in range(4):
            if step:
                z_copy(part, step).wait_send()
            for chip in range(4):
                if chip:
                    plane_copy(part, step, chip).wait_send()
                sibling_copy(part, step, chip).wait_send()

    token_arrays = (cot_all, n2_all)

    parts = (0, 512, 1024)

    def cube_device(bits):
        return (xor(plane, bits & 1), xor(member, bits & 6))

    def part_order(part):
        return [1 << ((part + k) % 3) for k in range(3)]

    def token_z(kind):
        block = token_arrays[kind].at[token_rows(0, 0)]
        return remote(block, block, tz_sems, (kind,), (xor(plane, 1), member))

    def token_where(kind, plane_step):
        base = xor(parity, plane_step) * 8 * tokens
        return token_arrays[kind], tok_sems, (kind, plane_step), 0, None, base

    quarter = w_in_ref.shape[0]
    quarter_out = w_out_ref.shape[0]

    def win_copy(step, piece):
        other = xor(parity, step % 2)
        source = w_in_ref.at[:, at_rows(piece * FF + other * half, half, 128)]
        target = w_in_half.at[at_rows(plane * quarter, quarter), pl.ds(piece * half, half)]
        if step == 0:
            return pltpu.make_async_copy(source, target, local_sems.at[piece])
        return remote(source, target, win_sems, (step, piece), (xor(plane, step), member))

    out_half = lax.div(plane, 2)

    def wout_send(turn):
        target = w_out_half.at[at_rows(parity * quarter_out, quarter_out)]
        device = (out_half + 2 * turn, member)
        return remote(w_out_ref, target, wout_sems, (turn,), device, (parity,))

    def wout_arrived(slot):
        target = w_out_half.at[at_rows(slot * quarter_out, quarter_out)]
        return remote(w_out_ref, target, wout_sems, (slot,), (xor(plane, 1), member))

    def wout_local():
        return pltpu.make_async_copy(
            w_out_ref,
            w_out_half.at[at_rows(parity * quarter_out, quarter_out)],
            local_sems.at[2],
        )

    def expert_start():
        for step in (1, 3, 2):
            for piece in (0, 1):
                win_copy(step, piece).start()
        for piece in (0, 1):
            win_copy(0, piece).start()
        for turn in (0, 1):

            @pl.when(out_half + 2 * turn != plane)
            def _():
                wout_send(turn).start()

        @pl.when(out_half == parity)
        def _():
            wout_local().start()

    def expert_finish():
        for step in (1, 3, 2):
            for piece in (0, 1):
                win_copy(step, piece).wait()
        for piece in (0, 1):
            win_copy(0, piece).wait()
        for slot in (0, 1):

            @pl.when(parity * 2 + slot != plane)
            def _():
                wout_arrived(slot).wait_recv()

        for turn in (0, 1):

            @pl.when(out_half + 2 * turn != plane)
            def _():
                wout_send(turn).wait_send()

        @pl.when(out_half == parity)
        def _():
            wout_local().wait()

    def gather_copy(array, sems, index, lead=(), start=0, stop=None, base=0):
        stop = array.shape[1] if stop is None else stop
        middle = (start + stop) // 256 * 128
        owner_step, device_step = ((0, 2), (0, 4), (2, 4), (4, 2), (0, 1), (2, 1), (4, 1), (6, 1))[
            index
        ]
        if index == 2:
            stop = middle
        if index == 3:
            start = middle
        block = at_rows(base + xor(member, owner_step) * tokens, tokens, 128)
        piece = array.at[block, pl.ds(start, stop - start)]
        return remote(piece, piece, sems, lead + (index,), in_plane(device_step))

    def gather_start(*where):
        for index in (0, 1, 4):
            gather_copy(where[0], where[1], index, *where[2:]).start()

    def gather_pass(*where):
        for index in (0, 1):
            gather_copy(where[0], where[1], index, *where[2:]).wait_recv()
            gather_copy(where[0], where[1], 2 + index, *where[2:]).start()
            gather_copy(where[0], where[1], 5 + index, *where[2:]).start()

    def gather_pass_last(*where):
        for index in (2, 3):
            gather_copy(where[0], where[1], index, *where[2:]).wait_recv()
        gather_copy(where[0], where[1], 7, *where[2:]).start()

    def gather_sent(*where):
        for index in range(8):
            gather_copy(where[0], where[1], index, *where[2:]).wait_send()

    def gather_finish(*where):
        gather_sent(*where)
        for index in range(4, 8):
            gather_copy(where[0], where[1], index, *where[2:]).wait_recv()

    pass_on_plane(0)
    pass_on_plane(1)
    pass_on_diagonal(0, range(4))
    pass_on_sibling(0)
    arrived_dense(0)
    token_z(0).start()
    expert_start()
    aux = full_a[:, pl.ds(2 * kv_width, 128)]
    pick = (
        lax.broadcasted_iota(jnp.int32, (16, 128), 1)
        == lax.broadcasted_iota(jnp.int32, (16, 128), 0) + EXPERT_LANES
    ).astype(bf16)
    gain_buf[...] = product_rows(pick, aux)
    gain_a = gain_buf[pl.ds(0, 1), :]
    gain_m = gain_buf[pl.ds(1, 1), :]
    residual = x_ref[...].astype(f32)
    normed = (residual * norm_factor(residual) * gain_a).astype(bf16)
    normed_buf[...] = normed
    cos_part = rope_ref[:, pl.ds(0, HEAD_DIM)]
    sin_part = rope_ref[:, pl.ds(HEAD_DIM, HEAD_DIM)]

    def turned(values, orient):
        swapped = pltpu.roll(values, HEAD_DIM // 2, 1)
        return values * cos_part + swapped * (sin_part * orient)

    kv_rows = product(normed, full_a[:, pl.ds(0, 2 * kv_width)])
    own_block = at_rows(member * tokens, tokens, 128)
    for part in range(2 * KEY_VALUE_HEADS):
        piece = kv_rows[:, part * HEAD_DIM : (part + 1) * HEAD_DIM]
        if part < KEY_VALUE_HEADS:
            piece = turned(piece, 1.0)
        kv_all[own_block, pl.ds(part * HEAD_DIM, HEAD_DIM)] = piece.astype(bf16)
    gather_start(kv_all, kv_sems)
    turn_send[0] = jnp.transpose(normed).reshape(turn_send.shape[1:])

    def turn_copy(kind, step):
        return remote(
            turn_send.at[kind, :, xor(member, step)],
            turn_recv.at[kind, :, :, at_rows(member * tokens, tokens, 128)],
            turn_sems,
            (kind, step),
            in_plane(step),
        )

    def turn_start(kind):
        for step in range(1, 8):
            turn_copy(kind, step).start()
        turn_recv[kind, :, :, at_rows(member * tokens, tokens, 128)] = turn_send[
            kind, :, pl.ds(member, 1)
        ].reshape(turn_recv.shape[1], rows, tokens)

    turn_start(0)
    pass_on_plane(2)
    gather_pass(kv_all, kv_sems)
    pass_on_diagonal(1, range(4))
    gather_start(*token_where(0, 0))
    gather_pass_last(kv_all, kv_sems)
    pass_on_sibling(1)
    token_z(0).wait_recv()
    gather_start(*token_where(0, 1))
    arrived_dense(1)
    spill_b_copy = pltpu.make_async_copy(
        arena.at[pl.ds(0, width)], spill_b, local_sems.at[3]
    )
    spill_b_copy.start()
    for head in range(QUERY_HEADS):
        if head % 2 == 0:
            pair = product(normed, arena[pl.ds(0, width), pl.ds(head * HEAD_DIM, 2 * HEAD_DIM)])
        piece = pair[:, (head % 2) * HEAD_DIM : (head % 2 + 1) * HEAD_DIM]
        q_rows[pl.ds(head * tokens, tokens)] = turned(piece, 1.0).astype(bf16)
    gather_finish(kv_all, kv_sems)
    for group in range(KEY_VALUE_HEADS):
        k_t[group] = jnp.transpose(kv_all[:, pl.ds(group * HEAD_DIM, HEAD_DIM)])
        v_t[group] = jnp.transpose(kv_all[:, pl.ds(kv_width + group * HEAD_DIM, HEAD_DIM)])
    pass_on_diagonal(2, range(4))

    seq_len = kv_all.shape[0]
    pairs = QUERY_HEADS // 2
    pairs_per_group = pairs // KEY_VALUE_HEADS
    key_index = lax.broadcasted_iota(jnp.int32, (seq_len, 2 * tokens), 0)
    query_index = member * tokens + lax.rem(
        lax.broadcasted_iota(jnp.int32, (seq_len, 2 * tokens), 1), tokens
    )
    allowed = key_index <= query_index

    def pair_scores(pair, group):
        queries = q_rows[at_rows(pair * 2 * tokens, 2 * tokens, 128)]
        keys = kv_all[:, at_rows(group * HEAD_DIM, HEAD_DIM, 128)]
        scores = product_rows(keys, queries) * score_scale
        return jnp.where(allowed, scores, masked_score), queries

    def attend(pair, carry):
        group = lax.div(pair, pairs_per_group)
        scores, _ = pair_scores(pair, group)
        peak = jnp.max(scores, axis=0, keepdims=True)
        expo_vals = jnp.exp(scores - peak)
        sums = jnp.sum(expo_vals, axis=0, keepdims=True)
        probs = (expo_vals / sums).astype(bf16)
        lse_buf[pair] = jnp.broadcast_to(peak + jnp.log(sums), (8, 2 * tokens))
        part = product(v_t[group], probs)
        for inner in (0, 1):
            piece = part[:, inner * tokens : (inner + 1) * tokens].astype(bf16)
            attn_buf[2 * pair + inner] = piece
        return carry

    lax.fori_loop(0, pairs, attend, 0)
    pass_on_sibling(2)
    gather_pass(*token_where(0, 0))
    attn_t = attn_buf[...].reshape(width, tokens)
    turn_send[1] = attn_t.reshape(turn_send.shape[1:])
    attn = jnp.transpose(attn_t)
    arrived_dense(2)
    spill_c_copy = pltpu.make_async_copy(
        arena.at[pl.ds(width, width)], spill_c, local_sems.at[4]
    )
    spill_c_copy.start()
    for start in range(0, width, 512):
        after_buf[:, pl.ds(start, 512)] = x_ref[:, pl.ds(start, 512)].astype(f32) + product(
            attn, arena[pl.ds(width, width), pl.ds(start, 512)]
        )
    after = after_buf[...]
    normed_two = (after * norm_factor(after) * gain_m).astype(bf16)
    n2_all[token_rows(0, 0)] = normed_two
    spill_b_copy.wait()
    spill_c_copy.wait()
    for part in range(3):
        sent_dense(part)
    token_z(1).start()
    gather_start(*token_where(1, 0))
    turn_send[2] = jnp.transpose(normed_two).reshape(turn_send.shape[1:])
    gather_pass(*token_where(0, 1))
    gather_pass_last(*token_where(0, 0))
    gather_pass_last(*token_where(0, 1))
    token_z(1).wait_recv()
    gather_start(*token_where(1, 1))
    for plane_step in (0, 1):
        gather_finish(*token_where(0, plane_step))
    expert_finish()

    own_lane = lax.broadcasted_iota(jnp.int32, (2 * tokens, 128), 1) == member
    low_lane = lax.broadcasted_iota(jnp.int32, (2 * tokens, 128), 1) == member + 64
    message = 2 * tokens
    stage_base, sib_base, sum_base, recv_base = 0, 2 * message, 4 * message, 12 * message

    def arena_slot(base, slot):
        return at_rows(base + slot * message, message, 128)

    def sib_copy(slot):
        return remote(
            arena.at[arena_slot(stage_base, slot)],
            arena.at[arena_slot(sib_base, slot)],
            sib_sems,
            (slot,),
            sibling,
        )

    def sib_gate_copy():
        return remote(
            gate_buf.at[pl.ds(8, 8)], gate_buf.at[pl.ds(16, 8)], sib_sems, (2,), sibling
        )

    def ret_copy(part, held, stage):
        first, second, third = part_order(part)
        far = lambda bit: jnp.where(held & bit > 0, 1, 0) if not isinstance(held, int) else held // bit % 2
        slot = (far(second) + 2 * far(third), 4 + far(third), 6)[stage]
        columns = pl.ds(parts[part], 512)
        return remote(
            arena.at[arena_slot(sum_base, held), columns],
            arena.at[arena_slot(recv_base, slot), columns],
            ret_sems,
            (part, slot),
            cube_device((first, second, third)[stage]),
        )

    def ret_arrived(part, slot):
        columns = pl.ds(parts[part], 512)
        block = arena.at[arena_slot(recv_base, slot), columns]
        return remote(block, block, ret_sems, (part, slot), sibling)

    def ret_gate_copy(held):
        return remote(
            gate_buf.at[held], gate_buf.at[24 + held], gate_sems, (held,), cube_device(held)
        )

    def halves(values, first):
        return jnp.where(first, values[:tokens], values[tokens:])

    def block_rows(held):
        other_plane = xor(parity, held & 1)
        chip = xor(lax.div(member, 2), lax.div(held, 2))
        return at_rows((other_plane * 4 + chip) * 2 * tokens, 2 * tokens, 128)

    def first_step(held, carry):
        @pl.when(held == 1)
        def _():
            gather_pass(*token_where(1, 0))

        @pl.when(held == 2)
        def _():
            gather_pass(*token_where(1, 1))

        @pl.when(held == 4)
        def _():
            gather_pass_last(*token_where(1, 0))
            gather_pass_last(*token_where(1, 1))

        own = token_rows(held & 1, held & 6)
        remote(
            n2_all.at[own],
            n2_all.at[own],
            tok_sems,
            (1, held & 1, 4 + lax.div(held, 2)),
            sibling,
        ).wait_recv()
        here = block_rows(held)
        token_block = n2_all[here, :]
        gate_up = product(token_block, w_in_half[...])
        gates = masked_gates(
            token_block,
            full_a[:, pl.ds(2 * kv_width, 128)],
            cot_all[here, pl.ds(width, 128)],
        )
        gate = jnp.sum(jnp.where(own_lane, gates, 0.0), axis=1, keepdims=True)
        gate_half = gate_up[:, :half]
        up_half = gate_up[:, half:]
        sigmoid_vals = 1.0 / (1.0 + jnp.exp(-gate_half))
        silu_vals = gate_half * sigmoid_vals
        hidden = silu_vals * up_half
        hidden_all[here, :] = (gate * hidden).astype(bf16)
        back = product_rows(cot_all[here, pl.ds(0, width)], w_out_half[...])
        gate_grad = jnp.sum(hidden * back, axis=1, keepdims=True)
        act_grad = gate * back
        gate_part = act_grad * up_half * sigmoid_vals * (1.0 + gate_half * (1.0 - sigmoid_vals))
        g_all[here, pl.ds(0, half)] = gate_part.astype(bf16)
        g_all[here, pl.ds(half, half)] = (act_grad * silu_vals).astype(bf16)
        gate_high = gate_grad.astype(bf16).astype(f32)
        gate_lanes = jnp.where(own_lane, gate_high, 0.0) + jnp.where(
            low_lane, gate_grad - gate_high, 0.0
        )
        gate_buf[held] = halves(gate_lanes, core == 0).astype(bf16)
        gate_buf[8 + held] = halves(gate_lanes, core == 1).astype(bf16)
        return carry

    lax.fori_loop(0, 8, first_step, 0)
    token_z(0).wait_send()
    token_z(1).wait_send()
    for plane_step in (0, 1):
        gather_sent(*token_where(1, plane_step))
    sib_gate_copy().start()

    def second_step(turn, carry):
        slot2 = lax.rem(turn, 2)
        held = 7 - turn
        here = block_rows(held)
        hidden = hidden_all[here, :]
        g_block = g_all[here, :]

        @pl.when(turn >= 2)
        def _():
            sib_copy(slot2).wait_send()
            pl.semaphore_wait(credit_sem, 1)

        send_first = core == 1
        stage = stage_base + slot2 * message
        place = sum_base + held * message
        sib_start = sib_base + slot2 * message
        for start in range(0, width, 512):
            columns = pl.ds(start, 512)
            out_part = product(hidden, w_out_half[:, columns])
            in_part = product_rows(g_block, w_in_half[columns, :])
            arena[at_rows(stage, tokens, 128), columns] = halves(out_part, send_first).astype(bf16)
            arena[at_rows(stage + tokens, tokens, 128), columns] = halves(
                in_part, send_first
            ).astype(bf16)
            arena[at_rows(place, tokens, 128), columns] = halves(out_part, core == 0).astype(bf16)
            arena[at_rows(place + tokens, tokens, 128), columns] = halves(
                in_part, core == 0
            ).astype(bf16)
        sib_copy(slot2).start()
        sib_copy(slot2).wait_recv()
        both = at_rows(place, message, 128)
        arena[both] = (
            arena[both].astype(f32) + arena[at_rows(sib_start, message, 128)].astype(f32)
        ).astype(bf16)

        @pl.when(turn < 6)
        def _():
            pl.semaphore_signal(credit_sem, inc=1, device_id=sibling, device_id_type=MESH)

        for part in range(3):

            @pl.when(held & (1 << part) > 0)
            def _():
                ret_copy(part, held, 0).start()

        return carry

    for kind in (1, 2):
        turn_start(kind)
    lax.fori_loop(0, 8, second_step, 0)
    for slot in (0, 1):
        sib_copy(slot).wait_send()
    sib_gate_copy().wait()
    gate_buf[pl.ds(0, 8)] = (
        gate_buf[pl.ds(0, 8)].astype(f32) + gate_buf[pl.ds(16, 8)].astype(f32)
    ).astype(bf16)
    for held in range(1, 8):
        ret_gate_copy(held).start()

    def ret_sum(part, held, slots):
        columns = pl.ds(parts[part], 512)
        total = arena[arena_slot(sum_base, held), columns].astype(f32)
        for slot in slots:
            total = total + arena[arena_slot(recv_base, slot), columns].astype(f32)
        return total

    for part in range(3):
        first, second, third = part_order(part)
        for held, slot in ((second, 1), (second | third, 3)):
            ret_arrived(part, slot).wait_recv()
            arena[arena_slot(sum_base, held), pl.ds(parts[part], 512)] = ret_sum(
                part, held, (slot,)
            ).astype(bf16)
            ret_copy(part, held, 1).start()

    def gin_copy(step):
        source = w_in_half.at[at_rows(xor(plane, step) * quarter, quarter)]
        if step == 0:
            return pltpu.make_async_copy(source, grad_in_ref.at[0], local_sems.at[5])
        return remote(
            source, grad_in_ref.at[step], gin_sems, (step,), (xor(plane, step), member)
        )

    for step in (2, 1, 3, 0):
        start = xor(plane, step) * quarter
        for piece in range(0, quarter, 128):
            columns = n2_all[:, at_rows(start + piece, 128, 128)]
            w_in_half[at_rows(start + piece, 128, 128)] = product_columns(
                columns, g_all[...]
            ).astype(bf16)
        if step == 2:
            gin_copy(2).start()

    def gout_copy(slot):
        source = w_out_half.at[pl.ds(slot * quarter_out, quarter_out)]
        target = grad_out_ref.at[out_half]
        device = (parity * 2 + slot, member)
        return remote(source, target, gout_sems, (slot,), device, (out_half,))

    def gout_local(slot):
        return pltpu.make_async_copy(
            w_out_half.at[pl.ds(slot * quarter_out, quarter_out)],
            grad_out_ref.at[out_half],
            local_sems.at[6],
        )

    def gout_arrived(turn):
        source = w_out_half.at[pl.ds(0, quarter_out)]
        return remote(source, grad_out_ref.at[turn], gout_sems, (turn,), (xor(plane, 1), member))

    for start in range(0, half, 128):
        w_out_half[pl.ds(start, 128)] = product_columns(
            hidden_all[:, pl.ds(start, 128)], cot_all[:, pl.ds(0, width)]
        ).astype(bf16)
    own_n2 = n2_all[token_rows(0, 0), :]
    own_mask = mask_ref[...]
    own_gates = masked_gates(own_n2, full_a[:, pl.ds(2 * kv_width, 128)], own_mask)
    for part in range(3):
        third = part_order(part)[2]
        for slot in (2, 5):
            ret_arrived(part, slot).wait_recv()
        arena[arena_slot(sum_base, third), pl.ds(parts[part], 512)] = ret_sum(
            part, third, (2, 5)
        ).astype(bf16)
        ret_copy(part, third, 2).start()
    gin_copy(0).start()

    load_b = pltpu.make_async_copy(
        spill_b, cot_all.at[pl.ds(0, width), pl.ds(0, width)], local_sems.at[3]
    )
    load_c = pltpu.make_async_copy(spill_c, n2_all.at[pl.ds(0, width)], local_sems.at[4])
    load_b.start()
    load_c.start()

    for part in range(3):
        for slot in (0, 4, 6):
            ret_arrived(part, slot).wait_recv()
    totals = [ret_sum(part, 0, (0, 4, 6)) for part in range(3)]
    total_out = after_buf[...] + jnp.concatenate([total[:tokens] for total in totals], axis=1)
    total_in = jnp.concatenate([total[tokens:] for total in totals], axis=1)
    total_gate = gate_buf[0].astype(f32)
    for held in range(1, 8):
        ret_gate_copy(held).wait_recv()
        total_gate = total_gate + gate_buf[24 + held].astype(f32)
    for step in (3, 1):
        gin_copy(step).start()
    for slot in (0, 1):

        @pl.when(parity * 2 + slot != plane)
        def _():
            gout_copy(slot).start()

        @pl.when(parity * 2 + slot == plane)
        def _():
            gout_local(slot).start()

    block_out_ref[...] = total_out.astype(bf16)
    gate_grad = total_gate + pltpu.roll(total_gate, 64, 1)
    gate_inner = jnp.sum(own_gates * gate_grad, axis=1, keepdims=True)
    logit_grad = own_gates * (gate_grad - gate_inner)
    lg_parts = split_three(logit_grad)
    aux_now = full_a[:, pl.ds(2 * kv_width, 128)]
    for part in lg_parts:
        total_in = total_in + product_rows(part, aux_now)
    after = after_buf[...]

    def norm_backward(values, gain, grad):
        factor = norm_factor(values)
        scaled = grad * gain
        gain_row = jnp.sum(grad * values * factor, axis=0, keepdims=True)
        inner = jnp.mean(scaled * values, axis=-1, keepdims=True)
        return factor * scaled - values * factor * factor * factor * inner, gain_row

    two_back, gain_m_row = norm_backward(after, gain_buf[pl.ds(1, 1), :], total_in)
    mid = cot_ref[...].astype(f32) + two_back
    after_buf[...] = mid
    out_grad = mid.astype(bf16)
    og_all[own_block, pl.ds(0, width)] = out_grad
    og_all[own_block, pl.ds(width, 128)] = (
        lg_parts[0].astype(f32)
        + pltpu.roll(lg_parts[1].astype(f32), 8, 1)
        + pltpu.roll(lg_parts[2].astype(f32), 16, 1)
    ).astype(bf16)

    gather_start(og_all, og_sems)
    load_c.wait()
    for head in range(0, QUERY_HEADS, 2):
        pair = product_rows(out_grad, n2_all[pl.ds(head * HEAD_DIM, 2 * HEAD_DIM), :])
        for inner in (0, 1):
            do_rows[pl.ds((head + inner) * tokens, tokens)] = pair[
                :, inner * HEAD_DIM : (inner + 1) * HEAD_DIM
            ].astype(bf16)
    gather_pass(og_all, og_sems)

    def dkv_copy(group, step):
        return remote(
            g_all.at[
                at_rows(xor(member, step) * tokens, tokens, 128),
                pl.ds(group * 2 * HEAD_DIM, 2 * HEAD_DIM),
            ],
            dkv_recv.at[group, step],
            dkv_sems,
            (group, step),
            in_plane(step),
        )

    planes = turn_recv.shape[1]

    def dense_rows(piece, step):
        return at_rows((piece * planes + xor(plane, step)) * rows, rows)

    def kv_grad_copy(step):
        source = arena.at[dense_rows(0, step), pl.ds(0, 2 * kv_width)]
        if step == 0:
            return pltpu.make_async_copy(source, grad_kv_ref.at[0], local_sems.at[0])
        device = (xor(plane, step), member)
        return remote(source, grad_kv_ref.at[step], dense_sems, (0, step), device)

    def pair_rows(piece, which):
        return pl.ds(width + ((piece - 1) * 2 + which) * rows, rows)

    def dense_copy(piece, step):
        columns = pl.ds((piece - 1) * width, width)
        if step == 2:
            target = grad_dense_ref.at[1, :, columns]
            device = (xor(plane, 2), member)
        else:
            target = n2_all.at[pair_rows(piece, step // 2)]
            device = (xor(plane, 1), member)
        return remote(arena.at[dense_rows(piece, step)], target, dense_sems, (piece, step), device)

    def dense_own(piece):
        return pltpu.make_async_copy(
            arena.at[dense_rows(piece, 0)],
            grad_dense_ref.at[0, :, pl.ds((piece - 1) * width, width)],
            local_sems.at[piece],
        )

    def dense_start(piece):
        for step in (3, 1):
            dense_copy(piece, step).start()

    def dense_pass(piece):
        for which, step in ((1, 2), (0, 0)):
            dense_copy(piece, 1 + 2 * which).wait_recv()
            block = dense_rows(piece, step)
            arena[block] = (
                arena[block].astype(f32) + n2_all[pair_rows(piece, which)].astype(f32)
            ).astype(bf16)
            if step:
                dense_copy(piece, 2).start()
            else:
                dense_own(piece).start()

    for group in range(KEY_VALUE_HEADS):
        values = kv_all[:, pl.ds(kv_width + group * HEAD_DIM, HEAD_DIM)]
        dk = jnp.zeros((seq_len, HEAD_DIM), f32)
        dv = jnp.zeros((seq_len, HEAD_DIM), f32)
        for pair in range(group * pairs_per_group, (group + 1) * pairs_per_group):
            scores, queries = pair_scores(pair, group)
            probs = jnp.exp(scores - lse_buf[pair][0:1])
            grads = do_rows[pl.ds(pair * 2 * tokens, 2 * tokens)]
            prob_grad = product_rows(values, grads)
            row_dot = jnp.sum(probs * prob_grad, axis=0, keepdims=True)
            score_grad = (probs * (prob_grad - row_dot)).astype(bf16)
            dk = dk + product(score_grad, queries)
            dv = dv + product(probs.astype(bf16), grads)
            dq = product(k_t[group], score_grad) * score_scale
            for inner in (0, 1):
                piece = jnp.transpose(dq[:, inner * tokens : (inner + 1) * tokens])
                qg_all[own_block, pl.ds((2 * pair + inner) * HEAD_DIM, HEAD_DIM)] = turned(
                    piece, -1.0
                ).astype(bf16)
        start = group * 2 * HEAD_DIM
        g_all[pl.ds(0, seq_len), pl.ds(start, HEAD_DIM)] = (dk * score_scale).astype(bf16)
        g_all[pl.ds(0, seq_len), pl.ds(start + HEAD_DIM, HEAD_DIM)] = dv.astype(bf16)
        for step in range(1, 8):
            dkv_copy(group, step).start()
        span = width // KEY_VALUE_HEADS
        gather_start(qg_all, qg_sems, (group,), group * span, (group + 1) * span)
        if group == 0:
            gather_pass_last(og_all, og_sems)

    gather_pass(qg_all, qg_sems, (0,), 0, span)

    for group in range(KEY_VALUE_HEADS):
        start = group * 2 * HEAD_DIM
        dk = g_all[own_block, pl.ds(start, HEAD_DIM)].astype(f32)
        dv = g_all[own_block, pl.ds(start + HEAD_DIM, HEAD_DIM)].astype(f32)
        for step in range(1, 8):
            dkv_copy(group, step).wait_recv()
            dk = dk + dkv_recv[group, step, :, pl.ds(0, HEAD_DIM)].astype(f32)
            dv = dv + dkv_recv[group, step, :, pl.ds(HEAD_DIM, HEAD_DIM)].astype(f32)
        kvg_all[own_block, pl.ds(group * HEAD_DIM, HEAD_DIM)] = turned(dk, -1.0).astype(bf16)
        kvg_all[own_block, pl.ds(kv_width + group * HEAD_DIM, HEAD_DIM)] = dv.astype(bf16)
    gather_start(kvg_all, kvg_sems)
    gather_finish(og_all, og_sems)
    for kind in range(3):
        for step in range(1, 8):
            turn_copy(kind, step).wait()
    turned_attn = turn_recv[1].reshape(planes * rows, seq_len)
    for start in range(0, width, 512):
        arena[pl.ds(2 * planes * rows, planes * rows), pl.ds(start, 512)] = product(
            turned_attn, og_all[:, pl.ds(start, 512)]
        ).astype(bf16)
    dense_start(2)
    router_part = product(
        turn_recv[2].reshape(planes * rows, seq_len), og_all[:, pl.ds(width, 128)]
    )

    gather_pass(qg_all, qg_sems, (1,), span, 2 * span)
    gather_pass(kvg_all, kvg_sems)
    for group in range(KEY_VALUE_HEADS):
        gather_pass_last(qg_all, qg_sems, (group,), group * span, (group + 1) * span)
    gather_pass_last(kvg_all, kvg_sems)

    load_b.wait()
    own_kvg = kvg_all[own_block, :]
    own_qg = qg_all[own_block, :]
    normed_grad = product_rows(own_kvg, full_a[:, pl.ds(0, 2 * kv_width)]) + product_rows(
        own_qg, cot_all[pl.ds(0, width), pl.ds(0, width)]
    )
    one_back, gain_a_row = norm_backward(
        x_ref[...].astype(f32), gain_buf[pl.ds(0, 1), :], normed_grad
    )
    dx_ref[...] = after_buf[...] + one_back
    line = lax.broadcasted_iota(jnp.int32, (128, width), 0)
    gain_lines = jnp.zeros((128, width), f32)
    for offset, part in enumerate(split_three(gain_a_row) + split_three(gain_m_row)):
        gain_lines = jnp.where(line == 32 + offset, part.astype(f32), gain_lines)
    turn_send[3] = jnp.transpose(gain_lines.astype(bf16)).reshape(turn_send.shape[1:])
    turn_start(3)

    turned_normed = turn_recv[0].reshape(planes * rows, seq_len)
    for group in range(KEY_VALUE_HEADS):
        gather_finish(qg_all, qg_sems, (group,), group * span, (group + 1) * span)
    for start in range(0, width, 512):
        arena[pl.ds(planes * rows, planes * rows), pl.ds(start, 512)] = product(
            turned_normed, qg_all[:, pl.ds(start, 512)]
        ).astype(bf16)
    dense_start(1)
    dense_pass(2)
    gather_finish(kvg_all, kvg_sems)
    arena[pl.ds(0, planes * rows), pl.ds(0, 2 * kv_width)] = product(
        turned_normed, kvg_all[...]
    ).astype(bf16)
    for step in (2, 3, 1, 0):
        kv_grad_copy(step).start()
    dense_pass(1)
    for step in range(1, 8):
        turn_copy(3, step).wait()
    aux_total = router_part
    for block in range(8):
        aux_total = aux_total + turn_recv[3, :, :, pl.ds(block * tokens, tokens)].reshape(
            planes * rows, tokens
        ).astype(f32)
    aux_send[...] = aux_total.reshape(planes, rows, 128)

    def aux_copy(step):
        return remote(
            aux_send.at[xor(plane, step)],
            grad_aux_ref.at[step],
            aux_sems,
            (step,),
            (xor(plane, step), member),
        )

    for step in (1, 2, 3):
        aux_copy(step).start()
    own_aux = pltpu.make_async_copy(aux_send.at[plane], grad_aux_ref.at[0], local_sems.at[7])
    own_aux.start()

    for held in range(1, 8):
        ret_gate_copy(held).wait_send()
    for part in range(3):
        first, second, third = part_order(part)
        for held in range(8):
            if held & first:
                ret_copy(part, held, 0).wait_send()
        for held in (second, second | third):
            ret_copy(part, held, 1).wait_send()
        ret_copy(part, third, 2).wait_send()
    for group in range(KEY_VALUE_HEADS):
        for step in range(1, 8):
            dkv_copy(group, step).wait_send()
    gin_copy(0).wait()
    for step in (1, 2, 3):
        gin_copy(step).wait()
    for slot in (0, 1):

        @pl.when(parity * 2 + slot != plane)
        def _():
            gout_copy(slot).wait_send()

        @pl.when(parity * 2 + slot == plane)
        def _():
            gout_local(slot).wait()

    for turn in (0, 1):

        @pl.when(out_half + 2 * turn != plane)
        def _():
            gout_arrived(turn).wait_recv()

    for step in range(4):
        kv_grad_copy(step).wait()
    for piece in (1, 2):
        dense_own(piece).wait()
        dense_copy(piece, 2).wait()
        for step in (1, 3):
            dense_copy(piece, step).wait_send()
    for step in (1, 2, 3):
        aux_copy(step).wait()
    own_aux.wait()


EXPERT_LANES = 8


def fast_body(
    tokens,
    cotangent,
    routes,
    gain_attn,
    w_query,
    key_weight,
    value_weight,
    w_output,
    gain_moe,
    w_router,
    w_in,
    w_out,
):
    f32, bf16 = jnp.float32, jnp.bfloat16
    total_rows, width = tokens.shape
    rows = w_query.shape[1]
    planes = lax.axis_size("dp")
    members = lax.axis_size("expert")
    seq_len = total_rows * members
    kv_width = key_weight.shape[2]
    quarter = w_in.shape[1]
    quarter_out = w_out.shape[1]
    half = FF // 2
    positions = lax.axis_index("expert") * total_rows + jnp.arange(total_rows, dtype=jnp.int32)
    cos_table, sin_table = rope_tables(positions, HEAD_DIM)
    rope = jnp.concatenate([cos_table, cos_table, -sin_table, sin_table], axis=1)
    lanes = jnp.arange(128, dtype=jnp.int32)
    mask = jnp.any(routes[0][:, :, None] == lanes[None, None, :], axis=1).astype(bf16)
    padding = jnp.zeros((rows, 128 - EXPERT_LANES - 2), bf16)
    shard_a = jnp.concatenate(
        [
            key_weight[0],
            value_weight[0],
            w_router[0],
            gain_attn[0][:, None],
            gain_moe[0][:, None],
            padding,
        ],
        axis=1,
    )
    in_vmem = pl.BlockSpec(memory_space=pltpu.VMEM)
    anywhere = pl.BlockSpec(memory_space=pl.ANY)
    pair_rows = 2 * seq_len
    shape = jax.ShapeDtypeStruct
    dma = pltpu.SemaphoreType.DMA
    heads = QUERY_HEADS
    (
        block_out,
        tokens_grad,
        grad_in,
        grad_out,
        grad_dense,
        grad_kv,
        grad_aux,
        _,
        _,
    ) = pl.pallas_call(
        layer_kernel,
        out_shape=(
            shape((total_rows, width), bf16),
            shape((total_rows, width), f32),
            shape((planes, quarter, 2 * half), bf16),
            shape((2, quarter_out, width), bf16),
            shape((2, rows, 2 * width), bf16),
            shape((planes, rows, 2 * kv_width), bf16),
            shape((planes, rows, 128), f32),
            shape((width, width), bf16),
            shape((width, width), bf16),
        ),
        in_specs=[in_vmem] * 7 + [anywhere] * 2,
        out_specs=(in_vmem,) * 2 + (anywhere,) * 7,
        scratch_shapes=[
            pltpu.VMEM((pair_rows, width), bf16),
            pltpu.VMEM((pair_rows, width + 128), bf16),
            pltpu.VMEM((width, 2 * kv_width + 128), bf16),
            pltpu.VMEM((38 * total_rows, width), bf16),
            pltpu.VMEM((32, total_rows, 128), bf16),
            pltpu.VMEM((width, 2 * half), bf16),
            pltpu.VMEM((half, width), bf16),
            pltpu.VMEM((pair_rows, half), bf16),
            pltpu.VMEM((pair_rows, 2 * half), bf16),
            pltpu.VMEM((seq_len, 2 * kv_width), bf16),
            pltpu.VMEM((KEY_VALUE_HEADS, HEAD_DIM, seq_len), bf16),
            pltpu.VMEM((KEY_VALUE_HEADS, HEAD_DIM, seq_len), bf16),
            pltpu.VMEM((heads * total_rows, HEAD_DIM), bf16),
            pltpu.VMEM((heads * total_rows, HEAD_DIM), bf16),
            pltpu.VMEM((total_rows, width), bf16),
            pltpu.VMEM((heads, HEAD_DIM, total_rows), bf16),
            pltpu.VMEM((total_rows, width), f32),
            pltpu.VMEM((heads // 2, 8, 2 * total_rows), f32),
            pltpu.VMEM((4, planes, members, rows, total_rows), bf16),
            pltpu.VMEM((4, planes, rows, seq_len), bf16),
            pltpu.VMEM((seq_len, width + 128), bf16),
            pltpu.VMEM((seq_len, width), bf16),
            pltpu.VMEM((seq_len, 2 * kv_width), bf16),
            pltpu.VMEM((KEY_VALUE_HEADS, members, total_rows, 2 * HEAD_DIM), bf16),
            pltpu.VMEM((planes, rows, 128), f32),
            pltpu.VMEM((16, width), f32),
            dma((2, 3, 4)),
            dma((2, 3, 4, 4)),
            dma((2, 3, 4, 4)),
            dma((2, 8)),
            dma((2, 2, 2, 8)),
            dma((2, 2)),
            dma((2, 4, 8)),
            dma((2, 4, 2)),
            dma((2, 2)),
            dma((2, 4)),
            dma((2, 3, 7)),
            dma((2, 8)),
            dma((2, 4)),
            dma((2, 2)),
            dma((2, 8)),
            dma((2, 2, 8)),
            dma((2, 8)),
            dma((2, 2, 8)),
            dma((2, 3, 4)),
            dma((2, 4)),
            dma((8,)),
            pltpu.SemaphoreType.REGULAR,
        ],
        compiler_params=pltpu.CompilerParams(
            collective_id=0, has_side_effects=True, vmem_limit_bytes=63 * 2**20
        ),
    )(
        tokens,
        cotangent,
        mask,
        rope,
        shard_a,
        w_query[0],
        w_output[0],
        w_in.reshape(quarter, 2 * FF),
        w_out.reshape(quarter_out, width),
    )
    own = grad_in[0].astype(f32) + grad_in[2].astype(f32)
    other = grad_in[1].astype(f32) + grad_in[3].astype(f32)
    even = lax.rem(lax.axis_index("dp"), 2) == 0
    low, high = jnp.where(even, own, other), jnp.where(even, other, own)
    w_in_grad = jnp.concatenate(
        [low[:, :half], high[:, :half], low[:, half:], high[:, half:]], axis=1
    )
    w_out_grad = grad_out[0].astype(f32) + grad_out[1].astype(f32)
    dense = grad_dense[0].astype(f32) + grad_dense[1].astype(f32)
    dense_kv = jnp.sum(grad_kv.astype(f32), axis=0)
    aux = jnp.sum(grad_aux, axis=0)
    return (
        block_out,
        tokens_grad,
        jnp.sum(aux[:, 32:35], axis=1)[None],
        dense[None, :, :width],
        dense_kv[None, :, :kv_width],
        dense_kv[None, :, kv_width:],
        dense[None, :, width:],
        jnp.sum(aux[:, 35:38], axis=1)[None],
        (aux[:, :8] + aux[:, 8:16] + aux[:, 16:24])[None],
        w_in_grad[None, :, None, :],
        w_out_grad[None, :, None, :],
    )


def solution(mesh):
    in_specs = (
        P(("dp", "expert"), None),
        P(("dp", "expert"), None),
        P(None, ("dp", "expert"), None),
        P(None, ("dp", "expert")),
        P(None, ("dp", "expert"), None),
        P(None, ("dp", "expert"), None),
        P(None, ("dp", "expert"), None),
        P(None, ("dp", "expert"), None),
        P(None, ("dp", "expert")),
        P(None, ("dp", "expert"), None),
        P(None, "dp", "expert", None),
        P(None, "dp", "expert", None),
    )
    out_specs = (
        P(("dp", "expert"), None),
        P(("dp", "expert"), None),
        P(None, ("dp", "expert")),
        P(None, ("dp", "expert"), None),
        P(None, ("dp", "expert"), None),
        P(None, ("dp", "expert"), None),
        P(None, ("dp", "expert"), None),
        P(None, ("dp", "expert")),
        P(None, ("dp", "expert"), None),
        P(None, "dp", "expert", None),
        P(None, "dp", "expert", None),
    )
    body = fast_body if mesh.shape["dp"] == 4 and mesh.shape["expert"] == 8 else general_body
    return jax.shard_map(body, mesh=mesh, in_specs=in_specs, out_specs=out_specs, check_vma=False)
```

```python
import functools

import jax
import jax.numpy as jnp
from jax import lax
from jax.experimental import pallas as pl
from jax.experimental.pallas import tpu as pltpu
from jax.sharding import PartitionSpec as P

MESH = pl.DeviceIdType.MESH

QUERY_HEADS = 12
KEY_VALUE_HEADS = 2
HEAD_DIM = 128
FF = 768
TOP = 4


norm_eps = 1e-06
rope_base = 1000000.0
masked_score = -1e30
top_precision = lax.Precision.HIGHEST


def norm_factor(values):
    return lax.rsqrt(jnp.mean(values * values, axis=-1, keepdims=True) + norm_eps)


def norm_back(values, gain, grad_out):
    factor = norm_factor(values)
    scaled = grad_out * gain
    gain_grad = jnp.sum(grad_out * values * factor, axis=0)
    inner_mean = jnp.mean(scaled * values, axis=-1, keepdims=True)
    return (factor * scaled - values * factor * factor * factor * inner_mean, gain_grad)


def rope_tables(positions, head_size):
    half_size = head_size // 2
    inverse = rope_base ** (-(jnp.arange(half_size, dtype=jnp.float32) * 2.0 / head_size))
    angles = positions.astype(jnp.float32)[:, None] * inverse[None, :]
    return (jnp.cos(angles), jnp.sin(angles))


def rotate(values, cos_table, sin_table, orient):
    half_size = values.shape[-1] // 2
    first_half = values[..., :half_size]
    second = values[..., half_size:]
    cos_part = cos_table[:, None, :]
    sin_part = orient * sin_table[:, None, :]
    return jnp.concatenate(
        [first_half * cos_part - second * sin_part, second * cos_part + first_half * sin_part],
        axis=-1,
    )


def plan_slots(route, expert_count, capacity):
    flat_route = route.reshape(-1)
    slot_total = flat_route.shape[0]
    onehot = (flat_route[:, None] == jnp.arange(expert_count, dtype=jnp.int32)[None, :]).astype(
        jnp.int32
    )
    before = jnp.cumsum(onehot, axis=0) - onehot
    target = flat_route * capacity + jnp.sum(before * onehot, axis=1)
    source = (
        jnp.full((expert_count * capacity,), slot_total, jnp.int32)
        .at[target]
        .set(jnp.arange(slot_total, dtype=jnp.int32))
    )
    filled = source < slot_total
    return (target, jnp.minimum(source, slot_total - 1), filled)


def general_body(
    tokens,
    cotangent,
    routes,
    gain_attn,
    w_query,
    key_weight,
    value_weight,
    w_output,
    gain_moe,
    w_router,
    w_in,
    w_out,
):
    total_rows, model_width = tokens.shape
    layer_count = w_query.shape[0]
    group_count = lax.axis_size("expert")
    seq_len = total_rows * group_count
    experts_local = w_in.shape[2]
    expert_count = experts_local * group_count
    capacity = min(total_rows, total_rows * TOP * 3 // (2 * expert_count))
    heads_per_group = QUERY_HEADS // KEY_VALUE_HEADS
    score_scale = HEAD_DIM ** (-0.5)
    positions = lax.axis_index("expert") * total_rows + jnp.arange(total_rows, dtype=jnp.int32)
    cos_table, sin_table = rope_tables(positions, HEAD_DIM)
    allowed = jnp.arange(seq_len, dtype=jnp.int32)[None, :] <= positions[:, None]
    zero_bf = jnp.zeros((), jnp.bfloat16)

    def score_block(query_rows, all_keys, group_of_heads):
        grouped_q = query_rows[
            :, group_of_heads * heads_per_group : (group_of_heads + 1) * heads_per_group, :
        ]
        scores = (
            jnp.einsum(
                "rgd,kd->grk",
                grouped_q,
                all_keys[:, group_of_heads, :],
                preferred_element_type=jnp.float32,
            )
            * score_scale
        )
        return (jnp.where(allowed[None], scores, masked_score), grouped_q)

    residual = tokens.astype(jnp.float32)
    layer_number = 0
    dense_w = (
        lax.all_gather(gain_attn[layer_number], ("dp", "expert"), axis=0, tiled=True),
        lax.all_gather(w_query[layer_number], ("dp", "expert"), axis=0, tiled=True),
        lax.all_gather(key_weight[layer_number], ("dp", "expert"), axis=0, tiled=True),
        lax.all_gather(value_weight[layer_number], ("dp", "expert"), axis=0, tiled=True),
        lax.all_gather(w_output[layer_number], ("dp", "expert"), axis=0, tiled=True),
        lax.all_gather(gain_moe[layer_number], ("dp", "expert"), axis=0, tiled=True),
        lax.all_gather(w_router[layer_number], ("dp", "expert"), axis=0, tiled=True),
    )
    expert_w = (
        lax.all_gather(w_in[layer_number], "dp", axis=0, tiled=True),
        lax.all_gather(w_out[layer_number], "dp", axis=0, tiled=True),
    )
    route = routes[layer_number]
    gain_a = dense_w[0].astype(jnp.float32)
    norm_result = (residual * norm_factor(residual) * gain_a).astype(jnp.bfloat16)
    query_rows = jnp.dot(norm_result, dense_w[1], preferred_element_type=jnp.float32).reshape(
        total_rows, QUERY_HEADS, HEAD_DIM
    )
    query_rows = rotate(query_rows, cos_table, sin_table, 1.0).astype(jnp.bfloat16)
    key_matrix_rows = jnp.dot(norm_result, dense_w[2], preferred_element_type=jnp.float32).reshape(
        total_rows, KEY_VALUE_HEADS, HEAD_DIM
    )
    key_matrix_rows = rotate(key_matrix_rows, cos_table, sin_table, 1.0).astype(jnp.bfloat16)
    value_matrix_rows = (
        jnp.dot(norm_result, dense_w[3], preferred_element_type=jnp.float32)
        .astype(jnp.bfloat16)
        .reshape(total_rows, KEY_VALUE_HEADS, HEAD_DIM)
    )
    all_keys = lax.all_gather(key_matrix_rows, "expert", axis=0, tiled=True)
    all_values = lax.all_gather(value_matrix_rows, "expert", axis=0, tiled=True)
    heads_out = []
    log_totals = []
    for group_of_heads in range(KEY_VALUE_HEADS):
        scores, grouped_q = score_block(query_rows, all_keys, group_of_heads)
        row_peak = jnp.max(scores, axis=-1, keepdims=True)
        expo_vals = jnp.exp(scores - row_peak)
        row_sums = jnp.sum(expo_vals, axis=-1, keepdims=True)
        attn_probs = (expo_vals / row_sums).astype(jnp.bfloat16)
        log_totals.append(row_peak + jnp.log(row_sums))
        heads_out.append(
            jnp.einsum(
                "grk,kd->rgd",
                attn_probs,
                all_values[:, group_of_heads, :],
                preferred_element_type=jnp.float32,
            )
        )
    attn = (
        jnp.concatenate(heads_out, axis=1)
        .reshape(total_rows, QUERY_HEADS * HEAD_DIM)
        .astype(jnp.bfloat16)
    )
    after_attn = residual + jnp.dot(attn, dense_w[4], preferred_element_type=jnp.float32)
    gain_m = dense_w[5].astype(jnp.float32)
    normed_two = (after_attn * norm_factor(after_attn) * gain_m).astype(jnp.bfloat16)
    logits = jnp.dot(normed_two, dense_w[6], preferred_element_type=jnp.float32)
    gate_probs = jax.nn.softmax(jnp.take_along_axis(logits, route, axis=1), axis=-1)
    target, source, filled = plan_slots(route, expert_count, capacity)
    send_rows = jnp.where(filled[:, None], normed_two[source // TOP], zero_bf)
    send_rows = send_rows.reshape(group_count, experts_local, capacity, model_width)
    arrived_rows = lax.all_to_all(send_rows, "expert", split_axis=0, concat_axis=0, tiled=True)
    gate_up_vals = jnp.einsum(
        "secd,def->secf", arrived_rows, expert_w[0], preferred_element_type=jnp.float32
    )
    expert_gate_half = gate_up_vals[..., :FF]
    expert_hidden_act = (
        expert_gate_half * jax.nn.sigmoid(expert_gate_half) * gate_up_vals[..., FF:]
    ).astype(jnp.bfloat16)
    expert_out = jnp.einsum(
        "secf,fed->secd", expert_hidden_act, expert_w[1], preferred_element_type=jnp.float32
    ).astype(jnp.bfloat16)
    arrived, gate_up, expert_out = (arrived_rows, gate_up_vals, expert_out)
    returned = lax.all_to_all(expert_out, "expert", split_axis=0, concat_axis=0, tiled=True)
    slot_out = returned.reshape(expert_count * capacity, model_width)[target].reshape(
        total_rows, TOP, model_width
    )
    new_residual = after_attn + jnp.sum(
        gate_probs[:, :, None] * slot_out.astype(jnp.float32), axis=1
    )
    saved_layers = [
        (
            residual,
            norm_result,
            query_rows,
            key_matrix_rows,
            value_matrix_rows,
            all_keys,
            all_values,
            log_totals,
            attn,
            after_attn,
            normed_two,
            route,
            gate_probs,
            target,
            source,
            filled,
            arrived,
            gate_up,
            slot_out,
            dense_w,
            expert_w,
        )
    ]
    block_out = new_residual.astype(jnp.bfloat16)
    grad_resid = cotangent.astype(jnp.float32)
    grad_lists = [[None] * layer_count for _ in range(9)]
    for layer_number in reversed(range(layer_count)):
        (
            resid_in,
            norm_result,
            query_rows,
            key_matrix_rows,
            value_matrix_rows,
            all_keys,
            all_values,
            log_totals,
            attn,
            after_attn,
            normed_two,
            route,
            gate_probs,
            target,
            source,
            filled,
            arrived,
            gate_up,
            slot_out,
            dense_w,
            expert_w,
        ) = saved_layers[layer_number]
        dense_w = (
            lax.all_gather(gain_attn[layer_number], ("dp", "expert"), axis=0, tiled=True),
            lax.all_gather(w_query[layer_number], ("dp", "expert"), axis=0, tiled=True),
            lax.all_gather(key_weight[layer_number], ("dp", "expert"), axis=0, tiled=True),
            lax.all_gather(value_weight[layer_number], ("dp", "expert"), axis=0, tiled=True),
            lax.all_gather(w_output[layer_number], ("dp", "expert"), axis=0, tiled=True),
            lax.all_gather(gain_moe[layer_number], ("dp", "expert"), axis=0, tiled=True),
            lax.all_gather(w_router[layer_number], ("dp", "expert"), axis=0, tiled=True),
        )
        expert_w = (
            lax.all_gather(w_in[layer_number], "dp", axis=0, tiled=True),
            lax.all_gather(w_out[layer_number], "dp", axis=0, tiled=True),
        )
        all_keys, all_values = (
            lax.all_gather(key_matrix_rows, "expert", axis=0, tiled=True),
            lax.all_gather(value_matrix_rows, "expert", axis=0, tiled=True),
        )
        gate_grad = jnp.sum(slot_out.astype(jnp.float32) * grad_resid[:, None, :], axis=-1)
        slot_grad = (
            (gate_probs[:, :, None] * grad_resid[:, None, :])
            .astype(jnp.bfloat16)
            .reshape(total_rows * TOP, model_width)
        )
        grad_rows = jnp.where(filled[:, None], slot_grad[source], zero_bf)
        grad_rows = grad_rows.reshape(group_count, experts_local, capacity, model_width)
        grad_arrived = lax.all_to_all(grad_rows, "expert", split_axis=0, concat_axis=0, tiled=True)
        gate_half = gate_up[..., :FF]
        up_half = gate_up[..., FF:]
        sigmoid_vals = jax.nn.sigmoid(gate_half)
        silu_vals = gate_half * sigmoid_vals
        hidden_act = (silu_vals * up_half).astype(jnp.bfloat16)
        act_grad = jnp.einsum(
            "secd,fed->secf", grad_arrived, expert_w[1], preferred_element_type=jnp.float32
        )
        gate_part = act_grad * up_half * sigmoid_vals * (1.0 + gate_half * (1.0 - sigmoid_vals))
        gate_up_grad = jnp.concatenate([gate_part, act_grad * silu_vals], axis=-1).astype(
            jnp.bfloat16
        )
        input_grad = jnp.einsum(
            "secf,def->secd", gate_up_grad, expert_w[0], preferred_element_type=jnp.float32
        ).astype(jnp.bfloat16)
        returned_grad = lax.all_to_all(
            input_grad, "expert", split_axis=0, concat_axis=0, tiled=True
        )
        grad_lists[7][layer_number] = lax.psum_scatter(
            jnp.einsum(
                "secd,secf->def", arrived, gate_up_grad, preferred_element_type=jnp.float32
            ).astype(jnp.bfloat16),
            "dp",
            scatter_dimension=0,
            tiled=True,
        ).astype(jnp.float32)
        grad_lists[8][layer_number] = lax.psum_scatter(
            jnp.einsum(
                "secf,secd->fed", hidden_act, grad_arrived, preferred_element_type=jnp.float32
            ).astype(jnp.bfloat16),
            "dp",
            scatter_dimension=0,
            tiled=True,
        ).astype(jnp.float32)
        slot_back = returned_grad.reshape(expert_count * capacity, model_width)[target].reshape(
            total_rows, TOP, model_width
        )
        normed_two_grad = jnp.sum(slot_back.astype(jnp.float32), axis=1)
        gate_inner = jnp.sum(gate_probs * gate_grad, axis=-1, keepdims=True)
        chosen_grad = gate_probs * (gate_grad - gate_inner)
        route_hot = (
            route[:, :, None] == jnp.arange(expert_count, dtype=jnp.int32)[None, None, :]
        ).astype(jnp.float32)
        logit_grad = jnp.sum(route_hot * chosen_grad[:, :, None], axis=1)
        router_f = dense_w[6].astype(jnp.float32)
        normed_two_grad = normed_two_grad + jnp.einsum(
            "re,de->rd", logit_grad, router_f, precision=top_precision
        )
        router_grad = jnp.einsum(
            "rd,re->de", normed_two.astype(jnp.float32), logit_grad, precision=top_precision
        )
        gain_m = dense_w[5].astype(jnp.float32)
        norm_two_back, gain_m_grad = norm_back(after_attn, gain_m, normed_two_grad)
        mid_grad = grad_resid + norm_two_back
        out_grad = mid_grad.astype(jnp.bfloat16)
        output_grad = jnp.einsum("rq,rd->qd", attn, out_grad, preferred_element_type=jnp.float32)
        attn_grad = (
            jnp.einsum("rd,qd->rq", out_grad, dense_w[4], preferred_element_type=jnp.float32)
            .astype(jnp.bfloat16)
            .reshape(total_rows, QUERY_HEADS, HEAD_DIM)
        )
        query_grads = []
        key_grads = []
        value_grads = []
        for group_of_heads in range(KEY_VALUE_HEADS):
            scores, grouped_q = score_block(query_rows, all_keys, group_of_heads)
            grouped_do = attn_grad[
                :, group_of_heads * heads_per_group : (group_of_heads + 1) * heads_per_group, :
            ]
            probs = jnp.exp(scores - log_totals[group_of_heads])
            prob_bf = probs.astype(jnp.bfloat16)
            prob_grad = jnp.einsum(
                "rgd,kd->grk",
                grouped_do,
                all_values[:, group_of_heads, :],
                preferred_element_type=jnp.float32,
            )
            row_dot = jnp.sum(probs * prob_grad, axis=-1, keepdims=True)
            score_grad = (probs * (prob_grad - row_dot)).astype(jnp.bfloat16)
            query_grads.append(
                jnp.einsum(
                    "grk,kd->rgd",
                    score_grad,
                    all_keys[:, group_of_heads, :],
                    preferred_element_type=jnp.float32,
                )
                * score_scale
            )
            key_grads.append(
                jnp.einsum("grk,rgd->kd", score_grad, grouped_q, preferred_element_type=jnp.float32)
                * score_scale
            )
            value_grads.append(
                jnp.einsum("grk,rgd->kd", prob_bf, grouped_do, preferred_element_type=jnp.float32)
            )
        key_sum, value_total_sum = (
            lax.psum_scatter(
                jnp.stack(key_grads, axis=1).astype(jnp.bfloat16),
                "expert",
                scatter_dimension=0,
                tiled=True,
            ).astype(jnp.float32),
            lax.psum_scatter(
                jnp.stack(value_grads, axis=1).astype(jnp.bfloat16),
                "expert",
                scatter_dimension=0,
                tiled=True,
            ).astype(jnp.float32),
        )
        query_grad = (
            rotate(jnp.concatenate(query_grads, axis=1), cos_table, sin_table, -1.0)
            .astype(jnp.bfloat16)
            .reshape(total_rows, QUERY_HEADS * HEAD_DIM)
        )
        key_grad = (
            rotate(key_sum, cos_table, sin_table, -1.0)
            .astype(jnp.bfloat16)
            .reshape(total_rows, KEY_VALUE_HEADS * HEAD_DIM)
        )
        value_rows_gradient = value_total_sum.astype(jnp.bfloat16).reshape(
            total_rows, KEY_VALUE_HEADS * HEAD_DIM
        )
        normed_grad = jnp.einsum(
            "rq,dq->rd", query_grad, dense_w[1], preferred_element_type=jnp.float32
        )
        normed_grad = normed_grad + jnp.einsum(
            "rq,dq->rd", key_grad, dense_w[2], preferred_element_type=jnp.float32
        )
        normed_grad = normed_grad + jnp.einsum(
            "rq,dq->rd", value_rows_gradient, dense_w[3], preferred_element_type=jnp.float32
        )
        query_w_grad = jnp.einsum(
            "rd,rq->dq", norm_result, query_grad, preferred_element_type=jnp.float32
        )
        key_w_grad = jnp.einsum(
            "rd,rq->dq", norm_result, key_grad, preferred_element_type=jnp.float32
        )
        value_w_grad = jnp.einsum(
            "rd,rq->dq", norm_result, value_rows_gradient, preferred_element_type=jnp.float32
        )
        gain_a = dense_w[0].astype(jnp.float32)
        norm_one_back, gain_a_grad = norm_back(resid_in, gain_a, normed_grad)
        grad_resid = mid_grad + norm_one_back
        shares = (
            lax.psum_scatter(gain_a_grad, ("dp", "expert"), scatter_dimension=0, tiled=True),
            lax.psum_scatter(query_w_grad, ("dp", "expert"), scatter_dimension=0, tiled=True),
            lax.psum_scatter(key_w_grad, ("dp", "expert"), scatter_dimension=0, tiled=True),
            lax.psum_scatter(value_w_grad, ("dp", "expert"), scatter_dimension=0, tiled=True),
            lax.psum_scatter(output_grad, ("dp", "expert"), scatter_dimension=0, tiled=True),
            lax.psum_scatter(gain_m_grad, ("dp", "expert"), scatter_dimension=0, tiled=True),
            lax.psum_scatter(router_grad, ("dp", "expert"), scatter_dimension=0, tiled=True),
        )
        for member in range(7):
            grad_lists[member][layer_number] = shares[member]
    stacked = [jnp.stack(grad_lists[member], axis=0) for member in range(9)]
    return (
        block_out,
        grad_resid,
        stacked[0],
        stacked[1],
        stacked[2],
        stacked[3],
        stacked[4],
        stacked[5],
        stacked[6],
        stacked[7],
        stacked[8],
    )


def product(left, right):
    return lax.dot_general(
        left, right, (((1,), (0,)), ((), ())), preferred_element_type=jnp.float32
    )


def product_rows(left, right):
    return lax.dot_general(
        left, right, (((1,), (1,)), ((), ())), preferred_element_type=jnp.float32
    )


def product_columns(left, right):
    return lax.dot_general(
        left, right, (((0,), (0,)), ((), ())), preferred_element_type=jnp.float32
    )


def split_three(values):
    high = values.astype(jnp.bfloat16)
    rest = values - high.astype(jnp.float32)
    middle = rest.astype(jnp.bfloat16)
    low = (rest - middle.astype(jnp.float32)).astype(jnp.bfloat16)
    return high, middle, low


def masked_gates(rows, router, mask):
    chosen = mask.astype(jnp.float32) > 0.5
    logits = jnp.where(chosen, product(rows, router), masked_score)
    expo_vals = jnp.where(chosen, jnp.exp(logits - jnp.max(logits, axis=1, keepdims=True)), 0.0)
    return expo_vals / jnp.sum(expo_vals, axis=1, keepdims=True)


def layer_kernel(
    x_ref,
    cot_ref,
    routes_ref,
    rope_ref,
    key_ref,
    value_ref,
    router_ref,
    gain_a_ref,
    gain_m_ref,
    shard_b,
    shard_c,
    w_in_ref,
    w_out_ref,
    block_out_ref,
    dx_ref,
    grad_in_ref,
    grad_out_ref,
    grad_dense_ref,
    grad_kv_ref,
    grad_aux_ref,
    spill_b,
    spill_c,
    n2_all,
    cot_all,
    full_a,
    arena,
    gate_buf,
    w_in_half,
    w_out_half,
    hidden_all,
    g_all,
    kv_all,
    k_t,
    v_t,
    q_rows,
    do_rows,
    normed_buf,
    attn_buf,
    after_buf,
    lse_buf,
    turn_send,
    turn_recv,
    og_all,
    qg_all,
    kvg_all,
    dkv_recv,
    aux_send,
    gain_buf,
    z_sems,
    p_sems,
    s_sems,
    kv_sems,
    tok_sems,
    tz_sems,
    turn_sems,
    win_sems,
    wout_sems,
    sib_sems,
    ret_sems,
    gate_sems,
    gin_sems,
    gout_sems,
    og_sems,
    qg_sems,
    kvg_sems,
    dkv_sems,
    dense_sems,
    aux_sems,
    local_sems,
    credit_sem,
):
    plane = lax.axis_index("dp")
    member = lax.axis_index("expert")
    core = lax.rem(member, 2)
    parity = lax.rem(plane, 2)
    tokens, width = x_ref.shape
    rows = shard_b.shape[0]
    xor = lax.bitwise_xor
    f32, bf16 = jnp.float32, jnp.bfloat16
    half = FF // 2
    score_scale = HEAD_DIM ** (-0.5)
    kv_width = KEY_VALUE_HEADS * HEAD_DIM

    def at_rows(start, count, step=16):
        return pl.ds(pl.multiple_of(start, step), count)

    def remote(source, target, sems, index, device, recv_index=None):
        return pltpu.make_async_remote_copy(
            src_ref=source,
            dst_ref=target,
            send_sem=sems.at[(0,) + index],
            recv_sem=sems.at[(1,) + (index if recv_index is None else recv_index)],
            device_id=device,
            device_id_type=MESH,
        )

    in_plane = lambda step: (plane, xor(member, step))
    sibling = in_plane(1)

    barrier = pltpu.get_barrier_semaphore()
    greeted = [(xor(plane, s), member) for s in (1, 2, 3)]
    greeted += [in_plane(s) for s in range(1, 8)]
    greeted += [(xor(plane, 1), xor(member, s)) for s in (2, 4, 6)]
    for device in greeted:
        pl.semaphore_signal(barrier, inc=1, device_id=device, device_id_type=MESH)

    def dense_block(part, step, chip_step):
        start = (xor(plane, step) * 8 + xor(member, chip_step)) * rows
        if part == 0:
            return full_a.at[at_rows(start, rows)]
        return arena.at[at_rows(start + (part - 1) * width, rows)]

    def z_copy(part, step):
        block = dense_block(part, 0, 0)
        return remote(block, block, z_sems, (part, step), (xor(plane, step), member))

    def plane_copy(part, step, chip):
        if chip < 3:
            block = dense_block(part, step, 0)
            return remote(block, block, p_sems, (part, step, chip), in_plane(2 * chip))
        via = 1 + step % 2
        block = dense_block(part, step, 2 * via)
        return remote(block, block, p_sems, (part, step, 3), in_plane(2 * (3 - via)))

    def sibling_copy(part, step, chip):
        block = dense_block(part, step, 2 * chip)
        return remote(block, block, s_sems, (part, step, chip), sibling)

    own_rows = (plane * 8 + member) * rows
    full_a[at_rows(own_rows, rows), pl.ds(0, kv_width)] = key_ref[...]
    full_a[at_rows(own_rows, rows), pl.ds(kv_width, kv_width)] = value_ref[...]
    line = lax.broadcasted_iota(jnp.int32, (128, rows), 0)
    gains = jnp.where(line == EXPERT_LANES, gain_a_ref[...].astype(f32), 0.0) + jnp.where(
        line == EXPERT_LANES + 1, gain_m_ref[...].astype(f32), 0.0
    )
    lines = jnp.concatenate(
        [router_ref[...].astype(f32), gains[EXPERT_LANES:]], axis=0
    ).astype(bf16)
    square = (
        lax.broadcasted_iota(jnp.int32, (rows, rows), 0)
        == lax.broadcasted_iota(jnp.int32, (rows, rows), 1)
    ).astype(bf16)
    full_a[at_rows(own_rows, rows), pl.ds(2 * kv_width, 128)] = product_rows(
        square, lines
    ).astype(bf16)
    arena[at_rows(own_rows, rows)] = shard_b[...]
    arena[at_rows(own_rows + width, rows)] = shard_c[...]

    def token_rows(plane_step, member_step):
        start = (xor(parity, plane_step) * 8 + xor(member, member_step)) * tokens
        return at_rows(start, tokens, 128)

    cot_all[token_rows(0, 0), pl.ds(0, width)] = cot_ref[...]
    expert_line = lax.broadcasted_iota(jnp.int32, (128, tokens), 0)
    named = jnp.zeros((128, tokens), f32)
    for slot in range(TOP):
        named = jnp.where(expert_line == routes_ref[pl.ds(slot, 1), :], 1.0, named)
    cot_all[token_rows(0, 0), pl.ds(width, 128)] = jnp.transpose(named).astype(bf16)
    pl.semaphore_wait(barrier, len(greeted))

    for part in range(3):
        for step in (3, 2, 1):
            z_copy(part, step).start()
    for part in range(3):
        for chip in (1, 2):
            plane_copy(part, 0, chip).start()
        sibling_copy(part, 0, 0).start()

    def pass_on_plane(part):
        for step in (1, 2, 3):
            z_copy(part, step).wait_recv()
            for chip in (1, 2):
                plane_copy(part, step, chip).start()
            sibling_copy(part, step, 0).start()

    def pass_on_diagonal(part, steps):
        for step in steps:
            for chip in (1, 2):
                plane_copy(part, step, chip).wait_recv()
                if chip == 1 + step % 2:
                    plane_copy(part, step, 3).start()
                sibling_copy(part, step, chip).start()

    def pass_on_sibling(part):
        for step in range(4):
            plane_copy(part, step, 3).wait_recv()
            sibling_copy(part, step, 3).start()

    def arrived_dense(part):
        for step in range(4):
            for chip in range(4):
                sibling_copy(part, step, chip).wait_recv()

    def sent_dense(part):
        for step in range(4):
            if step:
                z_copy(part, step).wait_send()
            for chip in range(4):
                if chip:
                    plane_copy(part, step, chip).wait_send()
                sibling_copy(part, step, chip).wait_send()

    token_arrays = (cot_all, n2_all)

    parts = (0, 512, 1024)

    def cube_device(bits):
        return (xor(plane, bits & 1), xor(member, bits & 6))

    def part_order(part):
        return [1 << ((part + k) % 3) for k in range(3)]

    def token_z(kind):
        block = token_arrays[kind].at[token_rows(0, 0)]
        return remote(block, block, tz_sems, (kind,), (xor(plane, 1), member))

    def token_where(kind, plane_step):
        base = xor(parity, plane_step) * 8 * tokens
        return token_arrays[kind], tok_sems, (kind, plane_step), 0, None, base

    quarter = w_in_ref.shape[0]
    quarter_out = w_out_ref.shape[0]

    def win_copy(step, piece):
        other = xor(parity, step % 2)
        source = w_in_ref.at[:, at_rows(piece * FF + other * half, half, 128)]
        target = w_in_half.at[at_rows(plane * quarter, quarter), pl.ds(piece * half, half)]
        if step == 0:
            return pltpu.make_async_copy(source, target, local_sems.at[piece])
        return remote(source, target, win_sems, (step, piece), (xor(plane, step), member))

    out_half = lax.div(plane, 2)

    def wout_send(turn):
        target = w_out_half.at[at_rows(parity * quarter_out, quarter_out)]
        device = (out_half + 2 * turn, member)
        return remote(w_out_ref, target, wout_sems, (turn,), device, (parity,))

    def wout_arrived(slot):
        target = w_out_half.at[at_rows(slot * quarter_out, quarter_out)]
        return remote(w_out_ref, target, wout_sems, (slot,), (xor(plane, 1), member))

    def wout_local():
        return pltpu.make_async_copy(
            w_out_ref,
            w_out_half.at[at_rows(parity * quarter_out, quarter_out)],
            local_sems.at[2],
        )

    def expert_start():
        for step in (1, 3, 2):
            for piece in (0, 1):
                win_copy(step, piece).start()
        for piece in (0, 1):
            win_copy(0, piece).start()
        for turn in (0, 1):

            @pl.when(out_half + 2 * turn != plane)
            def _():
                wout_send(turn).start()

        @pl.when(out_half == parity)
        def _():
            wout_local().start()

    def expert_finish():
        for step in (1, 3, 2):
            for piece in (0, 1):
                win_copy(step, piece).wait()
        for piece in (0, 1):
            win_copy(0, piece).wait()
        for slot in (0, 1):

            @pl.when(parity * 2 + slot != plane)
            def _():
                wout_arrived(slot).wait_recv()

        for turn in (0, 1):

            @pl.when(out_half + 2 * turn != plane)
            def _():
                wout_send(turn).wait_send()

        @pl.when(out_half == parity)
        def _():
            wout_local().wait()

    def gather_copy(array, sems, index, lead=(), start=0, stop=None, base=0):
        stop = array.shape[1] if stop is None else stop
        middle = (start + stop) // 256 * 128
        owner_step, device_step = ((0, 2), (0, 4), (2, 4), (4, 2), (0, 1), (2, 1), (4, 1), (6, 1))[
            index
        ]
        if index == 2:
            stop = middle
        if index == 3:
            start = middle
        block = at_rows(base + xor(member, owner_step) * tokens, tokens, 128)
        piece = array.at[block, pl.ds(start, stop - start)]
        return remote(piece, piece, sems, lead + (index,), in_plane(device_step))

    def gather_start(*where):
        for index in (0, 1, 4):
            gather_copy(where[0], where[1], index, *where[2:]).start()

    def gather_pass(*where):
        for index in (0, 1):
            gather_copy(where[0], where[1], index, *where[2:]).wait_recv()
            gather_copy(where[0], where[1], 2 + index, *where[2:]).start()
            gather_copy(where[0], where[1], 5 + index, *where[2:]).start()

    def gather_pass_last(*where):
        for index in (2, 3):
            gather_copy(where[0], where[1], index, *where[2:]).wait_recv()
        gather_copy(where[0], where[1], 7, *where[2:]).start()

    def gather_sent(*where):
        for index in range(8):
            gather_copy(where[0], where[1], index, *where[2:]).wait_send()

    def gather_finish(*where):
        gather_sent(*where)
        for index in range(4, 8):
            gather_copy(where[0], where[1], index, *where[2:]).wait_recv()

    pass_on_plane(0)
    pass_on_plane(1)
    pass_on_diagonal(0, range(4))
    pass_on_sibling(0)
    arrived_dense(0)
    token_z(0).start()
    expert_start()
    aux = full_a[:, pl.ds(2 * kv_width, 128)]
    pick = (
        lax.broadcasted_iota(jnp.int32, (16, 128), 1)
        == lax.broadcasted_iota(jnp.int32, (16, 128), 0) + EXPERT_LANES
    ).astype(bf16)
    gain_buf[...] = product_rows(pick, aux)
    gain_a = gain_buf[pl.ds(0, 1), :]
    gain_m = gain_buf[pl.ds(1, 1), :]
    residual = x_ref[...].astype(f32)
    normed = (residual * norm_factor(residual) * gain_a).astype(bf16)
    normed_buf[...] = normed
    cos_part = rope_ref[:, pl.ds(0, HEAD_DIM)]
    sin_part = rope_ref[:, pl.ds(HEAD_DIM, HEAD_DIM)]

    def turned(values, orient):
        swapped = pltpu.roll(values, HEAD_DIM // 2, 1)
        return values * cos_part + swapped * (sin_part * orient)

    kv_rows = product(normed, full_a[:, pl.ds(0, 2 * kv_width)])
    own_block = at_rows(member * tokens, tokens, 128)
    for part in range(2 * KEY_VALUE_HEADS):
        piece = kv_rows[:, part * HEAD_DIM : (part + 1) * HEAD_DIM]
        if part < KEY_VALUE_HEADS:
            piece = turned(piece, 1.0)
        kv_all[own_block, pl.ds(part * HEAD_DIM, HEAD_DIM)] = piece.astype(bf16)
    gather_start(kv_all, kv_sems)
    turn_send[0] = jnp.transpose(normed).reshape(turn_send.shape[1:])

    def turn_copy(kind, step):
        return remote(
            turn_send.at[kind, :, xor(member, step)],
            turn_recv.at[kind, :, :, at_rows(member * tokens, tokens, 128)],
            turn_sems,
            (kind, step),
            in_plane(step),
        )

    def turn_start(kind):
        for step in range(1, 8):
            turn_copy(kind, step).start()
        turn_recv[kind, :, :, at_rows(member * tokens, tokens, 128)] = turn_send[
            kind, :, pl.ds(member, 1)
        ].reshape(turn_recv.shape[1], rows, tokens)

    turn_start(0)
    pass_on_plane(2)
    gather_pass(kv_all, kv_sems)
    pass_on_diagonal(1, range(4))
    gather_start(*token_where(0, 0))
    gather_pass_last(kv_all, kv_sems)
    pass_on_sibling(1)
    token_z(0).wait_recv()
    gather_start(*token_where(0, 1))
    arrived_dense(1)
    spill_b_copy = pltpu.make_async_copy(
        arena.at[pl.ds(0, width)], spill_b, local_sems.at[3]
    )
    spill_b_copy.start()
    for head in range(QUERY_HEADS):
        if head % 2 == 0:
            pair = product(normed, arena[pl.ds(0, width), pl.ds(head * HEAD_DIM, 2 * HEAD_DIM)])
        piece = pair[:, (head % 2) * HEAD_DIM : (head % 2 + 1) * HEAD_DIM]
        q_rows[pl.ds(head * tokens, tokens)] = turned(piece, 1.0).astype(bf16)
    gather_finish(kv_all, kv_sems)
    for group in range(KEY_VALUE_HEADS):
        k_t[group] = jnp.transpose(kv_all[:, pl.ds(group * HEAD_DIM, HEAD_DIM)])
        v_t[group] = jnp.transpose(kv_all[:, pl.ds(kv_width + group * HEAD_DIM, HEAD_DIM)])
    pass_on_diagonal(2, range(4))

    seq_len = kv_all.shape[0]
    pairs = QUERY_HEADS // 2
    pairs_per_group = pairs // KEY_VALUE_HEADS
    key_index = lax.broadcasted_iota(jnp.int32, (seq_len, 2 * tokens), 0)
    query_index = member * tokens + lax.rem(
        lax.broadcasted_iota(jnp.int32, (seq_len, 2 * tokens), 1), tokens
    )
    allowed = key_index <= query_index

    def pair_scores(pair, group):
        queries = q_rows[at_rows(pair * 2 * tokens, 2 * tokens, 128)]
        keys = kv_all[:, at_rows(group * HEAD_DIM, HEAD_DIM, 128)]
        scores = product_rows(keys, queries) * score_scale
        return jnp.where(allowed, scores, masked_score), queries

    def attend(pair, carry):
        group = lax.div(pair, pairs_per_group)
        scores, _ = pair_scores(pair, group)
        peak = jnp.max(scores, axis=0, keepdims=True)
        expo_vals = jnp.exp(scores - peak)
        sums = jnp.sum(expo_vals, axis=0, keepdims=True)
        probs = (expo_vals / sums).astype(bf16)
        lse_buf[pair] = jnp.broadcast_to(peak + jnp.log(sums), (8, 2 * tokens))
        part = product(v_t[group], probs)
        for inner in (0, 1):
            piece = part[:, inner * tokens : (inner + 1) * tokens].astype(bf16)
            attn_buf[2 * pair + inner] = piece
        return carry

    lax.fori_loop(0, pairs, attend, 0)
    pass_on_sibling(2)
    gather_pass(*token_where(0, 0))
    attn_t = attn_buf[...].reshape(width, tokens)
    turn_send[1] = attn_t.reshape(turn_send.shape[1:])
    attn = jnp.transpose(attn_t)
    arrived_dense(2)
    spill_c_copy = pltpu.make_async_copy(
        arena.at[pl.ds(width, width)], spill_c, local_sems.at[4]
    )
    spill_c_copy.start()
    for start in range(0, width, 512):
        after_buf[:, pl.ds(start, 512)] = x_ref[:, pl.ds(start, 512)].astype(f32) + product(
            attn, arena[pl.ds(width, width), pl.ds(start, 512)]
        )
    after = after_buf[...]
    normed_two = (after * norm_factor(after) * gain_m).astype(bf16)
    n2_all[token_rows(0, 0)] = normed_two
    spill_b_copy.wait()
    spill_c_copy.wait()
    for part in range(3):
        sent_dense(part)
    token_z(1).start()
    gather_start(*token_where(1, 0))
    turn_send[2] = jnp.transpose(normed_two).reshape(turn_send.shape[1:])
    gather_pass(*token_where(0, 1))
    gather_pass_last(*token_where(0, 0))
    gather_pass_last(*token_where(0, 1))
    token_z(1).wait_recv()
    gather_start(*token_where(1, 1))
    for plane_step in (0, 1):
        gather_finish(*token_where(0, plane_step))
    expert_finish()

    own_lane = lax.broadcasted_iota(jnp.int32, (2 * tokens, 128), 1) == member
    low_lane = lax.broadcasted_iota(jnp.int32, (2 * tokens, 128), 1) == member + 64
    def arena_slot(base, kind, slot):
        first, each = {"stage": (0, 2), "sib": (4, 2), "sum": (8, 8), "recv": (24, 7)}[base]
        return at_rows((first + kind * each + slot) * tokens, tokens, 128)

    def sib_copy(kind, slot):
        return remote(
            arena.at[arena_slot("stage", kind, slot)],
            arena.at[arena_slot("sib", kind, slot)],
            sib_sems,
            (kind, slot),
            sibling,
        )

    def sib_gate_copy():
        return remote(
            gate_buf.at[pl.ds(8, 8)], gate_buf.at[pl.ds(16, 8)], sib_sems, (2, 0), sibling
        )

    def bit_of(held, bit):
        if isinstance(held, int):
            return held // bit % 2
        return jnp.where(held & bit > 0, 1, 0)

    def ret_copy(kind, part, held, stage):
        first, second, third = part_order(part)
        slot = (
            bit_of(held, second) + 2 * bit_of(held, third),
            4 + bit_of(held, third),
            6,
        )[stage]
        columns = pl.ds(parts[part], 512)
        return remote(
            arena.at[arena_slot("sum", kind, held), columns],
            arena.at[arena_slot("recv", kind, slot), columns],
            ret_sems,
            (kind, part, slot),
            cube_device((first, second, third)[stage]),
        )

    def ret_arrived(kind, part, slot):
        columns = pl.ds(parts[part], 512)
        block = arena.at[arena_slot("recv", kind, slot), columns]
        return remote(block, block, ret_sems, (kind, part, slot), sibling)

    def ret_sum(kind, part, held, slots):
        columns = pl.ds(parts[part], 512)
        total = arena[arena_slot("sum", kind, held), columns].astype(f32)
        for slot in slots:
            total = total + arena[arena_slot("recv", kind, slot), columns].astype(f32)
        return total

    def ret_second(kind):
        for part in range(3):
            first, second, third = part_order(part)
            for held, slot in ((second, 1), (second | third, 3)):
                ret_arrived(kind, part, slot).wait_recv()
                arena[arena_slot("sum", kind, held), pl.ds(parts[part], 512)] = ret_sum(
                    kind, part, held, (slot,)
                ).astype(bf16)
                ret_copy(kind, part, held, 1).start()

    def ret_third(kind):
        for part in range(3):
            third = part_order(part)[2]
            for slot in (2, 5):
                ret_arrived(kind, part, slot).wait_recv()
            arena[arena_slot("sum", kind, third), pl.ds(parts[part], 512)] = ret_sum(
                kind, part, third, (2, 5)
            ).astype(bf16)
            ret_copy(kind, part, third, 2).start()

    def ret_total(kind):
        for part in range(3):
            for slot in (0, 4, 6):
                ret_arrived(kind, part, slot).wait_recv()
        return jnp.concatenate([ret_sum(kind, part, 0, (0, 4, 6)) for part in range(3)], axis=1)

    def ret_sent(kind):
        for part in range(3):
            first, second, third = part_order(part)
            for held in range(8):
                if held & first:
                    ret_copy(kind, part, held, 0).wait_send()
            for held in (second, second | third):
                ret_copy(kind, part, held, 1).wait_send()
            ret_copy(kind, part, third, 2).wait_send()

    def ret_gate_copy(held):
        return remote(
            gate_buf.at[held], gate_buf.at[24 + held], gate_sems, (held,), cube_device(held)
        )

    def halves(values, first):
        return jnp.where(first, values[:tokens], values[tokens:])

    def block_rows(held):
        other_plane = xor(parity, held & 1)
        chip = xor(lax.div(member, 2), lax.div(held, 2))
        return at_rows((other_plane * 4 + chip) * 2 * tokens, 2 * tokens, 128)

    def first_step(held, carry):
        @pl.when(held == 1)
        def _():
            gather_pass(*token_where(1, 0))

        @pl.when(held == 2)
        def _():
            gather_pass(*token_where(1, 1))

        @pl.when(held == 4)
        def _():
            gather_pass_last(*token_where(1, 0))
            gather_pass_last(*token_where(1, 1))

        own = token_rows(held & 1, held & 6)
        remote(
            n2_all.at[own],
            n2_all.at[own],
            tok_sems,
            (1, held & 1, 4 + lax.div(held, 2)),
            sibling,
        ).wait_recv()
        here = block_rows(held)
        token_block = n2_all[here, :]
        gate_up = product(token_block, w_in_half[...])
        gates = masked_gates(
            token_block,
            full_a[:, pl.ds(2 * kv_width, 128)],
            cot_all[here, pl.ds(width, 128)],
        )
        gate = jnp.sum(jnp.where(own_lane, gates, 0.0), axis=1, keepdims=True)
        gate_half = gate_up[:, :half]
        up_half = gate_up[:, half:]
        sigmoid_vals = 1.0 / (1.0 + jnp.exp(-gate_half))
        silu_vals = gate_half * sigmoid_vals
        hidden = silu_vals * up_half
        hidden_all[here, :] = (gate * hidden).astype(bf16)
        back = product_rows(cot_all[here, pl.ds(0, width)], w_out_half[...])
        gate_grad = jnp.sum(hidden * back, axis=1, keepdims=True)
        act_grad = gate * back
        gate_part = act_grad * up_half * sigmoid_vals * (1.0 + gate_half * (1.0 - sigmoid_vals))
        g_all[here, pl.ds(0, half)] = gate_part.astype(bf16)
        g_all[here, pl.ds(half, half)] = (act_grad * silu_vals).astype(bf16)
        gate_high = gate_grad.astype(bf16).astype(f32)
        gate_lanes = jnp.where(own_lane, gate_high, 0.0) + jnp.where(
            low_lane, gate_grad - gate_high, 0.0
        )
        gate_buf[held] = halves(gate_lanes, core == 0).astype(bf16)
        gate_buf[8 + held] = halves(gate_lanes, core == 1).astype(bf16)
        return carry

    lax.fori_loop(0, 8, first_step, 0)
    token_z(0).wait_send()
    token_z(1).wait_send()
    for plane_step in (0, 1):
        gather_sent(*token_where(1, plane_step))
    sib_gate_copy().start()

    def turn_held(turn):
        return jnp.where(turn == 3, 3, jnp.where(turn == 4, 4, 7 - turn))

    def second_step(kind, turn, carry):
        @pl.when(turn < 8)
        def _():
            slot2 = lax.rem(turn, 2)
            held = turn_held(turn)
            here = block_rows(held)

            @pl.when(turn >= 2)
            def _():
                sib_copy(kind, slot2).wait_send()
                pl.semaphore_wait(credit_sem, 1)

            place = arena_slot("sum", kind, held)
            for start in range(0, width, 512):
                columns = pl.ds(start, 512)
                if kind == 0:
                    result = product_rows(g_all[here, :], w_in_half[columns, :])
                else:
                    result = product(hidden_all[here, :], w_out_half[:, columns])
                arena[arena_slot("stage", kind, slot2), columns] = halves(
                    result, core == 1
                ).astype(bf16)
                arena[place, columns] = halves(result, core == 0).astype(bf16)
            sib_copy(kind, slot2).start()

        @pl.when(turn > 0)
        def _():
            last = turn - 1
            slot2 = lax.rem(last, 2)
            held = turn_held(last)
            place = arena_slot("sum", kind, held)
            sib_copy(kind, slot2).wait_recv()
            arena[place] = (
                arena[place].astype(f32) + arena[arena_slot("sib", kind, slot2)].astype(f32)
            ).astype(bf16)

            @pl.when(last < 6)
            def _():
                pl.semaphore_signal(credit_sem, inc=1, device_id=sibling, device_id_type=MESH)

            for part in range(3):

                @pl.when(held & (1 << part) > 0)
                def _():
                    ret_copy(kind, part, held, 0).start()

        return carry

    def second_loop(kind):
        lax.fori_loop(0, 9, functools.partial(second_step, kind), 0)
        for slot in (0, 1):
            sib_copy(kind, slot).wait_send()

    for kind in (1, 2):
        turn_start(kind)
    second_loop(0)
    sib_gate_copy().wait()
    gate_buf[pl.ds(0, 8)] = (
        gate_buf[pl.ds(0, 8)].astype(f32) + gate_buf[pl.ds(16, 8)].astype(f32)
    ).astype(bf16)
    for held in range(1, 8):
        ret_gate_copy(held).start()
    ret_second(0)

    def gin_copy(step):
        source = w_in_half.at[at_rows(xor(plane, step) * quarter, quarter)]
        if step == 0:
            return pltpu.make_async_copy(source, grad_in_ref.at[0], local_sems.at[5])
        return remote(
            source, grad_in_ref.at[step], gin_sems, (step,), (xor(plane, step), member)
        )

    for step in (2, 3, 1, 0):
        start = xor(plane, step) * quarter
        for piece in range(0, quarter, 128):
            columns = n2_all[:, at_rows(start + piece, 128, 128)]
            w_in_half[at_rows(start + piece, 128, 128)] = product_columns(
                columns, g_all[...]
            ).astype(bf16)
        if step in (2, 3):
            gin_copy(step).start()

    def gout_copy(slot):
        source = w_out_half.at[pl.ds(slot * quarter_out, quarter_out)]
        target = grad_out_ref.at[out_half]
        device = (parity * 2 + slot, member)
        return remote(source, target, gout_sems, (slot,), device, (out_half,))

    def gout_local(slot):
        return pltpu.make_async_copy(
            w_out_half.at[pl.ds(slot * quarter_out, quarter_out)],
            grad_out_ref.at[out_half],
            local_sems.at[6],
        )

    def gout_arrived(turn):
        source = w_out_half.at[pl.ds(0, quarter_out)]
        return remote(source, grad_out_ref.at[turn], gout_sems, (turn,), (xor(plane, 1), member))

    own_n2 = n2_all[token_rows(0, 0), :]
    own_mask = cot_all[token_rows(0, 0), pl.ds(width, 128)]
    own_gates = masked_gates(own_n2, full_a[:, pl.ds(2 * kv_width, 128)], own_mask)
    gin_copy(0).start()
    ret_third(0)
    second_loop(1)
    for start in range(0, half, 128):
        w_out_half[pl.ds(start, 128)] = product_columns(
            hidden_all[:, pl.ds(start, 128)], cot_all[:, pl.ds(0, width)]
        ).astype(bf16)

    load_b = pltpu.make_async_copy(
        spill_b, cot_all.at[pl.ds(0, width), pl.ds(0, width)], local_sems.at[3]
    )
    load_c = pltpu.make_async_copy(spill_c, n2_all.at[pl.ds(0, width)], local_sems.at[4])
    load_b.start()
    load_c.start()

    total_in = ret_total(0)
    total_gate = gate_buf[0].astype(f32)
    for held in range(1, 8):
        ret_gate_copy(held).wait_recv()
        total_gate = total_gate + gate_buf[24 + held].astype(f32)
    gin_copy(1).start()
    for slot in (0, 1):

        @pl.when(parity * 2 + slot != plane)
        def _():
            gout_copy(slot).start()

        @pl.when(parity * 2 + slot == plane)
        def _():
            gout_local(slot).start()

    gate_grad = total_gate + pltpu.roll(total_gate, 64, 1)
    gate_inner = jnp.sum(own_gates * gate_grad, axis=1, keepdims=True)
    logit_grad = own_gates * (gate_grad - gate_inner)
    lg_parts = split_three(logit_grad)
    aux_now = full_a[:, pl.ds(2 * kv_width, 128)]
    for part in lg_parts:
        total_in = total_in + product_rows(part, aux_now)
    after = after_buf[...]

    def norm_backward(values, gain, grad):
        factor = norm_factor(values)
        scaled = grad * gain
        gain_row = jnp.sum(grad * values * factor, axis=0, keepdims=True)
        inner = jnp.mean(scaled * values, axis=-1, keepdims=True)
        return factor * scaled - values * factor * factor * factor * inner, gain_row

    two_back, gain_m_row = norm_backward(after, gain_buf[pl.ds(1, 1), :], total_in)
    mid = cot_ref[...].astype(f32) + two_back
    dx_ref[...] = mid
    out_grad = mid.astype(bf16)
    og_all[own_block, pl.ds(0, width)] = out_grad
    og_all[own_block, pl.ds(width, 128)] = (
        lg_parts[0].astype(f32)
        + pltpu.roll(lg_parts[1].astype(f32), 8, 1)
        + pltpu.roll(lg_parts[2].astype(f32), 16, 1)
    ).astype(bf16)

    gather_start(og_all, og_sems)
    load_c.wait()
    for head in range(0, QUERY_HEADS, 2):
        pair = product_rows(out_grad, n2_all[pl.ds(head * HEAD_DIM, 2 * HEAD_DIM), :])
        for inner in (0, 1):
            do_rows[pl.ds((head + inner) * tokens, tokens)] = pair[
                :, inner * HEAD_DIM : (inner + 1) * HEAD_DIM
            ].astype(bf16)
    gather_pass(og_all, og_sems)

    def dkv_rows(kind_core, chip):
        return at_rows((kind_core * 4 + chip) * tokens, tokens, 128)

    def dkv_columns(group):
        return pl.ds(group * 2 * HEAD_DIM, 2 * HEAD_DIM)

    def dkv_sibling(group):
        source = g_all.at[at_rows((1 - core) * 4 * tokens, 4 * tokens, 128), dkv_columns(group)]
        target = dkv_recv.at[group, pl.ds(4 * tokens, 4 * tokens)]
        return remote(source, target, dkv_sems, (group, 0), sibling)

    def dkv_copy(group, step):
        chip = xor(lax.div(member, 2), step)
        return remote(
            g_all.at[dkv_rows(core, chip), dkv_columns(group)],
            dkv_recv.at[group, pl.ds(step * tokens, tokens)],
            dkv_sems,
            (group, step),
            in_plane(2 * step),
        )

    def dkv_pass(group):
        dkv_sibling(group).wait_recv()
        mine = at_rows(core * 4 * tokens, 4 * tokens, 128)
        g_all[mine, dkv_columns(group)] = (
            g_all[mine, dkv_columns(group)].astype(f32)
            + dkv_recv[group, pl.ds(4 * tokens, 4 * tokens)].astype(f32)
        ).astype(bf16)
        for step in (1, 2, 3):
            dkv_copy(group, step).start()

    planes = turn_recv.shape[1]

    def dense_rows(piece, step):
        return at_rows((piece * planes + xor(plane, step)) * rows, rows)

    def kv_grad_copy(step):
        source = arena.at[dense_rows(0, step), pl.ds(0, 2 * kv_width)]
        if step == 0:
            return pltpu.make_async_copy(source, grad_kv_ref.at[0], local_sems.at[0])
        device = (xor(plane, step), member)
        return remote(source, grad_kv_ref.at[step], dense_sems, (0, step), device)

    def pair_rows(piece, which):
        return pl.ds(width + ((piece - 1) * 2 + which) * rows, rows)

    def dense_copy(piece, step):
        columns = pl.ds((piece - 1) * width, width)
        if step == 2:
            target = grad_dense_ref.at[1, :, columns]
            device = (xor(plane, 2), member)
        else:
            target = n2_all.at[pair_rows(piece, step // 2)]
            device = (xor(plane, 1), member)
        return remote(arena.at[dense_rows(piece, step)], target, dense_sems, (piece, step), device)

    def dense_own(piece):
        return pltpu.make_async_copy(
            arena.at[dense_rows(piece, 0)],
            grad_dense_ref.at[0, :, pl.ds((piece - 1) * width, width)],
            local_sems.at[piece],
        )

    def dense_start(piece):
        for step in (3, 1):
            dense_copy(piece, step).start()

    def dense_pass(piece):
        for which, step in ((1, 2), (0, 0)):
            dense_copy(piece, 1 + 2 * which).wait_recv()
            block = dense_rows(piece, step)
            arena[block] = (
                arena[block].astype(f32) + n2_all[pair_rows(piece, which)].astype(f32)
            ).astype(bf16)
            if step:
                dense_copy(piece, 2).start()
            else:
                dense_own(piece).start()

    for group in range(KEY_VALUE_HEADS):
        values = kv_all[:, pl.ds(kv_width + group * HEAD_DIM, HEAD_DIM)]
        dk = jnp.zeros((seq_len, HEAD_DIM), f32)
        dv = jnp.zeros((seq_len, HEAD_DIM), f32)
        for pair in range(group * pairs_per_group, (group + 1) * pairs_per_group):
            scores, queries = pair_scores(pair, group)
            probs = jnp.exp(scores - lse_buf[pair][0:1])
            grads = do_rows[pl.ds(pair * 2 * tokens, 2 * tokens)]
            prob_grad = product_rows(values, grads)
            row_dot = jnp.sum(probs * prob_grad, axis=0, keepdims=True)
            score_grad = (probs * (prob_grad - row_dot)).astype(bf16)
            dk = dk + product(score_grad, queries)
            dv = dv + product(probs.astype(bf16), grads)
            dq = product(k_t[group], score_grad) * score_scale
            for inner in (0, 1):
                piece = jnp.transpose(dq[:, inner * tokens : (inner + 1) * tokens])
                qg_all[own_block, pl.ds((2 * pair + inner) * HEAD_DIM, HEAD_DIM)] = turned(
                    piece, -1.0
                ).astype(bf16)
        start = group * 2 * HEAD_DIM
        dk = (dk * score_scale).astype(bf16)
        dv = dv.astype(bf16)
        for block in range(8):
            place = pl.ds((block % 2 * 4 + block // 2) * tokens, tokens)
            here = slice(block * tokens, (block + 1) * tokens)
            g_all[place, pl.ds(start, HEAD_DIM)] = dk[here]
            g_all[place, pl.ds(start + HEAD_DIM, HEAD_DIM)] = dv[here]
        dkv_sibling(group).start()
        span = width // KEY_VALUE_HEADS
        gather_start(qg_all, qg_sems, (group,), group * span, (group + 1) * span)
        if group == 0:
            gather_pass_last(og_all, og_sems)
            dkv_pass(0)
            ret_second(1)

    dkv_pass(1)
    gather_pass(qg_all, qg_sems, (0,), 0, span)

    for group in range(KEY_VALUE_HEADS):
        start = group * 2 * HEAD_DIM
        mine = dkv_rows(core, lax.div(member, 2))
        dk = g_all[mine, pl.ds(start, HEAD_DIM)].astype(f32)
        dv = g_all[mine, pl.ds(start + HEAD_DIM, HEAD_DIM)].astype(f32)
        for step in (1, 2, 3):
            dkv_copy(group, step).wait_recv()
            block = pl.ds(step * tokens, tokens)
            dk = dk + dkv_recv[group, block, pl.ds(0, HEAD_DIM)].astype(f32)
            dv = dv + dkv_recv[group, block, pl.ds(HEAD_DIM, HEAD_DIM)].astype(f32)
        kvg_all[own_block, pl.ds(group * HEAD_DIM, HEAD_DIM)] = turned(dk, -1.0).astype(bf16)
        kvg_all[own_block, pl.ds(kv_width + group * HEAD_DIM, HEAD_DIM)] = dv.astype(bf16)
    gather_start(kvg_all, kvg_sems)
    ret_third(1)
    gather_finish(og_all, og_sems)
    for kind in range(3):
        for step in range(1, 8):
            turn_copy(kind, step).wait()
    turned_attn = turn_recv[1].reshape(planes * rows, seq_len)
    for start in range(0, width, 512):
        arena[pl.ds(2 * planes * rows, planes * rows), pl.ds(start, 512)] = product(
            turned_attn, og_all[:, pl.ds(start, 512)]
        ).astype(bf16)
    dense_start(2)
    router_part = product(
        turn_recv[2].reshape(planes * rows, seq_len), og_all[:, pl.ds(width, 128)]
    )

    gather_pass(qg_all, qg_sems, (1,), span, 2 * span)
    gather_pass(kvg_all, kvg_sems)
    for group in range(KEY_VALUE_HEADS):
        gather_pass_last(qg_all, qg_sems, (group,), group * span, (group + 1) * span)
    gather_pass_last(kvg_all, kvg_sems)

    load_b.wait()
    own_kvg = kvg_all[own_block, :]
    own_qg = qg_all[own_block, :]
    normed_grad = product_rows(own_kvg, full_a[:, pl.ds(0, 2 * kv_width)]) + product_rows(
        own_qg, cot_all[pl.ds(0, width), pl.ds(0, width)]
    )
    one_back, gain_a_row = norm_backward(
        x_ref[...].astype(f32), gain_buf[pl.ds(0, 1), :], normed_grad
    )
    dx_ref[...] = dx_ref[...] + one_back
    line = lax.broadcasted_iota(jnp.int32, (128, width), 0)
    gain_lines = jnp.zeros((128, width), f32)
    for offset, part in enumerate(split_three(gain_a_row) + split_three(gain_m_row)):
        gain_lines = jnp.where(line == 32 + offset, part.astype(f32), gain_lines)
    turn_send[3] = jnp.transpose(gain_lines.astype(bf16)).reshape(turn_send.shape[1:])
    turn_start(3)

    turned_normed = turn_recv[0].reshape(planes * rows, seq_len)
    for group in range(KEY_VALUE_HEADS):
        gather_finish(qg_all, qg_sems, (group,), group * span, (group + 1) * span)
    for start in range(0, width, 512):
        arena[pl.ds(planes * rows, planes * rows), pl.ds(start, 512)] = product(
            turned_normed, qg_all[:, pl.ds(start, 512)]
        ).astype(bf16)
    dense_start(1)
    dense_pass(2)
    gather_finish(kvg_all, kvg_sems)
    arena[pl.ds(0, planes * rows), pl.ds(0, 2 * kv_width)] = product(
        turned_normed, kvg_all[...]
    ).astype(bf16)
    for step in (2, 3, 1, 0):
        kv_grad_copy(step).start()
    dense_pass(1)
    for step in range(1, 8):
        turn_copy(3, step).wait()
    aux_total = router_part
    for block in range(8):
        aux_total = aux_total + turn_recv[3, :, :, pl.ds(block * tokens, tokens)].reshape(
            planes * rows, tokens
        ).astype(f32)
    aux_send[...] = aux_total.reshape(planes, rows, 128)

    def aux_copy(step):
        return remote(
            aux_send.at[xor(plane, step)],
            grad_aux_ref.at[step],
            aux_sems,
            (step,),
            (xor(plane, step), member),
        )

    for step in (1, 2, 3):
        aux_copy(step).start()
    own_aux = pltpu.make_async_copy(aux_send.at[plane], grad_aux_ref.at[0], local_sems.at[7])
    own_aux.start()

    block_out_ref[...] = (after_buf[...] + ret_total(1)).astype(bf16)

    for held in range(1, 8):
        ret_gate_copy(held).wait_send()
    for kind in (0, 1):
        ret_sent(kind)
    for group in range(KEY_VALUE_HEADS):
        dkv_sibling(group).wait_send()
        for step in (1, 2, 3):
            dkv_copy(group, step).wait_send()
    gin_copy(0).wait()
    for step in (1, 2, 3):
        gin_copy(step).wait()
    for slot in (0, 1):

        @pl.when(parity * 2 + slot != plane)
        def _():
            gout_copy(slot).wait_send()

        @pl.when(parity * 2 + slot == plane)
        def _():
            gout_local(slot).wait()

    for turn in (0, 1):

        @pl.when(out_half + 2 * turn != plane)
        def _():
            gout_arrived(turn).wait_recv()

    for step in range(4):
        kv_grad_copy(step).wait()
    for piece in (1, 2):
        dense_own(piece).wait()
        dense_copy(piece, 2).wait()
        for step in (1, 3):
            dense_copy(piece, step).wait_send()
    for step in (1, 2, 3):
        aux_copy(step).wait()
    own_aux.wait()


EXPERT_LANES = 8


def fast_body(
    tokens,
    cotangent,
    routes,
    gain_attn,
    w_query,
    key_weight,
    value_weight,
    w_output,
    gain_moe,
    w_router,
    w_in,
    w_out,
):
    f32, bf16 = jnp.float32, jnp.bfloat16
    total_rows, width = tokens.shape
    rows = w_query.shape[1]
    planes = lax.axis_size("dp")
    members = lax.axis_size("expert")
    seq_len = total_rows * members
    kv_width = key_weight.shape[2]
    quarter = w_in.shape[1]
    quarter_out = w_out.shape[1]
    half = FF // 2
    positions = lax.axis_index("expert") * total_rows + jnp.arange(total_rows, dtype=jnp.int32)
    cos_table, sin_table = rope_tables(positions, HEAD_DIM)
    rope = jnp.concatenate([cos_table, cos_table, -sin_table, sin_table], axis=1)
    in_vmem = pl.BlockSpec(memory_space=pltpu.VMEM)
    anywhere = pl.BlockSpec(memory_space=pl.ANY)
    pair_rows = 2 * seq_len
    shape = jax.ShapeDtypeStruct
    dma = pltpu.SemaphoreType.DMA
    heads = QUERY_HEADS
    (
        block_out,
        tokens_grad,
        grad_in,
        grad_out,
        grad_dense,
        grad_kv,
        grad_aux,
        _,
        _,
    ) = pl.pallas_call(
        layer_kernel,
        out_shape=(
            shape((total_rows, width), bf16),
            shape((total_rows, width), f32),
            shape((planes, quarter, 2 * half), bf16),
            shape((2, quarter_out, width), bf16),
            shape((2, rows, 2 * width), bf16),
            shape((planes, rows, 2 * kv_width), bf16),
            shape((planes, rows, 128), f32),
            shape((width, width), bf16),
            shape((width, width), bf16),
        ),
        in_specs=[in_vmem] * 11 + [anywhere] * 2,
        out_specs=(in_vmem,) * 2 + (anywhere,) * 7,
        scratch_shapes=[
            pltpu.VMEM((pair_rows, width), bf16),
            pltpu.VMEM((pair_rows, width + 128), bf16),
            pltpu.VMEM((width, 2 * kv_width + 128), bf16),
            pltpu.VMEM((38 * total_rows, width), bf16),
            pltpu.VMEM((32, total_rows, 128), bf16),
            pltpu.VMEM((width, 2 * half), bf16),
            pltpu.VMEM((half, width), bf16),
            pltpu.VMEM((pair_rows, half), bf16),
            pltpu.VMEM((pair_rows, 2 * half), bf16),
            pltpu.VMEM((seq_len, 2 * kv_width), bf16),
            pltpu.VMEM((KEY_VALUE_HEADS, HEAD_DIM, seq_len), bf16),
            pltpu.VMEM((KEY_VALUE_HEADS, HEAD_DIM, seq_len), bf16),
            pltpu.VMEM((heads * total_rows, HEAD_DIM), bf16),
            pltpu.VMEM((heads * total_rows, HEAD_DIM), bf16),
            pltpu.VMEM((total_rows, width), bf16),
            pltpu.VMEM((heads, HEAD_DIM, total_rows), bf16),
            pltpu.VMEM((total_rows, width), f32),
            pltpu.VMEM((heads // 2, 8, 2 * total_rows), f32),
            pltpu.VMEM((4, planes, members, rows, total_rows), bf16),
            pltpu.VMEM((4, planes, rows, seq_len), bf16),
            pltpu.VMEM((seq_len, width + 128), bf16),
            pltpu.VMEM((seq_len, width), bf16),
            pltpu.VMEM((seq_len, 2 * kv_width), bf16),
            pltpu.VMEM((KEY_VALUE_HEADS, seq_len, 2 * HEAD_DIM), bf16),
            pltpu.VMEM((planes, rows, 128), f32),
            pltpu.VMEM((16, width), f32),
            dma((2, 3, 4)),
            dma((2, 3, 4, 4)),
            dma((2, 3, 4, 4)),
            dma((2, 8)),
            dma((2, 2, 2, 8)),
            dma((2, 2)),
            dma((2, 4, 8)),
            dma((2, 4, 2)),
            dma((2, 2)),
            dma((2, 3, 2)),
            dma((2, 2, 3, 7)),
            dma((2, 8)),
            dma((2, 4)),
            dma((2, 2)),
            dma((2, 8)),
            dma((2, 2, 8)),
            dma((2, 8)),
            dma((2, 2, 8)),
            dma((2, 3, 4)),
            dma((2, 4)),
            dma((8,)),
            pltpu.SemaphoreType.REGULAR,
        ],
        compiler_params=pltpu.CompilerParams(
            collective_id=0, has_side_effects=True, vmem_limit_bytes=63 * 2**20
        ),
    )(
        tokens,
        cotangent,
        routes[0].T,
        rope,
        key_weight[0],
        value_weight[0],
        w_router[0].T,
        gain_attn,
        gain_moe,
        w_query[0],
        w_output[0],
        w_in.reshape(quarter, 2 * FF),
        w_out.reshape(quarter_out, width),
    )
    own = grad_in[0].astype(f32) + grad_in[2].astype(f32)
    other = grad_in[1].astype(f32) + grad_in[3].astype(f32)
    even = lax.rem(lax.axis_index("dp"), 2) == 0
    low, high = jnp.where(even, own, other), jnp.where(even, other, own)
    w_in_grad = jnp.concatenate(
        [low[:, :half], high[:, :half], low[:, half:], high[:, half:]], axis=1
    )
    w_out_grad = grad_out[0].astype(f32) + grad_out[1].astype(f32)
    dense = grad_dense[0].astype(f32) + grad_dense[1].astype(f32)
    dense_kv = jnp.sum(grad_kv.astype(f32), axis=0)
    aux = jnp.sum(grad_aux, axis=0)
    return (
        block_out,
        tokens_grad,
        jnp.sum(aux[:, 32:35], axis=1)[None],
        dense[None, :, :width],
        dense_kv[None, :, :kv_width],
        dense_kv[None, :, kv_width:],
        dense[None, :, width:],
        jnp.sum(aux[:, 35:38], axis=1)[None],
        (aux[:, :8] + aux[:, 8:16] + aux[:, 16:24])[None],
        w_in_grad[None, :, None, :],
        w_out_grad[None, :, None, :],
    )


def solution(mesh):
    in_specs = (
        P(("dp", "expert"), None),
        P(("dp", "expert"), None),
        P(None, ("dp", "expert"), None),
        P(None, ("dp", "expert")),
        P(None, ("dp", "expert"), None),
        P(None, ("dp", "expert"), None),
        P(None, ("dp", "expert"), None),
        P(None, ("dp", "expert"), None),
        P(None, ("dp", "expert")),
        P(None, ("dp", "expert"), None),
        P(None, "dp", "expert", None),
        P(None, "dp", "expert", None),
    )
    out_specs = (
        P(("dp", "expert"), None),
        P(("dp", "expert"), None),
        P(None, ("dp", "expert")),
        P(None, ("dp", "expert"), None),
        P(None, ("dp", "expert"), None),
        P(None, ("dp", "expert"), None),
        P(None, ("dp", "expert"), None),
        P(None, ("dp", "expert")),
        P(None, ("dp", "expert"), None),
        P(None, "dp", "expert", None),
        P(None, "dp", "expert", None),
    )
    body = fast_body if mesh.shape["dp"] == 4 and mesh.shape["expert"] == 8 else general_body
    return jax.shard_map(body, mesh=mesh, in_specs=in_specs, out_specs=out_specs, check_vma=False)
```

```python
import functools

import jax
import jax.numpy as jnp
from jax import lax
from jax.experimental import pallas as pl
from jax.experimental.pallas import tpu as pltpu
from jax.sharding import PartitionSpec as P

MESH = pl.DeviceIdType.MESH

QUERY_HEADS = 12
KEY_VALUE_HEADS = 2
HEAD_DIM = 128
FF = 768
TOP = 4


norm_eps = 1e-06
rope_base = 1000000.0
masked_score = -1e30
top_precision = lax.Precision.HIGHEST


def norm_factor(values):
    return lax.rsqrt(jnp.mean(values * values, axis=-1, keepdims=True) + norm_eps)


def norm_back(values, gain, grad_out):
    factor = norm_factor(values)
    scaled = grad_out * gain
    gain_grad = jnp.sum(grad_out * values * factor, axis=0)
    inner_mean = jnp.mean(scaled * values, axis=-1, keepdims=True)
    return (factor * scaled - values * factor * factor * factor * inner_mean, gain_grad)


def rope_tables(positions, head_size):
    half_size = head_size // 2
    inverse = rope_base ** (-(jnp.arange(half_size, dtype=jnp.float32) * 2.0 / head_size))
    angles = positions.astype(jnp.float32)[:, None] * inverse[None, :]
    return (jnp.cos(angles), jnp.sin(angles))


def rotate(values, cos_table, sin_table, orient):
    half_size = values.shape[-1] // 2
    first_half = values[..., :half_size]
    second = values[..., half_size:]
    cos_part = cos_table[:, None, :]
    sin_part = orient * sin_table[:, None, :]
    return jnp.concatenate(
        [first_half * cos_part - second * sin_part, second * cos_part + first_half * sin_part],
        axis=-1,
    )


def plan_slots(route, expert_count, capacity):
    flat_route = route.reshape(-1)
    slot_total = flat_route.shape[0]
    onehot = (flat_route[:, None] == jnp.arange(expert_count, dtype=jnp.int32)[None, :]).astype(
        jnp.int32
    )
    before = jnp.cumsum(onehot, axis=0) - onehot
    target = flat_route * capacity + jnp.sum(before * onehot, axis=1)
    source = (
        jnp.full((expert_count * capacity,), slot_total, jnp.int32)
        .at[target]
        .set(jnp.arange(slot_total, dtype=jnp.int32))
    )
    filled = source < slot_total
    return (target, jnp.minimum(source, slot_total - 1), filled)


def general_body(
    tokens,
    cotangent,
    routes,
    gain_attn,
    w_query,
    key_weight,
    value_weight,
    w_output,
    gain_moe,
    w_router,
    w_in,
    w_out,
):
    total_rows, model_width = tokens.shape
    layer_count = w_query.shape[0]
    group_count = lax.axis_size("expert")
    seq_len = total_rows * group_count
    experts_local = w_in.shape[2]
    expert_count = experts_local * group_count
    capacity = min(total_rows, total_rows * TOP * 3 // (2 * expert_count))
    heads_per_group = QUERY_HEADS // KEY_VALUE_HEADS
    score_scale = HEAD_DIM ** (-0.5)
    positions = lax.axis_index("expert") * total_rows + jnp.arange(total_rows, dtype=jnp.int32)
    cos_table, sin_table = rope_tables(positions, HEAD_DIM)
    allowed = jnp.arange(seq_len, dtype=jnp.int32)[None, :] <= positions[:, None]
    zero_bf = jnp.zeros((), jnp.bfloat16)

    def score_block(query_rows, all_keys, group_of_heads):
        grouped_q = query_rows[
            :, group_of_heads * heads_per_group : (group_of_heads + 1) * heads_per_group, :
        ]
        scores = (
            jnp.einsum(
                "rgd,kd->grk",
                grouped_q,
                all_keys[:, group_of_heads, :],
                preferred_element_type=jnp.float32,
            )
            * score_scale
        )
        return (jnp.where(allowed[None], scores, masked_score), grouped_q)

    residual = tokens.astype(jnp.float32)
    layer_number = 0
    dense_w = (
        lax.all_gather(gain_attn[layer_number], ("dp", "expert"), axis=0, tiled=True),
        lax.all_gather(w_query[layer_number], ("dp", "expert"), axis=0, tiled=True),
        lax.all_gather(key_weight[layer_number], ("dp", "expert"), axis=0, tiled=True),
        lax.all_gather(value_weight[layer_number], ("dp", "expert"), axis=0, tiled=True),
        lax.all_gather(w_output[layer_number], ("dp", "expert"), axis=0, tiled=True),
        lax.all_gather(gain_moe[layer_number], ("dp", "expert"), axis=0, tiled=True),
        lax.all_gather(w_router[layer_number], ("dp", "expert"), axis=0, tiled=True),
    )
    expert_w = (
        lax.all_gather(w_in[layer_number], "dp", axis=0, tiled=True),
        lax.all_gather(w_out[layer_number], "dp", axis=0, tiled=True),
    )
    route = routes[layer_number]
    gain_a = dense_w[0].astype(jnp.float32)
    norm_result = (residual * norm_factor(residual) * gain_a).astype(jnp.bfloat16)
    query_rows = jnp.dot(norm_result, dense_w[1], preferred_element_type=jnp.float32).reshape(
        total_rows, QUERY_HEADS, HEAD_DIM
    )
    query_rows = rotate(query_rows, cos_table, sin_table, 1.0).astype(jnp.bfloat16)
    key_matrix_rows = jnp.dot(norm_result, dense_w[2], preferred_element_type=jnp.float32).reshape(
        total_rows, KEY_VALUE_HEADS, HEAD_DIM
    )
    key_matrix_rows = rotate(key_matrix_rows, cos_table, sin_table, 1.0).astype(jnp.bfloat16)
    value_matrix_rows = (
        jnp.dot(norm_result, dense_w[3], preferred_element_type=jnp.float32)
        .astype(jnp.bfloat16)
        .reshape(total_rows, KEY_VALUE_HEADS, HEAD_DIM)
    )
    all_keys = lax.all_gather(key_matrix_rows, "expert", axis=0, tiled=True)
    all_values = lax.all_gather(value_matrix_rows, "expert", axis=0, tiled=True)
    heads_out = []
    log_totals = []
    for group_of_heads in range(KEY_VALUE_HEADS):
        scores, grouped_q = score_block(query_rows, all_keys, group_of_heads)
        row_peak = jnp.max(scores, axis=-1, keepdims=True)
        expo_vals = jnp.exp(scores - row_peak)
        row_sums = jnp.sum(expo_vals, axis=-1, keepdims=True)
        attn_probs = (expo_vals / row_sums).astype(jnp.bfloat16)
        log_totals.append(row_peak + jnp.log(row_sums))
        heads_out.append(
            jnp.einsum(
                "grk,kd->rgd",
                attn_probs,
                all_values[:, group_of_heads, :],
                preferred_element_type=jnp.float32,
            )
        )
    attn = (
        jnp.concatenate(heads_out, axis=1)
        .reshape(total_rows, QUERY_HEADS * HEAD_DIM)
        .astype(jnp.bfloat16)
    )
    after_attn = residual + jnp.dot(attn, dense_w[4], preferred_element_type=jnp.float32)
    gain_m = dense_w[5].astype(jnp.float32)
    normed_two = (after_attn * norm_factor(after_attn) * gain_m).astype(jnp.bfloat16)
    logits = jnp.dot(normed_two, dense_w[6], preferred_element_type=jnp.float32)
    gate_probs = jax.nn.softmax(jnp.take_along_axis(logits, route, axis=1), axis=-1)
    target, source, filled = plan_slots(route, expert_count, capacity)
    send_rows = jnp.where(filled[:, None], normed_two[source // TOP], zero_bf)
    send_rows = send_rows.reshape(group_count, experts_local, capacity, model_width)
    arrived_rows = lax.all_to_all(send_rows, "expert", split_axis=0, concat_axis=0, tiled=True)
    gate_up_vals = jnp.einsum(
        "secd,def->secf", arrived_rows, expert_w[0], preferred_element_type=jnp.float32
    )
    expert_gate_half = gate_up_vals[..., :FF]
    expert_hidden_act = (
        expert_gate_half * jax.nn.sigmoid(expert_gate_half) * gate_up_vals[..., FF:]
    ).astype(jnp.bfloat16)
    expert_out = jnp.einsum(
        "secf,fed->secd", expert_hidden_act, expert_w[1], preferred_element_type=jnp.float32
    ).astype(jnp.bfloat16)
    arrived, gate_up, expert_out = (arrived_rows, gate_up_vals, expert_out)
    returned = lax.all_to_all(expert_out, "expert", split_axis=0, concat_axis=0, tiled=True)
    slot_out = returned.reshape(expert_count * capacity, model_width)[target].reshape(
        total_rows, TOP, model_width
    )
    new_residual = after_attn + jnp.sum(
        gate_probs[:, :, None] * slot_out.astype(jnp.float32), axis=1
    )
    saved_layers = [
        (
            residual,
            norm_result,
            query_rows,
            key_matrix_rows,
            value_matrix_rows,
            all_keys,
            all_values,
            log_totals,
            attn,
            after_attn,
            normed_two,
            route,
            gate_probs,
            target,
            source,
            filled,
            arrived,
            gate_up,
            slot_out,
            dense_w,
            expert_w,
        )
    ]
    block_out = new_residual.astype(jnp.bfloat16)
    grad_resid = cotangent.astype(jnp.float32)
    grad_lists = [[None] * layer_count for _ in range(9)]
    for layer_number in reversed(range(layer_count)):
        (
            resid_in,
            norm_result,
            query_rows,
            key_matrix_rows,
            value_matrix_rows,
            all_keys,
            all_values,
            log_totals,
            attn,
            after_attn,
            normed_two,
            route,
            gate_probs,
            target,
            source,
            filled,
            arrived,
            gate_up,
            slot_out,
            dense_w,
            expert_w,
        ) = saved_layers[layer_number]
        dense_w = (
            lax.all_gather(gain_attn[layer_number], ("dp", "expert"), axis=0, tiled=True),
            lax.all_gather(w_query[layer_number], ("dp", "expert"), axis=0, tiled=True),
            lax.all_gather(key_weight[layer_number], ("dp", "expert"), axis=0, tiled=True),
            lax.all_gather(value_weight[layer_number], ("dp", "expert"), axis=0, tiled=True),
            lax.all_gather(w_output[layer_number], ("dp", "expert"), axis=0, tiled=True),
            lax.all_gather(gain_moe[layer_number], ("dp", "expert"), axis=0, tiled=True),
            lax.all_gather(w_router[layer_number], ("dp", "expert"), axis=0, tiled=True),
        )
        expert_w = (
            lax.all_gather(w_in[layer_number], "dp", axis=0, tiled=True),
            lax.all_gather(w_out[layer_number], "dp", axis=0, tiled=True),
        )
        all_keys, all_values = (
            lax.all_gather(key_matrix_rows, "expert", axis=0, tiled=True),
            lax.all_gather(value_matrix_rows, "expert", axis=0, tiled=True),
        )
        gate_grad = jnp.sum(slot_out.astype(jnp.float32) * grad_resid[:, None, :], axis=-1)
        slot_grad = (
            (gate_probs[:, :, None] * grad_resid[:, None, :])
            .astype(jnp.bfloat16)
            .reshape(total_rows * TOP, model_width)
        )
        grad_rows = jnp.where(filled[:, None], slot_grad[source], zero_bf)
        grad_rows = grad_rows.reshape(group_count, experts_local, capacity, model_width)
        grad_arrived = lax.all_to_all(grad_rows, "expert", split_axis=0, concat_axis=0, tiled=True)
        gate_half = gate_up[..., :FF]
        up_half = gate_up[..., FF:]
        sigmoid_vals = jax.nn.sigmoid(gate_half)
        silu_vals = gate_half * sigmoid_vals
        hidden_act = (silu_vals * up_half).astype(jnp.bfloat16)
        act_grad = jnp.einsum(
            "secd,fed->secf", grad_arrived, expert_w[1], preferred_element_type=jnp.float32
        )
        gate_part = act_grad * up_half * sigmoid_vals * (1.0 + gate_half * (1.0 - sigmoid_vals))
        gate_up_grad = jnp.concatenate([gate_part, act_grad * silu_vals], axis=-1).astype(
            jnp.bfloat16
        )
        input_grad = jnp.einsum(
            "secf,def->secd", gate_up_grad, expert_w[0], preferred_element_type=jnp.float32
        ).astype(jnp.bfloat16)
        returned_grad = lax.all_to_all(
            input_grad, "expert", split_axis=0, concat_axis=0, tiled=True
        )
        grad_lists[7][layer_number] = lax.psum_scatter(
            jnp.einsum(
                "secd,secf->def", arrived, gate_up_grad, preferred_element_type=jnp.float32
            ).astype(jnp.bfloat16),
            "dp",
            scatter_dimension=0,
            tiled=True,
        ).astype(jnp.float32)
        grad_lists[8][layer_number] = lax.psum_scatter(
            jnp.einsum(
                "secf,secd->fed", hidden_act, grad_arrived, preferred_element_type=jnp.float32
            ).astype(jnp.bfloat16),
            "dp",
            scatter_dimension=0,
            tiled=True,
        ).astype(jnp.float32)
        slot_back = returned_grad.reshape(expert_count * capacity, model_width)[target].reshape(
            total_rows, TOP, model_width
        )
        normed_two_grad = jnp.sum(slot_back.astype(jnp.float32), axis=1)
        gate_inner = jnp.sum(gate_probs * gate_grad, axis=-1, keepdims=True)
        chosen_grad = gate_probs * (gate_grad - gate_inner)
        route_hot = (
            route[:, :, None] == jnp.arange(expert_count, dtype=jnp.int32)[None, None, :]
        ).astype(jnp.float32)
        logit_grad = jnp.sum(route_hot * chosen_grad[:, :, None], axis=1)
        router_f = dense_w[6].astype(jnp.float32)
        normed_two_grad = normed_two_grad + jnp.einsum(
            "re,de->rd", logit_grad, router_f, precision=top_precision
        )
        router_grad = jnp.einsum(
            "rd,re->de", normed_two.astype(jnp.float32), logit_grad, precision=top_precision
        )
        gain_m = dense_w[5].astype(jnp.float32)
        norm_two_back, gain_m_grad = norm_back(after_attn, gain_m, normed_two_grad)
        mid_grad = grad_resid + norm_two_back
        out_grad = mid_grad.astype(jnp.bfloat16)
        output_grad = jnp.einsum("rq,rd->qd", attn, out_grad, preferred_element_type=jnp.float32)
        attn_grad = (
            jnp.einsum("rd,qd->rq", out_grad, dense_w[4], preferred_element_type=jnp.float32)
            .astype(jnp.bfloat16)
            .reshape(total_rows, QUERY_HEADS, HEAD_DIM)
        )
        query_grads = []
        key_grads = []
        value_grads = []
        for group_of_heads in range(KEY_VALUE_HEADS):
            scores, grouped_q = score_block(query_rows, all_keys, group_of_heads)
            grouped_do = attn_grad[
                :, group_of_heads * heads_per_group : (group_of_heads + 1) * heads_per_group, :
            ]
            probs = jnp.exp(scores - log_totals[group_of_heads])
            prob_bf = probs.astype(jnp.bfloat16)
            prob_grad = jnp.einsum(
                "rgd,kd->grk",
                grouped_do,
                all_values[:, group_of_heads, :],
                preferred_element_type=jnp.float32,
            )
            row_dot = jnp.sum(probs * prob_grad, axis=-1, keepdims=True)
            score_grad = (probs * (prob_grad - row_dot)).astype(jnp.bfloat16)
            query_grads.append(
                jnp.einsum(
                    "grk,kd->rgd",
                    score_grad,
                    all_keys[:, group_of_heads, :],
                    preferred_element_type=jnp.float32,
                )
                * score_scale
            )
            key_grads.append(
                jnp.einsum("grk,rgd->kd", score_grad, grouped_q, preferred_element_type=jnp.float32)
                * score_scale
            )
            value_grads.append(
                jnp.einsum("grk,rgd->kd", prob_bf, grouped_do, preferred_element_type=jnp.float32)
            )
        key_sum, value_total_sum = (
            lax.psum_scatter(
                jnp.stack(key_grads, axis=1).astype(jnp.bfloat16),
                "expert",
                scatter_dimension=0,
                tiled=True,
            ).astype(jnp.float32),
            lax.psum_scatter(
                jnp.stack(value_grads, axis=1).astype(jnp.bfloat16),
                "expert",
                scatter_dimension=0,
                tiled=True,
            ).astype(jnp.float32),
        )
        query_grad = (
            rotate(jnp.concatenate(query_grads, axis=1), cos_table, sin_table, -1.0)
            .astype(jnp.bfloat16)
            .reshape(total_rows, QUERY_HEADS * HEAD_DIM)
        )
        key_grad = (
            rotate(key_sum, cos_table, sin_table, -1.0)
            .astype(jnp.bfloat16)
            .reshape(total_rows, KEY_VALUE_HEADS * HEAD_DIM)
        )
        value_rows_gradient = value_total_sum.astype(jnp.bfloat16).reshape(
            total_rows, KEY_VALUE_HEADS * HEAD_DIM
        )
        normed_grad = jnp.einsum(
            "rq,dq->rd", query_grad, dense_w[1], preferred_element_type=jnp.float32
        )
        normed_grad = normed_grad + jnp.einsum(
            "rq,dq->rd", key_grad, dense_w[2], preferred_element_type=jnp.float32
        )
        normed_grad = normed_grad + jnp.einsum(
            "rq,dq->rd", value_rows_gradient, dense_w[3], preferred_element_type=jnp.float32
        )
        query_w_grad = jnp.einsum(
            "rd,rq->dq", norm_result, query_grad, preferred_element_type=jnp.float32
        )
        key_w_grad = jnp.einsum(
            "rd,rq->dq", norm_result, key_grad, preferred_element_type=jnp.float32
        )
        value_w_grad = jnp.einsum(
            "rd,rq->dq", norm_result, value_rows_gradient, preferred_element_type=jnp.float32
        )
        gain_a = dense_w[0].astype(jnp.float32)
        norm_one_back, gain_a_grad = norm_back(resid_in, gain_a, normed_grad)
        grad_resid = mid_grad + norm_one_back
        shares = (
            lax.psum_scatter(gain_a_grad, ("dp", "expert"), scatter_dimension=0, tiled=True),
            lax.psum_scatter(query_w_grad, ("dp", "expert"), scatter_dimension=0, tiled=True),
            lax.psum_scatter(key_w_grad, ("dp", "expert"), scatter_dimension=0, tiled=True),
            lax.psum_scatter(value_w_grad, ("dp", "expert"), scatter_dimension=0, tiled=True),
            lax.psum_scatter(output_grad, ("dp", "expert"), scatter_dimension=0, tiled=True),
            lax.psum_scatter(gain_m_grad, ("dp", "expert"), scatter_dimension=0, tiled=True),
            lax.psum_scatter(router_grad, ("dp", "expert"), scatter_dimension=0, tiled=True),
        )
        for member in range(7):
            grad_lists[member][layer_number] = shares[member]
    stacked = [jnp.stack(grad_lists[member], axis=0) for member in range(9)]
    return (
        block_out,
        grad_resid,
        stacked[0],
        stacked[1],
        stacked[2],
        stacked[3],
        stacked[4],
        stacked[5],
        stacked[6],
        stacked[7],
        stacked[8],
    )


def product(left, right):
    return lax.dot_general(
        left, right, (((1,), (0,)), ((), ())), preferred_element_type=jnp.float32
    )


def product_rows(left, right):
    return lax.dot_general(
        left, right, (((1,), (1,)), ((), ())), preferred_element_type=jnp.float32
    )


def product_columns(left, right):
    return lax.dot_general(
        left, right, (((0,), (0,)), ((), ())), preferred_element_type=jnp.float32
    )


def split_three(values):
    high = values.astype(jnp.bfloat16)
    rest = values - high.astype(jnp.float32)
    middle = rest.astype(jnp.bfloat16)
    low = (rest - middle.astype(jnp.float32)).astype(jnp.bfloat16)
    return high, middle, low


def masked_gates(rows, router, mask):
    chosen = mask.astype(jnp.float32) > 0.5
    logits = jnp.where(chosen, product(rows, router), masked_score)
    expo_vals = jnp.where(chosen, jnp.exp(logits - jnp.max(logits, axis=1, keepdims=True)), 0.0)
    return expo_vals / jnp.sum(expo_vals, axis=1, keepdims=True)


def layer_kernel(
    x_ref,
    cot_ref,
    routes_ref,
    rope_ref,
    key_ref,
    value_ref,
    router_ref,
    gain_a_ref,
    gain_m_ref,
    shard_b,
    shard_c,
    w_in_ref,
    w_out_ref,
    block_out_ref,
    dx_ref,
    grad_in_ref,
    grad_out_ref,
    grad_dense_ref,
    grad_kv_ref,
    grad_aux_ref,
    spill_b,
    spill_c,
    n2_all,
    cot_all,
    full_a,
    arena,
    gate_buf,
    w_in_half,
    w_out_half,
    hidden_all,
    g_all,
    kv_all,
    k_t,
    v_t,
    q_rows,
    do_rows,
    normed_buf,
    attn_buf,
    after_buf,
    lse_buf,
    turn_send,
    turn_recv,
    og_all,
    qg_all,
    kvg_all,
    dkv_recv,
    aux_send,
    gain_buf,
    z_sems,
    p_sems,
    s_sems,
    kv_sems,
    tok_sems,
    tz_sems,
    turn_sems,
    win_sems,
    wout_sems,
    sib_sems,
    ret_sems,
    gate_sems,
    gin_sems,
    gout_sems,
    og_sems,
    qg_sems,
    kvg_sems,
    dkv_sems,
    dense_sems,
    aux_sems,
    local_sems,
    credit_sem,
):
    plane = lax.axis_index("dp")
    member = lax.axis_index("expert")
    core = lax.rem(member, 2)
    parity = lax.rem(plane, 2)
    tokens, width = x_ref.shape
    rows = shard_b.shape[0]
    xor = lax.bitwise_xor
    f32, bf16 = jnp.float32, jnp.bfloat16
    half = FF // 2
    score_scale = HEAD_DIM ** (-0.5)
    kv_width = KEY_VALUE_HEADS * HEAD_DIM

    def at_rows(start, count, step=16):
        return pl.ds(pl.multiple_of(start, step), count)

    def remote(source, target, sems, index, device, recv_index=None):
        return pltpu.make_async_remote_copy(
            src_ref=source,
            dst_ref=target,
            send_sem=sems.at[(0,) + index],
            recv_sem=sems.at[(1,) + (index if recv_index is None else recv_index)],
            device_id=device,
            device_id_type=MESH,
        )

    in_plane = lambda step: (plane, xor(member, step))
    sibling = in_plane(1)

    barrier = pltpu.get_barrier_semaphore()
    greeted = [(xor(plane, s), member) for s in (1, 2, 3)]
    greeted += [in_plane(s) for s in range(1, 8)]
    greeted += [(xor(plane, 1), xor(member, s)) for s in (2, 4, 6)]
    for device in greeted:
        pl.semaphore_signal(barrier, inc=1, device_id=device, device_id_type=MESH)

    def dense_block(part, step, chip_step):
        start = (xor(plane, step) * 8 + xor(member, chip_step)) * rows
        if part == 0:
            return full_a.at[at_rows(start, rows)]
        return arena.at[at_rows(start + (part - 1) * width, rows)]

    def z_copy(part, step):
        block = dense_block(part, 0, 0)
        return remote(block, block, z_sems, (part, step), (xor(plane, step), member))

    def plane_copy(part, step, chip):
        if chip < 3:
            block = dense_block(part, step, 0)
            return remote(block, block, p_sems, (part, step, chip), in_plane(2 * chip))
        via = 1 + step % 2
        block = dense_block(part, step, 2 * via)
        return remote(block, block, p_sems, (part, step, 3), in_plane(2 * (3 - via)))

    def sibling_copy(part, step, chip):
        block = dense_block(part, step, 2 * chip)
        return remote(block, block, s_sems, (part, step, chip), sibling)

    own_rows = (plane * 8 + member) * rows
    full_a[at_rows(own_rows, rows), pl.ds(0, kv_width)] = key_ref[...]
    full_a[at_rows(own_rows, rows), pl.ds(kv_width, kv_width)] = value_ref[...]
    line = lax.broadcasted_iota(jnp.int32, (128, rows), 0)
    gains = jnp.where(line == EXPERT_LANES, gain_a_ref[...].astype(f32), 0.0) + jnp.where(
        line == EXPERT_LANES + 1, gain_m_ref[...].astype(f32), 0.0
    )
    lines = jnp.concatenate(
        [router_ref[...].astype(f32), gains[EXPERT_LANES:]], axis=0
    ).astype(bf16)
    square = (
        lax.broadcasted_iota(jnp.int32, (rows, rows), 0)
        == lax.broadcasted_iota(jnp.int32, (rows, rows), 1)
    ).astype(bf16)
    full_a[at_rows(own_rows, rows), pl.ds(2 * kv_width, 128)] = product_rows(
        square, lines
    ).astype(bf16)
    arena[at_rows(own_rows, rows)] = shard_b[...]
    arena[at_rows(own_rows + width, rows)] = shard_c[...]

    def token_rows(plane_step, member_step):
        start = (xor(parity, plane_step) * 8 + xor(member, member_step)) * tokens
        return at_rows(start, tokens, 128)

    cot_all[token_rows(0, 0), pl.ds(0, width)] = cot_ref[...]
    expert_line = lax.broadcasted_iota(jnp.int32, (128, tokens), 0)
    named = jnp.zeros((128, tokens), f32)
    for slot in range(TOP):
        named = jnp.where(expert_line == routes_ref[pl.ds(slot, 1), :], 1.0, named)
    cot_all[token_rows(0, 0), pl.ds(width, 128)] = jnp.transpose(named).astype(bf16)
    pl.semaphore_wait(barrier, len(greeted))

    for part in range(3):
        for step in (3, 2, 1):
            z_copy(part, step).start()
    for part in range(3):
        for chip in (1, 2):
            plane_copy(part, 0, chip).start()
        sibling_copy(part, 0, 0).start()

    def pass_on_plane(part):
        for step in (1, 2, 3):
            z_copy(part, step).wait_recv()
            for chip in (1, 2):
                plane_copy(part, step, chip).start()
            sibling_copy(part, step, 0).start()

    def pass_on_diagonal(part, steps):
        for step in steps:
            for chip in (1, 2):
                plane_copy(part, step, chip).wait_recv()
                if chip == 1 + step % 2:
                    plane_copy(part, step, 3).start()
                sibling_copy(part, step, chip).start()

    def pass_on_sibling(part):
        for step in range(4):
            plane_copy(part, step, 3).wait_recv()
            sibling_copy(part, step, 3).start()

    def arrived_dense(part):
        for step in range(4):
            for chip in range(4):
                sibling_copy(part, step, chip).wait_recv()

    def sent_dense(part):
        for step in range(4):
            if step:
                z_copy(part, step).wait_send()
            for chip in range(4):
                if chip:
                    plane_copy(part, step, chip).wait_send()
                sibling_copy(part, step, chip).wait_send()

    token_arrays = (cot_all, n2_all)

    parts = (0, 512, 1024)

    def cube_device(bits):
        return (xor(plane, bits & 1), xor(member, bits & 6))

    def part_order(part):
        return [1 << ((part + k) % 3) for k in range(3)]

    def token_z(kind):
        block = token_arrays[kind].at[token_rows(0, 0)]
        return remote(block, block, tz_sems, (kind,), (xor(plane, 1), member))

    def token_where(kind, plane_step):
        base = xor(parity, plane_step) * 8 * tokens
        return token_arrays[kind], tok_sems, (kind, plane_step), 0, None, base

    quarter = w_in_ref.shape[0]
    quarter_out = w_out_ref.shape[0]

    def win_copy(step, piece):
        other = xor(parity, step % 2)
        source = w_in_ref.at[:, at_rows(piece * FF + other * half, half, 128)]
        target = w_in_half.at[at_rows(plane * quarter, quarter), pl.ds(piece * half, half)]
        if step == 0:
            return pltpu.make_async_copy(source, target, local_sems.at[piece])
        return remote(source, target, win_sems, (step, piece), (xor(plane, step), member))

    out_half = lax.div(plane, 2)

    def wout_send(turn):
        target = w_out_half.at[at_rows(parity * quarter_out, quarter_out)]
        device = (out_half + 2 * turn, member)
        return remote(w_out_ref, target, wout_sems, (turn,), device, (parity,))

    def wout_arrived(slot):
        target = w_out_half.at[at_rows(slot * quarter_out, quarter_out)]
        return remote(w_out_ref, target, wout_sems, (slot,), (xor(plane, 1), member))

    def wout_local():
        return pltpu.make_async_copy(
            w_out_ref,
            w_out_half.at[at_rows(parity * quarter_out, quarter_out)],
            local_sems.at[2],
        )

    def expert_start():
        for step in (1, 3, 2):
            for piece in (0, 1):
                win_copy(step, piece).start()
        for piece in (0, 1):
            win_copy(0, piece).start()
        for turn in (0, 1):

            @pl.when(out_half + 2 * turn != plane)
            def _():
                wout_send(turn).start()

        @pl.when(out_half == parity)
        def _():
            wout_local().start()

    def expert_finish():
        for step in (1, 3, 2):
            for piece in (0, 1):
                win_copy(step, piece).wait()
        for piece in (0, 1):
            win_copy(0, piece).wait()
        for slot in (0, 1):

            @pl.when(parity * 2 + slot != plane)
            def _():
                wout_arrived(slot).wait_recv()

        for turn in (0, 1):

            @pl.when(out_half + 2 * turn != plane)
            def _():
                wout_send(turn).wait_send()

        @pl.when(out_half == parity)
        def _():
            wout_local().wait()

    def gather_copy(array, sems, index, lead=(), start=0, stop=None, base=0):
        stop = array.shape[1] if stop is None else stop
        middle = (start + stop) // 256 * 128
        owner_step, device_step = ((0, 2), (0, 4), (2, 4), (4, 2), (0, 1), (2, 1), (4, 1), (6, 1))[
            index
        ]
        if index == 2:
            stop = middle
        if index == 3:
            start = middle
        block = at_rows(base + xor(member, owner_step) * tokens, tokens, 128)
        piece = array.at[block, pl.ds(start, stop - start)]
        return remote(piece, piece, sems, lead + (index,), in_plane(device_step))

    def gather_start(*where):
        for index in (0, 1, 4):
            gather_copy(where[0], where[1], index, *where[2:]).start()

    def gather_pass(*where):
        for index in (0, 1):
            gather_copy(where[0], where[1], index, *where[2:]).wait_recv()
            gather_copy(where[0], where[1], 2 + index, *where[2:]).start()
            gather_copy(where[0], where[1], 5 + index, *where[2:]).start()

    def gather_pass_last(*where):
        for index in (2, 3):
            gather_copy(where[0], where[1], index, *where[2:]).wait_recv()
        gather_copy(where[0], where[1], 7, *where[2:]).start()

    def gather_sent(*where):
        for index in range(8):
            gather_copy(where[0], where[1], index, *where[2:]).wait_send()

    def gather_finish(*where):
        gather_sent(*where)
        for index in range(4, 8):
            gather_copy(where[0], where[1], index, *where[2:]).wait_recv()

    pass_on_plane(0)
    pass_on_plane(1)
    pass_on_diagonal(0, range(4))
    pass_on_sibling(0)
    arrived_dense(0)
    token_z(0).start()
    expert_start()
    aux = full_a[:, pl.ds(2 * kv_width, 128)]
    pick = (
        lax.broadcasted_iota(jnp.int32, (16, 128), 1)
        == lax.broadcasted_iota(jnp.int32, (16, 128), 0) + EXPERT_LANES
    ).astype(bf16)
    gain_buf[...] = product_rows(pick, aux)
    gain_a = gain_buf[pl.ds(0, 1), :]
    gain_m = gain_buf[pl.ds(1, 1), :]
    residual = x_ref[...].astype(f32)
    normed = (residual * norm_factor(residual) * gain_a).astype(bf16)
    normed_buf[...] = normed
    cos_part = rope_ref[:, pl.ds(0, HEAD_DIM)]
    sin_part = rope_ref[:, pl.ds(HEAD_DIM, HEAD_DIM)]

    def turned(values, orient):
        swapped = pltpu.roll(values, HEAD_DIM // 2, 1)
        return values * cos_part + swapped * (sin_part * orient)

    kv_rows = product(normed, full_a[:, pl.ds(0, 2 * kv_width)])
    own_block = at_rows(member * tokens, tokens, 128)
    for part in range(2 * KEY_VALUE_HEADS):
        piece = kv_rows[:, part * HEAD_DIM : (part + 1) * HEAD_DIM]
        if part < KEY_VALUE_HEADS:
            piece = turned(piece, 1.0)
        kv_all[own_block, pl.ds(part * HEAD_DIM, HEAD_DIM)] = piece.astype(bf16)
    gather_start(kv_all, kv_sems)
    turn_send[0] = jnp.transpose(normed).reshape(turn_send.shape[1:])

    def turn_copy(kind, step):
        return remote(
            turn_send.at[kind, :, xor(member, step)],
            turn_recv.at[kind, :, :, at_rows(member * tokens, tokens, 128)],
            turn_sems,
            (kind, step),
            in_plane(step),
        )

    def turn_start(kind):
        for step in range(1, 8):
            turn_copy(kind, step).start()
        turn_recv[kind, :, :, at_rows(member * tokens, tokens, 128)] = turn_send[
            kind, :, pl.ds(member, 1)
        ].reshape(turn_recv.shape[1], rows, tokens)

    turn_start(0)
    pass_on_plane(2)
    gather_pass(kv_all, kv_sems)
    pass_on_diagonal(1, range(4))
    gather_start(*token_where(0, 0))
    gather_pass_last(kv_all, kv_sems)
    pass_on_sibling(1)
    token_z(0).wait_recv()
    gather_start(*token_where(0, 1))
    arrived_dense(1)
    spill_b_copy = pltpu.make_async_copy(
        arena.at[pl.ds(0, width)], spill_b, local_sems.at[3]
    )
    spill_b_copy.start()
    for head in range(QUERY_HEADS):
        if head % 2 == 0:
            pair = product(normed, arena[pl.ds(0, width), pl.ds(head * HEAD_DIM, 2 * HEAD_DIM)])
        piece = pair[:, (head % 2) * HEAD_DIM : (head % 2 + 1) * HEAD_DIM]
        q_rows[pl.ds(head * tokens, tokens)] = turned(piece, 1.0).astype(bf16)
    gather_finish(kv_all, kv_sems)
    for group in range(KEY_VALUE_HEADS):
        k_t[group] = jnp.transpose(kv_all[:, pl.ds(group * HEAD_DIM, HEAD_DIM)])
        v_t[group] = jnp.transpose(kv_all[:, pl.ds(kv_width + group * HEAD_DIM, HEAD_DIM)])
    pass_on_diagonal(2, range(4))

    seq_len = kv_all.shape[0]
    pairs = QUERY_HEADS // 2
    pairs_per_group = pairs // KEY_VALUE_HEADS
    key_index = lax.broadcasted_iota(jnp.int32, (seq_len, 2 * tokens), 0)
    query_index = member * tokens + lax.rem(
        lax.broadcasted_iota(jnp.int32, (seq_len, 2 * tokens), 1), tokens
    )
    allowed = key_index <= query_index

    def pair_scores(pair, group):
        queries = q_rows[at_rows(pair * 2 * tokens, 2 * tokens, 128)]
        keys = kv_all[:, at_rows(group * HEAD_DIM, HEAD_DIM, 128)]
        scores = product_rows(keys, queries) * score_scale
        return jnp.where(allowed, scores, masked_score), queries

    def attend(pair, carry):
        group = lax.div(pair, pairs_per_group)
        scores, _ = pair_scores(pair, group)
        peak = jnp.max(scores, axis=0, keepdims=True)
        expo_vals = jnp.exp(scores - peak)
        sums = jnp.sum(expo_vals, axis=0, keepdims=True)
        probs = (expo_vals / sums).astype(bf16)
        lse_buf[pair] = jnp.broadcast_to(peak + jnp.log(sums), (8, 2 * tokens))
        part = product(v_t[group], probs)
        for inner in (0, 1):
            piece = part[:, inner * tokens : (inner + 1) * tokens].astype(bf16)
            attn_buf[2 * pair + inner] = piece
        return carry

    lax.fori_loop(0, pairs, attend, 0)
    pass_on_sibling(2)
    gather_pass(*token_where(0, 0))
    attn_t = attn_buf[...].reshape(width, tokens)
    turn_send[1] = attn_t.reshape(turn_send.shape[1:])
    attn = jnp.transpose(attn_t)
    arrived_dense(2)
    spill_c_copy = pltpu.make_async_copy(
        arena.at[pl.ds(width, width)], spill_c, local_sems.at[4]
    )
    spill_c_copy.start()
    for start in range(0, width, 512):
        after_buf[:, pl.ds(start, 512)] = x_ref[:, pl.ds(start, 512)].astype(f32) + product(
            attn, arena[pl.ds(width, width), pl.ds(start, 512)]
        )
    after = after_buf[...]
    normed_two = (after * norm_factor(after) * gain_m).astype(bf16)
    n2_all[token_rows(0, 0)] = normed_two
    spill_b_copy.wait()
    spill_c_copy.wait()
    for part in range(3):
        sent_dense(part)
    token_z(1).start()
    gather_start(*token_where(1, 0))
    turn_send[2] = jnp.transpose(normed_two).reshape(turn_send.shape[1:])
    gather_pass(*token_where(0, 1))
    gather_pass_last(*token_where(0, 0))
    gather_pass_last(*token_where(0, 1))
    token_z(1).wait_recv()
    gather_start(*token_where(1, 1))
    for plane_step in (0, 1):
        gather_finish(*token_where(0, plane_step))
    expert_finish()

    own_lane = lax.broadcasted_iota(jnp.int32, (2 * tokens, 128), 1) == member
    low_lane = lax.broadcasted_iota(jnp.int32, (2 * tokens, 128), 1) == member + 64
    def arena_slot(base, kind, slot):
        first, each = {"stage": (0, 2), "sib": (4, 2), "sum": (8, 8), "recv": (24, 7)}[base]
        return at_rows((first + kind * each + slot) * tokens, tokens, 128)

    def sib_copy(kind, slot):
        return remote(
            arena.at[arena_slot("stage", kind, slot)],
            arena.at[arena_slot("sib", kind, slot)],
            sib_sems,
            (kind, slot),
            sibling,
        )

    def sib_gate_copy():
        return remote(
            gate_buf.at[pl.ds(8, 8)], gate_buf.at[pl.ds(16, 8)], sib_sems, (2, 0), sibling
        )

    def bit_of(held, bit):
        if isinstance(held, int):
            return held // bit % 2
        return jnp.where(held & bit > 0, 1, 0)

    def ret_copy(kind, part, held, stage):
        first, second, third = part_order(part)
        slot = (
            bit_of(held, second) + 2 * bit_of(held, third),
            4 + bit_of(held, third),
            6,
        )[stage]
        columns = pl.ds(parts[part], 512)
        return remote(
            arena.at[arena_slot("sum", kind, held), columns],
            arena.at[arena_slot("recv", kind, slot), columns],
            ret_sems,
            (kind, part, slot),
            cube_device((first, second, third)[stage]),
        )

    def ret_arrived(kind, part, slot):
        columns = pl.ds(parts[part], 512)
        block = arena.at[arena_slot("recv", kind, slot), columns]
        return remote(block, block, ret_sems, (kind, part, slot), sibling)

    def ret_sum(kind, part, held, slots):
        columns = pl.ds(parts[part], 512)
        total = arena[arena_slot("sum", kind, held), columns].astype(f32)
        for slot in slots:
            total = total + arena[arena_slot("recv", kind, slot), columns].astype(f32)
        return total

    def ret_second(kind):
        for part in range(3):
            first, second, third = part_order(part)
            for held, slot in ((second, 1), (second | third, 3)):
                ret_arrived(kind, part, slot).wait_recv()
                arena[arena_slot("sum", kind, held), pl.ds(parts[part], 512)] = ret_sum(
                    kind, part, held, (slot,)
                ).astype(bf16)
                ret_copy(kind, part, held, 1).start()

    def ret_third(kind):
        for part in range(3):
            third = part_order(part)[2]
            for slot in (2, 5):
                ret_arrived(kind, part, slot).wait_recv()
            arena[arena_slot("sum", kind, third), pl.ds(parts[part], 512)] = ret_sum(
                kind, part, third, (2, 5)
            ).astype(bf16)
            ret_copy(kind, part, third, 2).start()

    def ret_total(kind):
        for part in range(3):
            for slot in (0, 4, 6):
                ret_arrived(kind, part, slot).wait_recv()
        return jnp.concatenate([ret_sum(kind, part, 0, (0, 4, 6)) for part in range(3)], axis=1)

    def ret_sent(kind):
        for part in range(3):
            first, second, third = part_order(part)
            for held in range(8):
                if held & first:
                    ret_copy(kind, part, held, 0).wait_send()
            for held in (second, second | third):
                ret_copy(kind, part, held, 1).wait_send()
            ret_copy(kind, part, third, 2).wait_send()

    def ret_gate_copy(held):
        return remote(
            gate_buf.at[held], gate_buf.at[24 + held], gate_sems, (held,), cube_device(held)
        )

    def halves(values, first):
        return jnp.where(first, values[:tokens], values[tokens:])

    def block_rows(held):
        other_plane = xor(parity, held & 1)
        chip = xor(lax.div(member, 2), lax.div(held, 2))
        return at_rows((other_plane * 4 + chip) * 2 * tokens, 2 * tokens, 128)

    def first_step(held, carry):
        @pl.when(held == 1)
        def _():
            gather_pass(*token_where(1, 0))

        @pl.when(held == 2)
        def _():
            gather_pass(*token_where(1, 1))

        @pl.when(held == 4)
        def _():
            gather_pass_last(*token_where(1, 0))
            gather_pass_last(*token_where(1, 1))

        own = token_rows(held & 1, held & 6)
        remote(
            n2_all.at[own],
            n2_all.at[own],
            tok_sems,
            (1, held & 1, 4 + lax.div(held, 2)),
            sibling,
        ).wait_recv()
        here = block_rows(held)
        token_block = n2_all[here, :]
        gate_up = product(token_block, w_in_half[...])
        gates = masked_gates(
            token_block,
            full_a[:, pl.ds(2 * kv_width, 128)],
            cot_all[here, pl.ds(width, 128)],
        )
        gate = jnp.sum(jnp.where(own_lane, gates, 0.0), axis=1, keepdims=True)
        gate_half = gate_up[:, :half]
        up_half = gate_up[:, half:]
        sigmoid_vals = 1.0 / (1.0 + jnp.exp(-gate_half))
        silu_vals = gate_half * sigmoid_vals
        hidden = silu_vals * up_half
        hidden_all[here, :] = (gate * hidden).astype(bf16)
        back = product_rows(cot_all[here, pl.ds(0, width)], w_out_half[...])
        gate_grad = jnp.sum(hidden * back, axis=1, keepdims=True)
        act_grad = gate * back
        gate_part = act_grad * up_half * sigmoid_vals * (1.0 + gate_half * (1.0 - sigmoid_vals))
        g_all[here, pl.ds(0, half)] = gate_part.astype(bf16)
        g_all[here, pl.ds(half, half)] = (act_grad * silu_vals).astype(bf16)
        gate_high = gate_grad.astype(bf16).astype(f32)
        gate_lanes = jnp.where(own_lane, gate_high, 0.0) + jnp.where(
            low_lane, gate_grad - gate_high, 0.0
        )
        gate_buf[held] = halves(gate_lanes, core == 0).astype(bf16)
        gate_buf[8 + held] = halves(gate_lanes, core == 1).astype(bf16)
        return carry

    lax.fori_loop(0, 8, first_step, 0)
    token_z(0).wait_send()
    token_z(1).wait_send()
    for plane_step in (0, 1):
        gather_sent(*token_where(1, plane_step))
    sib_gate_copy().start()

    def turn_held(turn):
        return jnp.where(turn == 3, 3, jnp.where(turn == 4, 4, 7 - turn))

    def second_step(kind, turn, carry):
        @pl.when(turn < 8)
        def _():
            slot2 = lax.rem(turn, 2)
            held = turn_held(turn)
            here = block_rows(held)

            @pl.when(turn >= 2)
            def _():
                sib_copy(kind, slot2).wait_send()
                pl.semaphore_wait(credit_sem, 1)

            place = arena_slot("sum", kind, held)
            for start in range(0, width, 512):
                columns = pl.ds(start, 512)
                if kind == 0:
                    result = product_rows(g_all[here, :], w_in_half[columns, :])
                else:
                    result = product(hidden_all[here, :], w_out_half[:, columns])
                arena[arena_slot("stage", kind, slot2), columns] = halves(
                    result, core == 1
                ).astype(bf16)
                arena[place, columns] = halves(result, core == 0).astype(bf16)
            sib_copy(kind, slot2).start()

        @pl.when(turn > 0)
        def _():
            last = turn - 1
            slot2 = lax.rem(last, 2)
            held = turn_held(last)
            place = arena_slot("sum", kind, held)
            sib_copy(kind, slot2).wait_recv()
            arena[place] = (
                arena[place].astype(f32) + arena[arena_slot("sib", kind, slot2)].astype(f32)
            ).astype(bf16)

            @pl.when(last < 6)
            def _():
                pl.semaphore_signal(credit_sem, inc=1, device_id=sibling, device_id_type=MESH)

            for part in range(3):

                @pl.when(held & (1 << part) > 0)
                def _():
                    ret_copy(kind, part, held, 0).start()

        return carry

    def second_loop(kind):
        lax.fori_loop(0, 9, functools.partial(second_step, kind), 0)
        for slot in (0, 1):
            sib_copy(kind, slot).wait_send()

    for kind in (1, 2):
        turn_start(kind)
    second_loop(0)
    sib_gate_copy().wait()
    gate_buf[pl.ds(0, 8)] = (
        gate_buf[pl.ds(0, 8)].astype(f32) + gate_buf[pl.ds(16, 8)].astype(f32)
    ).astype(bf16)
    for held in range(1, 8):
        ret_gate_copy(held).start()
    ret_second(0)

    def gin_copy(step):
        source = w_in_half.at[at_rows(xor(plane, step) * quarter, quarter)]
        if step == 0:
            return pltpu.make_async_copy(source, grad_in_ref.at[0], local_sems.at[5])
        return remote(
            source, grad_in_ref.at[step], gin_sems, (step,), (xor(plane, step), member)
        )

    for step in (2, 3, 1, 0):
        start = xor(plane, step) * quarter
        for piece in range(0, quarter, 128):
            columns = n2_all[:, at_rows(start + piece, 128, 128)]
            w_in_half[at_rows(start + piece, 128, 128)] = product_columns(
                columns, g_all[...]
            ).astype(bf16)
        if step in (2, 3):
            gin_copy(step).start()

    def gout_copy(slot):
        source = w_out_half.at[pl.ds(slot * quarter_out, quarter_out)]
        target = grad_out_ref.at[out_half]
        device = (parity * 2 + slot, member)
        return remote(source, target, gout_sems, (slot,), device, (out_half,))

    def gout_local(slot):
        return pltpu.make_async_copy(
            w_out_half.at[pl.ds(slot * quarter_out, quarter_out)],
            grad_out_ref.at[out_half],
            local_sems.at[6],
        )

    def gout_arrived(turn):
        source = w_out_half.at[pl.ds(0, quarter_out)]
        return remote(source, grad_out_ref.at[turn], gout_sems, (turn,), (xor(plane, 1), member))

    own_n2 = n2_all[token_rows(0, 0), :]
    own_mask = cot_all[token_rows(0, 0), pl.ds(width, 128)]
    own_gates = masked_gates(own_n2, full_a[:, pl.ds(2 * kv_width, 128)], own_mask)
    gin_copy(0).start()
    ret_third(0)
    second_loop(1)
    for start in range(0, half, 128):
        w_out_half[pl.ds(start, 128)] = product_columns(
            hidden_all[:, pl.ds(start, 128)], cot_all[:, pl.ds(0, width)]
        ).astype(bf16)

    load_b = pltpu.make_async_copy(
        spill_b, cot_all.at[pl.ds(0, width), pl.ds(0, width)], local_sems.at[3]
    )
    load_c = pltpu.make_async_copy(spill_c, n2_all.at[pl.ds(0, width)], local_sems.at[4])
    load_b.start()
    load_c.start()

    total_in = ret_total(0)
    total_gate = gate_buf[0].astype(f32)
    for held in range(1, 8):
        ret_gate_copy(held).wait_recv()
        total_gate = total_gate + gate_buf[24 + held].astype(f32)
    gin_copy(1).start()
    for slot in (0, 1):

        @pl.when(parity * 2 + slot != plane)
        def _():
            gout_copy(slot).start()

        @pl.when(parity * 2 + slot == plane)
        def _():
            gout_local(slot).start()

    gate_grad = total_gate + pltpu.roll(total_gate, 64, 1)
    gate_inner = jnp.sum(own_gates * gate_grad, axis=1, keepdims=True)
    logit_grad = own_gates * (gate_grad - gate_inner)
    lg_parts = split_three(logit_grad)
    aux_now = full_a[:, pl.ds(2 * kv_width, 128)]
    for part in lg_parts:
        total_in = total_in + product_rows(part, aux_now)
    after = after_buf[...]

    def norm_backward(values, gain, grad):
        factor = norm_factor(values)
        scaled = grad * gain
        gain_row = jnp.sum(grad * values * factor, axis=0, keepdims=True)
        inner = jnp.mean(scaled * values, axis=-1, keepdims=True)
        return factor * scaled - values * factor * factor * factor * inner, gain_row

    two_back, gain_m_row = norm_backward(after, gain_buf[pl.ds(1, 1), :], total_in)
    mid = cot_ref[...].astype(f32) + two_back
    dx_ref[...] = mid
    out_grad = mid.astype(bf16)
    og_all[own_block, pl.ds(0, width)] = out_grad
    og_all[own_block, pl.ds(width, 128)] = (
        lg_parts[0].astype(f32)
        + pltpu.roll(lg_parts[1].astype(f32), 8, 1)
        + pltpu.roll(lg_parts[2].astype(f32), 16, 1)
    ).astype(bf16)

    gather_start(og_all, og_sems)
    load_c.wait()
    for head in range(0, QUERY_HEADS, 2):
        pair = product_rows(out_grad, n2_all[pl.ds(head * HEAD_DIM, 2 * HEAD_DIM), :])
        for inner in (0, 1):
            do_rows[pl.ds((head + inner) * tokens, tokens)] = pair[
                :, inner * HEAD_DIM : (inner + 1) * HEAD_DIM
            ].astype(bf16)
    gather_pass(og_all, og_sems)

    def dkv_rows(kind_core, chip):
        return at_rows((kind_core * 4 + chip) * tokens, tokens, 128)

    def dkv_columns(group):
        return pl.ds(group * 2 * HEAD_DIM, 2 * HEAD_DIM)

    def dkv_sibling(group):
        source = g_all.at[at_rows((1 - core) * 4 * tokens, 4 * tokens, 128), dkv_columns(group)]
        target = dkv_recv.at[group, pl.ds(4 * tokens, 4 * tokens)]
        return remote(source, target, dkv_sems, (group, 0), sibling)

    def dkv_copy(group, step):
        chip = xor(lax.div(member, 2), step)
        return remote(
            g_all.at[dkv_rows(core, chip), dkv_columns(group)],
            dkv_recv.at[group, pl.ds(step * tokens, tokens)],
            dkv_sems,
            (group, step),
            in_plane(2 * step),
        )

    def dkv_pass(group):
        dkv_sibling(group).wait_recv()
        mine = at_rows(core * 4 * tokens, 4 * tokens, 128)
        g_all[mine, dkv_columns(group)] = (
            g_all[mine, dkv_columns(group)].astype(f32)
            + dkv_recv[group, pl.ds(4 * tokens, 4 * tokens)].astype(f32)
        ).astype(bf16)
        for step in (1, 2, 3):
            dkv_copy(group, step).start()

    planes = turn_recv.shape[1]

    def dense_rows(piece, step):
        return at_rows((piece * planes + xor(plane, step)) * rows, rows)

    def kv_grad_copy(step):
        source = arena.at[dense_rows(0, step), pl.ds(0, 2 * kv_width)]
        if step == 0:
            return pltpu.make_async_copy(source, grad_kv_ref.at[0], local_sems.at[0])
        device = (xor(plane, step), member)
        return remote(source, grad_kv_ref.at[step], dense_sems, (0, step), device)

    def pair_rows(piece, which):
        return pl.ds(width + ((piece - 1) * 2 + which) * rows, rows)

    def dense_copy(piece, step):
        columns = pl.ds((piece - 1) * width, width)
        if step == 2:
            target = grad_dense_ref.at[1, :, columns]
            device = (xor(plane, 2), member)
        else:
            target = n2_all.at[pair_rows(piece, step // 2)]
            device = (xor(plane, 1), member)
        return remote(arena.at[dense_rows(piece, step)], target, dense_sems, (piece, step), device)

    def dense_own(piece):
        return pltpu.make_async_copy(
            arena.at[dense_rows(piece, 0)],
            grad_dense_ref.at[0, :, pl.ds((piece - 1) * width, width)],
            local_sems.at[piece],
        )

    def dense_start(piece):
        for step in (3, 1):
            dense_copy(piece, step).start()

    def dense_pass(piece):
        for which, step in ((1, 2), (0, 0)):
            dense_copy(piece, 1 + 2 * which).wait_recv()
            block = dense_rows(piece, step)
            arena[block] = (
                arena[block].astype(f32) + n2_all[pair_rows(piece, which)].astype(f32)
            ).astype(bf16)
            if step:
                dense_copy(piece, 2).start()
            else:
                dense_own(piece).start()

    for group in range(KEY_VALUE_HEADS):
        values = kv_all[:, pl.ds(kv_width + group * HEAD_DIM, HEAD_DIM)]
        dk = jnp.zeros((seq_len, HEAD_DIM), f32)
        dv = jnp.zeros((seq_len, HEAD_DIM), f32)
        for pair in range(group * pairs_per_group, (group + 1) * pairs_per_group):
            scores, queries = pair_scores(pair, group)
            probs = jnp.exp(scores - lse_buf[pair][0:1])
            grads = do_rows[pl.ds(pair * 2 * tokens, 2 * tokens)]
            prob_grad = product_rows(values, grads)
            row_dot = jnp.sum(probs * prob_grad, axis=0, keepdims=True)
            score_grad = (probs * (prob_grad - row_dot)).astype(bf16)
            dk = dk + product(score_grad, queries)
            dv = dv + product(probs.astype(bf16), grads)
            dq = product(k_t[group], score_grad) * score_scale
            for inner in (0, 1):
                piece = jnp.transpose(dq[:, inner * tokens : (inner + 1) * tokens])
                qg_all[own_block, pl.ds((2 * pair + inner) * HEAD_DIM, HEAD_DIM)] = turned(
                    piece, -1.0
                ).astype(bf16)
        start = group * 2 * HEAD_DIM
        dk = (dk * score_scale).astype(bf16)
        dv = dv.astype(bf16)
        for block in range(8):
            place = pl.ds((block % 2 * 4 + block // 2) * tokens, tokens)
            here = slice(block * tokens, (block + 1) * tokens)
            g_all[place, pl.ds(start, HEAD_DIM)] = dk[here]
            g_all[place, pl.ds(start + HEAD_DIM, HEAD_DIM)] = dv[here]
        dkv_sibling(group).start()
        span = width // KEY_VALUE_HEADS
        gather_start(qg_all, qg_sems, (group,), group * span, (group + 1) * span)
        if group == 0:
            gather_pass_last(og_all, og_sems)
            dkv_pass(0)
            ret_second(1)

    dkv_pass(1)
    gather_pass(qg_all, qg_sems, (0,), 0, span)

    for group in range(KEY_VALUE_HEADS):
        start = group * 2 * HEAD_DIM
        mine = dkv_rows(core, lax.div(member, 2))
        dk = g_all[mine, pl.ds(start, HEAD_DIM)].astype(f32)
        dv = g_all[mine, pl.ds(start + HEAD_DIM, HEAD_DIM)].astype(f32)
        for step in (1, 2, 3):
            dkv_copy(group, step).wait_recv()
            block = pl.ds(step * tokens, tokens)
            dk = dk + dkv_recv[group, block, pl.ds(0, HEAD_DIM)].astype(f32)
            dv = dv + dkv_recv[group, block, pl.ds(HEAD_DIM, HEAD_DIM)].astype(f32)
        kvg_all[own_block, pl.ds(group * HEAD_DIM, HEAD_DIM)] = turned(dk, -1.0).astype(bf16)
        kvg_all[own_block, pl.ds(kv_width + group * HEAD_DIM, HEAD_DIM)] = dv.astype(bf16)
    gather_start(kvg_all, kvg_sems)
    ret_third(1)
    gather_finish(og_all, og_sems)
    for kind in range(3):
        for step in range(1, 8):
            turn_copy(kind, step).wait()
    turned_attn = turn_recv[1].reshape(planes * rows, seq_len)
    for start in range(0, width, 512):
        arena[pl.ds(2 * planes * rows, planes * rows), pl.ds(start, 512)] = product(
            turned_attn, og_all[:, pl.ds(start, 512)]
        ).astype(bf16)
    dense_start(2)
    router_part = product(
        turn_recv[2].reshape(planes * rows, seq_len), og_all[:, pl.ds(width, 128)]
    )

    gather_pass(qg_all, qg_sems, (1,), span, 2 * span)
    gather_pass(kvg_all, kvg_sems)
    for group in range(KEY_VALUE_HEADS):
        gather_pass_last(qg_all, qg_sems, (group,), group * span, (group + 1) * span)
    gather_pass_last(kvg_all, kvg_sems)

    load_b.wait()
    own_kvg = kvg_all[own_block, :]
    own_qg = qg_all[own_block, :]
    normed_grad = product_rows(own_kvg, full_a[:, pl.ds(0, 2 * kv_width)]) + product_rows(
        own_qg, cot_all[pl.ds(0, width), pl.ds(0, width)]
    )
    one_back, gain_a_row = norm_backward(
        x_ref[...].astype(f32), gain_buf[pl.ds(0, 1), :], normed_grad
    )
    dx_ref[...] = dx_ref[...] + one_back
    line = lax.broadcasted_iota(jnp.int32, (128, width), 0)
    gain_lines = jnp.zeros((128, width), f32)
    for offset, part in enumerate(split_three(gain_a_row) + split_three(gain_m_row)):
        gain_lines = jnp.where(line == 32 + offset, part.astype(f32), gain_lines)
    turn_send[3] = jnp.transpose(gain_lines.astype(bf16)).reshape(turn_send.shape[1:])
    turn_start(3)

    turned_normed = turn_recv[0].reshape(planes * rows, seq_len)
    for group in range(KEY_VALUE_HEADS):
        gather_finish(qg_all, qg_sems, (group,), group * span, (group + 1) * span)
    for start in range(0, width, 512):
        arena[pl.ds(planes * rows, planes * rows), pl.ds(start, 512)] = product(
            turned_normed, qg_all[:, pl.ds(start, 512)]
        ).astype(bf16)
    dense_start(1)
    dense_pass(2)
    gather_finish(kvg_all, kvg_sems)
    arena[pl.ds(0, planes * rows), pl.ds(0, 2 * kv_width)] = product(
        turned_normed, kvg_all[...]
    ).astype(bf16)
    for step in (2, 3, 1, 0):
        kv_grad_copy(step).start()
    dense_pass(1)
    for step in range(1, 8):
        turn_copy(3, step).wait()
    aux_total = router_part
    for block in range(8):
        aux_total = aux_total + turn_recv[3, :, :, pl.ds(block * tokens, tokens)].reshape(
            planes * rows, tokens
        ).astype(f32)
    aux_send[...] = aux_total.reshape(planes, rows, 128)

    def aux_copy(step):
        return remote(
            aux_send.at[xor(plane, step)],
            grad_aux_ref.at[step],
            aux_sems,
            (step,),
            (xor(plane, step), member),
        )

    for step in (1, 2, 3):
        aux_copy(step).start()
    own_aux = pltpu.make_async_copy(aux_send.at[plane], grad_aux_ref.at[0], local_sems.at[7])
    own_aux.start()

    block_out_ref[...] = (after_buf[...] + ret_total(1)).astype(bf16)

    for held in range(1, 8):
        ret_gate_copy(held).wait_send()
    for kind in (0, 1):
        ret_sent(kind)
    for group in range(KEY_VALUE_HEADS):
        dkv_sibling(group).wait_send()
        for step in (1, 2, 3):
            dkv_copy(group, step).wait_send()
    gin_copy(0).wait()
    for step in (1, 2, 3):
        gin_copy(step).wait()
    for slot in (0, 1):

        @pl.when(parity * 2 + slot != plane)
        def _():
            gout_copy(slot).wait_send()

        @pl.when(parity * 2 + slot == plane)
        def _():
            gout_local(slot).wait()

    for turn in (0, 1):

        @pl.when(out_half + 2 * turn != plane)
        def _():
            gout_arrived(turn).wait_recv()

    for step in range(4):
        kv_grad_copy(step).wait()
    for piece in (1, 2):
        dense_own(piece).wait()
        dense_copy(piece, 2).wait()
        for step in (1, 3):
            dense_copy(piece, step).wait_send()
    for step in (1, 2, 3):
        aux_copy(step).wait()
    own_aux.wait()


EXPERT_LANES = 8


def final_kernel(
    block_ref,
    dx_ref,
    in_ref,
    out_ref,
    dense_ref,
    kv_ref,
    aux_ref,
    block_out,
    tokens_grad,
    gain_a_out,
    query_out,
    key_out,
    value_out,
    output_out,
    gain_m_out,
    router_out,
    w_in_out,
    w_out_out,
):
    f32 = jnp.float32
    half = FF // 2
    block_out[...] = block_ref[...]
    tokens_grad[...] = dx_ref[...]
    even = lax.rem(lax.axis_index("dp"), 2) == 0
    own = in_ref[0].astype(f32) + in_ref[2].astype(f32)
    other = in_ref[1].astype(f32) + in_ref[3].astype(f32)
    halves = (jnp.where(even, own, other), jnp.where(even, other, own))
    count = own.shape[0]
    tiles = half // 128
    for tile in range(4 * tiles):
        piece, rest = divmod(tile, 2 * tiles)
        which, lane = divmod(rest, tiles)
        start = piece * half + lane * 128
        w_in_out[pl.ds(tile, count, 4 * tiles), :] = halves[which][:, start : start + 128]
    total = out_ref[0].astype(f32) + out_ref[1].astype(f32)
    count, width = total.shape
    for tile in range(width // 128):
        w_out_out[pl.ds(tile, count, width // 128), :] = total[:, tile * 128 : tile * 128 + 128]

    @pl.when(pl.program_id(0) == 0)
    def _():
        dense = dense_ref[0].astype(f32) + dense_ref[1].astype(f32)
        query_out[0] = dense[:, :width]
        output_out[0] = dense[:, width:]
        kv = (
            kv_ref[0].astype(f32)
            + kv_ref[1].astype(f32)
            + kv_ref[2].astype(f32)
            + kv_ref[3].astype(f32)
        )
        key_out[0] = kv[:, : kv.shape[1] // 2]
        value_out[0] = kv[:, kv.shape[1] // 2 :]
        aux = aux_ref[0] + aux_ref[1] + aux_ref[2] + aux_ref[3]
        rows = aux.shape[0]
        lines = jnp.transpose(
            jnp.concatenate([aux, jnp.zeros((128 - rows, 128), f32)], axis=0)
        )
        router_out[...] = (lines[0:8] + lines[8:16] + lines[16:24])[:, :rows]
        gain_a_out[...] = (lines[32:33] + lines[33:34] + lines[34:35])[:, :rows]
        gain_m_out[...] = (lines[35:36] + lines[36:37] + lines[37:38])[:, :rows]


def fast_body(
    tokens,
    cotangent,
    routes,
    gain_attn,
    w_query,
    key_weight,
    value_weight,
    w_output,
    gain_moe,
    w_router,
    w_in,
    w_out,
):
    f32, bf16 = jnp.float32, jnp.bfloat16
    total_rows, width = tokens.shape
    rows = w_query.shape[1]
    planes = lax.axis_size("dp")
    members = lax.axis_size("expert")
    seq_len = total_rows * members
    kv_width = key_weight.shape[2]
    quarter = w_in.shape[1]
    quarter_out = w_out.shape[1]
    half = FF // 2
    positions = lax.axis_index("expert") * total_rows + jnp.arange(total_rows, dtype=jnp.int32)
    cos_table, sin_table = rope_tables(positions, HEAD_DIM)
    rope = jnp.concatenate([cos_table, cos_table, -sin_table, sin_table], axis=1)
    in_vmem = pl.BlockSpec(memory_space=pltpu.VMEM)
    anywhere = pl.BlockSpec(memory_space=pl.ANY)
    pair_rows = 2 * seq_len
    shape = jax.ShapeDtypeStruct
    dma = pltpu.SemaphoreType.DMA
    heads = QUERY_HEADS
    (
        block_out,
        tokens_grad,
        grad_in,
        grad_out,
        grad_dense,
        grad_kv,
        grad_aux,
        _,
        _,
    ) = pl.pallas_call(
        layer_kernel,
        out_shape=(
            shape((total_rows, width), bf16),
            shape((total_rows, width), f32),
            shape((planes, quarter, 2 * half), bf16),
            shape((2, quarter_out, width), bf16),
            shape((2, rows, 2 * width), bf16),
            shape((planes, rows, 2 * kv_width), bf16),
            shape((planes, rows, 128), f32),
            shape((width, width), bf16),
            shape((width, width), bf16),
        ),
        in_specs=[in_vmem] * 11 + [anywhere] * 2,
        out_specs=(in_vmem,) * 2 + (anywhere,) * 7,
        scratch_shapes=[
            pltpu.VMEM((pair_rows, width), bf16),
            pltpu.VMEM((pair_rows, width + 128), bf16),
            pltpu.VMEM((width, 2 * kv_width + 128), bf16),
            pltpu.VMEM((38 * total_rows, width), bf16),
            pltpu.VMEM((32, total_rows, 128), bf16),
            pltpu.VMEM((width, 2 * half), bf16),
            pltpu.VMEM((half, width), bf16),
            pltpu.VMEM((pair_rows, half), bf16),
            pltpu.VMEM((pair_rows, 2 * half), bf16),
            pltpu.VMEM((seq_len, 2 * kv_width), bf16),
            pltpu.VMEM((KEY_VALUE_HEADS, HEAD_DIM, seq_len), bf16),
            pltpu.VMEM((KEY_VALUE_HEADS, HEAD_DIM, seq_len), bf16),
            pltpu.VMEM((heads * total_rows, HEAD_DIM), bf16),
            pltpu.VMEM((heads * total_rows, HEAD_DIM), bf16),
            pltpu.VMEM((total_rows, width), bf16),
            pltpu.VMEM((heads, HEAD_DIM, total_rows), bf16),
            pltpu.VMEM((total_rows, width), f32),
            pltpu.VMEM((heads // 2, 8, 2 * total_rows), f32),
            pltpu.VMEM((4, planes, members, rows, total_rows), bf16),
            pltpu.VMEM((4, planes, rows, seq_len), bf16),
            pltpu.VMEM((seq_len, width + 128), bf16),
            pltpu.VMEM((seq_len, width), bf16),
            pltpu.VMEM((seq_len, 2 * kv_width), bf16),
            pltpu.VMEM((KEY_VALUE_HEADS, seq_len, 2 * HEAD_DIM), bf16),
            pltpu.VMEM((planes, rows, 128), f32),
            pltpu.VMEM((16, width), f32),
            dma((2, 3, 4)),
            dma((2, 3, 4, 4)),
            dma((2, 3, 4, 4)),
            dma((2, 8)),
            dma((2, 2, 2, 8)),
            dma((2, 2)),
            dma((2, 4, 8)),
            dma((2, 4, 2)),
            dma((2, 2)),
            dma((2, 3, 2)),
            dma((2, 2, 3, 7)),
            dma((2, 8)),
            dma((2, 4)),
            dma((2, 2)),
            dma((2, 8)),
            dma((2, 2, 8)),
            dma((2, 8)),
            dma((2, 2, 8)),
            dma((2, 3, 4)),
            dma((2, 4)),
            dma((8,)),
            pltpu.SemaphoreType.REGULAR,
        ],
        compiler_params=pltpu.CompilerParams(
            collective_id=0, has_side_effects=True, vmem_limit_bytes=63 * 2**20
        ),
    )(
        tokens,
        cotangent,
        routes[0].T,
        rope,
        key_weight[0],
        value_weight[0],
        w_router[0].T,
        gain_attn,
        gain_moe,
        w_query[0],
        w_output[0],
        w_in.reshape(quarter, 2 * FF),
        w_out.reshape(quarter_out, width),
    )
    steps = 4
    whole = lambda *dims: pl.BlockSpec(dims, lambda i: (0,) * len(dims))
    final = pl.pallas_call(
        final_kernel,
        grid=(steps,),
        out_shape=(
            shape((total_rows, width), bf16),
            shape((total_rows, width), f32),
            shape((1, rows), f32),
            shape((1, rows, width), f32),
            shape((1, rows, kv_width), f32),
            shape((1, rows, kv_width), f32),
            shape((1, rows, width), f32),
            shape((1, rows), f32),
            shape((EXPERT_LANES, rows), f32),
            shape((quarter * 2 * FF // 128, 128), f32),
            shape((quarter_out * width // 128, 128), f32),
        ),
        in_specs=[
            pl.BlockSpec((total_rows // steps, width), lambda i: (i, 0)),
            pl.BlockSpec((total_rows // steps, width), lambda i: (i, 0)),
            pl.BlockSpec((planes, quarter // steps, 2 * half), lambda i: (0, i, 0)),
            pl.BlockSpec((2, quarter_out // steps, width), lambda i: (0, i, 0)),
            whole(2, rows, 2 * width),
            whole(planes, rows, 2 * kv_width),
            whole(planes, rows, 128),
        ],
        out_specs=(
            pl.BlockSpec((total_rows // steps, width), lambda i: (i, 0)),
            pl.BlockSpec((total_rows // steps, width), lambda i: (i, 0)),
            whole(1, rows),
            whole(1, rows, width),
            whole(1, rows, kv_width),
            whole(1, rows, kv_width),
            whole(1, rows, width),
            whole(1, rows),
            whole(EXPERT_LANES, rows),
            pl.BlockSpec((quarter * 2 * FF // 128 // steps, 128), lambda i: (i, 0)),
            pl.BlockSpec((quarter_out * width // 128 // steps, 128), lambda i: (i, 0)),
        ),
        compiler_params=pltpu.CompilerParams(vmem_limit_bytes=63 * 2**20),
    )(block_out, tokens_grad, grad_in, grad_out, grad_dense, grad_kv, grad_aux)
    return final[:8] + (
        final[8].T[None],
        final[9].reshape(1, quarter, 1, 2 * FF),
        final[10].reshape(1, quarter_out, 1, width),
    )


def solution(mesh):
    in_specs = (
        P(("dp", "expert"), None),
        P(("dp", "expert"), None),
        P(None, ("dp", "expert"), None),
        P(None, ("dp", "expert")),
        P(None, ("dp", "expert"), None),
        P(None, ("dp", "expert"), None),
        P(None, ("dp", "expert"), None),
        P(None, ("dp", "expert"), None),
        P(None, ("dp", "expert")),
        P(None, ("dp", "expert"), None),
        P(None, "dp", "expert", None),
        P(None, "dp", "expert", None),
    )
    out_specs = (
        P(("dp", "expert"), None),
        P(("dp", "expert"), None),
        P(None, ("dp", "expert")),
        P(None, ("dp", "expert"), None),
        P(None, ("dp", "expert"), None),
        P(None, ("dp", "expert"), None),
        P(None, ("dp", "expert"), None),
        P(None, ("dp", "expert")),
        P(None, ("dp", "expert"), None),
        P(None, "dp", "expert", None),
        P(None, "dp", "expert", None),
    )
    body = fast_body if mesh.shape["dp"] == 4 and mesh.shape["expert"] == 8 else general_body
    return jax.shard_map(body, mesh=mesh, in_specs=in_specs, out_specs=out_specs, check_vma=False)
```

```python
import functools

import jax
import jax.numpy as jnp
from jax import lax
from jax.experimental import pallas as pl
from jax.experimental.pallas import tpu as pltpu
from jax.sharding import PartitionSpec as P

MESH = pl.DeviceIdType.MESH

QUERY_HEADS = 12
KEY_VALUE_HEADS = 2
HEAD_DIM = 128
FF = 768
TOP = 4


norm_eps = 1e-06
rope_base = 1000000.0
masked_score = -1e30
top_precision = lax.Precision.HIGHEST


def norm_factor(values):
    return lax.rsqrt(jnp.mean(values * values, axis=-1, keepdims=True) + norm_eps)


def norm_back(values, gain, grad_out):
    factor = norm_factor(values)
    scaled = grad_out * gain
    gain_grad = jnp.sum(grad_out * values * factor, axis=0)
    inner_mean = jnp.mean(scaled * values, axis=-1, keepdims=True)
    return (factor * scaled - values * factor * factor * factor * inner_mean, gain_grad)


def rope_tables(positions, head_size):
    half_size = head_size // 2
    inverse = rope_base ** (-(jnp.arange(half_size, dtype=jnp.float32) * 2.0 / head_size))
    angles = positions.astype(jnp.float32)[:, None] * inverse[None, :]
    return (jnp.cos(angles), jnp.sin(angles))


def rotate(values, cos_table, sin_table, orient):
    half_size = values.shape[-1] // 2
    first_half = values[..., :half_size]
    second = values[..., half_size:]
    cos_part = cos_table[:, None, :]
    sin_part = orient * sin_table[:, None, :]
    return jnp.concatenate(
        [first_half * cos_part - second * sin_part, second * cos_part + first_half * sin_part],
        axis=-1,
    )


def plan_slots(route, expert_count, capacity):
    flat_route = route.reshape(-1)
    slot_total = flat_route.shape[0]
    onehot = (flat_route[:, None] == jnp.arange(expert_count, dtype=jnp.int32)[None, :]).astype(
        jnp.int32
    )
    before = jnp.cumsum(onehot, axis=0) - onehot
    target = flat_route * capacity + jnp.sum(before * onehot, axis=1)
    source = (
        jnp.full((expert_count * capacity,), slot_total, jnp.int32)
        .at[target]
        .set(jnp.arange(slot_total, dtype=jnp.int32))
    )
    filled = source < slot_total
    return (target, jnp.minimum(source, slot_total - 1), filled)


def general_body(
    tokens,
    cotangent,
    routes,
    gain_attn,
    w_query,
    key_weight,
    value_weight,
    w_output,
    gain_moe,
    w_router,
    w_in,
    w_out,
):
    total_rows, model_width = tokens.shape
    layer_count = w_query.shape[0]
    group_count = lax.axis_size("expert")
    seq_len = total_rows * group_count
    experts_local = w_in.shape[2]
    expert_count = experts_local * group_count
    capacity = min(total_rows, total_rows * TOP * 3 // (2 * expert_count))
    heads_per_group = QUERY_HEADS // KEY_VALUE_HEADS
    score_scale = HEAD_DIM ** (-0.5)
    positions = lax.axis_index("expert") * total_rows + jnp.arange(total_rows, dtype=jnp.int32)
    cos_table, sin_table = rope_tables(positions, HEAD_DIM)
    allowed = jnp.arange(seq_len, dtype=jnp.int32)[None, :] <= positions[:, None]
    zero_bf = jnp.zeros((), jnp.bfloat16)

    def score_block(query_rows, all_keys, group_of_heads):
        grouped_q = query_rows[
            :, group_of_heads * heads_per_group : (group_of_heads + 1) * heads_per_group, :
        ]
        scores = (
            jnp.einsum(
                "rgd,kd->grk",
                grouped_q,
                all_keys[:, group_of_heads, :],
                preferred_element_type=jnp.float32,
            )
            * score_scale
        )
        return (jnp.where(allowed[None], scores, masked_score), grouped_q)

    residual = tokens.astype(jnp.float32)
    layer_number = 0
    dense_w = (
        lax.all_gather(gain_attn[layer_number], ("dp", "expert"), axis=0, tiled=True),
        lax.all_gather(w_query[layer_number], ("dp", "expert"), axis=0, tiled=True),
        lax.all_gather(key_weight[layer_number], ("dp", "expert"), axis=0, tiled=True),
        lax.all_gather(value_weight[layer_number], ("dp", "expert"), axis=0, tiled=True),
        lax.all_gather(w_output[layer_number], ("dp", "expert"), axis=0, tiled=True),
        lax.all_gather(gain_moe[layer_number], ("dp", "expert"), axis=0, tiled=True),
        lax.all_gather(w_router[layer_number], ("dp", "expert"), axis=0, tiled=True),
    )
    expert_w = (
        lax.all_gather(w_in[layer_number], "dp", axis=0, tiled=True),
        lax.all_gather(w_out[layer_number], "dp", axis=0, tiled=True),
    )
    route = routes[layer_number]
    gain_a = dense_w[0].astype(jnp.float32)
    norm_result = (residual * norm_factor(residual) * gain_a).astype(jnp.bfloat16)
    query_rows = jnp.dot(norm_result, dense_w[1], preferred_element_type=jnp.float32).reshape(
        total_rows, QUERY_HEADS, HEAD_DIM
    )
    query_rows = rotate(query_rows, cos_table, sin_table, 1.0).astype(jnp.bfloat16)
    key_matrix_rows = jnp.dot(norm_result, dense_w[2], preferred_element_type=jnp.float32).reshape(
        total_rows, KEY_VALUE_HEADS, HEAD_DIM
    )
    key_matrix_rows = rotate(key_matrix_rows, cos_table, sin_table, 1.0).astype(jnp.bfloat16)
    value_matrix_rows = (
        jnp.dot(norm_result, dense_w[3], preferred_element_type=jnp.float32)
        .astype(jnp.bfloat16)
        .reshape(total_rows, KEY_VALUE_HEADS, HEAD_DIM)
    )
    all_keys = lax.all_gather(key_matrix_rows, "expert", axis=0, tiled=True)
    all_values = lax.all_gather(value_matrix_rows, "expert", axis=0, tiled=True)
    heads_out = []
    log_totals = []
    for group_of_heads in range(KEY_VALUE_HEADS):
        scores, grouped_q = score_block(query_rows, all_keys, group_of_heads)
        row_peak = jnp.max(scores, axis=-1, keepdims=True)
        expo_vals = jnp.exp(scores - row_peak)
        row_sums = jnp.sum(expo_vals, axis=-1, keepdims=True)
        attn_probs = (expo_vals / row_sums).astype(jnp.bfloat16)
        log_totals.append(row_peak + jnp.log(row_sums))
        heads_out.append(
            jnp.einsum(
                "grk,kd->rgd",
                attn_probs,
                all_values[:, group_of_heads, :],
                preferred_element_type=jnp.float32,
            )
        )
    attn = (
        jnp.concatenate(heads_out, axis=1)
        .reshape(total_rows, QUERY_HEADS * HEAD_DIM)
        .astype(jnp.bfloat16)
    )
    after_attn = residual + jnp.dot(attn, dense_w[4], preferred_element_type=jnp.float32)
    gain_m = dense_w[5].astype(jnp.float32)
    normed_two = (after_attn * norm_factor(after_attn) * gain_m).astype(jnp.bfloat16)
    logits = jnp.dot(normed_two, dense_w[6], preferred_element_type=jnp.float32)
    gate_probs = jax.nn.softmax(jnp.take_along_axis(logits, route, axis=1), axis=-1)
    target, source, filled = plan_slots(route, expert_count, capacity)
    send_rows = jnp.where(filled[:, None], normed_two[source // TOP], zero_bf)
    send_rows = send_rows.reshape(group_count, experts_local, capacity, model_width)
    arrived_rows = lax.all_to_all(send_rows, "expert", split_axis=0, concat_axis=0, tiled=True)
    gate_up_vals = jnp.einsum(
        "secd,def->secf", arrived_rows, expert_w[0], preferred_element_type=jnp.float32
    )
    expert_gate_half = gate_up_vals[..., :FF]
    expert_hidden_act = (
        expert_gate_half * jax.nn.sigmoid(expert_gate_half) * gate_up_vals[..., FF:]
    ).astype(jnp.bfloat16)
    expert_out = jnp.einsum(
        "secf,fed->secd", expert_hidden_act, expert_w[1], preferred_element_type=jnp.float32
    ).astype(jnp.bfloat16)
    arrived, gate_up, expert_out = (arrived_rows, gate_up_vals, expert_out)
    returned = lax.all_to_all(expert_out, "expert", split_axis=0, concat_axis=0, tiled=True)
    slot_out = returned.reshape(expert_count * capacity, model_width)[target].reshape(
        total_rows, TOP, model_width
    )
    new_residual = after_attn + jnp.sum(
        gate_probs[:, :, None] * slot_out.astype(jnp.float32), axis=1
    )
    saved_layers = [
        (
            residual,
            norm_result,
            query_rows,
            key_matrix_rows,
            value_matrix_rows,
            all_keys,
            all_values,
            log_totals,
            attn,
            after_attn,
            normed_two,
            route,
            gate_probs,
            target,
            source,
            filled,
            arrived,
            gate_up,
            slot_out,
            dense_w,
            expert_w,
        )
    ]
    block_out = new_residual.astype(jnp.bfloat16)
    grad_resid = cotangent.astype(jnp.float32)
    grad_lists = [[None] * layer_count for _ in range(9)]
    for layer_number in reversed(range(layer_count)):
        (
            resid_in,
            norm_result,
            query_rows,
            key_matrix_rows,
            value_matrix_rows,
            all_keys,
            all_values,
            log_totals,
            attn,
            after_attn,
            normed_two,
            route,
            gate_probs,
            target,
            source,
            filled,
            arrived,
            gate_up,
            slot_out,
            dense_w,
            expert_w,
        ) = saved_layers[layer_number]
        dense_w = (
            lax.all_gather(gain_attn[layer_number], ("dp", "expert"), axis=0, tiled=True),
            lax.all_gather(w_query[layer_number], ("dp", "expert"), axis=0, tiled=True),
            lax.all_gather(key_weight[layer_number], ("dp", "expert"), axis=0, tiled=True),
            lax.all_gather(value_weight[layer_number], ("dp", "expert"), axis=0, tiled=True),
            lax.all_gather(w_output[layer_number], ("dp", "expert"), axis=0, tiled=True),
            lax.all_gather(gain_moe[layer_number], ("dp", "expert"), axis=0, tiled=True),
            lax.all_gather(w_router[layer_number], ("dp", "expert"), axis=0, tiled=True),
        )
        expert_w = (
            lax.all_gather(w_in[layer_number], "dp", axis=0, tiled=True),
            lax.all_gather(w_out[layer_number], "dp", axis=0, tiled=True),
        )
        all_keys, all_values = (
            lax.all_gather(key_matrix_rows, "expert", axis=0, tiled=True),
            lax.all_gather(value_matrix_rows, "expert", axis=0, tiled=True),
        )
        gate_grad = jnp.sum(slot_out.astype(jnp.float32) * grad_resid[:, None, :], axis=-1)
        slot_grad = (
            (gate_probs[:, :, None] * grad_resid[:, None, :])
            .astype(jnp.bfloat16)
            .reshape(total_rows * TOP, model_width)
        )
        grad_rows = jnp.where(filled[:, None], slot_grad[source], zero_bf)
        grad_rows = grad_rows.reshape(group_count, experts_local, capacity, model_width)
        grad_arrived = lax.all_to_all(grad_rows, "expert", split_axis=0, concat_axis=0, tiled=True)
        gate_half = gate_up[..., :FF]
        up_half = gate_up[..., FF:]
        sigmoid_vals = jax.nn.sigmoid(gate_half)
        silu_vals = gate_half * sigmoid_vals
        hidden_act = (silu_vals * up_half).astype(jnp.bfloat16)
        act_grad = jnp.einsum(
            "secd,fed->secf", grad_arrived, expert_w[1], preferred_element_type=jnp.float32
        )
        gate_part = act_grad * up_half * sigmoid_vals * (1.0 + gate_half * (1.0 - sigmoid_vals))
        gate_up_grad = jnp.concatenate([gate_part, act_grad * silu_vals], axis=-1).astype(
            jnp.bfloat16
        )
        input_grad = jnp.einsum(
            "secf,def->secd", gate_up_grad, expert_w[0], preferred_element_type=jnp.float32
        ).astype(jnp.bfloat16)
        returned_grad = lax.all_to_all(
            input_grad, "expert", split_axis=0, concat_axis=0, tiled=True
        )
        grad_lists[7][layer_number] = lax.psum_scatter(
            jnp.einsum(
                "secd,secf->def", arrived, gate_up_grad, preferred_element_type=jnp.float32
            ).astype(jnp.bfloat16),
            "dp",
            scatter_dimension=0,
            tiled=True,
        ).astype(jnp.float32)
        grad_lists[8][layer_number] = lax.psum_scatter(
            jnp.einsum(
                "secf,secd->fed", hidden_act, grad_arrived, preferred_element_type=jnp.float32
            ).astype(jnp.bfloat16),
            "dp",
            scatter_dimension=0,
            tiled=True,
        ).astype(jnp.float32)
        slot_back = returned_grad.reshape(expert_count * capacity, model_width)[target].reshape(
            total_rows, TOP, model_width
        )
        normed_two_grad = jnp.sum(slot_back.astype(jnp.float32), axis=1)
        gate_inner = jnp.sum(gate_probs * gate_grad, axis=-1, keepdims=True)
        chosen_grad = gate_probs * (gate_grad - gate_inner)
        route_hot = (
            route[:, :, None] == jnp.arange(expert_count, dtype=jnp.int32)[None, None, :]
        ).astype(jnp.float32)
        logit_grad = jnp.sum(route_hot * chosen_grad[:, :, None], axis=1)
        router_f = dense_w[6].astype(jnp.float32)
        normed_two_grad = normed_two_grad + jnp.einsum(
            "re,de->rd", logit_grad, router_f, precision=top_precision
        )
        router_grad = jnp.einsum(
            "rd,re->de", normed_two.astype(jnp.float32), logit_grad, precision=top_precision
        )
        gain_m = dense_w[5].astype(jnp.float32)
        norm_two_back, gain_m_grad = norm_back(after_attn, gain_m, normed_two_grad)
        mid_grad = grad_resid + norm_two_back
        out_grad = mid_grad.astype(jnp.bfloat16)
        output_grad = jnp.einsum("rq,rd->qd", attn, out_grad, preferred_element_type=jnp.float32)
        attn_grad = (
            jnp.einsum("rd,qd->rq", out_grad, dense_w[4], preferred_element_type=jnp.float32)
            .astype(jnp.bfloat16)
            .reshape(total_rows, QUERY_HEADS, HEAD_DIM)
        )
        query_grads = []
        key_grads = []
        value_grads = []
        for group_of_heads in range(KEY_VALUE_HEADS):
            scores, grouped_q = score_block(query_rows, all_keys, group_of_heads)
            grouped_do = attn_grad[
                :, group_of_heads * heads_per_group : (group_of_heads + 1) * heads_per_group, :
            ]
            probs = jnp.exp(scores - log_totals[group_of_heads])
            prob_bf = probs.astype(jnp.bfloat16)
            prob_grad = jnp.einsum(
                "rgd,kd->grk",
                grouped_do,
                all_values[:, group_of_heads, :],
                preferred_element_type=jnp.float32,
            )
            row_dot = jnp.sum(probs * prob_grad, axis=-1, keepdims=True)
            score_grad = (probs * (prob_grad - row_dot)).astype(jnp.bfloat16)
            query_grads.append(
                jnp.einsum(
                    "grk,kd->rgd",
                    score_grad,
                    all_keys[:, group_of_heads, :],
                    preferred_element_type=jnp.float32,
                )
                * score_scale
            )
            key_grads.append(
                jnp.einsum("grk,rgd->kd", score_grad, grouped_q, preferred_element_type=jnp.float32)
                * score_scale
            )
            value_grads.append(
                jnp.einsum("grk,rgd->kd", prob_bf, grouped_do, preferred_element_type=jnp.float32)
            )
        key_sum, value_total_sum = (
            lax.psum_scatter(
                jnp.stack(key_grads, axis=1).astype(jnp.bfloat16),
                "expert",
                scatter_dimension=0,
                tiled=True,
            ).astype(jnp.float32),
            lax.psum_scatter(
                jnp.stack(value_grads, axis=1).astype(jnp.bfloat16),
                "expert",
                scatter_dimension=0,
                tiled=True,
            ).astype(jnp.float32),
        )
        query_grad = (
            rotate(jnp.concatenate(query_grads, axis=1), cos_table, sin_table, -1.0)
            .astype(jnp.bfloat16)
            .reshape(total_rows, QUERY_HEADS * HEAD_DIM)
        )
        key_grad = (
            rotate(key_sum, cos_table, sin_table, -1.0)
            .astype(jnp.bfloat16)
            .reshape(total_rows, KEY_VALUE_HEADS * HEAD_DIM)
        )
        value_rows_gradient = value_total_sum.astype(jnp.bfloat16).reshape(
            total_rows, KEY_VALUE_HEADS * HEAD_DIM
        )
        normed_grad = jnp.einsum(
            "rq,dq->rd", query_grad, dense_w[1], preferred_element_type=jnp.float32
        )
        normed_grad = normed_grad + jnp.einsum(
            "rq,dq->rd", key_grad, dense_w[2], preferred_element_type=jnp.float32
        )
        normed_grad = normed_grad + jnp.einsum(
            "rq,dq->rd", value_rows_gradient, dense_w[3], preferred_element_type=jnp.float32
        )
        query_w_grad = jnp.einsum(
            "rd,rq->dq", norm_result, query_grad, preferred_element_type=jnp.float32
        )
        key_w_grad = jnp.einsum(
            "rd,rq->dq", norm_result, key_grad, preferred_element_type=jnp.float32
        )
        value_w_grad = jnp.einsum(
            "rd,rq->dq", norm_result, value_rows_gradient, preferred_element_type=jnp.float32
        )
        gain_a = dense_w[0].astype(jnp.float32)
        norm_one_back, gain_a_grad = norm_back(resid_in, gain_a, normed_grad)
        grad_resid = mid_grad + norm_one_back
        shares = (
            lax.psum_scatter(gain_a_grad, ("dp", "expert"), scatter_dimension=0, tiled=True),
            lax.psum_scatter(query_w_grad, ("dp", "expert"), scatter_dimension=0, tiled=True),
            lax.psum_scatter(key_w_grad, ("dp", "expert"), scatter_dimension=0, tiled=True),
            lax.psum_scatter(value_w_grad, ("dp", "expert"), scatter_dimension=0, tiled=True),
            lax.psum_scatter(output_grad, ("dp", "expert"), scatter_dimension=0, tiled=True),
            lax.psum_scatter(gain_m_grad, ("dp", "expert"), scatter_dimension=0, tiled=True),
            lax.psum_scatter(router_grad, ("dp", "expert"), scatter_dimension=0, tiled=True),
        )
        for member in range(7):
            grad_lists[member][layer_number] = shares[member]
    stacked = [jnp.stack(grad_lists[member], axis=0) for member in range(9)]
    return (
        block_out,
        grad_resid,
        stacked[0],
        stacked[1],
        stacked[2],
        stacked[3],
        stacked[4],
        stacked[5],
        stacked[6],
        stacked[7],
        stacked[8],
    )


def product(left, right):
    return lax.dot_general(
        left, right, (((1,), (0,)), ((), ())), preferred_element_type=jnp.float32
    )


def product_rows(left, right):
    return lax.dot_general(
        left, right, (((1,), (1,)), ((), ())), preferred_element_type=jnp.float32
    )


def product_columns(left, right):
    return lax.dot_general(
        left, right, (((0,), (0,)), ((), ())), preferred_element_type=jnp.float32
    )


def split_three(values):
    high = values.astype(jnp.bfloat16)
    rest = values - high.astype(jnp.float32)
    middle = rest.astype(jnp.bfloat16)
    low = (rest - middle.astype(jnp.float32)).astype(jnp.bfloat16)
    return high, middle, low


def masked_gates(rows, router, mask):
    chosen = mask.astype(jnp.float32) > 0.5
    logits = jnp.where(chosen, product(rows, router), masked_score)
    expo_vals = jnp.where(chosen, jnp.exp(logits - jnp.max(logits, axis=1, keepdims=True)), 0.0)
    return expo_vals / jnp.sum(expo_vals, axis=1, keepdims=True)


def layer_kernel(
    x_ref,
    cot_ref,
    routes_ref,
    rope_ref,
    key_ref,
    value_ref,
    router_ref,
    gain_a_ref,
    gain_m_ref,
    shard_b,
    shard_c,
    w_in_ref,
    w_out_ref,
    block_out_ref,
    dx_ref,
    grad_in_ref,
    grad_out_ref,
    grad_dense_ref,
    grad_kv_ref,
    grad_aux_ref,
    spill_b,
    spill_c,
    n2_all,
    cot_all,
    full_a,
    arena,
    gate_buf,
    w_in_half,
    w_out_half,
    hidden_all,
    g_all,
    gin_early,
    kv_all,
    k_t,
    v_t,
    q_rows,
    do_rows,
    attn_buf,
    after_buf,
    lse_buf,
    turn_send,
    turn_recv,
    og_all,
    qg_all,
    kvg_all,
    dkv_recv,
    aux_send,
    gain_buf,
    z_sems,
    p_sems,
    s_sems,
    kv_sems,
    tok_sems,
    tz_sems,
    turn_sems,
    win_sems,
    wout_sems,
    sib_sems,
    ret_sems,
    gate_sems,
    gin_sems,
    gout_sems,
    og_sems,
    qg_sems,
    kvg_sems,
    dkv_sems,
    dense_sems,
    aux_sems,
    local_sems,
    credit_sem,
):
    plane = lax.axis_index("dp")
    member = lax.axis_index("expert")
    core = lax.rem(member, 2)
    parity = lax.rem(plane, 2)
    tokens, width = x_ref.shape
    rows = shard_b.shape[0]
    xor = lax.bitwise_xor
    f32, bf16 = jnp.float32, jnp.bfloat16
    half = FF // 2
    score_scale = HEAD_DIM ** (-0.5)
    kv_width = KEY_VALUE_HEADS * HEAD_DIM

    def at_rows(start, count, step=16):
        return pl.ds(pl.multiple_of(start, step), count)

    def remote(source, target, sems, index, device, recv_index=None):
        return pltpu.make_async_remote_copy(
            src_ref=source,
            dst_ref=target,
            send_sem=sems.at[(0,) + index],
            recv_sem=sems.at[(1,) + (index if recv_index is None else recv_index)],
            device_id=device,
            device_id_type=MESH,
        )

    in_plane = lambda step: (plane, xor(member, step))
    sibling = in_plane(1)

    barrier = pltpu.get_barrier_semaphore()
    greeted = [(xor(plane, s), member) for s in (1, 2, 3)]
    greeted += [in_plane(s) for s in range(1, 8)]
    greeted += [(xor(plane, 1), xor(member, s)) for s in (2, 4, 6)]
    for device in greeted:
        pl.semaphore_signal(barrier, inc=1, device_id=device, device_id_type=MESH)

    def dense_block(part, step, chip_step):
        start = (xor(plane, step) * 8 + xor(member, chip_step)) * rows
        if part == 0:
            return full_a.at[at_rows(start, rows)]
        return arena.at[at_rows(start + (part - 1) * width, rows)]

    def z_copy(part, step):
        block = dense_block(part, 0, 0)
        return remote(block, block, z_sems, (part, step), (xor(plane, step), member))

    def plane_copy(part, step, chip):
        if chip < 3:
            block = dense_block(part, step, 0)
            return remote(block, block, p_sems, (part, step, chip), in_plane(2 * chip))
        via = 1 + step % 2
        block = dense_block(part, step, 2 * via)
        return remote(block, block, p_sems, (part, step, 3), in_plane(2 * (3 - via)))

    def sibling_copy(part, step, chip):
        block = dense_block(part, step, 2 * chip)
        return remote(block, block, s_sems, (part, step, chip), sibling)

    own_rows = (plane * 8 + member) * rows
    full_a[at_rows(own_rows, rows), pl.ds(0, kv_width)] = key_ref[...]
    full_a[at_rows(own_rows, rows), pl.ds(kv_width, kv_width)] = value_ref[...]
    line = lax.broadcasted_iota(jnp.int32, (128, rows), 0)
    gains = jnp.where(line == EXPERT_LANES, gain_a_ref[...].astype(f32), 0.0) + jnp.where(
        line == EXPERT_LANES + 1, gain_m_ref[...].astype(f32), 0.0
    )
    lines = jnp.concatenate(
        [router_ref[...].astype(f32), gains[EXPERT_LANES:]], axis=0
    ).astype(bf16)
    square = (
        lax.broadcasted_iota(jnp.int32, (rows, rows), 0)
        == lax.broadcasted_iota(jnp.int32, (rows, rows), 1)
    ).astype(bf16)
    full_a[at_rows(own_rows, rows), pl.ds(2 * kv_width, 128)] = product_rows(
        square, lines
    ).astype(bf16)
    arena[at_rows(own_rows, rows)] = shard_b[...]
    arena[at_rows(own_rows + width, rows)] = shard_c[...]

    def token_rows(plane_step, member_step):
        start = (xor(parity, plane_step) * 8 + xor(member, member_step)) * tokens
        return at_rows(start, tokens, 128)

    cot_all[token_rows(0, 0), pl.ds(0, width)] = cot_ref[...]
    expert_line = lax.broadcasted_iota(jnp.int32, (128, tokens), 0)
    named = jnp.zeros((128, tokens), f32)
    for slot in range(TOP):
        named = jnp.where(expert_line == routes_ref[pl.ds(slot, 1), :], 1.0, named)
    cot_all[token_rows(0, 0), pl.ds(width, 128)] = jnp.transpose(named).astype(bf16)
    pl.semaphore_wait(barrier, len(greeted))

    for part in range(3):
        for step in (3, 2, 1):
            z_copy(part, step).start()
    for part in range(3):
        for chip in (1, 2):
            plane_copy(part, 0, chip).start()
        sibling_copy(part, 0, 0).start()

    def pass_on_plane(part):
        for step in (1, 2, 3):
            z_copy(part, step).wait_recv()
            for chip in (1, 2):
                plane_copy(part, step, chip).start()
            sibling_copy(part, step, 0).start()

    def pass_on_diagonal(part, steps):
        for step in steps:
            for chip in (1, 2):
                plane_copy(part, step, chip).wait_recv()
                if chip == 1 + step % 2:
                    plane_copy(part, step, 3).start()
                sibling_copy(part, step, chip).start()

    def pass_on_sibling(part):
        for step in range(4):
            plane_copy(part, step, 3).wait_recv()
            sibling_copy(part, step, 3).start()

    def arrived_dense(part):
        for step in range(4):
            for chip in range(4):
                sibling_copy(part, step, chip).wait_recv()

    def sent_dense(part):
        for step in range(4):
            if step:
                z_copy(part, step).wait_send()
            for chip in range(4):
                if chip:
                    plane_copy(part, step, chip).wait_send()
                sibling_copy(part, step, chip).wait_send()

    token_arrays = (cot_all, n2_all)

    parts = (0, 512, 1024)

    def cube_device(bits):
        return (xor(plane, bits & 1), xor(member, bits & 6))

    def part_order(part):
        return [1 << ((part + k) % 3) for k in range(3)]

    def token_z(kind):
        block = token_arrays[kind].at[token_rows(0, 0)]
        return remote(block, block, tz_sems, (kind,), (xor(plane, 1), member))

    def token_where(kind, plane_step):
        base = xor(parity, plane_step) * 8 * tokens
        return token_arrays[kind], tok_sems, (kind, plane_step), 0, None, base

    quarter = w_in_ref.shape[0]
    quarter_out = w_out_ref.shape[0]

    def win_copy(step, piece):
        other = xor(parity, step % 2)
        source = w_in_ref.at[:, at_rows(piece * FF + other * half, half, 128)]
        target = w_in_half.at[at_rows(plane * quarter, quarter), pl.ds(piece * half, half)]
        if step == 0:
            return pltpu.make_async_copy(source, target, local_sems.at[piece])
        return remote(source, target, win_sems, (step, piece), (xor(plane, step), member))

    out_half = lax.div(plane, 2)

    def wout_send(turn):
        target = w_out_half.at[at_rows(parity * quarter_out, quarter_out)]
        device = (out_half + 2 * turn, member)
        return remote(w_out_ref, target, wout_sems, (turn,), device, (parity,))

    def wout_arrived(slot):
        target = w_out_half.at[at_rows(slot * quarter_out, quarter_out)]
        return remote(w_out_ref, target, wout_sems, (slot,), (xor(plane, 1), member))

    def wout_local():
        return pltpu.make_async_copy(
            w_out_ref,
            w_out_half.at[at_rows(parity * quarter_out, quarter_out)],
            local_sems.at[2],
        )

    def expert_start():
        for step in (1, 3, 2):
            for piece in (0, 1):
                win_copy(step, piece).start()
        for piece in (0, 1):
            win_copy(0, piece).start()
        for turn in (0, 1):

            @pl.when(out_half + 2 * turn != plane)
            def _():
                wout_send(turn).start()

        @pl.when(out_half == parity)
        def _():
            wout_local().start()

    def expert_finish():
        for step in (1, 3, 2):
            for piece in (0, 1):
                win_copy(step, piece).wait()
        for piece in (0, 1):
            win_copy(0, piece).wait()
        for slot in (0, 1):

            @pl.when(parity * 2 + slot != plane)
            def _():
                wout_arrived(slot).wait_recv()

        for turn in (0, 1):

            @pl.when(out_half + 2 * turn != plane)
            def _():
                wout_send(turn).wait_send()

        @pl.when(out_half == parity)
        def _():
            wout_local().wait()

    def gather_copy(array, sems, index, lead=(), start=0, stop=None, base=0):
        stop = array.shape[1] if stop is None else stop
        middle = (start + stop) // 256 * 128
        owner_step, device_step = ((0, 2), (0, 4), (2, 4), (4, 2), (0, 1), (2, 1), (4, 1), (6, 1))[
            index
        ]
        if index == 2:
            stop = middle
        if index == 3:
            start = middle
        block = at_rows(base + xor(member, owner_step) * tokens, tokens, 128)
        piece = array.at[block, pl.ds(start, stop - start)]
        return remote(piece, piece, sems, lead + (index,), in_plane(device_step))

    def gather_start(*where):
        for index in (0, 1, 4):
            gather_copy(where[0], where[1], index, *where[2:]).start()

    def gather_pass(*where):
        for index in (0, 1):
            gather_copy(where[0], where[1], index, *where[2:]).wait_recv()
            gather_copy(where[0], where[1], 2 + index, *where[2:]).start()
            gather_copy(where[0], where[1], 5 + index, *where[2:]).start()

    def gather_pass_last(*where):
        for index in (2, 3):
            gather_copy(where[0], where[1], index, *where[2:]).wait_recv()
        gather_copy(where[0], where[1], 7, *where[2:]).start()

    def gather_sent(*where):
        for index in range(8):
            gather_copy(where[0], where[1], index, *where[2:]).wait_send()

    def gather_finish(*where):
        gather_sent(*where)
        for index in range(4, 8):
            gather_copy(where[0], where[1], index, *where[2:]).wait_recv()

    pass_on_plane(0)
    pass_on_plane(1)
    pass_on_diagonal(0, range(4))
    pass_on_sibling(0)
    arrived_dense(0)
    token_z(0).start()
    expert_start()
    aux = full_a[:, pl.ds(2 * kv_width, 128)]
    pick = (
        lax.broadcasted_iota(jnp.int32, (16, 128), 1)
        == lax.broadcasted_iota(jnp.int32, (16, 128), 0) + EXPERT_LANES
    ).astype(bf16)
    gain_buf[...] = product_rows(pick, aux)
    gain_a = gain_buf[pl.ds(0, 1), :]
    gain_m = gain_buf[pl.ds(1, 1), :]
    residual = x_ref[...].astype(f32)
    normed = (residual * norm_factor(residual) * gain_a).astype(bf16)
    cos_part = rope_ref[:, pl.ds(0, HEAD_DIM)]
    sin_part = rope_ref[:, pl.ds(HEAD_DIM, HEAD_DIM)]

    def turned(values, orient):
        swapped = pltpu.roll(values, HEAD_DIM // 2, 1)
        return values * cos_part + swapped * (sin_part * orient)

    kv_rows = product(normed, full_a[:, pl.ds(0, 2 * kv_width)])
    own_block = at_rows(member * tokens, tokens, 128)
    for part in range(2 * KEY_VALUE_HEADS):
        piece = kv_rows[:, part * HEAD_DIM : (part + 1) * HEAD_DIM]
        if part < KEY_VALUE_HEADS:
            piece = turned(piece, 1.0)
        kv_all[own_block, pl.ds(part * HEAD_DIM, HEAD_DIM)] = piece.astype(bf16)
    gather_start(kv_all, kv_sems)
    turn_send[0] = jnp.transpose(normed).reshape(turn_send.shape[1:])

    def turn_copy(kind, step):
        return remote(
            turn_send.at[kind % 3, :, xor(member, step)],
            turn_recv.at[kind, :, :, at_rows(member * tokens, tokens, 128)],
            turn_sems,
            (kind, step),
            in_plane(step),
        )

    def turn_start(kind):
        for step in range(1, 8):
            turn_copy(kind, step).start()
        turn_recv[kind, :, :, at_rows(member * tokens, tokens, 128)] = turn_send[
            kind % 3, :, pl.ds(member, 1)
        ].reshape(turn_recv.shape[1], rows, tokens)

    turn_start(0)
    pass_on_plane(2)
    gather_pass(kv_all, kv_sems)
    pass_on_diagonal(1, range(4))
    gather_start(*token_where(0, 0))
    gather_pass_last(kv_all, kv_sems)
    pass_on_sibling(1)
    token_z(0).wait_recv()
    gather_start(*token_where(0, 1))
    arrived_dense(1)
    spill_b_copy = pltpu.make_async_copy(
        arena.at[pl.ds(0, width)], spill_b, local_sems.at[3]
    )
    spill_b_copy.start()
    for head in range(QUERY_HEADS):
        if head % 2 == 0:
            pair = product(normed, arena[pl.ds(0, width), pl.ds(head * HEAD_DIM, 2 * HEAD_DIM)])
        piece = pair[:, (head % 2) * HEAD_DIM : (head % 2 + 1) * HEAD_DIM]
        q_rows[pl.ds(head * tokens, tokens)] = turned(piece, 1.0).astype(bf16)
    gather_finish(kv_all, kv_sems)
    for group in range(KEY_VALUE_HEADS):
        k_t[group] = jnp.transpose(kv_all[:, pl.ds(group * HEAD_DIM, HEAD_DIM)])
        v_t[group] = jnp.transpose(kv_all[:, pl.ds(kv_width + group * HEAD_DIM, HEAD_DIM)])
    pass_on_diagonal(2, range(4))

    seq_len = kv_all.shape[0]
    pairs = QUERY_HEADS // 2
    pairs_per_group = pairs // KEY_VALUE_HEADS
    key_index = lax.broadcasted_iota(jnp.int32, (seq_len, 2 * tokens), 0)
    query_index = member * tokens + lax.rem(
        lax.broadcasted_iota(jnp.int32, (seq_len, 2 * tokens), 1), tokens
    )
    allowed = key_index <= query_index

    def pair_scores(pair, group):
        queries = q_rows[at_rows(pair * 2 * tokens, 2 * tokens, 128)]
        keys = kv_all[:, at_rows(group * HEAD_DIM, HEAD_DIM, 128)]
        scores = product_rows(keys, queries) * score_scale
        return jnp.where(allowed, scores, masked_score), queries

    def attend(pair, carry):
        group = lax.div(pair, pairs_per_group)
        scores, _ = pair_scores(pair, group)
        peak = jnp.max(scores, axis=0, keepdims=True)
        expo_vals = jnp.exp(scores - peak)
        sums = jnp.sum(expo_vals, axis=0, keepdims=True)
        probs = (expo_vals / sums).astype(bf16)
        lse_buf[pair] = jnp.broadcast_to(peak + jnp.log(sums), (8, 2 * tokens))
        part = product(v_t[group], probs)
        for inner in (0, 1):
            piece = part[:, inner * tokens : (inner + 1) * tokens].astype(bf16)
            attn_buf[2 * pair + inner] = piece
        return carry

    lax.fori_loop(0, pairs, attend, 0)
    pass_on_sibling(2)
    gather_pass(*token_where(0, 0))
    attn_t = attn_buf[...].reshape(width, tokens)
    turn_send[1] = attn_t.reshape(turn_send.shape[1:])
    attn = jnp.transpose(attn_t)
    arrived_dense(2)
    spill_c_copy = pltpu.make_async_copy(
        arena.at[pl.ds(width, width)], spill_c, local_sems.at[4]
    )
    spill_c_copy.start()
    for start in range(0, width, 512):
        after_buf[:, pl.ds(start, 512)] = x_ref[:, pl.ds(start, 512)].astype(f32) + product(
            attn, arena[pl.ds(width, width), pl.ds(start, 512)]
        )
    after = after_buf[...]
    normed_two = (after * norm_factor(after) * gain_m).astype(bf16)
    n2_all[token_rows(0, 0)] = normed_two
    spill_b_copy.wait()
    spill_c_copy.wait()
    for part in range(3):
        sent_dense(part)
    token_z(1).start()
    gather_start(*token_where(1, 0))
    turn_send[2] = jnp.transpose(normed_two).reshape(turn_send.shape[1:])
    gather_pass(*token_where(0, 1))
    gather_pass_last(*token_where(0, 0))
    gather_pass_last(*token_where(0, 1))
    token_z(1).wait_recv()
    gather_start(*token_where(1, 1))
    for plane_step in (0, 1):
        gather_finish(*token_where(0, plane_step))
    expert_finish()

    own_lane = lax.broadcasted_iota(jnp.int32, (2 * tokens, 128), 1) == member
    low_lane = lax.broadcasted_iota(jnp.int32, (2 * tokens, 128), 1) == member + 64
    def arena_slot(base, kind, slot):
        first, each = {"stage": (0, 2), "sib": (4, 2), "sum": (8, 8), "recv": (24, 7)}[base]
        return at_rows((first + kind * each + slot) * tokens, tokens, 128)

    def sib_copy(kind, slot):
        return remote(
            arena.at[arena_slot("stage", kind, slot)],
            arena.at[arena_slot("sib", kind, slot)],
            sib_sems,
            (kind, slot),
            sibling,
        )

    def sib_gate_copy():
        return remote(
            gate_buf.at[pl.ds(8, 8)], gate_buf.at[pl.ds(16, 8)], sib_sems, (2, 0), sibling
        )

    def bit_of(held, bit):
        if isinstance(held, int):
            return held // bit % 2
        return jnp.where(held & bit > 0, 1, 0)

    def ret_copy(kind, part, held, stage):
        first, second, third = part_order(part)
        slot = (
            bit_of(held, second) + 2 * bit_of(held, third),
            4 + bit_of(held, third),
            6,
        )[stage]
        columns = pl.ds(parts[part], 512)
        return remote(
            arena.at[arena_slot("sum", kind, held), columns],
            arena.at[arena_slot("recv", kind, slot), columns],
            ret_sems,
            (kind, part, slot),
            cube_device((first, second, third)[stage]),
        )

    def ret_arrived(kind, part, slot):
        columns = pl.ds(parts[part], 512)
        block = arena.at[arena_slot("recv", kind, slot), columns]
        return remote(block, block, ret_sems, (kind, part, slot), sibling)

    def ret_sum(kind, part, held, slots):
        columns = pl.ds(parts[part], 512)
        total = arena[arena_slot("sum", kind, held), columns].astype(f32)
        for slot in slots:
            total = total + arena[arena_slot("recv", kind, slot), columns].astype(f32)
        return total

    def ret_second(kind):
        for part in range(3):
            first, second, third = part_order(part)
            for held, slot in ((second, 1), (second | third, 3)):
                ret_arrived(kind, part, slot).wait_recv()
                arena[arena_slot("sum", kind, held), pl.ds(parts[part], 512)] = ret_sum(
                    kind, part, held, (slot,)
                ).astype(bf16)
                ret_copy(kind, part, held, 1).start()

    def ret_third(kind):
        for part in range(3):
            third = part_order(part)[2]
            for slot in (2, 5):
                ret_arrived(kind, part, slot).wait_recv()
            arena[arena_slot("sum", kind, third), pl.ds(parts[part], 512)] = ret_sum(
                kind, part, third, (2, 5)
            ).astype(bf16)
            ret_copy(kind, part, third, 2).start()

    def ret_total(kind):
        for part in range(3):
            for slot in (0, 4, 6):
                ret_arrived(kind, part, slot).wait_recv()
        return jnp.concatenate([ret_sum(kind, part, 0, (0, 4, 6)) for part in range(3)], axis=1)

    def ret_sent(kind):
        for part in range(3):
            first, second, third = part_order(part)
            for held in range(8):
                if held & first:
                    ret_copy(kind, part, held, 0).wait_send()
            for held in (second, second | third):
                ret_copy(kind, part, held, 1).wait_send()
            ret_copy(kind, part, third, 2).wait_send()

    def ret_gate_copy(held):
        return remote(
            gate_buf.at[held], gate_buf.at[24 + held], gate_sems, (held,), cube_device(held)
        )

    def halves(values, first):
        return jnp.where(first, values[:tokens], values[tokens:])

    def block_rows(held):
        other_plane = xor(parity, held & 1)
        chip = xor(lax.div(member, 2), lax.div(held, 2))
        return at_rows((other_plane * 4 + chip) * 2 * tokens, 2 * tokens, 128)

    def first_step(held, carry):
        @pl.when(held == 1)
        def _():
            gather_pass(*token_where(1, 0))

        @pl.when(held == 2)
        def _():
            gather_pass(*token_where(1, 1))

        @pl.when(held == 4)
        def _():
            gather_pass_last(*token_where(1, 0))
            gather_pass_last(*token_where(1, 1))

        own = token_rows(held & 1, held & 6)
        remote(
            n2_all.at[own],
            n2_all.at[own],
            tok_sems,
            (1, held & 1, 4 + lax.div(held, 2)),
            sibling,
        ).wait_recv()
        here = block_rows(held)
        token_block = n2_all[here, :]
        gate_up = product(token_block, w_in_half[...])
        gates = masked_gates(
            token_block,
            full_a[:, pl.ds(2 * kv_width, 128)],
            cot_all[here, pl.ds(width, 128)],
        )
        gate = jnp.sum(jnp.where(own_lane, gates, 0.0), axis=1, keepdims=True)
        gate_half = gate_up[:, :half]
        up_half = gate_up[:, half:]
        sigmoid_vals = 1.0 / (1.0 + jnp.exp(-gate_half))
        silu_vals = gate_half * sigmoid_vals
        hidden = silu_vals * up_half
        hidden_all[here, :] = (gate * hidden).astype(bf16)
        back = product_rows(cot_all[here, pl.ds(0, width)], w_out_half[...])
        gate_grad = jnp.sum(hidden * back, axis=1, keepdims=True)
        act_grad = gate * back
        gate_part = act_grad * up_half * sigmoid_vals * (1.0 + gate_half * (1.0 - sigmoid_vals))
        g_all[here, pl.ds(0, half)] = gate_part.astype(bf16)
        g_all[here, pl.ds(half, half)] = (act_grad * silu_vals).astype(bf16)
        gate_high = gate_grad.astype(bf16).astype(f32)
        gate_lanes = jnp.where(own_lane, gate_high, 0.0) + jnp.where(
            low_lane, gate_grad - gate_high, 0.0
        )
        gate_buf[held] = halves(gate_lanes, core == 0).astype(bf16)
        gate_buf[8 + held] = halves(gate_lanes, core == 1).astype(bf16)
        return carry

    lax.fori_loop(0, 8, first_step, 0)
    token_z(0).wait_send()
    token_z(1).wait_send()
    for plane_step in (0, 1):
        gather_sent(*token_where(1, plane_step))
    sib_gate_copy().start()

    def turn_held(turn):
        return jnp.where(turn == 3, 3, jnp.where(turn == 4, 4, 7 - turn))

    def second_step(kind, turn, carry):
        @pl.when(turn < 8)
        def _():
            slot2 = lax.rem(turn, 2)
            held = turn_held(turn)
            here = block_rows(held)

            @pl.when(turn >= 2)
            def _():
                sib_copy(kind, slot2).wait_send()
                pl.semaphore_wait(credit_sem, 1)

            place = arena_slot("sum", kind, held)
            for start in range(0, width, 512):
                columns = pl.ds(start, 512)
                if kind == 0:
                    result = product_rows(g_all[here, :], w_in_half[columns, :])
                else:
                    result = product(hidden_all[here, :], w_out_half[:, columns])
                arena[arena_slot("stage", kind, slot2), columns] = halves(
                    result, core == 1
                ).astype(bf16)
                arena[place, columns] = halves(result, core == 0).astype(bf16)
            sib_copy(kind, slot2).start()

        @pl.when(turn > 0)
        def _():
            last = turn - 1
            slot2 = lax.rem(last, 2)
            held = turn_held(last)
            place = arena_slot("sum", kind, held)
            sib_copy(kind, slot2).wait_recv()
            arena[place] = (
                arena[place].astype(f32) + arena[arena_slot("sib", kind, slot2)].astype(f32)
            ).astype(bf16)

            @pl.when(last < 6)
            def _():
                pl.semaphore_signal(credit_sem, inc=1, device_id=sibling, device_id_type=MESH)

            for part in range(3):

                @pl.when(held & (1 << part) > 0)
                def _():
                    ret_copy(kind, part, held, 0).start()

        return carry

    def gin_copy(step):
        if step >= 2:
            source = gin_early.at[step - 2]
        else:
            source = w_in_half.at[at_rows(xor(plane, step) * quarter, quarter)]
        if step == 0:
            return pltpu.make_async_copy(source, grad_in_ref.at[0], local_sems.at[5])
        return remote(
            source, grad_in_ref.at[step], gin_sems, (step,), (xor(plane, step), member)
        )

    def gin_quarter(step):
        start = xor(plane, step) * quarter
        for piece in range(0, quarter, 128):
            columns = n2_all[:, at_rows(start + piece, 128, 128)]
            result = product_columns(columns, g_all[...]).astype(bf16)
            if step >= 2:
                gin_early[step - 2, pl.ds(piece, 128)] = result
            else:
                w_in_half[at_rows(start + piece, 128, 128)] = result

    def second_loop(kind):
        lax.fori_loop(0, 9, functools.partial(second_step, kind), 0)
        for slot in (0, 1):
            sib_copy(kind, slot).wait_send()

    for kind in (1, 2):
        turn_start(kind)
    gin_quarter(2)
    gin_copy(2).start()
    second_loop(0)
    sib_gate_copy().wait()
    gate_buf[pl.ds(0, 8)] = (
        gate_buf[pl.ds(0, 8)].astype(f32) + gate_buf[pl.ds(16, 8)].astype(f32)
    ).astype(bf16)
    for held in range(1, 8):
        ret_gate_copy(held).start()
    ret_second(0)

    gin_quarter(3)
    gin_copy(3).start()
    for step in (1, 0):
        gin_quarter(step)
    gin_copy(0).start()

    def gout_copy(slot):
        source = w_out_half.at[pl.ds(slot * quarter_out, quarter_out)]
        target = grad_out_ref.at[out_half]
        device = (parity * 2 + slot, member)
        return remote(source, target, gout_sems, (slot,), device, (out_half,))

    def gout_local(slot):
        return pltpu.make_async_copy(
            w_out_half.at[pl.ds(slot * quarter_out, quarter_out)],
            grad_out_ref.at[out_half],
            local_sems.at[6],
        )

    def gout_arrived(turn):
        source = w_out_half.at[pl.ds(0, quarter_out)]
        return remote(source, grad_out_ref.at[turn], gout_sems, (turn,), (xor(plane, 1), member))

    own_n2 = n2_all[token_rows(0, 0), :]
    own_mask = cot_all[token_rows(0, 0), pl.ds(width, 128)]
    own_gates = masked_gates(own_n2, full_a[:, pl.ds(2 * kv_width, 128)], own_mask)
    ret_third(0)
    second_loop(1)
    for start in range(0, half, 128):
        w_out_half[pl.ds(start, 128)] = product_columns(
            hidden_all[:, pl.ds(start, 128)], cot_all[:, pl.ds(0, width)]
        ).astype(bf16)

    load_b = pltpu.make_async_copy(
        spill_b, cot_all.at[pl.ds(0, width), pl.ds(0, width)], local_sems.at[3]
    )
    load_c = pltpu.make_async_copy(spill_c, n2_all.at[pl.ds(0, width)], local_sems.at[4])
    load_b.start()
    load_c.start()

    total_in = ret_total(0)
    total_gate = gate_buf[0].astype(f32)
    for held in range(1, 8):
        ret_gate_copy(held).wait_recv()
        total_gate = total_gate + gate_buf[24 + held].astype(f32)
    gin_copy(1).start()
    for slot in (0, 1):

        @pl.when(parity * 2 + slot != plane)
        def _():
            gout_copy(slot).start()

        @pl.when(parity * 2 + slot == plane)
        def _():
            gout_local(slot).start()

    gate_grad = total_gate + pltpu.roll(total_gate, 64, 1)
    gate_inner = jnp.sum(own_gates * gate_grad, axis=1, keepdims=True)
    logit_grad = own_gates * (gate_grad - gate_inner)
    lg_parts = split_three(logit_grad)
    aux_now = full_a[:, pl.ds(2 * kv_width, 128)]
    for part in lg_parts:
        total_in = total_in + product_rows(part, aux_now)
    after = after_buf[...]

    def norm_backward(values, gain, grad):
        factor = norm_factor(values)
        scaled = grad * gain
        gain_row = jnp.sum(grad * values * factor, axis=0, keepdims=True)
        inner = jnp.mean(scaled * values, axis=-1, keepdims=True)
        return factor * scaled - values * factor * factor * factor * inner, gain_row

    two_back, gain_m_row = norm_backward(after, gain_buf[pl.ds(1, 1), :], total_in)
    mid = cot_ref[...].astype(f32) + two_back
    dx_ref[...] = mid
    out_grad = mid.astype(bf16)
    og_all[own_block, pl.ds(0, width)] = out_grad
    og_all[own_block, pl.ds(width, 128)] = (
        lg_parts[0].astype(f32)
        + pltpu.roll(lg_parts[1].astype(f32), 8, 1)
        + pltpu.roll(lg_parts[2].astype(f32), 16, 1)
    ).astype(bf16)

    gather_start(og_all, og_sems)
    load_c.wait()
    for head in range(0, QUERY_HEADS, 2):
        pair = product_rows(out_grad, n2_all[pl.ds(head * HEAD_DIM, 2 * HEAD_DIM), :])
        for inner in (0, 1):
            do_rows[pl.ds((head + inner) * tokens, tokens)] = pair[
                :, inner * HEAD_DIM : (inner + 1) * HEAD_DIM
            ].astype(bf16)
    gather_pass(og_all, og_sems)

    def dkv_rows(kind_core, chip):
        return at_rows((kind_core * 4 + chip) * tokens, tokens, 128)

    def dkv_columns(group):
        return pl.ds(group * 2 * HEAD_DIM, 2 * HEAD_DIM)

    def dkv_sibling(group):
        source = g_all.at[at_rows((1 - core) * 4 * tokens, 4 * tokens, 128), dkv_columns(group)]
        target = dkv_recv.at[group, pl.ds(4 * tokens, 4 * tokens)]
        return remote(source, target, dkv_sems, (group, 0), sibling)

    def dkv_copy(group, step):
        chip = xor(lax.div(member, 2), step)
        return remote(
            g_all.at[dkv_rows(core, chip), dkv_columns(group)],
            dkv_recv.at[group, pl.ds(step * tokens, tokens)],
            dkv_sems,
            (group, step),
            in_plane(2 * step),
        )

    def dkv_pass(group):
        dkv_sibling(group).wait_recv()
        mine = at_rows(core * 4 * tokens, 4 * tokens, 128)
        g_all[mine, dkv_columns(group)] = (
            g_all[mine, dkv_columns(group)].astype(f32)
            + dkv_recv[group, pl.ds(4 * tokens, 4 * tokens)].astype(f32)
        ).astype(bf16)
        for step in (1, 2, 3):
            dkv_copy(group, step).start()

    planes = turn_recv.shape[1]

    def dense_rows(piece, step):
        return at_rows((piece * planes + xor(plane, step)) * rows, rows)

    def kv_grad_copy(step):
        source = arena.at[dense_rows(0, step), pl.ds(0, 2 * kv_width)]
        if step == 0:
            return pltpu.make_async_copy(source, grad_kv_ref.at[0], local_sems.at[0])
        device = (xor(plane, step), member)
        return remote(source, grad_kv_ref.at[step], dense_sems, (0, step), device)

    def pair_rows(piece, which):
        return pl.ds(width + ((piece - 1) * 2 + which) * rows, rows)

    def dense_copy(piece, step):
        columns = pl.ds((piece - 1) * width, width)
        if step == 2:
            target = grad_dense_ref.at[1, :, columns]
            device = (xor(plane, 2), member)
        else:
            target = n2_all.at[pair_rows(piece, step // 2)]
            device = (xor(plane, 1), member)
        return remote(arena.at[dense_rows(piece, step)], target, dense_sems, (piece, step), device)

    def dense_own(piece):
        return pltpu.make_async_copy(
            arena.at[dense_rows(piece, 0)],
            grad_dense_ref.at[0, :, pl.ds((piece - 1) * width, width)],
            local_sems.at[piece],
        )

    def dense_start(piece):
        for step in (3, 1):
            dense_copy(piece, step).start()

    def dense_pass(piece):
        for which, step in ((1, 2), (0, 0)):
            dense_copy(piece, 1 + 2 * which).wait_recv()
            block = dense_rows(piece, step)
            arena[block] = (
                arena[block].astype(f32) + n2_all[pair_rows(piece, which)].astype(f32)
            ).astype(bf16)
            if step:
                dense_copy(piece, 2).start()
            else:
                dense_own(piece).start()

    for group in range(KEY_VALUE_HEADS):
        values = kv_all[:, pl.ds(kv_width + group * HEAD_DIM, HEAD_DIM)]
        dk = jnp.zeros((seq_len, HEAD_DIM), f32)
        dv = jnp.zeros((seq_len, HEAD_DIM), f32)
        for pair in range(group * pairs_per_group, (group + 1) * pairs_per_group):
            scores, queries = pair_scores(pair, group)
            probs = jnp.exp(scores - lse_buf[pair][0:1])
            grads = do_rows[pl.ds(pair * 2 * tokens, 2 * tokens)]
            prob_grad = product_rows(values, grads)
            row_dot = jnp.sum(probs * prob_grad, axis=0, keepdims=True)
            score_grad = (probs * (prob_grad - row_dot)).astype(bf16)
            dk = dk + product(score_grad, queries)
            dv = dv + product(probs.astype(bf16), grads)
            dq = product(k_t[group], score_grad) * score_scale
            for inner in (0, 1):
                piece = jnp.transpose(dq[:, inner * tokens : (inner + 1) * tokens])
                qg_all[own_block, pl.ds((2 * pair + inner) * HEAD_DIM, HEAD_DIM)] = turned(
                    piece, -1.0
                ).astype(bf16)
        start = group * 2 * HEAD_DIM
        dk = (dk * score_scale).astype(bf16)
        dv = dv.astype(bf16)
        for block in range(8):
            place = pl.ds((block % 2 * 4 + block // 2) * tokens, tokens)
            here = slice(block * tokens, (block + 1) * tokens)
            g_all[place, pl.ds(start, HEAD_DIM)] = dk[here]
            g_all[place, pl.ds(start + HEAD_DIM, HEAD_DIM)] = dv[here]
        dkv_sibling(group).start()
        span = width // KEY_VALUE_HEADS
        gather_start(qg_all, qg_sems, (group,), group * span, (group + 1) * span)
        if group == 0:
            gather_pass_last(og_all, og_sems)
            dkv_pass(0)
            ret_second(1)

    dkv_pass(1)
    gather_pass(qg_all, qg_sems, (0,), 0, span)

    for group in range(KEY_VALUE_HEADS):
        start = group * 2 * HEAD_DIM
        mine = dkv_rows(core, lax.div(member, 2))
        dk = g_all[mine, pl.ds(start, HEAD_DIM)].astype(f32)
        dv = g_all[mine, pl.ds(start + HEAD_DIM, HEAD_DIM)].astype(f32)
        for step in (1, 2, 3):
            dkv_copy(group, step).wait_recv()
            block = pl.ds(step * tokens, tokens)
            dk = dk + dkv_recv[group, block, pl.ds(0, HEAD_DIM)].astype(f32)
            dv = dv + dkv_recv[group, block, pl.ds(HEAD_DIM, HEAD_DIM)].astype(f32)
        kvg_all[own_block, pl.ds(group * HEAD_DIM, HEAD_DIM)] = turned(dk, -1.0).astype(bf16)
        kvg_all[own_block, pl.ds(kv_width + group * HEAD_DIM, HEAD_DIM)] = dv.astype(bf16)
    gather_start(kvg_all, kvg_sems)
    ret_third(1)
    gather_finish(og_all, og_sems)
    for kind in range(3):
        for step in range(1, 8):
            turn_copy(kind, step).wait()
    turned_attn = turn_recv[1].reshape(planes * rows, seq_len)
    for start in range(0, width, 512):
        arena[pl.ds(2 * planes * rows, planes * rows), pl.ds(start, 512)] = product(
            turned_attn, og_all[:, pl.ds(start, 512)]
        ).astype(bf16)
    dense_start(2)
    router_part = product(
        turn_recv[2].reshape(planes * rows, seq_len), og_all[:, pl.ds(width, 128)]
    )

    gather_pass(qg_all, qg_sems, (1,), span, 2 * span)
    gather_pass(kvg_all, kvg_sems)
    for group in range(KEY_VALUE_HEADS):
        gather_pass_last(qg_all, qg_sems, (group,), group * span, (group + 1) * span)
    gather_pass_last(kvg_all, kvg_sems)

    load_b.wait()
    own_kvg = kvg_all[own_block, :]
    own_qg = qg_all[own_block, :]
    normed_grad = product_rows(own_kvg, full_a[:, pl.ds(0, 2 * kv_width)]) + product_rows(
        own_qg, cot_all[pl.ds(0, width), pl.ds(0, width)]
    )
    one_back, gain_a_row = norm_backward(
        x_ref[...].astype(f32), gain_buf[pl.ds(0, 1), :], normed_grad
    )
    dx_ref[...] = dx_ref[...] + one_back
    line = lax.broadcasted_iota(jnp.int32, (128, width), 0)
    gain_lines = jnp.zeros((128, width), f32)
    for offset, part in enumerate(split_three(gain_a_row) + split_three(gain_m_row)):
        gain_lines = jnp.where(line == 32 + offset, part.astype(f32), gain_lines)
    turn_send[0] = jnp.transpose(gain_lines.astype(bf16)).reshape(turn_send.shape[1:])
    turn_start(3)

    turned_normed = turn_recv[0].reshape(planes * rows, seq_len)
    for group in range(KEY_VALUE_HEADS):
        gather_finish(qg_all, qg_sems, (group,), group * span, (group + 1) * span)
    for start in range(0, width, 512):
        arena[pl.ds(planes * rows, planes * rows), pl.ds(start, 512)] = product(
            turned_normed, qg_all[:, pl.ds(start, 512)]
        ).astype(bf16)
    dense_start(1)
    dense_pass(2)
    gather_finish(kvg_all, kvg_sems)
    arena[pl.ds(0, planes * rows), pl.ds(0, 2 * kv_width)] = product(
        turned_normed, kvg_all[...]
    ).astype(bf16)
    for step in (2, 3, 1, 0):
        kv_grad_copy(step).start()
    dense_pass(1)
    for step in range(1, 8):
        turn_copy(3, step).wait()
    aux_total = router_part
    for block in range(8):
        aux_total = aux_total + turn_recv[3, :, :, pl.ds(block * tokens, tokens)].reshape(
            planes * rows, tokens
        ).astype(f32)
    aux_send[...] = aux_total.reshape(planes, rows, 128)

    def aux_copy(step):
        return remote(
            aux_send.at[xor(plane, step)],
            grad_aux_ref.at[step],
            aux_sems,
            (step,),
            (xor(plane, step), member),
        )

    for step in (1, 2, 3):
        aux_copy(step).start()
    own_aux = pltpu.make_async_copy(aux_send.at[plane], grad_aux_ref.at[0], local_sems.at[7])
    own_aux.start()

    block_out_ref[...] = (after_buf[...] + ret_total(1)).astype(bf16)

    for held in range(1, 8):
        ret_gate_copy(held).wait_send()
    for kind in (0, 1):
        ret_sent(kind)
    for group in range(KEY_VALUE_HEADS):
        dkv_sibling(group).wait_send()
        for step in (1, 2, 3):
            dkv_copy(group, step).wait_send()
    gin_copy(0).wait()
    for step in (1, 2, 3):
        gin_copy(step).wait()
    for slot in (0, 1):

        @pl.when(parity * 2 + slot != plane)
        def _():
            gout_copy(slot).wait_send()

        @pl.when(parity * 2 + slot == plane)
        def _():
            gout_local(slot).wait()

    for turn in (0, 1):

        @pl.when(out_half + 2 * turn != plane)
        def _():
            gout_arrived(turn).wait_recv()

    for step in range(4):
        kv_grad_copy(step).wait()
    for piece in (1, 2):
        dense_own(piece).wait()
        dense_copy(piece, 2).wait()
        for step in (1, 3):
            dense_copy(piece, step).wait_send()
    for step in (1, 2, 3):
        aux_copy(step).wait()
    own_aux.wait()


EXPERT_LANES = 8


def final_kernel(
    block_ref,
    dx_ref,
    in_ref,
    out_ref,
    dense_ref,
    kv_ref,
    aux_ref,
    block_out,
    tokens_grad,
    gain_a_out,
    query_out,
    key_out,
    value_out,
    output_out,
    gain_m_out,
    router_out,
    w_in_out,
    w_out_out,
):
    f32 = jnp.float32
    half = FF // 2
    block_out[...] = block_ref[...]
    tokens_grad[...] = dx_ref[...]
    even = lax.rem(lax.axis_index("dp"), 2) == 0
    own = in_ref[0].astype(f32) + in_ref[2].astype(f32)
    other = in_ref[1].astype(f32) + in_ref[3].astype(f32)
    halves = (jnp.where(even, own, other), jnp.where(even, other, own))
    count = own.shape[0]
    tiles = half // 128
    for tile in range(4 * tiles):
        piece, rest = divmod(tile, 2 * tiles)
        which, lane = divmod(rest, tiles)
        start = piece * half + lane * 128
        w_in_out[pl.ds(tile, count, 4 * tiles), :] = halves[which][:, start : start + 128]
    total = out_ref[0].astype(f32) + out_ref[1].astype(f32)
    count, width = total.shape
    for tile in range(width // 128):
        w_out_out[pl.ds(tile, count, width // 128), :] = total[:, tile * 128 : tile * 128 + 128]

    @pl.when(pl.program_id(0) == 0)
    def _():
        dense = dense_ref[0].astype(f32) + dense_ref[1].astype(f32)
        query_out[0] = dense[:, :width]
        output_out[0] = dense[:, width:]
        kv = (
            kv_ref[0].astype(f32)
            + kv_ref[1].astype(f32)
            + kv_ref[2].astype(f32)
            + kv_ref[3].astype(f32)
        )
        key_out[0] = kv[:, : kv.shape[1] // 2]
        value_out[0] = kv[:, kv.shape[1] // 2 :]
        aux = aux_ref[0] + aux_ref[1] + aux_ref[2] + aux_ref[3]
        rows = aux.shape[0]
        lines = jnp.transpose(
            jnp.concatenate([aux, jnp.zeros((128 - rows, 128), f32)], axis=0)
        )
        router_out[...] = (lines[0:8] + lines[8:16] + lines[16:24])[:, :rows]
        gain_a_out[...] = (lines[32:33] + lines[33:34] + lines[34:35])[:, :rows]
        gain_m_out[...] = (lines[35:36] + lines[36:37] + lines[37:38])[:, :rows]


def fast_body(
    tokens,
    cotangent,
    routes,
    gain_attn,
    w_query,
    key_weight,
    value_weight,
    w_output,
    gain_moe,
    w_router,
    w_in,
    w_out,
):
    f32, bf16 = jnp.float32, jnp.bfloat16
    total_rows, width = tokens.shape
    rows = w_query.shape[1]
    planes = lax.axis_size("dp")
    members = lax.axis_size("expert")
    seq_len = total_rows * members
    kv_width = key_weight.shape[2]
    quarter = w_in.shape[1]
    quarter_out = w_out.shape[1]
    half = FF // 2
    positions = lax.axis_index("expert") * total_rows + jnp.arange(total_rows, dtype=jnp.int32)
    cos_table, sin_table = rope_tables(positions, HEAD_DIM)
    rope = jnp.concatenate([cos_table, cos_table, -sin_table, sin_table], axis=1)
    in_vmem = pl.BlockSpec(memory_space=pltpu.VMEM)
    anywhere = pl.BlockSpec(memory_space=pl.ANY)
    pair_rows = 2 * seq_len
    shape = jax.ShapeDtypeStruct
    dma = pltpu.SemaphoreType.DMA
    heads = QUERY_HEADS
    (
        block_out,
        tokens_grad,
        grad_in,
        grad_out,
        grad_dense,
        grad_kv,
        grad_aux,
        _,
        _,
    ) = pl.pallas_call(
        layer_kernel,
        out_shape=(
            shape((total_rows, width), bf16),
            shape((total_rows, width), f32),
            shape((planes, quarter, 2 * half), bf16),
            shape((2, quarter_out, width), bf16),
            shape((2, rows, 2 * width), bf16),
            shape((planes, rows, 2 * kv_width), bf16),
            shape((planes, rows, 128), f32),
            shape((width, width), bf16),
            shape((width, width), bf16),
        ),
        in_specs=[in_vmem] * 11 + [anywhere] * 2,
        out_specs=(in_vmem,) * 2 + (anywhere,) * 7,
        scratch_shapes=[
            pltpu.VMEM((pair_rows, width), bf16),
            pltpu.VMEM((pair_rows, width + 128), bf16),
            pltpu.VMEM((width, 2 * kv_width + 128), bf16),
            pltpu.VMEM((38 * total_rows, width), bf16),
            pltpu.VMEM((32, total_rows, 128), bf16),
            pltpu.VMEM((width, 2 * half), bf16),
            pltpu.VMEM((half, width), bf16),
            pltpu.VMEM((pair_rows, half), bf16),
            pltpu.VMEM((pair_rows, 2 * half), bf16),
            pltpu.VMEM((2, quarter, 2 * half), bf16),
            pltpu.VMEM((seq_len, 2 * kv_width), bf16),
            pltpu.VMEM((KEY_VALUE_HEADS, HEAD_DIM, seq_len), bf16),
            pltpu.VMEM((KEY_VALUE_HEADS, HEAD_DIM, seq_len), bf16),
            pltpu.VMEM((heads * total_rows, HEAD_DIM), bf16),
            pltpu.VMEM((heads * total_rows, HEAD_DIM), bf16),
            pltpu.VMEM((heads, HEAD_DIM, total_rows), bf16),
            pltpu.VMEM((total_rows, width), f32),
            pltpu.VMEM((heads // 2, 8, 2 * total_rows), f32),
            pltpu.VMEM((3, planes, members, rows, total_rows), bf16),
            pltpu.VMEM((4, planes, rows, seq_len), bf16),
            pltpu.VMEM((seq_len, width + 128), bf16),
            pltpu.VMEM((seq_len, width), bf16),
            pltpu.VMEM((seq_len, 2 * kv_width), bf16),
            pltpu.VMEM((KEY_VALUE_HEADS, seq_len, 2 * HEAD_DIM), bf16),
            pltpu.VMEM((planes, rows, 128), f32),
            pltpu.VMEM((16, width), f32),
            dma((2, 3, 4)),
            dma((2, 3, 4, 4)),
            dma((2, 3, 4, 4)),
            dma((2, 8)),
            dma((2, 2, 2, 8)),
            dma((2, 2)),
            dma((2, 4, 8)),
            dma((2, 4, 2)),
            dma((2, 2)),
            dma((2, 3, 2)),
            dma((2, 2, 3, 7)),
            dma((2, 8)),
            dma((2, 4)),
            dma((2, 2)),
            dma((2, 8)),
            dma((2, 2, 8)),
            dma((2, 8)),
            dma((2, 2, 8)),
            dma((2, 3, 4)),
            dma((2, 4)),
            dma((8,)),
            pltpu.SemaphoreType.REGULAR,
        ],
        compiler_params=pltpu.CompilerParams(
            collective_id=0, has_side_effects=True, vmem_limit_bytes=63 * 2**20
        ),
    )(
        tokens,
        cotangent,
        routes[0].T,
        rope,
        key_weight[0],
        value_weight[0],
        w_router[0].T,
        gain_attn,
        gain_moe,
        w_query[0],
        w_output[0],
        w_in.reshape(quarter, 2 * FF),
        w_out.reshape(quarter_out, width),
    )
    steps = 4
    whole = lambda *dims: pl.BlockSpec(dims, lambda i: (0,) * len(dims))
    final = pl.pallas_call(
        final_kernel,
        grid=(steps,),
        out_shape=(
            shape((total_rows, width), bf16),
            shape((total_rows, width), f32),
            shape((1, rows), f32),
            shape((1, rows, width), f32),
            shape((1, rows, kv_width), f32),
            shape((1, rows, kv_width), f32),
            shape((1, rows, width), f32),
            shape((1, rows), f32),
            shape((EXPERT_LANES, rows), f32),
            shape((quarter * 2 * FF // 128, 128), f32),
            shape((quarter_out * width // 128, 128), f32),
        ),
        in_specs=[
            pl.BlockSpec((total_rows // steps, width), lambda i: (i, 0)),
            pl.BlockSpec((total_rows // steps, width), lambda i: (i, 0)),
            pl.BlockSpec((planes, quarter // steps, 2 * half), lambda i: (0, i, 0)),
            pl.BlockSpec((2, quarter_out // steps, width), lambda i: (0, i, 0)),
            whole(2, rows, 2 * width),
            whole(planes, rows, 2 * kv_width),
            whole(planes, rows, 128),
        ],
        out_specs=(
            pl.BlockSpec((total_rows // steps, width), lambda i: (i, 0)),
            pl.BlockSpec((total_rows // steps, width), lambda i: (i, 0)),
            whole(1, rows),
            whole(1, rows, width),
            whole(1, rows, kv_width),
            whole(1, rows, kv_width),
            whole(1, rows, width),
            whole(1, rows),
            whole(EXPERT_LANES, rows),
            pl.BlockSpec((quarter * 2 * FF // 128 // steps, 128), lambda i: (i, 0)),
            pl.BlockSpec((quarter_out * width // 128 // steps, 128), lambda i: (i, 0)),
        ),
        compiler_params=pltpu.CompilerParams(vmem_limit_bytes=63 * 2**20),
    )(block_out, tokens_grad, grad_in, grad_out, grad_dense, grad_kv, grad_aux)
    return final[:8] + (
        final[8].T[None],
        final[9].reshape(1, quarter, 1, 2 * FF),
        final[10].reshape(1, quarter_out, 1, width),
    )


def solution(mesh):
    in_specs = (
        P(("dp", "expert"), None),
        P(("dp", "expert"), None),
        P(None, ("dp", "expert"), None),
        P(None, ("dp", "expert")),
        P(None, ("dp", "expert"), None),
        P(None, ("dp", "expert"), None),
        P(None, ("dp", "expert"), None),
        P(None, ("dp", "expert"), None),
        P(None, ("dp", "expert")),
        P(None, ("dp", "expert"), None),
        P(None, "dp", "expert", None),
        P(None, "dp", "expert", None),
    )
    out_specs = (
        P(("dp", "expert"), None),
        P(("dp", "expert"), None),
        P(None, ("dp", "expert")),
        P(None, ("dp", "expert"), None),
        P(None, ("dp", "expert"), None),
        P(None, ("dp", "expert"), None),
        P(None, ("dp", "expert"), None),
        P(None, ("dp", "expert")),
        P(None, ("dp", "expert"), None),
        P(None, "dp", "expert", None),
        P(None, "dp", "expert", None),
    )
    body = fast_body if mesh.shape["dp"] == 4 and mesh.shape["expert"] == 8 else general_body
    return jax.shard_map(body, mesh=mesh, in_specs=in_specs, out_specs=out_specs, check_vma=False)
```

```python
import functools

import jax
import jax.numpy as jnp
from jax import lax
from jax.experimental import pallas as pl
from jax.experimental.pallas import tpu as pltpu
from jax.sharding import PartitionSpec as P

MESH = pl.DeviceIdType.MESH

QUERY_HEADS = 12
KEY_VALUE_HEADS = 2
HEAD_DIM = 128
FF = 768
TOP = 4


norm_eps = 1e-06
rope_base = 1000000.0
masked_score = -1e30
top_precision = lax.Precision.HIGHEST


def norm_factor(values):
    return lax.rsqrt(jnp.mean(values * values, axis=-1, keepdims=True) + norm_eps)


def norm_back(values, gain, grad_out):
    factor = norm_factor(values)
    scaled = grad_out * gain
    gain_grad = jnp.sum(grad_out * values * factor, axis=0)
    inner_mean = jnp.mean(scaled * values, axis=-1, keepdims=True)
    return (factor * scaled - values * factor * factor * factor * inner_mean, gain_grad)


def rope_tables(positions, head_size):
    half_size = head_size // 2
    inverse = rope_base ** (-(jnp.arange(half_size, dtype=jnp.float32) * 2.0 / head_size))
    angles = positions.astype(jnp.float32)[:, None] * inverse[None, :]
    return (jnp.cos(angles), jnp.sin(angles))


def rotate(values, cos_table, sin_table, orient):
    half_size = values.shape[-1] // 2
    first_half = values[..., :half_size]
    second = values[..., half_size:]
    cos_part = cos_table[:, None, :]
    sin_part = orient * sin_table[:, None, :]
    return jnp.concatenate(
        [first_half * cos_part - second * sin_part, second * cos_part + first_half * sin_part],
        axis=-1,
    )


def plan_slots(route, expert_count, capacity):
    flat_route = route.reshape(-1)
    slot_total = flat_route.shape[0]
    onehot = (flat_route[:, None] == jnp.arange(expert_count, dtype=jnp.int32)[None, :]).astype(
        jnp.int32
    )
    before = jnp.cumsum(onehot, axis=0) - onehot
    target = flat_route * capacity + jnp.sum(before * onehot, axis=1)
    source = (
        jnp.full((expert_count * capacity,), slot_total, jnp.int32)
        .at[target]
        .set(jnp.arange(slot_total, dtype=jnp.int32))
    )
    filled = source < slot_total
    return (target, jnp.minimum(source, slot_total - 1), filled)


def general_body(
    tokens,
    cotangent,
    routes,
    gain_attn,
    w_query,
    key_weight,
    value_weight,
    w_output,
    gain_moe,
    w_router,
    w_in,
    w_out,
):
    total_rows, model_width = tokens.shape
    layer_count = w_query.shape[0]
    group_count = lax.axis_size("expert")
    seq_len = total_rows * group_count
    experts_local = w_in.shape[2]
    expert_count = experts_local * group_count
    capacity = min(total_rows, total_rows * TOP * 3 // (2 * expert_count))
    heads_per_group = QUERY_HEADS // KEY_VALUE_HEADS
    score_scale = HEAD_DIM ** (-0.5)
    positions = lax.axis_index("expert") * total_rows + jnp.arange(total_rows, dtype=jnp.int32)
    cos_table, sin_table = rope_tables(positions, HEAD_DIM)
    allowed = jnp.arange(seq_len, dtype=jnp.int32)[None, :] <= positions[:, None]
    zero_bf = jnp.zeros((), jnp.bfloat16)

    def score_block(query_rows, all_keys, group_of_heads):
        grouped_q = query_rows[
            :, group_of_heads * heads_per_group : (group_of_heads + 1) * heads_per_group, :
        ]
        scores = (
            jnp.einsum(
                "rgd,kd->grk",
                grouped_q,
                all_keys[:, group_of_heads, :],
                preferred_element_type=jnp.float32,
            )
            * score_scale
        )
        return (jnp.where(allowed[None], scores, masked_score), grouped_q)

    residual = tokens.astype(jnp.float32)
    layer_number = 0
    dense_w = (
        lax.all_gather(gain_attn[layer_number], ("dp", "expert"), axis=0, tiled=True),
        lax.all_gather(w_query[layer_number], ("dp", "expert"), axis=0, tiled=True),
        lax.all_gather(key_weight[layer_number], ("dp", "expert"), axis=0, tiled=True),
        lax.all_gather(value_weight[layer_number], ("dp", "expert"), axis=0, tiled=True),
        lax.all_gather(w_output[layer_number], ("dp", "expert"), axis=0, tiled=True),
        lax.all_gather(gain_moe[layer_number], ("dp", "expert"), axis=0, tiled=True),
        lax.all_gather(w_router[layer_number], ("dp", "expert"), axis=0, tiled=True),
    )
    expert_w = (
        lax.all_gather(w_in[layer_number], "dp", axis=0, tiled=True),
        lax.all_gather(w_out[layer_number], "dp", axis=0, tiled=True),
    )
    route = routes[layer_number]
    gain_a = dense_w[0].astype(jnp.float32)
    norm_result = (residual * norm_factor(residual) * gain_a).astype(jnp.bfloat16)
    query_rows = jnp.dot(norm_result, dense_w[1], preferred_element_type=jnp.float32).reshape(
        total_rows, QUERY_HEADS, HEAD_DIM
    )
    query_rows = rotate(query_rows, cos_table, sin_table, 1.0).astype(jnp.bfloat16)
    key_matrix_rows = jnp.dot(norm_result, dense_w[2], preferred_element_type=jnp.float32).reshape(
        total_rows, KEY_VALUE_HEADS, HEAD_DIM
    )
    key_matrix_rows = rotate(key_matrix_rows, cos_table, sin_table, 1.0).astype(jnp.bfloat16)
    value_matrix_rows = (
        jnp.dot(norm_result, dense_w[3], preferred_element_type=jnp.float32)
        .astype(jnp.bfloat16)
        .reshape(total_rows, KEY_VALUE_HEADS, HEAD_DIM)
    )
    all_keys = lax.all_gather(key_matrix_rows, "expert", axis=0, tiled=True)
    all_values = lax.all_gather(value_matrix_rows, "expert", axis=0, tiled=True)
    heads_out = []
    log_totals = []
    for group_of_heads in range(KEY_VALUE_HEADS):
        scores, grouped_q = score_block(query_rows, all_keys, group_of_heads)
        row_peak = jnp.max(scores, axis=-1, keepdims=True)
        expo_vals = jnp.exp(scores - row_peak)
        row_sums = jnp.sum(expo_vals, axis=-1, keepdims=True)
        attn_probs = (expo_vals / row_sums).astype(jnp.bfloat16)
        log_totals.append(row_peak + jnp.log(row_sums))
        heads_out.append(
            jnp.einsum(
                "grk,kd->rgd",
                attn_probs,
                all_values[:, group_of_heads, :],
                preferred_element_type=jnp.float32,
            )
        )
    attn = (
        jnp.concatenate(heads_out, axis=1)
        .reshape(total_rows, QUERY_HEADS * HEAD_DIM)
        .astype(jnp.bfloat16)
    )
    after_attn = residual + jnp.dot(attn, dense_w[4], preferred_element_type=jnp.float32)
    gain_m = dense_w[5].astype(jnp.float32)
    normed_two = (after_attn * norm_factor(after_attn) * gain_m).astype(jnp.bfloat16)
    logits = jnp.dot(normed_two, dense_w[6], preferred_element_type=jnp.float32)
    gate_probs = jax.nn.softmax(jnp.take_along_axis(logits, route, axis=1), axis=-1)
    target, source, filled = plan_slots(route, expert_count, capacity)
    send_rows = jnp.where(filled[:, None], normed_two[source // TOP], zero_bf)
    send_rows = send_rows.reshape(group_count, experts_local, capacity, model_width)
    arrived_rows = lax.all_to_all(send_rows, "expert", split_axis=0, concat_axis=0, tiled=True)
    gate_up_vals = jnp.einsum(
        "secd,def->secf", arrived_rows, expert_w[0], preferred_element_type=jnp.float32
    )
    expert_gate_half = gate_up_vals[..., :FF]
    expert_hidden_act = (
        expert_gate_half * jax.nn.sigmoid(expert_gate_half) * gate_up_vals[..., FF:]
    ).astype(jnp.bfloat16)
    expert_out = jnp.einsum(
        "secf,fed->secd", expert_hidden_act, expert_w[1], preferred_element_type=jnp.float32
    ).astype(jnp.bfloat16)
    arrived, gate_up, expert_out = (arrived_rows, gate_up_vals, expert_out)
    returned = lax.all_to_all(expert_out, "expert", split_axis=0, concat_axis=0, tiled=True)
    slot_out = returned.reshape(expert_count * capacity, model_width)[target].reshape(
        total_rows, TOP, model_width
    )
    new_residual = after_attn + jnp.sum(
        gate_probs[:, :, None] * slot_out.astype(jnp.float32), axis=1
    )
    saved_layers = [
        (
            residual,
            norm_result,
            query_rows,
            key_matrix_rows,
            value_matrix_rows,
            all_keys,
            all_values,
            log_totals,
            attn,
            after_attn,
            normed_two,
            route,
            gate_probs,
            target,
            source,
            filled,
            arrived,
            gate_up,
            slot_out,
            dense_w,
            expert_w,
        )
    ]
    block_out = new_residual.astype(jnp.bfloat16)
    grad_resid = cotangent.astype(jnp.float32)
    grad_lists = [[None] * layer_count for _ in range(9)]
    for layer_number in reversed(range(layer_count)):
        (
            resid_in,
            norm_result,
            query_rows,
            key_matrix_rows,
            value_matrix_rows,
            all_keys,
            all_values,
            log_totals,
            attn,
            after_attn,
            normed_two,
            route,
            gate_probs,
            target,
            source,
            filled,
            arrived,
            gate_up,
            slot_out,
            dense_w,
            expert_w,
        ) = saved_layers[layer_number]
        dense_w = (
            lax.all_gather(gain_attn[layer_number], ("dp", "expert"), axis=0, tiled=True),
            lax.all_gather(w_query[layer_number], ("dp", "expert"), axis=0, tiled=True),
            lax.all_gather(key_weight[layer_number], ("dp", "expert"), axis=0, tiled=True),
            lax.all_gather(value_weight[layer_number], ("dp", "expert"), axis=0, tiled=True),
            lax.all_gather(w_output[layer_number], ("dp", "expert"), axis=0, tiled=True),
            lax.all_gather(gain_moe[layer_number], ("dp", "expert"), axis=0, tiled=True),
            lax.all_gather(w_router[layer_number], ("dp", "expert"), axis=0, tiled=True),
        )
        expert_w = (
            lax.all_gather(w_in[layer_number], "dp", axis=0, tiled=True),
            lax.all_gather(w_out[layer_number], "dp", axis=0, tiled=True),
        )
        all_keys, all_values = (
            lax.all_gather(key_matrix_rows, "expert", axis=0, tiled=True),
            lax.all_gather(value_matrix_rows, "expert", axis=0, tiled=True),
        )
        gate_grad = jnp.sum(slot_out.astype(jnp.float32) * grad_resid[:, None, :], axis=-1)
        slot_grad = (
            (gate_probs[:, :, None] * grad_resid[:, None, :])
            .astype(jnp.bfloat16)
            .reshape(total_rows * TOP, model_width)
        )
        grad_rows = jnp.where(filled[:, None], slot_grad[source], zero_bf)
        grad_rows = grad_rows.reshape(group_count, experts_local, capacity, model_width)
        grad_arrived = lax.all_to_all(grad_rows, "expert", split_axis=0, concat_axis=0, tiled=True)
        gate_half = gate_up[..., :FF]
        up_half = gate_up[..., FF:]
        sigmoid_vals = jax.nn.sigmoid(gate_half)
        silu_vals = gate_half * sigmoid_vals
        hidden_act = (silu_vals * up_half).astype(jnp.bfloat16)
        act_grad = jnp.einsum(
            "secd,fed->secf", grad_arrived, expert_w[1], preferred_element_type=jnp.float32
        )
        gate_part = act_grad * up_half * sigmoid_vals * (1.0 + gate_half * (1.0 - sigmoid_vals))
        gate_up_grad = jnp.concatenate([gate_part, act_grad * silu_vals], axis=-1).astype(
            jnp.bfloat16
        )
        input_grad = jnp.einsum(
            "secf,def->secd", gate_up_grad, expert_w[0], preferred_element_type=jnp.float32
        ).astype(jnp.bfloat16)
        returned_grad = lax.all_to_all(
            input_grad, "expert", split_axis=0, concat_axis=0, tiled=True
        )
        grad_lists[7][layer_number] = lax.psum_scatter(
            jnp.einsum(
                "secd,secf->def", arrived, gate_up_grad, preferred_element_type=jnp.float32
            ).astype(jnp.bfloat16),
            "dp",
            scatter_dimension=0,
            tiled=True,
        ).astype(jnp.float32)
        grad_lists[8][layer_number] = lax.psum_scatter(
            jnp.einsum(
                "secf,secd->fed", hidden_act, grad_arrived, preferred_element_type=jnp.float32
            ).astype(jnp.bfloat16),
            "dp",
            scatter_dimension=0,
            tiled=True,
        ).astype(jnp.float32)
        slot_back = returned_grad.reshape(expert_count * capacity, model_width)[target].reshape(
            total_rows, TOP, model_width
        )
        normed_two_grad = jnp.sum(slot_back.astype(jnp.float32), axis=1)
        gate_inner = jnp.sum(gate_probs * gate_grad, axis=-1, keepdims=True)
        chosen_grad = gate_probs * (gate_grad - gate_inner)
        route_hot = (
            route[:, :, None] == jnp.arange(expert_count, dtype=jnp.int32)[None, None, :]
        ).astype(jnp.float32)
        logit_grad = jnp.sum(route_hot * chosen_grad[:, :, None], axis=1)
        router_f = dense_w[6].astype(jnp.float32)
        normed_two_grad = normed_two_grad + jnp.einsum(
            "re,de->rd", logit_grad, router_f, precision=top_precision
        )
        router_grad = jnp.einsum(
            "rd,re->de", normed_two.astype(jnp.float32), logit_grad, precision=top_precision
        )
        gain_m = dense_w[5].astype(jnp.float32)
        norm_two_back, gain_m_grad = norm_back(after_attn, gain_m, normed_two_grad)
        mid_grad = grad_resid + norm_two_back
        out_grad = mid_grad.astype(jnp.bfloat16)
        output_grad = jnp.einsum("rq,rd->qd", attn, out_grad, preferred_element_type=jnp.float32)
        attn_grad = (
            jnp.einsum("rd,qd->rq", out_grad, dense_w[4], preferred_element_type=jnp.float32)
            .astype(jnp.bfloat16)
            .reshape(total_rows, QUERY_HEADS, HEAD_DIM)
        )
        query_grads = []
        key_grads = []
        value_grads = []
        for group_of_heads in range(KEY_VALUE_HEADS):
            scores, grouped_q = score_block(query_rows, all_keys, group_of_heads)
            grouped_do = attn_grad[
                :, group_of_heads * heads_per_group : (group_of_heads + 1) * heads_per_group, :
            ]
            probs = jnp.exp(scores - log_totals[group_of_heads])
            prob_bf = probs.astype(jnp.bfloat16)
            prob_grad = jnp.einsum(
                "rgd,kd->grk",
                grouped_do,
                all_values[:, group_of_heads, :],
                preferred_element_type=jnp.float32,
            )
            row_dot = jnp.sum(probs * prob_grad, axis=-1, keepdims=True)
            score_grad = (probs * (prob_grad - row_dot)).astype(jnp.bfloat16)
            query_grads.append(
                jnp.einsum(
                    "grk,kd->rgd",
                    score_grad,
                    all_keys[:, group_of_heads, :],
                    preferred_element_type=jnp.float32,
                )
                * score_scale
            )
            key_grads.append(
                jnp.einsum("grk,rgd->kd", score_grad, grouped_q, preferred_element_type=jnp.float32)
                * score_scale
            )
            value_grads.append(
                jnp.einsum("grk,rgd->kd", prob_bf, grouped_do, preferred_element_type=jnp.float32)
            )
        key_sum, value_total_sum = (
            lax.psum_scatter(
                jnp.stack(key_grads, axis=1).astype(jnp.bfloat16),
                "expert",
                scatter_dimension=0,
                tiled=True,
            ).astype(jnp.float32),
            lax.psum_scatter(
                jnp.stack(value_grads, axis=1).astype(jnp.bfloat16),
                "expert",
                scatter_dimension=0,
                tiled=True,
            ).astype(jnp.float32),
        )
        query_grad = (
            rotate(jnp.concatenate(query_grads, axis=1), cos_table, sin_table, -1.0)
            .astype(jnp.bfloat16)
            .reshape(total_rows, QUERY_HEADS * HEAD_DIM)
        )
        key_grad = (
            rotate(key_sum, cos_table, sin_table, -1.0)
            .astype(jnp.bfloat16)
            .reshape(total_rows, KEY_VALUE_HEADS * HEAD_DIM)
        )
        value_rows_gradient = value_total_sum.astype(jnp.bfloat16).reshape(
            total_rows, KEY_VALUE_HEADS * HEAD_DIM
        )
        normed_grad = jnp.einsum(
            "rq,dq->rd", query_grad, dense_w[1], preferred_element_type=jnp.float32
        )
        normed_grad = normed_grad + jnp.einsum(
            "rq,dq->rd", key_grad, dense_w[2], preferred_element_type=jnp.float32
        )
        normed_grad = normed_grad + jnp.einsum(
            "rq,dq->rd", value_rows_gradient, dense_w[3], preferred_element_type=jnp.float32
        )
        query_w_grad = jnp.einsum(
            "rd,rq->dq", norm_result, query_grad, preferred_element_type=jnp.float32
        )
        key_w_grad = jnp.einsum(
            "rd,rq->dq", norm_result, key_grad, preferred_element_type=jnp.float32
        )
        value_w_grad = jnp.einsum(
            "rd,rq->dq", norm_result, value_rows_gradient, preferred_element_type=jnp.float32
        )
        gain_a = dense_w[0].astype(jnp.float32)
        norm_one_back, gain_a_grad = norm_back(resid_in, gain_a, normed_grad)
        grad_resid = mid_grad + norm_one_back
        shares = (
            lax.psum_scatter(gain_a_grad, ("dp", "expert"), scatter_dimension=0, tiled=True),
            lax.psum_scatter(query_w_grad, ("dp", "expert"), scatter_dimension=0, tiled=True),
            lax.psum_scatter(key_w_grad, ("dp", "expert"), scatter_dimension=0, tiled=True),
            lax.psum_scatter(value_w_grad, ("dp", "expert"), scatter_dimension=0, tiled=True),
            lax.psum_scatter(output_grad, ("dp", "expert"), scatter_dimension=0, tiled=True),
            lax.psum_scatter(gain_m_grad, ("dp", "expert"), scatter_dimension=0, tiled=True),
            lax.psum_scatter(router_grad, ("dp", "expert"), scatter_dimension=0, tiled=True),
        )
        for member in range(7):
            grad_lists[member][layer_number] = shares[member]
    stacked = [jnp.stack(grad_lists[member], axis=0) for member in range(9)]
    return (
        block_out,
        grad_resid,
        stacked[0],
        stacked[1],
        stacked[2],
        stacked[3],
        stacked[4],
        stacked[5],
        stacked[6],
        stacked[7],
        stacked[8],
    )


def product(left, right):
    return lax.dot_general(
        left, right, (((1,), (0,)), ((), ())), preferred_element_type=jnp.float32
    )


def product_rows(left, right):
    return lax.dot_general(
        left, right, (((1,), (1,)), ((), ())), preferred_element_type=jnp.float32
    )


def product_columns(left, right):
    return lax.dot_general(
        left, right, (((0,), (0,)), ((), ())), preferred_element_type=jnp.float32
    )


def split_three(values):
    high = values.astype(jnp.bfloat16)
    rest = values - high.astype(jnp.float32)
    middle = rest.astype(jnp.bfloat16)
    low = (rest - middle.astype(jnp.float32)).astype(jnp.bfloat16)
    return high, middle, low


def masked_gates(rows, router, mask):
    chosen = mask.astype(jnp.float32) > 0.5
    logits = jnp.where(chosen, product(rows, router), masked_score)
    expo_vals = jnp.where(chosen, jnp.exp(logits - jnp.max(logits, axis=1, keepdims=True)), 0.0)
    return expo_vals / jnp.sum(expo_vals, axis=1, keepdims=True)


def layer_kernel(
    x_ref,
    cot_ref,
    routes_ref,
    rope_ref,
    key_ref,
    value_ref,
    router_ref,
    gain_a_ref,
    gain_m_ref,
    shard_b,
    shard_c,
    w_in_ref,
    w_out_ref,
    block_out_ref,
    dx_ref,
    grad_in_ref,
    grad_out_ref,
    grad_dense_ref,
    grad_kv_ref,
    grad_aux_ref,
    spill_b,
    spill_c,
    n2_all,
    cot_all,
    full_a,
    arena,
    gate_buf,
    w_in_half,
    w_out_half,
    hidden_all,
    g_all,
    gin_early,
    kv_all,
    k_t,
    v_t,
    q_rows,
    do_rows,
    attn_buf,
    after_buf,
    lse_buf,
    turn_send,
    turn_recv,
    og_all,
    qg_all,
    kvg_all,
    dkv_recv,
    aux_send,
    gain_buf,
    z_sems,
    p_sems,
    s_sems,
    kv_sems,
    tok_sems,
    tz_sems,
    turn_sems,
    win_sems,
    wout_sems,
    sib_sems,
    ret_sems,
    gate_sems,
    gin_sems,
    gout_sems,
    og_sems,
    qg_sems,
    kvg_sems,
    dkv_sems,
    dense_sems,
    aux_sems,
    local_sems,
    credit_sem,
):
    plane = lax.axis_index("dp")
    member = lax.axis_index("expert")
    core = lax.rem(member, 2)
    parity = lax.rem(plane, 2)
    tokens, width = x_ref.shape
    rows = shard_b.shape[0]
    xor = lax.bitwise_xor
    f32, bf16 = jnp.float32, jnp.bfloat16
    half = FF // 2
    score_scale = HEAD_DIM ** (-0.5)
    kv_width = KEY_VALUE_HEADS * HEAD_DIM

    def at_rows(start, count, step=16):
        return pl.ds(pl.multiple_of(start, step), count)

    def remote(source, target, sems, index, device, recv_index=None):
        return pltpu.make_async_remote_copy(
            src_ref=source,
            dst_ref=target,
            send_sem=sems.at[(0,) + index],
            recv_sem=sems.at[(1,) + (index if recv_index is None else recv_index)],
            device_id=device,
            device_id_type=MESH,
        )

    in_plane = lambda step: (plane, xor(member, step))
    sibling = in_plane(1)

    barrier = pltpu.get_barrier_semaphore()
    greeted = [(xor(plane, s), member) for s in (1, 2, 3)]
    greeted += [in_plane(s) for s in range(1, 8)]
    greeted += [(xor(plane, 1), xor(member, s)) for s in (2, 4, 6)]
    for device in greeted:
        pl.semaphore_signal(barrier, inc=1, device_id=device, device_id_type=MESH)

    def dense_block(part, step, chip_step):
        start = (xor(plane, step) * 8 + xor(member, chip_step)) * rows
        if part == 0:
            return full_a.at[at_rows(start, rows)]
        return arena.at[at_rows(start + (part - 1) * width, rows)]

    def z_copy(part, step):
        block = dense_block(part, 0, 0)
        return remote(block, block, z_sems, (part, step), (xor(plane, step), member))

    def plane_copy(part, step, chip):
        if chip < 3:
            block = dense_block(part, step, 0)
            return remote(block, block, p_sems, (part, step, chip), in_plane(2 * chip))
        via = 1 + step % 2
        block = dense_block(part, step, 2 * via)
        return remote(block, block, p_sems, (part, step, 3), in_plane(2 * (3 - via)))

    def sibling_copy(part, step, chip):
        block = dense_block(part, step, 2 * chip)
        return remote(block, block, s_sems, (part, step, chip), sibling)

    own_rows = (plane * 8 + member) * rows
    full_a[at_rows(own_rows, rows), pl.ds(0, kv_width)] = key_ref[...]
    full_a[at_rows(own_rows, rows), pl.ds(kv_width, kv_width)] = value_ref[...]
    line = lax.broadcasted_iota(jnp.int32, (128, rows), 0)
    gains = jnp.where(line == EXPERT_LANES, gain_a_ref[...].astype(f32), 0.0) + jnp.where(
        line == EXPERT_LANES + 1, gain_m_ref[...].astype(f32), 0.0
    )
    lines = jnp.concatenate(
        [router_ref[...].astype(f32), gains[EXPERT_LANES:]], axis=0
    ).astype(bf16)
    square = (
        lax.broadcasted_iota(jnp.int32, (rows, rows), 0)
        == lax.broadcasted_iota(jnp.int32, (rows, rows), 1)
    ).astype(bf16)
    full_a[at_rows(own_rows, rows), pl.ds(2 * kv_width, 128)] = product_rows(
        square, lines
    ).astype(bf16)
    arena[at_rows(own_rows, rows)] = shard_b[...]
    arena[at_rows(own_rows + width, rows)] = shard_c[...]

    def token_rows(plane_step, member_step):
        start = (xor(parity, plane_step) * 8 + xor(member, member_step)) * tokens
        return at_rows(start, tokens, 128)

    cot_all[token_rows(0, 0), pl.ds(0, width)] = cot_ref[...]
    expert_line = lax.broadcasted_iota(jnp.int32, (128, tokens), 0)
    named = jnp.zeros((128, tokens), f32)
    for slot in range(TOP):
        named = jnp.where(expert_line == routes_ref[pl.ds(slot, 1), :], 1.0, named)
    cot_all[token_rows(0, 0), pl.ds(width, 128)] = jnp.transpose(named).astype(bf16)
    pl.semaphore_wait(barrier, len(greeted))

    for part in range(3):
        for step in (3, 2, 1):
            z_copy(part, step).start()
    for part in range(3):
        for chip in (1, 2):
            plane_copy(part, 0, chip).start()
        sibling_copy(part, 0, 0).start()

    def pass_on_plane(part):
        for step in (1, 2, 3):
            z_copy(part, step).wait_recv()
            for chip in (1, 2):
                plane_copy(part, step, chip).start()
            sibling_copy(part, step, 0).start()

    def pass_on_diagonal(part, steps):
        for step in steps:
            for chip in (1, 2):
                plane_copy(part, step, chip).wait_recv()
                if chip == 1 + step % 2:
                    plane_copy(part, step, 3).start()
                sibling_copy(part, step, chip).start()

    def pass_on_sibling(part):
        for step in range(4):
            plane_copy(part, step, 3).wait_recv()
            sibling_copy(part, step, 3).start()

    def arrived_dense(part):
        for step in range(4):
            for chip in range(4):
                sibling_copy(part, step, chip).wait_recv()

    def sent_dense(part):
        for step in range(4):
            if step:
                z_copy(part, step).wait_send()
            for chip in range(4):
                if chip:
                    plane_copy(part, step, chip).wait_send()
                sibling_copy(part, step, chip).wait_send()

    token_arrays = (cot_all, n2_all)

    parts = (0, 512, 1024)

    def cube_device(bits):
        return (xor(plane, bits & 1), xor(member, bits & 6))

    def part_order(part):
        return [1 << ((part + k) % 3) for k in range(3)]

    def token_z(kind):
        block = token_arrays[kind].at[token_rows(0, 0)]
        return remote(block, block, tz_sems, (kind,), (xor(plane, 1), member))

    def token_where(kind, plane_step):
        base = xor(parity, plane_step) * 8 * tokens
        return token_arrays[kind], tok_sems, (kind, plane_step), 0, None, base

    quarter = w_in_ref.shape[0]
    quarter_out = w_out_ref.shape[0]

    def win_copy(step, piece):
        other = xor(parity, step % 2)
        source = w_in_ref.at[:, at_rows(piece * FF + other * half, half, 128)]
        target = w_in_half.at[at_rows(plane * quarter, quarter), pl.ds(piece * half, half)]
        if step == 0:
            return pltpu.make_async_copy(source, target, local_sems.at[piece])
        return remote(source, target, win_sems, (step, piece), (xor(plane, step), member))

    out_half = lax.div(plane, 2)

    def wout_send(turn):
        target = w_out_half.at[at_rows(parity * quarter_out, quarter_out)]
        device = (out_half + 2 * turn, member)
        return remote(w_out_ref, target, wout_sems, (turn,), device, (parity,))

    def wout_arrived(slot):
        target = w_out_half.at[at_rows(slot * quarter_out, quarter_out)]
        return remote(w_out_ref, target, wout_sems, (slot,), (xor(plane, 1), member))

    def wout_local():
        return pltpu.make_async_copy(
            w_out_ref,
            w_out_half.at[at_rows(parity * quarter_out, quarter_out)],
            local_sems.at[2],
        )

    def expert_start():
        for step in (1, 3, 2):
            for piece in (0, 1):
                win_copy(step, piece).start()
        for piece in (0, 1):
            win_copy(0, piece).start()
        for turn in (0, 1):

            @pl.when(out_half + 2 * turn != plane)
            def _():
                wout_send(turn).start()

        @pl.when(out_half == parity)
        def _():
            wout_local().start()

    def expert_finish():
        for step in (1, 3, 2):
            for piece in (0, 1):
                win_copy(step, piece).wait()
        for piece in (0, 1):
            win_copy(0, piece).wait()
        for slot in (0, 1):

            @pl.when(parity * 2 + slot != plane)
            def _():
                wout_arrived(slot).wait_recv()

        for turn in (0, 1):

            @pl.when(out_half + 2 * turn != plane)
            def _():
                wout_send(turn).wait_send()

        @pl.when(out_half == parity)
        def _():
            wout_local().wait()

    def gather_copy(array, sems, index, lead=(), start=0, stop=None, base=0):
        stop = array.shape[1] if stop is None else stop
        middle = (start + stop) // 256 * 128
        owner_step, device_step = ((0, 2), (0, 4), (2, 4), (4, 2), (0, 1), (2, 1), (4, 1), (6, 1))[
            index
        ]
        if index == 2:
            stop = middle
        if index == 3:
            start = middle
        block = at_rows(base + xor(member, owner_step) * tokens, tokens, 128)
        piece = array.at[block, pl.ds(start, stop - start)]
        return remote(piece, piece, sems, lead + (index,), in_plane(device_step))

    def gather_start(*where):
        for index in (0, 1, 4):
            gather_copy(where[0], where[1], index, *where[2:]).start()

    def gather_pass(*where):
        for index in (0, 1):
            gather_copy(where[0], where[1], index, *where[2:]).wait_recv()
            gather_copy(where[0], where[1], 2 + index, *where[2:]).start()
            gather_copy(where[0], where[1], 5 + index, *where[2:]).start()

    def gather_pass_last(*where):
        for index in (2, 3):
            gather_copy(where[0], where[1], index, *where[2:]).wait_recv()
        gather_copy(where[0], where[1], 7, *where[2:]).start()

    def gather_sent(*where):
        for index in range(8):
            gather_copy(where[0], where[1], index, *where[2:]).wait_send()

    def gather_finish(*where):
        gather_sent(*where)
        for index in range(4, 8):
            gather_copy(where[0], where[1], index, *where[2:]).wait_recv()

    pass_on_plane(0)
    pass_on_plane(1)
    pass_on_diagonal(0, range(4))
    pass_on_sibling(0)
    arrived_dense(0)
    token_z(0).start()
    expert_start()
    aux = full_a[:, pl.ds(2 * kv_width, 128)]
    pick = (
        lax.broadcasted_iota(jnp.int32, (16, 128), 1)
        == lax.broadcasted_iota(jnp.int32, (16, 128), 0) + EXPERT_LANES
    ).astype(bf16)
    gain_buf[...] = product_rows(pick, aux)
    gain_a = gain_buf[pl.ds(0, 1), :]
    gain_m = gain_buf[pl.ds(1, 1), :]
    residual = x_ref[...].astype(f32)
    normed = (residual * norm_factor(residual) * gain_a).astype(bf16)
    cos_part = rope_ref[:, pl.ds(0, HEAD_DIM)]
    sin_part = rope_ref[:, pl.ds(HEAD_DIM, HEAD_DIM)]

    def turned(values, orient):
        swapped = pltpu.roll(values, HEAD_DIM // 2, 1)
        return values * cos_part + swapped * (sin_part * orient)

    kv_rows = product(normed, full_a[:, pl.ds(0, 2 * kv_width)])
    own_block = at_rows(member * tokens, tokens, 128)
    for part in range(2 * KEY_VALUE_HEADS):
        piece = kv_rows[:, part * HEAD_DIM : (part + 1) * HEAD_DIM]
        if part < KEY_VALUE_HEADS:
            piece = turned(piece, 1.0)
        kv_all[own_block, pl.ds(part * HEAD_DIM, HEAD_DIM)] = piece.astype(bf16)
    gather_start(kv_all, kv_sems)
    turn_send[0] = jnp.transpose(normed).reshape(turn_send.shape[1:])

    def turn_copy(kind, step):
        return remote(
            turn_send.at[kind % 3, :, xor(member, step)],
            turn_recv.at[kind, :, :, at_rows(member * tokens, tokens, 128)],
            turn_sems,
            (kind, step),
            in_plane(step),
        )

    def turn_start(kind):
        for step in range(1, 8):
            turn_copy(kind, step).start()
        turn_recv[kind, :, :, at_rows(member * tokens, tokens, 128)] = turn_send[
            kind % 3, :, pl.ds(member, 1)
        ].reshape(turn_recv.shape[1], rows, tokens)

    turn_start(0)
    pass_on_plane(2)
    gather_pass(kv_all, kv_sems)
    pass_on_diagonal(1, range(4))
    gather_start(*token_where(0, 0))
    gather_pass_last(kv_all, kv_sems)
    pass_on_sibling(1)
    token_z(0).wait_recv()
    gather_start(*token_where(0, 1))
    arrived_dense(1)
    spill_b_copy = pltpu.make_async_copy(
        arena.at[pl.ds(0, width)], spill_b, local_sems.at[3]
    )
    spill_b_copy.start()
    for head in range(QUERY_HEADS):
        if head % 2 == 0:
            pair = product(normed, arena[pl.ds(0, width), pl.ds(head * HEAD_DIM, 2 * HEAD_DIM)])
        piece = pair[:, (head % 2) * HEAD_DIM : (head % 2 + 1) * HEAD_DIM]
        q_rows[pl.ds(head * tokens, tokens)] = turned(piece, 1.0).astype(bf16)
    gather_finish(kv_all, kv_sems)
    for group in range(KEY_VALUE_HEADS):
        k_t[group] = jnp.transpose(kv_all[:, pl.ds(group * HEAD_DIM, HEAD_DIM)])
        v_t[group] = jnp.transpose(kv_all[:, pl.ds(kv_width + group * HEAD_DIM, HEAD_DIM)])
    pass_on_diagonal(2, range(4))

    seq_len = kv_all.shape[0]
    pairs = QUERY_HEADS // 2
    pairs_per_group = pairs // KEY_VALUE_HEADS
    key_index = lax.broadcasted_iota(jnp.int32, (seq_len, 2 * tokens), 0)
    query_index = member * tokens + lax.rem(
        lax.broadcasted_iota(jnp.int32, (seq_len, 2 * tokens), 1), tokens
    )
    allowed = key_index <= query_index

    def pair_scores(pair, group):
        queries = q_rows[at_rows(pair * 2 * tokens, 2 * tokens, 128)]
        keys = kv_all[:, at_rows(group * HEAD_DIM, HEAD_DIM, 128)]
        scores = product_rows(keys, queries) * score_scale
        return jnp.where(allowed, scores, masked_score), queries

    def attend(pair, carry):
        group = lax.div(pair, pairs_per_group)
        scores, _ = pair_scores(pair, group)
        peak = jnp.max(scores, axis=0, keepdims=True)
        expo_vals = jnp.exp(scores - peak)
        sums = jnp.sum(expo_vals, axis=0, keepdims=True)
        probs = (expo_vals / sums).astype(bf16)
        lse_buf[pair] = jnp.broadcast_to(peak + jnp.log(sums), (8, 2 * tokens))
        part = product(v_t[group], probs)
        for inner in (0, 1):
            piece = part[:, inner * tokens : (inner + 1) * tokens].astype(bf16)
            attn_buf[2 * pair + inner] = piece
        return carry

    lax.fori_loop(0, pairs, attend, 0)
    pass_on_sibling(2)
    gather_pass(*token_where(0, 0))
    attn_t = attn_buf[...].reshape(width, tokens)
    turn_send[1] = attn_t.reshape(turn_send.shape[1:])
    attn = jnp.transpose(attn_t)
    arrived_dense(2)
    spill_c_copy = pltpu.make_async_copy(
        arena.at[pl.ds(width, width)], spill_c, local_sems.at[4]
    )
    spill_c_copy.start()
    for start in range(0, width, 512):
        after_buf[:, pl.ds(start, 512)] = x_ref[:, pl.ds(start, 512)].astype(f32) + product(
            attn, arena[pl.ds(width, width), pl.ds(start, 512)]
        )
    after = after_buf[...]
    normed_two = (after * norm_factor(after) * gain_m).astype(bf16)
    n2_all[token_rows(0, 0)] = normed_two
    spill_b_copy.wait()
    spill_c_copy.wait()
    for part in range(3):
        sent_dense(part)
    token_z(1).start()
    gather_start(*token_where(1, 0))
    turn_send[2] = jnp.transpose(normed_two).reshape(turn_send.shape[1:])
    gather_pass(*token_where(0, 1))
    gather_pass_last(*token_where(0, 0))
    gather_pass_last(*token_where(0, 1))
    token_z(1).wait_recv()
    gather_start(*token_where(1, 1))
    for plane_step in (0, 1):
        gather_finish(*token_where(0, plane_step))
    expert_finish()

    own_lane = lax.broadcasted_iota(jnp.int32, (2 * tokens, 128), 1) == member
    low_lane = lax.broadcasted_iota(jnp.int32, (2 * tokens, 128), 1) == member + 64
    def arena_slot(base, kind, slot):
        first, each = {"stage": (0, 2), "sib": (4, 2), "sum": (8, 8), "recv": (24, 7)}[base]
        return at_rows((first + kind * each + slot) * tokens, tokens, 128)

    def sib_copy(kind, slot):
        return remote(
            arena.at[arena_slot("stage", kind, slot)],
            arena.at[arena_slot("sib", kind, slot)],
            sib_sems,
            (kind, slot),
            sibling,
        )

    def sib_gate_copy():
        return remote(
            gate_buf.at[pl.ds(8, 8)], gate_buf.at[pl.ds(16, 8)], sib_sems, (2, 0), sibling
        )

    def bit_of(held, bit):
        if isinstance(held, int):
            return held // bit % 2
        return jnp.where(held & bit > 0, 1, 0)

    def ret_copy(kind, part, held, stage):
        first, second, third = part_order(part)
        slot = (
            bit_of(held, second) + 2 * bit_of(held, third),
            4 + bit_of(held, third),
            6,
        )[stage]
        columns = pl.ds(parts[part], 512)
        return remote(
            arena.at[arena_slot("sum", kind, held), columns],
            arena.at[arena_slot("recv", kind, slot), columns],
            ret_sems,
            (kind, part, slot),
            cube_device((first, second, third)[stage]),
        )

    def ret_arrived(kind, part, slot):
        columns = pl.ds(parts[part], 512)
        block = arena.at[arena_slot("recv", kind, slot), columns]
        return remote(block, block, ret_sems, (kind, part, slot), sibling)

    def ret_sum(kind, part, held, slots):
        columns = pl.ds(parts[part], 512)
        total = arena[arena_slot("sum", kind, held), columns].astype(f32)
        for slot in slots:
            total = total + arena[arena_slot("recv", kind, slot), columns].astype(f32)
        return total

    def ret_second(kind):
        for part in range(3):
            first, second, third = part_order(part)
            for held, slot in ((second, 1), (second | third, 3)):
                ret_arrived(kind, part, slot).wait_recv()
                arena[arena_slot("sum", kind, held), pl.ds(parts[part], 512)] = ret_sum(
                    kind, part, held, (slot,)
                ).astype(bf16)
                ret_copy(kind, part, held, 1).start()

    def ret_third(kind):
        for part in range(3):
            third = part_order(part)[2]
            for slot in (2, 5):
                ret_arrived(kind, part, slot).wait_recv()
            arena[arena_slot("sum", kind, third), pl.ds(parts[part], 512)] = ret_sum(
                kind, part, third, (2, 5)
            ).astype(bf16)
            ret_copy(kind, part, third, 2).start()

    def ret_total(kind):
        for part in range(3):
            for slot in (0, 4, 6):
                ret_arrived(kind, part, slot).wait_recv()
        return jnp.concatenate([ret_sum(kind, part, 0, (0, 4, 6)) for part in range(3)], axis=1)

    def ret_sent(kind):
        for part in range(3):
            first, second, third = part_order(part)
            for held in range(8):
                if held & first:
                    ret_copy(kind, part, held, 0).wait_send()
            for held in (second, second | third):
                ret_copy(kind, part, held, 1).wait_send()
            ret_copy(kind, part, third, 2).wait_send()

    def ret_gate_copy(held):
        return remote(
            gate_buf.at[held], gate_buf.at[24 + held], gate_sems, (held,), cube_device(held)
        )

    def halves(values, first):
        return jnp.where(first, values[:tokens], values[tokens:])

    def block_rows(held):
        other_plane = xor(parity, held & 1)
        chip = xor(lax.div(member, 2), lax.div(held, 2))
        return at_rows((other_plane * 4 + chip) * 2 * tokens, 2 * tokens, 128)

    def first_step(held, carry):
        @pl.when(held == 1)
        def _():
            gather_pass(*token_where(1, 0))

        @pl.when(held == 2)
        def _():
            gather_pass(*token_where(1, 1))

        @pl.when(held == 4)
        def _():
            gather_pass_last(*token_where(1, 0))
            gather_pass_last(*token_where(1, 1))

        own = token_rows(held & 1, held & 6)
        remote(
            n2_all.at[own],
            n2_all.at[own],
            tok_sems,
            (1, held & 1, 4 + lax.div(held, 2)),
            sibling,
        ).wait_recv()
        here = block_rows(held)
        token_block = n2_all[here, :]
        gate_up = product(token_block, w_in_half[...])
        gates = masked_gates(
            token_block,
            full_a[:, pl.ds(2 * kv_width, 128)],
            cot_all[here, pl.ds(width, 128)],
        )
        gate = jnp.sum(jnp.where(own_lane, gates, 0.0), axis=1, keepdims=True)
        gate_half = gate_up[:, :half]
        up_half = gate_up[:, half:]
        sigmoid_vals = 1.0 / (1.0 + jnp.exp(-gate_half))
        silu_vals = gate_half * sigmoid_vals
        hidden = silu_vals * up_half
        hidden_all[here, :] = (gate * hidden).astype(bf16)
        back = product_rows(cot_all[here, pl.ds(0, width)], w_out_half[...])
        gate_grad = jnp.sum(hidden * back, axis=1, keepdims=True)
        act_grad = gate * back
        gate_part = act_grad * up_half * sigmoid_vals * (1.0 + gate_half * (1.0 - sigmoid_vals))
        g_all[here, pl.ds(0, half)] = gate_part.astype(bf16)
        g_all[here, pl.ds(half, half)] = (act_grad * silu_vals).astype(bf16)
        gate_high = gate_grad.astype(bf16).astype(f32)
        gate_lanes = jnp.where(own_lane, gate_high, 0.0) + jnp.where(
            low_lane, gate_grad - gate_high, 0.0
        )
        gate_buf[held] = halves(gate_lanes, core == 0).astype(bf16)
        gate_buf[8 + held] = halves(gate_lanes, core == 1).astype(bf16)
        return carry

    lax.fori_loop(0, 8, first_step, 0)
    token_z(0).wait_send()
    token_z(1).wait_send()
    for plane_step in (0, 1):
        gather_sent(*token_where(1, plane_step))
    sib_gate_copy().start()

    def turn_held(turn):
        return jnp.where(turn == 3, 3, jnp.where(turn == 4, 4, 7 - turn))

    def second_step(kind, turn, carry):
        @pl.when(turn < 8)
        def _():
            slot2 = lax.rem(turn, 2)
            held = turn_held(turn)
            here = block_rows(held)

            @pl.when(turn >= 2)
            def _():
                sib_copy(kind, slot2).wait_send()
                pl.semaphore_wait(credit_sem, 1)

            place = arena_slot("sum", kind, held)
            for start in range(0, width, 512):
                columns = pl.ds(start, 512)
                if kind == 0:
                    result = product_rows(g_all[here, :], w_in_half[columns, :])
                else:
                    result = product(hidden_all[here, :], w_out_half[:, columns])
                arena[arena_slot("stage", kind, slot2), columns] = halves(
                    result, core == 1
                ).astype(bf16)
                arena[place, columns] = halves(result, core == 0).astype(bf16)
            sib_copy(kind, slot2).start()

        @pl.when(turn > 0)
        def _():
            last = turn - 1
            slot2 = lax.rem(last, 2)
            held = turn_held(last)
            place = arena_slot("sum", kind, held)
            sib_copy(kind, slot2).wait_recv()
            arena[place] = (
                arena[place].astype(f32) + arena[arena_slot("sib", kind, slot2)].astype(f32)
            ).astype(bf16)

            @pl.when(last < 6)
            def _():
                pl.semaphore_signal(credit_sem, inc=1, device_id=sibling, device_id_type=MESH)

            for part in range(3):

                @pl.when(held & (1 << part) > 0)
                def _():
                    ret_copy(kind, part, held, 0).start()

        return carry

    def gin_copy(step):
        if step >= 2:
            source = gin_early.at[step - 2]
        else:
            source = w_in_half.at[at_rows(xor(plane, step) * quarter, quarter)]
        if step == 0:
            return pltpu.make_async_copy(source, grad_in_ref.at[0], local_sems.at[5])
        return remote(
            source, grad_in_ref.at[step], gin_sems, (step,), (xor(plane, step), member)
        )

    def gin_quarter(step):
        start = xor(plane, step) * quarter
        for piece in range(0, quarter, 128):
            columns = n2_all[:, at_rows(start + piece, 128, 128)]
            result = product_columns(columns, g_all[...]).astype(bf16)
            if step >= 2:
                gin_early[step - 2, pl.ds(piece, 128)] = result
            else:
                w_in_half[at_rows(start + piece, 128, 128)] = result

    def second_loop(kind):
        lax.fori_loop(0, 9, functools.partial(second_step, kind), 0)
        for slot in (0, 1):
            sib_copy(kind, slot).wait_send()

    for kind in (1, 2):
        turn_start(kind)
    gin_quarter(2)
    gin_copy(2).start()
    second_loop(0)
    sib_gate_copy().wait()
    gate_buf[pl.ds(0, 8)] = (
        gate_buf[pl.ds(0, 8)].astype(f32) + gate_buf[pl.ds(16, 8)].astype(f32)
    ).astype(bf16)
    for held in range(1, 8):
        ret_gate_copy(held).start()
    ret_second(0)

    gin_quarter(3)
    gin_copy(3).start()
    for step in (1, 0):
        gin_quarter(step)
    gin_copy(0).start()

    def gout_copy(slot):
        source = w_out_half.at[pl.ds(slot * quarter_out, quarter_out)]
        target = grad_out_ref.at[out_half]
        device = (parity * 2 + slot, member)
        return remote(source, target, gout_sems, (slot,), device, (out_half,))

    def gout_local(slot):
        return pltpu.make_async_copy(
            w_out_half.at[pl.ds(slot * quarter_out, quarter_out)],
            grad_out_ref.at[out_half],
            local_sems.at[6],
        )

    def gout_arrived(turn):
        source = w_out_half.at[pl.ds(0, quarter_out)]
        return remote(source, grad_out_ref.at[turn], gout_sems, (turn,), (xor(plane, 1), member))

    own_n2 = n2_all[token_rows(0, 0), :]
    own_mask = cot_all[token_rows(0, 0), pl.ds(width, 128)]
    own_gates = masked_gates(own_n2, full_a[:, pl.ds(2 * kv_width, 128)], own_mask)
    ret_third(0)
    second_loop(1)
    for start in range(0, half, 128):
        w_out_half[pl.ds(start, 128)] = product_columns(
            hidden_all[:, pl.ds(start, 128)], cot_all[:, pl.ds(0, width)]
        ).astype(bf16)

    load_b = pltpu.make_async_copy(
        spill_b, cot_all.at[pl.ds(0, width), pl.ds(0, width)], local_sems.at[3]
    )
    load_c = pltpu.make_async_copy(spill_c, n2_all.at[pl.ds(0, width)], local_sems.at[4])
    load_b.start()
    load_c.start()

    total_in = ret_total(0)
    total_gate = gate_buf[0].astype(f32)
    for held in range(1, 8):
        ret_gate_copy(held).wait_recv()
        total_gate = total_gate + gate_buf[24 + held].astype(f32)
    gin_copy(1).start()
    for slot in (0, 1):

        @pl.when(parity * 2 + slot != plane)
        def _():
            gout_copy(slot).start()

        @pl.when(parity * 2 + slot == plane)
        def _():
            gout_local(slot).start()

    gate_grad = total_gate + pltpu.roll(total_gate, 64, 1)
    gate_inner = jnp.sum(own_gates * gate_grad, axis=1, keepdims=True)
    logit_grad = own_gates * (gate_grad - gate_inner)
    lg_parts = split_three(logit_grad)
    aux_now = full_a[:, pl.ds(2 * kv_width, 128)]
    for part in lg_parts:
        total_in = total_in + product_rows(part, aux_now)
    after = after_buf[...]

    def norm_backward(values, gain, grad):
        factor = norm_factor(values)
        scaled = grad * gain
        gain_row = jnp.sum(grad * values * factor, axis=0, keepdims=True)
        inner = jnp.mean(scaled * values, axis=-1, keepdims=True)
        return factor * scaled - values * factor * factor * factor * inner, gain_row

    two_back, gain_m_row = norm_backward(after, gain_buf[pl.ds(1, 1), :], total_in)
    mid = cot_ref[...].astype(f32) + two_back
    dx_ref[...] = mid
    out_grad = mid.astype(bf16)
    og_all[own_block, pl.ds(0, width)] = out_grad
    og_all[own_block, pl.ds(width, 128)] = (
        lg_parts[0].astype(f32)
        + pltpu.roll(lg_parts[1].astype(f32), 8, 1)
        + pltpu.roll(lg_parts[2].astype(f32), 16, 1)
    ).astype(bf16)

    gather_start(og_all, og_sems)
    load_c.wait()
    for head in range(0, QUERY_HEADS, 2):
        pair = product_rows(out_grad, n2_all[pl.ds(head * HEAD_DIM, 2 * HEAD_DIM), :])
        for inner in (0, 1):
            do_rows[pl.ds((head + inner) * tokens, tokens)] = pair[
                :, inner * HEAD_DIM : (inner + 1) * HEAD_DIM
            ].astype(bf16)
    gather_pass(og_all, og_sems)

    def dkv_rows(kind_core, chip):
        return at_rows((kind_core * 4 + chip) * tokens, tokens, 128)

    def dkv_columns(group):
        return pl.ds(group * 2 * HEAD_DIM, 2 * HEAD_DIM)

    def dkv_sibling(group):
        source = g_all.at[at_rows((1 - core) * 4 * tokens, 4 * tokens, 128), dkv_columns(group)]
        target = dkv_recv.at[group, pl.ds(4 * tokens, 4 * tokens)]
        return remote(source, target, dkv_sems, (group, 0), sibling)

    def dkv_copy(group, step):
        chip = xor(lax.div(member, 2), step)
        return remote(
            g_all.at[dkv_rows(core, chip), dkv_columns(group)],
            dkv_recv.at[group, pl.ds(step * tokens, tokens)],
            dkv_sems,
            (group, step),
            in_plane(2 * step),
        )

    def dkv_pass(group):
        dkv_sibling(group).wait_recv()
        mine = at_rows(core * 4 * tokens, 4 * tokens, 128)
        g_all[mine, dkv_columns(group)] = (
            g_all[mine, dkv_columns(group)].astype(f32)
            + dkv_recv[group, pl.ds(4 * tokens, 4 * tokens)].astype(f32)
        ).astype(bf16)
        for step in (1, 2, 3):
            dkv_copy(group, step).start()

    planes = turn_recv.shape[1]

    def dense_rows(piece, step):
        return at_rows((piece * planes + xor(plane, step)) * rows, rows)

    def kv_grad_copy(step):
        source = arena.at[dense_rows(0, step), pl.ds(0, 2 * kv_width)]
        if step == 0:
            return pltpu.make_async_copy(source, grad_kv_ref.at[0], local_sems.at[0])
        device = (xor(plane, step), member)
        return remote(source, grad_kv_ref.at[step], dense_sems, (0, step), device)

    def pair_rows(piece, which):
        return pl.ds(width + ((piece - 1) * 2 + which) * rows, rows)

    def dense_copy(piece, step):
        columns = pl.ds((piece - 1) * width, width)
        if step == 2:
            target = grad_dense_ref.at[1, :, columns]
            device = (xor(plane, 2), member)
        else:
            target = n2_all.at[pair_rows(piece, step // 2)]
            device = (xor(plane, 1), member)
        return remote(arena.at[dense_rows(piece, step)], target, dense_sems, (piece, step), device)

    def dense_own(piece):
        return pltpu.make_async_copy(
            arena.at[dense_rows(piece, 0)],
            grad_dense_ref.at[0, :, pl.ds((piece - 1) * width, width)],
            local_sems.at[piece],
        )

    def dense_start(piece):
        for step in (3, 1):
            dense_copy(piece, step).start()

    def dense_pass(piece):
        for which, step in ((1, 2), (0, 0)):
            dense_copy(piece, 1 + 2 * which).wait_recv()
            block = dense_rows(piece, step)
            arena[block] = (
                arena[block].astype(f32) + n2_all[pair_rows(piece, which)].astype(f32)
            ).astype(bf16)
            if step:
                dense_copy(piece, 2).start()
            else:
                dense_own(piece).start()

    for group in range(KEY_VALUE_HEADS):
        values = kv_all[:, pl.ds(kv_width + group * HEAD_DIM, HEAD_DIM)]
        dk = jnp.zeros((seq_len, HEAD_DIM), f32)
        dv = jnp.zeros((seq_len, HEAD_DIM), f32)
        for pair in range(group * pairs_per_group, (group + 1) * pairs_per_group):
            scores, queries = pair_scores(pair, group)
            probs = jnp.exp(scores - lse_buf[pair][0:1])
            grads = do_rows[pl.ds(pair * 2 * tokens, 2 * tokens)]
            prob_grad = product_rows(values, grads)
            row_dot = jnp.sum(probs * prob_grad, axis=0, keepdims=True)
            score_grad = (probs * (prob_grad - row_dot)).astype(bf16)
            dk = dk + product(score_grad, queries)
            dv = dv + product(probs.astype(bf16), grads)
            dq = product(k_t[group], score_grad) * score_scale
            for inner in (0, 1):
                piece = jnp.transpose(dq[:, inner * tokens : (inner + 1) * tokens])
                qg_all[own_block, pl.ds((2 * pair + inner) * HEAD_DIM, HEAD_DIM)] = turned(
                    piece, -1.0
                ).astype(bf16)
        start = group * 2 * HEAD_DIM
        dk = (dk * score_scale).astype(bf16)
        dv = dv.astype(bf16)
        for block in range(8):
            place = pl.ds((block % 2 * 4 + block // 2) * tokens, tokens)
            here = slice(block * tokens, (block + 1) * tokens)
            g_all[place, pl.ds(start, HEAD_DIM)] = dk[here]
            g_all[place, pl.ds(start + HEAD_DIM, HEAD_DIM)] = dv[here]
        dkv_sibling(group).start()
        span = width // KEY_VALUE_HEADS
        gather_start(qg_all, qg_sems, (group,), group * span, (group + 1) * span)
        if group == 0:
            gather_pass_last(og_all, og_sems)
            dkv_pass(0)
            ret_second(1)

    dkv_pass(1)
    gather_pass(qg_all, qg_sems, (0,), 0, span)

    for group in range(KEY_VALUE_HEADS):
        start = group * 2 * HEAD_DIM
        mine = dkv_rows(core, lax.div(member, 2))
        dk = g_all[mine, pl.ds(start, HEAD_DIM)].astype(f32)
        dv = g_all[mine, pl.ds(start + HEAD_DIM, HEAD_DIM)].astype(f32)
        for step in (1, 2, 3):
            dkv_copy(group, step).wait_recv()
            block = pl.ds(step * tokens, tokens)
            dk = dk + dkv_recv[group, block, pl.ds(0, HEAD_DIM)].astype(f32)
            dv = dv + dkv_recv[group, block, pl.ds(HEAD_DIM, HEAD_DIM)].astype(f32)
        kvg_all[own_block, pl.ds(group * HEAD_DIM, HEAD_DIM)] = turned(dk, -1.0).astype(bf16)
        kvg_all[own_block, pl.ds(kv_width + group * HEAD_DIM, HEAD_DIM)] = dv.astype(bf16)
    gather_start(kvg_all, kvg_sems)
    ret_third(1)
    gather_finish(og_all, og_sems)
    for kind in range(3):
        for step in range(1, 8):
            turn_copy(kind, step).wait()
    turned_attn = turn_recv[1].reshape(planes * rows, seq_len)
    for start in range(0, width, 512):
        arena[pl.ds(2 * planes * rows, planes * rows), pl.ds(start, 512)] = product(
            turned_attn, og_all[:, pl.ds(start, 512)]
        ).astype(bf16)
    dense_start(2)
    router_part = product(
        turn_recv[2].reshape(planes * rows, seq_len), og_all[:, pl.ds(width, 128)]
    )

    gather_pass(qg_all, qg_sems, (1,), span, 2 * span)
    gather_pass(kvg_all, kvg_sems)
    for group in range(KEY_VALUE_HEADS):
        gather_pass_last(qg_all, qg_sems, (group,), group * span, (group + 1) * span)
    gather_pass_last(kvg_all, kvg_sems)

    load_b.wait()
    own_kvg = kvg_all[own_block, :]
    own_qg = qg_all[own_block, :]
    normed_grad = product_rows(own_kvg, full_a[:, pl.ds(0, 2 * kv_width)]) + product_rows(
        own_qg, cot_all[pl.ds(0, width), pl.ds(0, width)]
    )
    one_back, gain_a_row = norm_backward(
        x_ref[...].astype(f32), gain_buf[pl.ds(0, 1), :], normed_grad
    )
    dx_ref[...] = dx_ref[...] + one_back
    line = lax.broadcasted_iota(jnp.int32, (128, width), 0)
    gain_lines = jnp.zeros((128, width), f32)
    for offset, part in enumerate(split_three(gain_a_row) + split_three(gain_m_row)):
        gain_lines = jnp.where(line == 32 + offset, part.astype(f32), gain_lines)
    turn_send[0] = jnp.transpose(gain_lines.astype(bf16)).reshape(turn_send.shape[1:])
    turn_start(3)

    turned_normed = turn_recv[0].reshape(planes * rows, seq_len)
    for group in range(KEY_VALUE_HEADS):
        gather_finish(qg_all, qg_sems, (group,), group * span, (group + 1) * span)
    for start in range(0, width, 512):
        arena[pl.ds(planes * rows, planes * rows), pl.ds(start, 512)] = product(
            turned_normed, qg_all[:, pl.ds(start, 512)]
        ).astype(bf16)
    dense_start(1)
    dense_pass(2)
    gather_finish(kvg_all, kvg_sems)
    arena[pl.ds(0, planes * rows), pl.ds(0, 2 * kv_width)] = product(
        turned_normed, kvg_all[...]
    ).astype(bf16)
    for step in (2, 3, 1, 0):
        kv_grad_copy(step).start()
    dense_pass(1)
    for step in range(1, 8):
        turn_copy(3, step).wait()
    aux_total = router_part
    for block in range(8):
        aux_total = aux_total + turn_recv[3, :, :, pl.ds(block * tokens, tokens)].reshape(
            planes * rows, tokens
        ).astype(f32)
    aux_send[...] = aux_total.reshape(planes, rows, 128)

    def aux_copy(step):
        return remote(
            aux_send.at[xor(plane, step)],
            grad_aux_ref.at[step],
            aux_sems,
            (step,),
            (xor(plane, step), member),
        )

    for step in (1, 2, 3):
        aux_copy(step).start()
    own_aux = pltpu.make_async_copy(aux_send.at[plane], grad_aux_ref.at[0], local_sems.at[7])
    own_aux.start()

    block_out_ref[...] = (after_buf[...] + ret_total(1)).astype(bf16)

    for held in range(1, 8):
        ret_gate_copy(held).wait_send()
    for kind in (0, 1):
        ret_sent(kind)
    for group in range(KEY_VALUE_HEADS):
        dkv_sibling(group).wait_send()
        for step in (1, 2, 3):
            dkv_copy(group, step).wait_send()
    gin_copy(0).wait()
    for step in (1, 2, 3):
        gin_copy(step).wait()
    for slot in (0, 1):

        @pl.when(parity * 2 + slot != plane)
        def _():
            gout_copy(slot).wait_send()

        @pl.when(parity * 2 + slot == plane)
        def _():
            gout_local(slot).wait()

    for turn in (0, 1):

        @pl.when(out_half + 2 * turn != plane)
        def _():
            gout_arrived(turn).wait_recv()

    for step in range(4):
        kv_grad_copy(step).wait()
    for piece in (1, 2):
        dense_own(piece).wait()
        dense_copy(piece, 2).wait()
        for step in (1, 3):
            dense_copy(piece, step).wait_send()
    for step in (1, 2, 3):
        aux_copy(step).wait()
    own_aux.wait()


EXPERT_LANES = 8


def final_kernel(
    block_ref,
    dx_ref,
    in_ref,
    out_ref,
    dense_ref,
    kv_ref,
    aux_ref,
    block_out,
    tokens_grad,
    gain_a_out,
    query_out,
    key_out,
    value_out,
    output_out,
    gain_m_out,
    router_out,
    w_in_out,
    w_out_out,
):
    f32 = jnp.float32
    half = FF // 2
    block_out[...] = block_ref[...]
    tokens_grad[...] = dx_ref[...]
    even = lax.rem(lax.axis_index("dp"), 2) == 0
    own = in_ref[0].astype(f32) + in_ref[2].astype(f32)
    other = in_ref[1].astype(f32) + in_ref[3].astype(f32)
    halves = (jnp.where(even, own, other), jnp.where(even, other, own))
    count = own.shape[0]
    tiles = half // 128
    for tile in range(4 * tiles):
        piece, rest = divmod(tile, 2 * tiles)
        which, lane = divmod(rest, tiles)
        start = piece * half + lane * 128
        w_in_out[pl.ds(tile, count, 4 * tiles), :] = halves[which][:, start : start + 128]
    total = out_ref[0].astype(f32) + out_ref[1].astype(f32)
    count, width = total.shape
    for tile in range(width // 128):
        w_out_out[pl.ds(tile, count, width // 128), :] = total[:, tile * 128 : tile * 128 + 128]

    @pl.when(pl.program_id(0) == 0)
    def _():
        dense = dense_ref[0].astype(f32) + dense_ref[1].astype(f32)
        query_out[0] = dense[:, :width]
        output_out[0] = dense[:, width:]
        kv = (
            kv_ref[0].astype(f32)
            + kv_ref[1].astype(f32)
            + kv_ref[2].astype(f32)
            + kv_ref[3].astype(f32)
        )
        key_out[0] = kv[:, : kv.shape[1] // 2]
        value_out[0] = kv[:, kv.shape[1] // 2 :]
        aux = aux_ref[0] + aux_ref[1] + aux_ref[2] + aux_ref[3]
        rows = aux.shape[0]
        lines = jnp.transpose(
            jnp.concatenate([aux, jnp.zeros((128 - rows, 128), f32)], axis=0)
        )
        router_out[...] = (lines[0:8] + lines[8:16] + lines[16:24])[:, :rows]
        gain_a_out[...] = (lines[32:33] + lines[33:34] + lines[34:35])[:, :rows]
        gain_m_out[...] = (lines[35:36] + lines[36:37] + lines[37:38])[:, :rows]


def fast_body(
    tokens,
    cotangent,
    routes,
    gain_attn,
    w_query,
    key_weight,
    value_weight,
    w_output,
    gain_moe,
    w_router,
    w_in,
    w_out,
):
    f32, bf16 = jnp.float32, jnp.bfloat16
    total_rows, width = tokens.shape
    rows = w_query.shape[1]
    planes = lax.axis_size("dp")
    members = lax.axis_size("expert")
    seq_len = total_rows * members
    kv_width = key_weight.shape[2]
    quarter = w_in.shape[1]
    quarter_out = w_out.shape[1]
    half = FF // 2
    positions = lax.axis_index("expert") * total_rows + jnp.arange(total_rows, dtype=jnp.int32)
    cos_table, sin_table = rope_tables(positions, HEAD_DIM)
    rope = jnp.concatenate([cos_table, cos_table, -sin_table, sin_table], axis=1)
    in_vmem = pl.BlockSpec(memory_space=pltpu.VMEM)
    anywhere = pl.BlockSpec(memory_space=pl.ANY)
    pair_rows = 2 * seq_len
    shape = jax.ShapeDtypeStruct
    dma = pltpu.SemaphoreType.DMA
    heads = QUERY_HEADS
    (
        block_out,
        tokens_grad,
        grad_in,
        grad_out,
        grad_dense,
        grad_kv,
        grad_aux,
        _,
        _,
    ) = pl.pallas_call(
        layer_kernel,
        out_shape=(
            shape((total_rows, width), bf16),
            shape((total_rows, width), f32),
            shape((planes, quarter, 2 * half), bf16),
            shape((2, quarter_out, width), bf16),
            shape((2, rows, 2 * width), bf16),
            shape((planes, rows, 2 * kv_width), bf16),
            shape((planes, rows, 128), f32),
            shape((width, width), bf16),
            shape((width, width), bf16),
        ),
        in_specs=[in_vmem] * 11 + [anywhere] * 2,
        out_specs=(in_vmem,) * 2 + (anywhere,) * 7,
        scratch_shapes=[
            pltpu.VMEM((pair_rows, width), bf16),
            pltpu.VMEM((pair_rows, width + 128), bf16),
            pltpu.VMEM((width, 2 * kv_width + 128), bf16),
            pltpu.VMEM((38 * total_rows, width), bf16),
            pltpu.VMEM((32, total_rows, 128), bf16),
            pltpu.VMEM((width, 2 * half), bf16),
            pltpu.VMEM((half, width), bf16),
            pltpu.VMEM((pair_rows, half), bf16),
            pltpu.VMEM((pair_rows, 2 * half), bf16),
            pltpu.VMEM((2, quarter, 2 * half), bf16),
            pltpu.VMEM((seq_len, 2 * kv_width), bf16),
            pltpu.VMEM((KEY_VALUE_HEADS, HEAD_DIM, seq_len), bf16),
            pltpu.VMEM((KEY_VALUE_HEADS, HEAD_DIM, seq_len), bf16),
            pltpu.VMEM((heads * total_rows, HEAD_DIM), bf16),
            pltpu.VMEM((heads * total_rows, HEAD_DIM), bf16),
            pltpu.VMEM((heads, HEAD_DIM, total_rows), bf16),
            pltpu.VMEM((total_rows, width), f32),
            pltpu.VMEM((heads // 2, 8, 2 * total_rows), f32),
            pltpu.VMEM((3, planes, members, rows, total_rows), bf16),
            pltpu.VMEM((4, planes, rows, seq_len), bf16),
            pltpu.VMEM((seq_len, width + 128), bf16),
            pltpu.VMEM((seq_len, width), bf16),
            pltpu.VMEM((seq_len, 2 * kv_width), bf16),
            pltpu.VMEM((KEY_VALUE_HEADS, seq_len, 2 * HEAD_DIM), bf16),
            pltpu.VMEM((planes, rows, 128), f32),
            pltpu.VMEM((16, width), f32),
            dma((2, 3, 4)),
            dma((2, 3, 4, 4)),
            dma((2, 3, 4, 4)),
            dma((2, 8)),
            dma((2, 2, 2, 8)),
            dma((2, 2)),
            dma((2, 4, 8)),
            dma((2, 4, 2)),
            dma((2, 2)),
            dma((2, 3, 2)),
            dma((2, 2, 3, 7)),
            dma((2, 8)),
            dma((2, 4)),
            dma((2, 2)),
            dma((2, 8)),
            dma((2, 2, 8)),
            dma((2, 8)),
            dma((2, 2, 8)),
            dma((2, 3, 4)),
            dma((2, 4)),
            dma((8,)),
            pltpu.SemaphoreType.REGULAR,
        ],
        compiler_params=pltpu.CompilerParams(
            collective_id=0, has_side_effects=True, vmem_limit_bytes=63 * 2**20
        ),
    )(
        tokens,
        cotangent,
        routes[0].T,
        rope,
        key_weight[0],
        value_weight[0],
        w_router[0].T,
        gain_attn,
        gain_moe,
        w_query[0],
        w_output[0],
        w_in.reshape(quarter, 2 * FF),
        w_out.reshape(quarter_out, width),
    )
    steps = 2
    whole = lambda *dims: pl.BlockSpec(dims, lambda i: (0,) * len(dims))
    final = pl.pallas_call(
        final_kernel,
        grid=(steps,),
        out_shape=(
            shape((total_rows, width), bf16),
            shape((total_rows, width), f32),
            shape((1, rows), f32),
            shape((1, rows, width), f32),
            shape((1, rows, kv_width), f32),
            shape((1, rows, kv_width), f32),
            shape((1, rows, width), f32),
            shape((1, rows), f32),
            shape((EXPERT_LANES, rows), f32),
            shape((quarter * 2 * FF // 128, 128), f32),
            shape((quarter_out * width // 128, 128), f32),
        ),
        in_specs=[
            pl.BlockSpec((total_rows // steps, width), lambda i: (i, 0)),
            pl.BlockSpec((total_rows // steps, width), lambda i: (i, 0)),
            pl.BlockSpec((planes, quarter // steps, 2 * half), lambda i: (0, i, 0)),
            pl.BlockSpec((2, quarter_out // steps, width), lambda i: (0, i, 0)),
            whole(2, rows, 2 * width),
            whole(planes, rows, 2 * kv_width),
            whole(planes, rows, 128),
        ],
        out_specs=(
            pl.BlockSpec((total_rows // steps, width), lambda i: (i, 0)),
            pl.BlockSpec((total_rows // steps, width), lambda i: (i, 0)),
            whole(1, rows),
            whole(1, rows, width),
            whole(1, rows, kv_width),
            whole(1, rows, kv_width),
            whole(1, rows, width),
            whole(1, rows),
            whole(EXPERT_LANES, rows),
            pl.BlockSpec((quarter * 2 * FF // 128 // steps, 128), lambda i: (i, 0)),
            pl.BlockSpec((quarter_out * width // 128 // steps, 128), lambda i: (i, 0)),
        ),
        compiler_params=pltpu.CompilerParams(vmem_limit_bytes=63 * 2**20),
    )(block_out, tokens_grad, grad_in, grad_out, grad_dense, grad_kv, grad_aux)
    return final[:8] + (
        final[8].T[None],
        final[9].reshape(1, quarter, 1, 2 * FF),
        final[10].reshape(1, quarter_out, 1, width),
    )


def solution(mesh):
    in_specs = (
        P(("dp", "expert"), None),
        P(("dp", "expert"), None),
        P(None, ("dp", "expert"), None),
        P(None, ("dp", "expert")),
        P(None, ("dp", "expert"), None),
        P(None, ("dp", "expert"), None),
        P(None, ("dp", "expert"), None),
        P(None, ("dp", "expert"), None),
        P(None, ("dp", "expert")),
        P(None, ("dp", "expert"), None),
        P(None, "dp", "expert", None),
        P(None, "dp", "expert", None),
    )
    out_specs = (
        P(("dp", "expert"), None),
        P(("dp", "expert"), None),
        P(None, ("dp", "expert")),
        P(None, ("dp", "expert"), None),
        P(None, ("dp", "expert"), None),
        P(None, ("dp", "expert"), None),
        P(None, ("dp", "expert"), None),
        P(None, ("dp", "expert")),
        P(None, ("dp", "expert"), None),
        P(None, "dp", "expert", None),
        P(None, "dp", "expert", None),
    )
    body = fast_body if mesh.shape["dp"] == 4 and mesh.shape["expert"] == 8 else general_body
    return jax.shard_map(body, mesh=mesh, in_specs=in_specs, out_specs=out_specs, check_vma=False)
```
